32 devices in a mesh: dp: 2 (over y), view: 4 (over x, core), head: 4 (over z).
Axes of the slice: x: 2, y: 2, z: 4, core: 2. Of those that a mesh axis runs over, the one named last changes fastest.
Arguments:
- normed: bfloat16 [2, 4, 256, 3072], P('dp', 'view'), may hold values from -6 to 6
- queries: bfloat16 [2, 4, 256, 3072], P('dp', 'view', None, 'head'), may hold values from -180 to 180
- saved_keys: bfloat16 [2, 4, 256, 3072], P('dp', 'view', None, 'head'), may hold values from -4.5 to 4.5
- saved_values: bfloat16 [2, 4, 256, 3072], P('dp', 'view', None, 'head'), may hold values from -6 to 6
- output_grad: bfloat16 [2, 4, 256, 3072], P('dp', 'view', None, 'head'), may hold values from -200 to 200
- view_links: int32 [4, 2], P('view'), may hold values from -1 to 3, as said below
- query_weight: bfloat16 [3072, 3072], P(('dp', 'view'), 'head'), may hold values from -0.109375 to 0.109375
- key_weight: bfloat16 [3072, 3072], P(('dp', 'view'), 'head'), may hold values from -0.109375 to 0.109375
- value_weight: bfloat16 [3072, 3072], P(('dp', 'view'), 'head'), may hold values from -0.109375 to 0.109375
Outputs:
- input_grad: bfloat16 [2, 4, 256, 3072], P('dp', 'view', None, 'head')
- grad_query: float32 [3072, 3072], P(('dp', 'view'), 'head')
- grad_key: float32 [3072, 3072], P(('dp', 'view'), 'head')
- grad_value: float32 [3072, 3072], P(('dp', 'view'), 'head')
The draws below stay inside these ranges and needn't reach their ends.
Inputs may be any that keep to these rules, and one draw needn't show every extreme that they name: `view_links`: row v holds (v - 1) mod 4 or -1 and then (v + 1) mod 4 or -1; -1 marks a link that view v does not attend.
All inputs are finite; a program needn't handle non-finite values.
Results may differ from the reference program's by a relative error of at most 0.0057.
Values may be sent and summed in bfloat16 or wider, within the bound.
No kernel may reach another device: no remote copies, remote signals or barrier semaphores. Data moves between devices by JAX's collectives and lax.ppermute only.
A program may use at most 128 MiB of HBM per device.

```python
import jax
import jax.numpy as jnp
from jax import lax

D = 3072
HEADS = 24
HD = 128
S = 256
VIEWS = 4
PROMPTS = 2


def clipped_normal(key, salt):
    values = jax.random.normal(jax.random.fold_in(key, salt), (PROMPTS, VIEWS, S, HEADS * HD), jnp.float32)
    return jnp.clip(values, -4.5, 4.5)


def draw_saved_keys(key, part):
    key_rows = clipped_normal(key, 3)
    return key_rows.astype(jnp.bfloat16)


def draw_queries(key, part):
    query_rows = clipped_normal(key, 4)
    return query_rows.astype(jnp.bfloat16)


def draw_view_links(key, part):
    numbers = jnp.arange(VIEWS, dtype=jnp.int32)
    previous = (numbers - 1) % VIEWS
    following = (numbers + 1) % VIEWS
    kept_link = jax.random.randint(key, (VIEWS, 2), 0, 4) != 0
    kept_link = kept_link.at[0, 0].set(True).at[0, 1].set(True)
    kept_link = kept_link.at[1, 0].set(True).at[1, 1].set(False)
    return jnp.where(kept_link, jnp.stack([previous, following], axis=1), -1).astype(jnp.int32)


def spiked(entries, stream_key, source, target, blocks, factor):
    owner, partner = [(jnp.arange(entries.shape[dim]) // (entries.shape[dim] // blocks)).reshape([-1 if axis == dim else 1 for axis in range(entries.ndim)]) for dim in (source, target)]
    chosen = jax.random.permutation(stream_key, blocks)[partner]
    strong = (owner == chosen) | (owner == (partner + blocks // 2) % blocks)
    return jnp.where(strong, factor * entries, entries)


def block_levels(key, shape, pieces, least, high):
    def one(dim, blocks):
        heights = jax.random.uniform(jax.random.fold_in(jax.random.fold_in(key, 6), dim), (blocks,), jnp.float32, least / len(pieces), high / len(pieces))
        return jnp.repeat(jnp.exp(heights), shape[dim] // blocks).reshape((-1,) + (1,) * (len(shape) - dim - 1))

    loudness = one(*pieces[0])
    for cut in pieces[1:]:
        loudness = loudness * one(*cut)
    return loudness


def centred(stream_key, shape, width, most, shards=(), held_as=jnp.bfloat16):
    entries = width * jax.random.normal(stream_key, shape, jnp.float32)
    if shards:
        entries = entries * block_levels(stream_key, shape, shards, -0.22, 0.18)
    return jnp.clip(entries, -most, most).astype(held_as)


def heavy_noise(own_key, dims, spread, reach, pieces, heavy, held_as=jnp.bfloat16):
    array = spread * jax.random.normal(own_key, dims, jnp.float32)
    if pieces:
        array = array * block_levels(own_key, dims, pieces, -0.22, 0.18)
    return jnp.clip(spiked(array, jax.random.fold_in(own_key, 3), *heavy), -reach, reach).astype(held_as)


def setup_inputs(seed: int = 0) -> dict:
    key_of = jax.random.split(jax.random.key(seed), 10)
    normed = heavy_noise(key_of[0], (PROMPTS, VIEWS, S, D), 1.0, 6.0, ((0, 2), (1, 4)), (1, 3, 4, 2.0))
    queries = draw_queries(jax.random.fold_in(key_of[9], 71), 0)
    saved_keys = draw_saved_keys(jax.random.fold_in(key_of[9], 71), 0)
    saved_values = centred(key_of[3], (PROMPTS, VIEWS, S, HEADS * HD), 1.0, 6.0, ((0, 2), (1, 4), (3, 4)))
    output_grad = centred(key_of[4], (PROMPTS, VIEWS, S, HEADS * HD), 32.0, 200.0, ((0, 2), (1, 4), (3, 4)))
    view_links = draw_view_links(jax.random.fold_in(key_of[9], 71), 0)
    query_weight = centred(key_of[6], (D, HEADS * HD), D ** -0.5, 0.109375, ((0, 8), (1, 4)))
    key_weight = centred(key_of[7], (D, HEADS * HD), D ** -0.5, 0.109375, ((0, 8), (1, 4)))
    value_weight = centred(key_of[8], (D, HEADS * HD), D ** -0.5, 0.109375, ((0, 8), (1, 4)))
    return dict(normed=normed, queries=queries, saved_keys=saved_keys, saved_values=saved_values, output_grad=output_grad, view_links=view_links, query_weight=query_weight, key_weight=key_weight, value_weight=value_weight)


def softmax_rows(scores):
    largest = jnp.max(scores, axis=-1, keepdims=True)
    powers = jnp.exp(scores - largest)
    return powers / jnp.sum(powers, axis=-1, keepdims=True)


def reference(normed, queries, saved_keys, saved_values, output_grad, view_links, query_weight, key_weight, value_weight):
    scaling = HD ** -0.5
    col_count = HEADS * HD
    block_index = jnp.arange(3 * S) // S

    def one_view(view):
        previous = (view - 1) % VIEWS
        following = (view + 1) % VIEWS

        def three_blocks(source):
            return jnp.stack([source[:, previous], source[:, view], source[:, following]], axis=1)

        key_heads = three_blocks(saved_keys).astype(jnp.float32).reshape(PROMPTS, 3 * S, HEADS, HD)
        value_heads = three_blocks(saved_values).astype(jnp.float32).reshape(PROMPTS, 3 * S, HEADS, HD)
        query_heads = queries[:, view].astype(jnp.float32).reshape(PROMPTS, S, HEADS, HD)
        grad_heads = output_grad[:, view].astype(jnp.float32).reshape(PROMPTS, S, HEADS, HD)
        link_flags = view_links[view] >= 0
        usable = jnp.where(block_index == 0, link_flags[0], jnp.where(block_index == 2, link_flags[1], True))
        scores = jnp.einsum("bshd,bthd->bhst", query_heads, key_heads) * scaling
        scores = jnp.where(usable, scores, -1e30)
        attn_probs = softmax_rows(scores)
        probs_half = lax.optimization_barrier(attn_probs.astype(jnp.bfloat16)).astype(jnp.float32)
        prob_grad = jnp.einsum("bshd,bthd->bhst", grad_heads, value_heads)
        row_delta = jnp.sum(attn_probs * prob_grad, axis=-1, keepdims=True)
        score_grad = lax.optimization_barrier((scaling * attn_probs * (prob_grad - row_delta)).astype(jnp.bfloat16)).astype(jnp.float32)
        query_grad = jnp.einsum("bhst,bthd->bshd", score_grad, key_heads).reshape(PROMPTS, S, col_count)
        key_grad = jnp.einsum("bhst,bshd->bthd", score_grad, query_heads).reshape(PROMPTS, 3, S, col_count)
        value_grad = jnp.einsum("bhst,bshd->bthd", probs_half, grad_heads).reshape(PROMPTS, 3, S, col_count)
        return query_grad, key_grad, value_grad

    query_all, key_parts, value_parts = lax.map(one_view, jnp.arange(VIEWS, dtype=jnp.int32))

    def gather_parts(parts):
        return parts[:, :, 1] + jnp.roll(parts[:, :, 0], -1, axis=0) + jnp.roll(parts[:, :, 2], 1, axis=0)

    row_count = PROMPTS * VIEWS * S
    query_half = jnp.moveaxis(query_all, 0, 1).astype(jnp.bfloat16).reshape(row_count, col_count)
    key_half = jnp.moveaxis(gather_parts(key_parts), 0, 1).astype(jnp.bfloat16).reshape(row_count, col_count)
    value_half = jnp.moveaxis(gather_parts(value_parts), 0, 1).astype(jnp.bfloat16).reshape(row_count, col_count)

    running = jnp.dot(query_half, query_weight.T, preferred_element_type=jnp.float32)
    running = running + jnp.dot(key_half, key_weight.T, preferred_element_type=jnp.float32)
    running = running + jnp.dot(value_half, value_weight.T, preferred_element_type=jnp.float32)
    input_grad = running.astype(jnp.bfloat16).reshape(PROMPTS, VIEWS, S, D)

    flat_input = normed.reshape(row_count, D)
    mean_scale = 1.0 / (PROMPTS * VIEWS)
    grad_query = jnp.dot(flat_input.T, query_half, preferred_element_type=jnp.float32) * mean_scale
    grad_key = jnp.dot(flat_input.T, key_half, preferred_element_type=jnp.float32) * mean_scale
    grad_value = jnp.dot(flat_input.T, value_half, preferred_element_type=jnp.float32) * mean_scale
    return (input_grad, grad_query, grad_key, grad_value)
```

```python
import functools

import jax
import jax.numpy as jnp
from jax import lax
from jax.experimental import pallas as pl
from jax.experimental.pallas import tpu as pltpu
from jax.sharding import PartitionSpec as P

HD = 128
LOG2E = 1.4426950408889634
MIB = 1024 * 1024


def shifted(value, axis, steps):
    count = lax.axis_size(axis)
    pairs = [(source, (source + steps) % count) for source in range(count)]
    return lax.ppermute(value, axis, pairs)


def attend(query_rows, grad_rows, blocks, usable, scaling):
    batch_size, length, col_count = query_rows.shape
    heads_here = col_count // HD
    key_heads = blocks[..., :col_count].reshape(batch_size, 3 * length, heads_here, HD)
    value_heads = blocks[..., col_count:].reshape(batch_size, 3 * length, heads_here, HD)
    query_heads = query_rows.reshape(batch_size, length, heads_here, HD)
    grad_heads = grad_rows.reshape(batch_size, length, heads_here, HD)
    scores = (
        jnp.einsum("bshd,bthd->bhst", query_heads, key_heads, preferred_element_type=jnp.float32)
        * scaling
    )
    scores = jnp.where(usable, scores, -1e30)
    largest = jnp.max(scores, axis=-1, keepdims=True)
    powers = jnp.exp(scores - largest)
    attn_probs = powers / jnp.sum(powers, axis=-1, keepdims=True)
    probs_half = attn_probs.astype(jnp.bfloat16)
    prob_grad = jnp.einsum(
        "bshd,bthd->bhst", grad_heads, value_heads, preferred_element_type=jnp.float32
    )
    row_delta = jnp.sum(attn_probs * prob_grad, axis=-1, keepdims=True)
    score_grad = (scaling * attn_probs * (prob_grad - row_delta)).astype(jnp.bfloat16)
    query_grad = jnp.einsum(
        "bhst,bthd->bshd", score_grad, key_heads, preferred_element_type=jnp.float32
    )
    key_grad = jnp.einsum(
        "bhst,bshd->bthd", score_grad, query_heads, preferred_element_type=jnp.float32
    )
    value_grad = jnp.einsum(
        "bhst,bshd->bthd", probs_half, grad_heads, preferred_element_type=jnp.float32
    )
    query_grad = query_grad.reshape(batch_size, length, col_count)
    key_grad = key_grad.reshape(batch_size, 3, length, col_count)
    value_grad = value_grad.reshape(batch_size, 3, length, col_count)
    return (query_grad, jnp.concatenate([key_grad, value_grad], axis=-1))


def halo_body(
    normed,
    queries,
    saved_keys,
    saved_values,
    output_grad,
    view_links,
    query_weight,
    key_weight,
    value_weight,
):
    scaling = HD ** (-0.5)
    batch_size, view_count, length, col_count = queries.shape
    model_width = normed.shape[-1]
    pairs = jnp.concatenate([saved_keys, saved_values], axis=-1)
    from_lower = shifted(pairs, "view", 1)
    from_upper = shifted(pairs, "view", -1)
    extended = jnp.concatenate([from_lower, pairs, from_upper], axis=1)
    block_index = jnp.arange(3 * length) // length
    pair_grads = jnp.zeros(extended.shape, jnp.float32)
    link_flags = view_links[0] >= 0
    usable = jnp.where(
        block_index == 0, link_flags[0], jnp.where(block_index == 2, link_flags[1], True)
    )
    query_grad, block_grad = attend(queries[:, 0], output_grad[:, 0], extended, usable, scaling)
    query_grads = [query_grad]
    pair_grads = pair_grads.at[:, 0:3].add(block_grad)
    row_count = batch_size * view_count * length
    query_half = jnp.stack(query_grads, axis=1).astype(jnp.bfloat16).reshape(row_count, col_count)
    flat_input = normed.reshape(row_count, model_width)
    mean_scale = 1.0 / (lax.axis_size("dp") * batch_size * lax.axis_size("view") * view_count)
    from_lower_grads = shifted(pair_grads[:, -1:], "view", 1)
    from_upper_grads = shifted(pair_grads[:, :1], "view", -1)
    own_grads = pair_grads[:, 1 : view_count + 1]
    own_grads = own_grads.at[:, :1].add(from_lower_grads)
    own_grads = own_grads.at[:, -1:].add(from_upper_grads)
    key_half = own_grads[..., :col_count].astype(jnp.bfloat16).reshape(row_count, col_count)
    value_half = own_grads[..., col_count:].astype(jnp.bfloat16).reshape(row_count, col_count)
    all_grads = jnp.concatenate([query_half, key_half, value_half], axis=-1)
    grads_three = all_grads.reshape(row_count, 3, col_count)
    stacked = jnp.stack([query_weight, key_weight, value_weight])
    partial_input = jnp.einsum(
        "ric,ipc->rp",
        grads_three,
        lax.all_gather(stacked, ("dp", "view"), axis=1, tiled=True),
        preferred_element_type=jnp.float32,
    )
    summed_input = lax.psum_scatter(partial_input, "head", scatter_dimension=1, tiled=True)
    input_grad = summed_input.astype(jnp.bfloat16).reshape(
        batch_size, view_count, length, model_width // lax.axis_size("head")
    )
    product = lax.dot_general(
        flat_input, all_grads, (((0,), (0,)), ((), ())), preferred_element_type=jnp.float32
    )
    together = lax.psum_scatter(
        product * mean_scale, ("dp", "view"), scatter_dimension=0, tiled=True
    )
    grad_query = together[:, :col_count]
    grad_key = together[:, col_count : 2 * col_count]
    grad_value = together[:, 2 * col_count :]
    return (input_grad, grad_query, grad_key, grad_value)


MATE, XSAME, XCROSS = (0, 1), (0, 2), (0, 3)
YSAME, YCROSS, DIAGONAL = (1, 0), (1, 1), (1, 2)


def flipped(value, flip):
    prompts, views = lax.axis_size("dp"), lax.axis_size("view")
    pairs = [
        (y * views + v, (y ^ flip[0]) * views + (v ^ flip[1]))
        for y in range(prompts)
        for v in range(views)
    ]
    return lax.ppermute(value, ("dp", "view"), pairs)


def core_of():
    return lax.rem(lax.axis_index("view"), 2)


def lanes(start, size):
    return pl.ds(pl.multiple_of(start, HD), size)


def whole(space=pltpu.VMEM):
    return pl.BlockSpec(memory_space=space)


def pack_kernel(per_core, core_ref, q_ref, k_ref, v_ref, g_ref, *out_refs):
    core = core_ref[0]
    width = per_core * HD
    for part, half in enumerate((core, 1 - core)):
        for head in range(per_core):
            out = out_refs[part * per_core + head]
            for place, source in enumerate((q_ref, k_ref, v_ref, g_ref)):
                out[:, place * HD : (place + 1) * HD] = source[
                    :, lanes(half * width + head * HD, HD)
                ]


def pack(core, q, k, v, g):
    length, cols = q.shape
    per_core = cols // HD // 2
    out = jax.ShapeDtypeStruct((length, 4 * HD), q.dtype)
    packed = pl.pallas_call(
        functools.partial(pack_kernel, per_core),
        out_shape=[out] * (2 * per_core),
        in_specs=[whole(pltpu.SMEM)] + [whole()] * 4,
        out_specs=[whole()] * (2 * per_core),
        name="pack_heads",
    )(core, q, k, v, g)
    return packed[:per_core], packed[per_core:]


def dot_last(a, b):
    return lax.dot_general(a, b, (((1,), (1,)), ((), ())), preferred_element_type=jnp.float32)


def dot_first(a, b):
    return lax.dot_general(a, b, (((0,), (0,)), ((), ())), preferred_element_type=jnp.float32)


def attention_kernel(scaling, links_ref, view_ref, x0, x1, x2, x3, keep_ref, send_ref, kacc, vacc):
    xs = (x0, x1, x2, x3)
    view = view_ref[0]
    odd = lax.rem(view, 2)
    factor = scaling * LOG2E
    seen = set()
    for e in range(4):
        place = jnp.bitwise_xor(view, e)
        below = links_ref[place, odd]
        above = links_ref[place, 1 - odd]
        far_below = jnp.where(below >= 0, 0.0, 1e30).astype(jnp.float32)
        far_above = jnp.where(above >= 0, 0.0, 1e30).astype(jnp.float32)
        blocks = ((e + 3) % 4, e, (e + 1) % 4)
        q = xs[e][:, 0:HD]
        g = xs[e][:, 3 * HD : 4 * HD]
        scores = [dot_last(xs[f][:, HD : 2 * HD], q) for f in blocks]
        tops = [jnp.max(s, axis=0, keepdims=True) for s in scores]
        top = jnp.maximum(tops[1], jnp.maximum(tops[0] - far_below, tops[2] - far_above))
        offsets = (top + far_below, top, top + far_above)
        powers = [jnp.exp2((s - o) * factor) for s, o in zip(scores, offsets)]
        total = sum(jnp.sum(p, axis=0, keepdims=True) for p in powers)
        inverse = 1.0 / total
        prob_grads = [dot_last(xs[f][:, 2 * HD : 3 * HD], g) for f in blocks]
        delta = inverse * sum(
            jnp.sum(p * d, axis=0, keepdims=True) for p, d in zip(powers, prob_grads)
        )
        query_grad = None
        for f, p, d in zip(blocks, powers, prob_grads):
            probs = p * inverse
            score_grad = (probs * (d - delta)).astype(jnp.bfloat16)
            probs_half = probs.astype(jnp.bfloat16)
            part = dot_first(score_grad, xs[f][:, HD : 2 * HD])
            query_grad = part if query_grad is None else query_grad + part
            key_part = jnp.dot(score_grad, q, preferred_element_type=jnp.float32)
            value_part = jnp.dot(probs_half, g, preferred_element_type=jnp.float32)
            if f in seen:
                kacc[f] += key_part
                vacc[f] += value_part
            else:
                seen.add(f)
                kacc[f] = key_part
                vacc[f] = value_part
        out = (keep_ref, send_ref)[e % 2]
        out[e // 2, :, 0:HD] = (query_grad * scaling).astype(out.dtype)
    for f in range(4):
        out = (keep_ref, send_ref)[f % 2]
        out[f // 2, :, HD : 2 * HD] = (kacc[f] * scaling).astype(out.dtype)
        out[f // 2, :, 2 * HD : 3 * HD] = vacc[f].astype(out.dtype)


def attention(links, view, blocks):
    length = blocks[0].shape[0]
    out = jax.ShapeDtypeStruct((2, length, 3 * HD), jnp.bfloat16)
    return pl.pallas_call(
        functools.partial(attention_kernel, HD ** (-0.5)),
        out_shape=[out, out],
        in_specs=[whole(pltpu.SMEM)] * 2 + [whole()] * 4,
        out_specs=[whole()] * 2,
        scratch_shapes=[pltpu.VMEM((4, length, HD), jnp.float32)] * 2,
        compiler_params=pltpu.CompilerParams(vmem_limit_bytes=32 * MIB),
        cost_estimate=pl.CostEstimate(
            flops=4 * 5 * 2 * length * 3 * length * HD * 2,
            bytes_accessed=2 * length * 7 * HD * 4,
            transcendentals=12 * length * length,
        ),
        name="attention_gradients",
    )(links, view, *blocks)


def input_kernel(per_core, core_ref, *refs):
    own_refs = refs[:per_core]
    other_refs = refs[per_core : 2 * per_core]
    own_weights = refs[2 * per_core : 2 * per_core + 3]
    mate_weights = refs[2 * per_core + 3 : 2 * per_core + 6]
    out_ref = refs[2 * per_core + 6]
    core = core_ref[0]
    width = per_core * HD
    rows = own_weights[0].shape[0]
    blocks, length, depth = own_refs[0].shape
    for weights, place in ((own_weights, core), (mate_weights, 1 - core)):
        total = None
        for grads, half in ((own_refs, core), (other_refs, 1 - core)):
            left = jnp.concatenate([g[...].reshape(blocks * length, depth) for g in grads], axis=1)
            right = jnp.concatenate(
                [
                    w[:, lanes(half * width + head * HD, HD)]
                    for head in range(per_core)
                    for w in weights
                ],
                axis=1,
            )
            part = dot_last(left, right)
            total = part if total is None else total + part
        out_ref[:, lanes(place * rows, rows)] = total.astype(out_ref.dtype)


def input_product(core, own, other, own_weights, mate_weights):
    per_core = len(own)
    blocks, length, _ = own[0].shape
    rows, cols = own_weights[0].shape
    return pl.pallas_call(
        functools.partial(input_kernel, per_core),
        out_shape=jax.ShapeDtypeStruct((blocks * length, 2 * rows), jnp.bfloat16),
        in_specs=[whole(pltpu.SMEM)] + [whole()] * (2 * per_core + 6),
        out_specs=whole(),
        compiler_params=pltpu.CompilerParams(vmem_limit_bytes=32 * MIB),
        cost_estimate=pl.CostEstimate(
            flops=2 * blocks * length * 2 * rows * 3 * cols,
            bytes_accessed=2 * (blocks * length * (2 * rows + 3 * cols) + 6 * rows * cols),
            transcendentals=0,
        ),
        name="input_gradient",
    )(core, *own, *other, *own_weights, *mate_weights)


def token_blocks(per_core, grad_refs):
    for prompt in range(2):
        for e in range(4):
            yield prompt * 4 + e, [
                grad_refs[(prompt * per_core + head) * 2 + e % 2][e // 2]
                for head in range(per_core)
            ]


def weight_kernel(per_core, mean_scale, core_ref, *refs):
    normed_refs = refs[:8]
    grad_refs = refs[8 : 8 + 4 * per_core]
    out_ref = refs[8 + 4 * per_core]
    rows = out_ref.shape[0]
    start = (1 - core_ref[0]) * rows
    total = None
    for block, grads in token_blocks(per_core, grad_refs):
        part = dot_first(normed_refs[block][:, lanes(start, rows)], jnp.concatenate(grads, axis=1))
        total = part if total is None else total + part
    out_ref[...] = total * mean_scale


def weight_final_kernel(per_core, mean_scale, core_ref, *refs):
    normed_refs = refs[:8]
    grad_refs = refs[8 : 8 + 4 * per_core]
    mate_ref = refs[8 + 4 * per_core]
    out_refs = refs[9 + 4 * per_core : 12 + 4 * per_core]
    core = core_ref[0]
    rows = mate_ref.shape[0]
    width = per_core * HD
    total = None
    for block, grads in token_blocks(per_core, grad_refs):
        part = dot_first(
            normed_refs[block][:, lanes(core * rows, rows)], jnp.concatenate(grads, axis=1)
        )
        total = part if total is None else total + part
    total = total * mean_scale
    for head in range(per_core):
        for kind in range(3):
            column = (head * 3 + kind) * HD
            out_refs[kind][:, lanes(core * width + head * HD, HD)] = total[:, column : column + HD]
            out_refs[kind][:, lanes((1 - core) * width + head * HD, HD)] = mate_ref[
                :, column : column + HD
            ]


def weight_cost(rows, cols, tokens):
    return pl.CostEstimate(
        flops=2 * rows * cols * tokens,
        bytes_accessed=2 * tokens * (2 * rows + cols) + 4 * rows * cols,
        transcendentals=0,
    )


def gather_body(
    normed,
    queries,
    saved_keys,
    saved_values,
    output_grad,
    view_links,
    query_weight,
    key_weight,
    value_weight,
):
    length, cols = queries.shape[2:]
    model_width = normed.shape[-1]
    rows = query_weight.shape[0]
    per_core = cols // HD // 2
    prompts, views, groups = (lax.axis_size(name) for name in ("dp", "view", "head"))
    mean_scale = 1.0 / (prompts * views)
    view = lax.axis_index("view")
    core = core_of()
    view_word = view.reshape(1).astype(jnp.int32)
    core_word = core.reshape(1).astype(jnp.int32)
    links = lax.all_gather(view_links, "view", axis=0, tiled=True)

    own_packs, mate_packs = pack(
        core_word, *(a.reshape(length, cols) for a in (queries, saved_keys, saved_values, output_grad))
    )
    own_sets, other_sets = [], []
    for head in range(per_core):
        mine, theirs = own_packs[head], mate_packs[head]
        across = flipped(theirs, XCROSS)
        beside = flipped(mine, YSAME)
        own_sets.append((mine, flipped(theirs, MATE), flipped(mine, XSAME), across))
        other_sets.append(
            (beside, flipped(theirs, YCROSS), flipped(beside, XSAME), flipped(across, YSAME))
        )

    own_weights = (query_weight, key_weight, value_weight)
    mate_weights = tuple(flipped(w, MATE) for w in own_weights)

    pieces, grads = [], []
    for sets in (own_sets, other_sets):
        kept, received = [], []
        for blocks in sets:
            keep, send = attention(links, view_word, blocks)
            kept.append(keep)
            received.append(flipped(send, MATE))
            grads += [keep, send]
        partial = input_product(core_word, kept, received, own_weights, mate_weights)
        pieces.append(lax.psum_scatter(partial, "head", scatter_dimension=0, tiled=True))

    def place(y, v, z):
        return (y * views + v) * groups + z

    halves = []
    for part in range(2):
        landed = []
        for other, piece in enumerate(pieces):
            pairs = [
                (
                    place(y, v, z),
                    place(y ^ other, v ^ (2 * (z // 2)), y * (views // 2) + v // 2),
                )
                for y in range(prompts)
                for v in range(views)
                for z in range(groups)
                if z % 2 == part
            ]
            landed.append(lax.ppermute(piece, ("dp", "view", "head"), pairs))
        halves.append(landed[0] + landed[1])
    input_grad = jnp.concatenate(halves, axis=0).reshape(
        1, 1, length, model_width // groups
    )

    chip = lax.axis_index("dp") * (views // 2) + view // 2
    flat = normed.reshape(length, model_width)

    def columns(of_chip):
        return lax.dynamic_slice_in_dim(flat, of_chip * (2 * rows), 2 * rows, axis=1)

    near = [columns(chip)]
    for shift, flip in ((1, XSAME), (2, YSAME), (3, DIAGONAL)):
        near.append(flipped(columns(jnp.bitwise_xor(chip, shift)), flip))
    far = [flipped(n, MATE) for n in near]
    tokens = [near[0], far[0], near[1], far[1], near[2], far[2], near[3], far[3]]
    half_cols = 3 * per_core * HD
    cost = weight_cost(rows, half_cols, 8 * length)
    params = pltpu.CompilerParams(vmem_limit_bytes=40 * MIB)
    for_mate = pl.pallas_call(
        functools.partial(weight_kernel, per_core, mean_scale),
        out_shape=jax.ShapeDtypeStruct((rows, half_cols), jnp.float32),
        in_specs=[whole(pltpu.SMEM)] + [whole()] * (8 + len(grads)),
        out_specs=whole(),
        compiler_params=params,
        cost_estimate=cost,
        name="weight_gradient_mate",
    )(core_word, *tokens, *grads)
    from_mate = flipped(for_mate, MATE)
    weight_grads = pl.pallas_call(
        functools.partial(weight_final_kernel, per_core, mean_scale),
        out_shape=[jax.ShapeDtypeStruct((rows, cols), jnp.float32)] * 3,
        in_specs=[whole(pltpu.SMEM)] + [whole()] * (9 + len(grads)),
        out_specs=[whole()] * 3,
        compiler_params=params,
        cost_estimate=cost,
        name="weight_gradient_own",
    )(core_word, *tokens, *grads, from_mate)
    return (input_grad, *weight_grads)


def solution(mesh):
    prompts, views, groups = (mesh.shape[name] for name in ("dp", "view", "head"))
    loop_of_four = prompts * 2 == views and prompts * views == 2 * groups and views == groups

    def choose(*arrays):
        heads_here = arrays[1].shape[-1] // HD
        one_view_each = arrays[1].shape[:2] == (1, 1)
        if loop_of_four and one_view_each and heads_here % 2 == 0:
            return gather_body(*arrays)
        return halo_body(*arrays)

    placed = (
        P("dp", "view", None, None),
        P("dp", "view", None, "head"),
        P("dp", "view", None, "head"),
        P("dp", "view", None, "head"),
        P("dp", "view", None, "head"),
        P("view", None),
        P(("dp", "view"), "head"),
        P(("dp", "view"), "head"),
        P(("dp", "view"), "head"),
    )
    return jax.shard_map(
        choose,
        mesh=mesh,
        in_specs=placed,
        out_specs=(
            P("dp", "view", None, "head"),
            P(("dp", "view"), "head"),
            P(("dp", "view"), "head"),
            P(("dp", "view"), "head"),
        ),
        check_vma=False,
    )
```

```python
import functools

import jax
import jax.numpy as jnp
from jax import lax
from jax.experimental import pallas as pl
from jax.experimental.pallas import tpu as pltpu
from jax.sharding import PartitionSpec as P

HD = 128
LOG2E = 1.4426950408889634
MIB = 1024 * 1024


def shifted(value, axis, steps):
    count = lax.axis_size(axis)
    pairs = [(source, (source + steps) % count) for source in range(count)]
    return lax.ppermute(value, axis, pairs)


def attend(query_rows, grad_rows, blocks, usable, scaling):
    batch_size, length, col_count = query_rows.shape
    heads_here = col_count // HD
    key_heads = blocks[..., :col_count].reshape(batch_size, 3 * length, heads_here, HD)
    value_heads = blocks[..., col_count:].reshape(batch_size, 3 * length, heads_here, HD)
    query_heads = query_rows.reshape(batch_size, length, heads_here, HD)
    grad_heads = grad_rows.reshape(batch_size, length, heads_here, HD)
    scores = (
        jnp.einsum("bshd,bthd->bhst", query_heads, key_heads, preferred_element_type=jnp.float32)
        * scaling
    )
    scores = jnp.where(usable, scores, -1e30)
    largest = jnp.max(scores, axis=-1, keepdims=True)
    powers = jnp.exp(scores - largest)
    attn_probs = powers / jnp.sum(powers, axis=-1, keepdims=True)
    probs_half = attn_probs.astype(jnp.bfloat16)
    prob_grad = jnp.einsum(
        "bshd,bthd->bhst", grad_heads, value_heads, preferred_element_type=jnp.float32
    )
    row_delta = jnp.sum(attn_probs * prob_grad, axis=-1, keepdims=True)
    score_grad = (scaling * attn_probs * (prob_grad - row_delta)).astype(jnp.bfloat16)
    query_grad = jnp.einsum(
        "bhst,bthd->bshd", score_grad, key_heads, preferred_element_type=jnp.float32
    )
    key_grad = jnp.einsum(
        "bhst,bshd->bthd", score_grad, query_heads, preferred_element_type=jnp.float32
    )
    value_grad = jnp.einsum(
        "bhst,bshd->bthd", probs_half, grad_heads, preferred_element_type=jnp.float32
    )
    query_grad = query_grad.reshape(batch_size, length, col_count)
    key_grad = key_grad.reshape(batch_size, 3, length, col_count)
    value_grad = value_grad.reshape(batch_size, 3, length, col_count)
    return (query_grad, jnp.concatenate([key_grad, value_grad], axis=-1))


def halo_body(
    normed,
    queries,
    saved_keys,
    saved_values,
    output_grad,
    view_links,
    query_weight,
    key_weight,
    value_weight,
):
    scaling = HD ** (-0.5)
    batch_size, view_count, length, col_count = queries.shape
    model_width = normed.shape[-1]
    pairs = jnp.concatenate([saved_keys, saved_values], axis=-1)
    from_lower = shifted(pairs, "view", 1)
    from_upper = shifted(pairs, "view", -1)
    extended = jnp.concatenate([from_lower, pairs, from_upper], axis=1)
    block_index = jnp.arange(3 * length) // length
    pair_grads = jnp.zeros(extended.shape, jnp.float32)
    link_flags = view_links[0] >= 0
    usable = jnp.where(
        block_index == 0, link_flags[0], jnp.where(block_index == 2, link_flags[1], True)
    )
    query_grad, block_grad = attend(queries[:, 0], output_grad[:, 0], extended, usable, scaling)
    query_grads = [query_grad]
    pair_grads = pair_grads.at[:, 0:3].add(block_grad)
    row_count = batch_size * view_count * length
    query_half = jnp.stack(query_grads, axis=1).astype(jnp.bfloat16).reshape(row_count, col_count)
    flat_input = normed.reshape(row_count, model_width)
    mean_scale = 1.0 / (lax.axis_size("dp") * batch_size * lax.axis_size("view") * view_count)
    from_lower_grads = shifted(pair_grads[:, -1:], "view", 1)
    from_upper_grads = shifted(pair_grads[:, :1], "view", -1)
    own_grads = pair_grads[:, 1 : view_count + 1]
    own_grads = own_grads.at[:, :1].add(from_lower_grads)
    own_grads = own_grads.at[:, -1:].add(from_upper_grads)
    key_half = own_grads[..., :col_count].astype(jnp.bfloat16).reshape(row_count, col_count)
    value_half = own_grads[..., col_count:].astype(jnp.bfloat16).reshape(row_count, col_count)
    all_grads = jnp.concatenate([query_half, key_half, value_half], axis=-1)
    grads_three = all_grads.reshape(row_count, 3, col_count)
    stacked = jnp.stack([query_weight, key_weight, value_weight])
    partial_input = jnp.einsum(
        "ric,ipc->rp",
        grads_three,
        lax.all_gather(stacked, ("dp", "view"), axis=1, tiled=True),
        preferred_element_type=jnp.float32,
    )
    summed_input = lax.psum_scatter(partial_input, "head", scatter_dimension=1, tiled=True)
    input_grad = summed_input.astype(jnp.bfloat16).reshape(
        batch_size, view_count, length, model_width // lax.axis_size("head")
    )
    product = lax.dot_general(
        flat_input, all_grads, (((0,), (0,)), ((), ())), preferred_element_type=jnp.float32
    )
    together = lax.psum_scatter(
        product * mean_scale, ("dp", "view"), scatter_dimension=0, tiled=True
    )
    grad_query = together[:, :col_count]
    grad_key = together[:, col_count : 2 * col_count]
    grad_value = together[:, 2 * col_count :]
    return (input_grad, grad_query, grad_key, grad_value)


def moved(value, target):
    prompts, views = lax.axis_size("dp"), lax.axis_size("view")
    pairs = []
    for y in range(prompts):
        for v in range(views):
            goal = target(y, v)
            if goal is not None:
                pairs.append((y * views + v, goal[0] * views + goal[1]))
    return lax.ppermute(value, ("dp", "view"), pairs)


def straight(y, v):
    return (y, v ^ 2) if v % 2 == 0 else (y ^ 1, v)


def crossed(y, v):
    return (y ^ 1, v ^ 1) if v % 2 == 0 else (y, v ^ 3)


def inwards(y, v):
    return None if v % 2 == 0 else (y, v ^ 1)


def relay_x(y, v):
    return None if v % 2 == 0 else (y, v ^ 2)


def relay_y(y, v):
    return (y ^ 1, v ^ 1) if v % 2 == 0 else None


def corner_same(y, v):
    return None if v % 2 == 0 else (y ^ 1, v ^ 2)


def corner_cross(y, v):
    return (y ^ 1, v ^ 3) if v % 2 == 0 else None


def mate(y, v):
    return (y, v ^ 1)


def lanes(start, size):
    return pl.ds(pl.multiple_of(start, HD), size)


def whole(space=pltpu.VMEM):
    return pl.BlockSpec(memory_space=space)


def dot_last(a, b):
    return lax.dot_general(a, b, (((1,), (1,)), ((), ())), preferred_element_type=jnp.float32)


def dot_first(a, b):
    return lax.dot_general(a, b, (((0,), (0,)), ((), ())), preferred_element_type=jnp.float32)


def dot(a, b):
    return jnp.dot(a, b, preferred_element_type=jnp.float32)


def run_copies(copies):
    for copy in copies:
        copy.start()
    for copy in copies:
        copy.wait()


FLAG_ROWS = 16


def pack_first_kernel(width, links_ref, q_ref, k_ref, v_ref, g_ref, out_ref, flags, sems):
    length = q_ref.shape[0]
    half = FLAG_ROWS // 2
    row = lax.broadcasted_iota(jnp.int32, (FLAG_ROWS, width), 0)
    gaps = [jnp.where(links_ref[0, side] >= 0, 0.0, 1.0).astype(jnp.float32) for side in range(2)]
    flags[...] = jnp.where(row < half, gaps[0], gaps[1]).astype(jnp.bfloat16)
    run_copies(
        [
            pltpu.make_async_copy(
                source.at[:, 0:width],
                out_ref.at[kind * length : (kind + 1) * length],
                sems.at[kind],
            )
            for kind, source in enumerate((q_ref, k_ref, v_ref, g_ref))
        ]
        + [pltpu.make_async_copy(flags, out_ref.at[4 * length : 4 * length + FLAG_ROWS], sems.at[4])]
    )


def pack_next_kernel(first, width, q_ref, k_ref, v_ref, g_ref, out_ref, sems):
    length = q_ref.shape[0]
    run_copies(
        [
            pltpu.make_async_copy(
                source.at[:, first : first + width],
                out_ref.at[kind * length : (kind + 1) * length],
                sems.at[kind],
            )
            for kind, source in enumerate((q_ref, k_ref, v_ref, g_ref))
        ]
    )


def pack(first, width, links, arrays):
    length = arrays[0].shape[0]
    any_space = [whole(pl.ANY)] * 4
    if first == 0:
        return pl.pallas_call(
            functools.partial(pack_first_kernel, width),
            out_shape=jax.ShapeDtypeStruct((4 * length + FLAG_ROWS, width), jnp.bfloat16),
            in_specs=[whole(pltpu.SMEM)] + any_space,
            out_specs=whole(pl.ANY),
            scratch_shapes=[
                pltpu.VMEM((FLAG_ROWS, width), jnp.bfloat16),
                pltpu.SemaphoreType.DMA((5,)),
            ],
            name="pack_first",
        )(links, *arrays)
    return pl.pallas_call(
        functools.partial(pack_next_kernel, first, width),
        out_shape=jax.ShapeDtypeStruct((4 * length, width), jnp.bfloat16),
        in_specs=any_space,
        out_specs=whole(pl.ANY),
        scratch_shapes=[pltpu.SemaphoreType.DMA((4,))],
        name="pack_next",
    )(*arrays)


def attention_kernel(scaling, opening, place_ref, *refs):
    sources = refs[:6]
    if opening:
        out_ref, flags_out, x, flags, kacc, vacc, sems = refs[6:]
    else:
        flags_in, out_ref, x, flags, kacc, vacc, sems = refs[6:]
    core, odd = place_ref[0], place_ref[1]
    _, length, width = out_ref.shape
    width = width // 3
    own, mate_in, first, second, relayed_x, relayed_y = sources
    chosen = ((own, mate_in, first, second), (first, second, relayed_x, relayed_y))

    for which in range(2):

        @pl.when(core == which)
        def _():
            copies = [
                pltpu.make_async_copy(source.at[0 : 4 * length], x.at[e], sems.at[e])
                for e, source in enumerate(chosen[which])
            ]
            if opening:
                copies += [
                    pltpu.make_async_copy(
                        source.at[4 * length : 4 * length + FLAG_ROWS], flags.at[e], sems.at[4 + e]
                    )
                    for e, source in enumerate(chosen[which])
                ]
            run_copies(copies)

    if opening:
        flags_out[...] = flags[...]
    else:
        flags[...] = flags_in[...]
    factor = scaling * LOG2E
    kacc[...] = jnp.zeros_like(kacc)
    vacc[...] = jnp.zeros_like(vacc)

    def rows(e, kind, head):
        return x[e, kind * length : (kind + 1) * length, head * HD : (head + 1) * HD]

    def one_view(e, carry):
        blocks = (jnp.bitwise_and(e + 3, 3), e, jnp.bitwise_and(e + 1, 3))
        gaps = flags[e].astype(jnp.float32) * 1e30
        before, after = gaps[0:1, :length], gaps[FLAG_ROWS // 2 : FLAG_ROWS // 2 + 1, :length]
        far_below = jnp.where(odd == 0, before, after)
        far_above = jnp.where(odd == 0, after, before)
        for head in range(width // HD):
            q = rows(e, 0, head)
            g = rows(e, 3, head)
            scores = [dot_last(rows(f, 1, head), q) for f in blocks]
            tops = [jnp.max(s, axis=0, keepdims=True) for s in scores]
            top = jnp.maximum(tops[1], jnp.maximum(tops[0] - far_below, tops[2] - far_above))
            offsets = (top + far_below, top, top + far_above)
            powers = [jnp.exp2((s - o) * factor) for s, o in zip(scores, offsets)]
            inverse = 1.0 / sum(jnp.sum(p, axis=0, keepdims=True) for p in powers)
            prob_grads = [dot_last(rows(f, 2, head), g) for f in blocks]
            delta = inverse * sum(
                jnp.sum(p * d, axis=0, keepdims=True) for p, d in zip(powers, prob_grads)
            )
            query_grad = None
            here = slice(head * HD, (head + 1) * HD)
            for f, p, d in zip(blocks, powers, prob_grads):
                probs = p * inverse
                score_grad = (probs * scaling * (d - delta)).astype(jnp.bfloat16)
                part = dot_first(score_grad, rows(f, 1, head))
                query_grad = part if query_grad is None else query_grad + part
                kacc[f, :, here] += dot(score_grad, q)
                vacc[f, :, here] += dot(probs.astype(jnp.bfloat16), g)
            out_ref[e, :, here] = query_grad.astype(out_ref.dtype)
        return carry

    lax.fori_loop(0, 4, one_view, 0)
    out_ref[:, :, width : 2 * width] = kacc[...].astype(out_ref.dtype)
    out_ref[:, :, 2 * width : 3 * width] = vacc[...].astype(out_ref.dtype)


def attention(place, sources, flags, length):
    width = sources[0].shape[1]
    opening = flags is None
    out = jax.ShapeDtypeStruct((4, length, 3 * width), jnp.bfloat16)
    flag_shape = (4, FLAG_ROWS, width)
    flag_out = jax.ShapeDtypeStruct(flag_shape, jnp.bfloat16)
    result = pl.pallas_call(
        functools.partial(attention_kernel, HD ** (-0.5), opening),
        out_shape=[out, flag_out] if opening else [out],
        in_specs=[whole(pltpu.SMEM)] + [whole(pl.ANY)] * 6 + ([] if opening else [whole()]),
        out_specs=[whole()] * (2 if opening else 1),
        scratch_shapes=[
            pltpu.VMEM((4, 4 * length, width), jnp.bfloat16),
            pltpu.VMEM(flag_shape, jnp.bfloat16),
            pltpu.VMEM((4, length, width), jnp.float32),
            pltpu.VMEM((4, length, width), jnp.float32),
            pltpu.SemaphoreType.DMA((8,)),
        ],
        compiler_params=pltpu.CompilerParams(vmem_limit_bytes=32 * MIB),
        cost_estimate=pl.CostEstimate(
            flops=4 * 5 * 2 * length * 3 * length * width * 2,
            bytes_accessed=2 * length * 7 * width * 4,
            transcendentals=12 * length * length * (width // HD),
        ),
        name="attention_gradients",
    )(place, *sources, *([] if opening else [flags]))
    return result if opening else (result[0], flags)


def input_kernel(place_ref, *refs):
    chunks = (len(refs) - 10) // 1
    grads = refs[:chunks]
    own_weights = refs[chunks : chunks + 3]
    mate_weights = refs[chunks + 3 : chunks + 6]
    out_refs = refs[chunks + 6 :]
    core = place_ref[0]
    rows = own_weights[0].shape[0]
    width = grads[0].shape[2] // 3
    slot = pl.program_id(0)
    parts = []
    for weights in (own_weights, mate_weights):
        total = None
        for chunk, grad in enumerate(grads):
            left = grad[0]
            right = jnp.concatenate(
                [w[:, chunk * width : (chunk + 1) * width] for w in weights], axis=1
            )
            part = dot_last(left, right)
            total = part if total is None else total + part
        parts.append(total.astype(jnp.bfloat16))
    for s, out_ref in enumerate(out_refs):

        @pl.when(slot == s)
        def _():
            for part, at in zip(parts, (core, 1 - core)):
                out_ref[:, lanes(at * rows, rows)] = part


def input_product(place, grads, own_weights, mate_weights):
    blocks, length, triple = grads[0].shape
    rows, cols = own_weights[0].shape
    fixed = pl.BlockSpec((rows, cols), lambda s, place: (0, 0))
    out = jax.ShapeDtypeStruct((length, 2 * rows), jnp.bfloat16)
    return pl.pallas_call(
        input_kernel,
        grid_spec=pltpu.PrefetchScalarGridSpec(
            num_scalar_prefetch=1,
            grid=(blocks,),
            in_specs=[
                pl.BlockSpec(
                    (1, length, triple), lambda s, place: (jnp.bitwise_xor(s, place[2]), 0, 0)
                )
            ]
            * len(grads)
            + [fixed] * 6,
            out_specs=[pl.BlockSpec((length, 2 * rows), lambda s, place: (0, 0))] * blocks,
        ),
        out_shape=[out] * blocks,
        compiler_params=pltpu.CompilerParams(vmem_limit_bytes=32 * MIB),
        cost_estimate=pl.CostEstimate(
            flops=2 * blocks * length * 2 * rows * 3 * cols,
            bytes_accessed=2 * (blocks * length * (2 * rows + 3 * cols) + 6 * rows * cols),
            transcendentals=0,
        ),
        name="input_gradient",
    )(place, *grads, *own_weights, *mate_weights)


def columns_kernel(place_ref, normed_ref, *refs):
    out_refs, sems = refs[:-1], refs[-1]
    width = out_refs[0].shape[1]
    run_copies(
        [
            pltpu.make_async_copy(
                normed_ref.at[:, lanes(place_ref[3 + at] * width, width)], out, sems.at[at]
            )
            for at, out in enumerate(out_refs)
        ]
    )


def columns(place, flat, width):
    out = jax.ShapeDtypeStruct((flat.shape[0], width), flat.dtype)
    return pl.pallas_call(
        columns_kernel,
        out_shape=[out] * 4,
        in_specs=[whole(pltpu.SMEM), whole(pl.ANY)],
        out_specs=[whole(pl.ANY)] * 4,
        scratch_shapes=[pltpu.SemaphoreType.DMA((4,))],
        name="normed_columns",
    )(place, flat)


def weight_kernel(mine, mean_scale, place_ref, *refs):
    sources, grad_refs = refs[:6], refs[6:9]
    if mine:
        received, out_refs, scratch = refs[9:12], refs[12:15], refs[15:]
    else:
        received, out_refs, scratch = None, refs[9:12], refs[12:]
    tokens, turned, grads, sems = scratch
    core = place_ref[0]
    rows = out_refs[0].shape[0]
    chunks, blocks, length, triple = grads.shape
    width = triple // 3
    start = (core if mine else 1 - core) * rows
    own, mate_in, first, second, corner, corner_far = sources
    chosen = ((own, mate_in, first, second), (first, second, corner, corner_far))
    loads = [
        pltpu.make_async_copy(source, grads.at[chunk], sems.at[4 + chunk])
        for chunk, source in enumerate(grad_refs)
    ]
    for which in range(2):

        @pl.when(core == which)
        def _():
            for e, source in enumerate(chosen[which]):
                pltpu.make_async_copy(
                    source.at[:, lanes(start, rows)], tokens.at[e], sems.at[e]
                ).start()

    for load in loads:
        load.start()
    for e in range(blocks):
        pltpu.make_async_copy(first.at[:, lanes(start, rows)], tokens.at[e], sems.at[e]).wait()
        turned[:, e * length : (e + 1) * length] = tokens[e].T
    for chunk, load in enumerate(loads):
        load.wait()
        for kind, out in enumerate(out_refs):
            right = grads[chunk, :, :, kind * width : (kind + 1) * width]
            here = slice(chunk * width, (chunk + 1) * width)
            total = dot(turned[...], right.reshape(blocks * length, width))
            if mine:
                total = (total + received[kind][:, here]) * mean_scale
            out[:, here] = total


def weight_product(place, mine, mean_scale, tokens, grads, received=()):
    blocks, length, triple = grads[0].shape
    width = triple // 3
    rows = tokens[0].shape[1] // 2
    cols = width * len(grads)
    return pl.pallas_call(
        functools.partial(weight_kernel, mine, mean_scale),
        out_shape=[jax.ShapeDtypeStruct((rows, cols), jnp.float32)] * 3,
        in_specs=[whole(pltpu.SMEM)] + [whole(pl.ANY)] * 9 + [whole()] * len(received),
        out_specs=[whole()] * 3,
        scratch_shapes=[
            pltpu.VMEM((blocks, length, rows), jnp.bfloat16),
            pltpu.VMEM((rows, blocks * length), jnp.bfloat16),
            pltpu.VMEM((len(grads), blocks, length, triple), jnp.bfloat16),
            pltpu.SemaphoreType.DMA((4 + len(grads),)),
        ],
        compiler_params=pltpu.CompilerParams(vmem_limit_bytes=40 * MIB),
        cost_estimate=pl.CostEstimate(
            flops=2 * rows * 3 * cols * blocks * length,
            bytes_accessed=2 * blocks * length * (rows + 3 * cols) + 12 * rows * cols,
            transcendentals=0,
        ),
        name="weight_gradient_own" if mine else "weight_gradient_mate",
    )(place, *tokens, *grads, *received)


def after(values, *earlier):
    return lax.optimization_barrier((tuple(values), tuple(earlier)))[0]


def gather_body(
    normed,
    queries,
    saved_keys,
    saved_values,
    output_grad,
    view_links,
    query_weight,
    key_weight,
    value_weight,
):
    length, cols = queries.shape[2:]
    model_width = normed.shape[-1]
    rows = query_weight.shape[0]
    prompts, views, groups = (lax.axis_size(name) for name in ("dp", "view", "head"))
    mean_scale = 1.0 / (prompts * views)
    width = length
    view = lax.axis_index("view")
    core = lax.rem(view, 2)
    chip = lax.axis_index("dp") * (views // 2) + view // 2
    toward_x, toward_y = jnp.bitwise_xor(chip, 1), jnp.bitwise_xor(chip, 2)
    place = jnp.stack(
        [
            core,
            core,
            lax.axis_index("head"),
            jnp.where(core == 0, toward_x, toward_y),
            jnp.where(core == 0, toward_y, toward_x),
            chip,
            jnp.bitwise_xor(chip, 3),
        ]
    ).astype(jnp.int32)

    arrays = tuple(a.reshape(length, cols) for a in (queries, saved_keys, saved_values, output_grad))
    sets = []
    for first in range(0, cols, width):
        if sets:
            arrays = after(arrays, sets[-1][2])
        own = pack(first, width, view_links, arrays)
        straight_in = moved(own, straight)
        crossed_in = moved(own, crossed)
        mate_in = moved(own, inwards)
        sets.append(
            (own, mate_in, straight_in, crossed_in)
            + (moved(straight_in, relay_x), moved(straight_in, relay_y))
        )

    own_weights = after((query_weight, key_weight, value_weight), sets[0][1])
    mate_weights = tuple(moved(w, mate) for w in own_weights)

    grads, flags = [], None
    for sources in sets:
        grad, flags = attention(place, sources, flags, length)
        grads.append(grad)

    slots = input_product(place, grads, own_weights, mate_weights)
    total = slots[0].astype(jnp.float32)
    for s in range(1, groups):
        total += lax.ppermute(slots[s], "head", [(z, z ^ s) for z in range(groups)]).astype(
            jnp.float32
        )

    def spot(y, v, z):
        return (y * views + v) * groups + z

    pairs = [
        (spot(y, v, z), spot(y ^ (v % 2), v ^ z, y * (views // 2) + v // 2))
        for y in range(prompts)
        for v in range(views)
        for z in range(groups)
    ]
    input_grad = lax.ppermute(total.astype(jnp.bfloat16), ("dp", "view", "head"), pairs)

    (flat,) = after((normed.reshape(length, model_width),), sets[-1][3])
    to_straight, to_crossed, here, to_corner = columns(place, flat, 2 * rows)
    tokens = (
        here,
        moved(here, inwards),
        moved(to_straight, straight),
        moved(to_crossed, crossed),
        moved(to_corner, corner_same),
        moved(to_corner, corner_cross),
    )
    for_mate = weight_product(place, False, mean_scale, tokens, grads)
    from_mate = [moved(w, mate) for w in for_mate]
    weight_grads = weight_product(place, True, mean_scale, tokens, grads, from_mate)
    return (
        input_grad.reshape(1, 1, length, model_width // groups),
        *weight_grads,
    )


def solution(mesh):
    prompts, views, groups = (mesh.shape[name] for name in ("dp", "view", "head"))
    loop_of_four = prompts * 2 == views and prompts * views == 2 * groups and views == groups

    def choose(*arrays):
        batch, held, length, cols = arrays[1].shape
        if loop_of_four and batch == held == 1 and length % HD == 0 and cols == 3 * length:
            return gather_body(*arrays)
        return halo_body(*arrays)

    placed = (
        P("dp", "view", None, None),
        P("dp", "view", None, "head"),
        P("dp", "view", None, "head"),
        P("dp", "view", None, "head"),
        P("dp", "view", None, "head"),
        P("view", None),
        P(("dp", "view"), "head"),
        P(("dp", "view"), "head"),
        P(("dp", "view"), "head"),
    )
    return jax.shard_map(
        choose,
        mesh=mesh,
        in_specs=placed,
        out_specs=(
            P("dp", "view", None, "head"),
            P(("dp", "view"), "head"),
            P(("dp", "view"), "head"),
            P(("dp", "view"), "head"),
        ),
        check_vma=False,
    )
```

```python
import functools

import jax
import jax.numpy as jnp
from jax import lax
from jax.experimental import pallas as pl
from jax.experimental.pallas import tpu as pltpu
from jax.sharding import PartitionSpec as P

HD = 128
LOG2E = 1.4426950408889634
MIB = 1024 * 1024


def shifted(value, axis, steps):
    count = lax.axis_size(axis)
    pairs = [(source, (source + steps) % count) for source in range(count)]
    return lax.ppermute(value, axis, pairs)


def attend(query_rows, grad_rows, blocks, usable, scaling):
    batch_size, length, col_count = query_rows.shape
    heads_here = col_count // HD
    key_heads = blocks[..., :col_count].reshape(batch_size, 3 * length, heads_here, HD)
    value_heads = blocks[..., col_count:].reshape(batch_size, 3 * length, heads_here, HD)
    query_heads = query_rows.reshape(batch_size, length, heads_here, HD)
    grad_heads = grad_rows.reshape(batch_size, length, heads_here, HD)
    scores = (
        jnp.einsum("bshd,bthd->bhst", query_heads, key_heads, preferred_element_type=jnp.float32)
        * scaling
    )
    scores = jnp.where(usable, scores, -1e30)
    largest = jnp.max(scores, axis=-1, keepdims=True)
    powers = jnp.exp(scores - largest)
    attn_probs = powers / jnp.sum(powers, axis=-1, keepdims=True)
    probs_half = attn_probs.astype(jnp.bfloat16)
    prob_grad = jnp.einsum(
        "bshd,bthd->bhst", grad_heads, value_heads, preferred_element_type=jnp.float32
    )
    row_delta = jnp.sum(attn_probs * prob_grad, axis=-1, keepdims=True)
    score_grad = (scaling * attn_probs * (prob_grad - row_delta)).astype(jnp.bfloat16)
    query_grad = jnp.einsum(
        "bhst,bthd->bshd", score_grad, key_heads, preferred_element_type=jnp.float32
    )
    key_grad = jnp.einsum(
        "bhst,bshd->bthd", score_grad, query_heads, preferred_element_type=jnp.float32
    )
    value_grad = jnp.einsum(
        "bhst,bshd->bthd", probs_half, grad_heads, preferred_element_type=jnp.float32
    )
    query_grad = query_grad.reshape(batch_size, length, col_count)
    key_grad = key_grad.reshape(batch_size, 3, length, col_count)
    value_grad = value_grad.reshape(batch_size, 3, length, col_count)
    return (query_grad, jnp.concatenate([key_grad, value_grad], axis=-1))


def halo_body(
    normed,
    queries,
    saved_keys,
    saved_values,
    output_grad,
    view_links,
    query_weight,
    key_weight,
    value_weight,
):
    scaling = HD ** (-0.5)
    batch_size, view_count, length, col_count = queries.shape
    model_width = normed.shape[-1]
    pairs = jnp.concatenate([saved_keys, saved_values], axis=-1)
    from_lower = shifted(pairs, "view", 1)
    from_upper = shifted(pairs, "view", -1)
    extended = jnp.concatenate([from_lower, pairs, from_upper], axis=1)
    block_index = jnp.arange(3 * length) // length
    pair_grads = jnp.zeros(extended.shape, jnp.float32)
    link_flags = view_links[0] >= 0
    usable = jnp.where(
        block_index == 0, link_flags[0], jnp.where(block_index == 2, link_flags[1], True)
    )
    query_grad, block_grad = attend(queries[:, 0], output_grad[:, 0], extended, usable, scaling)
    query_grads = [query_grad]
    pair_grads = pair_grads.at[:, 0:3].add(block_grad)
    row_count = batch_size * view_count * length
    query_half = jnp.stack(query_grads, axis=1).astype(jnp.bfloat16).reshape(row_count, col_count)
    flat_input = normed.reshape(row_count, model_width)
    mean_scale = 1.0 / (lax.axis_size("dp") * batch_size * lax.axis_size("view") * view_count)
    from_lower_grads = shifted(pair_grads[:, -1:], "view", 1)
    from_upper_grads = shifted(pair_grads[:, :1], "view", -1)
    own_grads = pair_grads[:, 1 : view_count + 1]
    own_grads = own_grads.at[:, :1].add(from_lower_grads)
    own_grads = own_grads.at[:, -1:].add(from_upper_grads)
    key_half = own_grads[..., :col_count].astype(jnp.bfloat16).reshape(row_count, col_count)
    value_half = own_grads[..., col_count:].astype(jnp.bfloat16).reshape(row_count, col_count)
    all_grads = jnp.concatenate([query_half, key_half, value_half], axis=-1)
    grads_three = all_grads.reshape(row_count, 3, col_count)
    stacked = jnp.stack([query_weight, key_weight, value_weight])
    partial_input = jnp.einsum(
        "ric,ipc->rp",
        grads_three,
        lax.all_gather(stacked, ("dp", "view"), axis=1, tiled=True),
        preferred_element_type=jnp.float32,
    )
    summed_input = lax.psum_scatter(partial_input, "head", scatter_dimension=1, tiled=True)
    input_grad = summed_input.astype(jnp.bfloat16).reshape(
        batch_size, view_count, length, model_width // lax.axis_size("head")
    )
    product = lax.dot_general(
        flat_input, all_grads, (((0,), (0,)), ((), ())), preferred_element_type=jnp.float32
    )
    together = lax.psum_scatter(
        product * mean_scale, ("dp", "view"), scatter_dimension=0, tiled=True
    )
    grad_query = together[:, :col_count]
    grad_key = together[:, col_count : 2 * col_count]
    grad_value = together[:, 2 * col_count :]
    return (input_grad, grad_query, grad_key, grad_value)


def moved(value, target):
    prompts, views = lax.axis_size("dp"), lax.axis_size("view")
    pairs = []
    for y in range(prompts):
        for v in range(views):
            goal = target(y, v)
            if goal is not None:
                pairs.append((y * views + v, goal[0] * views + goal[1]))
    return lax.ppermute(value, ("dp", "view"), pairs)


def straight(y, v):
    return (y, v ^ 2) if v % 2 == 0 else (y ^ 1, v)


def crossed(y, v):
    return (y ^ 1, v ^ 1) if v % 2 == 0 else (y, v ^ 3)


def inwards(y, v):
    return None if v % 2 == 0 else (y, v ^ 1)


def relay_x(y, v):
    return None if v % 2 == 0 else (y, v ^ 2)


def relay_y(y, v):
    return (y ^ 1, v ^ 1) if v % 2 == 0 else None


def corner_same(y, v):
    return None if v % 2 == 0 else (y ^ 1, v ^ 2)


def corner_cross(y, v):
    return (y ^ 1, v ^ 3) if v % 2 == 0 else None


def mate(y, v):
    return (y, v ^ 1)


def lanes(start, size):
    return pl.ds(pl.multiple_of(start, HD), size)


def whole(space=pltpu.VMEM):
    return pl.BlockSpec(memory_space=space)


def dot_last(a, b):
    return lax.dot_general(a, b, (((1,), (1,)), ((), ())), preferred_element_type=jnp.float32)


def dot_first(a, b):
    return lax.dot_general(a, b, (((0,), (0,)), ((), ())), preferred_element_type=jnp.float32)


def dot(a, b):
    return jnp.dot(a, b, preferred_element_type=jnp.float32)


def run_copies(copies):
    for copy in copies:
        copy.start()
    for copy in copies:
        copy.wait()


FLAG_ROWS = 16


def pack_kernel(opening, links_ref, q_ref, k_ref, v_ref, g_ref, out_ref):
    length, width = q_ref.shape
    for kind, source in enumerate((q_ref, k_ref, v_ref, g_ref)):
        out_ref[kind * length : (kind + 1) * length] = source[...]
    if opening:
        row = lax.broadcasted_iota(jnp.int32, (FLAG_ROWS, width), 0)
        gaps = [
            jnp.where(links_ref[0, side] >= 0, 0.0, 1.0).astype(jnp.float32) for side in range(2)
        ]
        flags = jnp.where(row < FLAG_ROWS // 2, gaps[0], gaps[1])
        out_ref[4 * length : 4 * length + FLAG_ROWS] = flags.astype(out_ref.dtype)


def pack(chunk, width, links, arrays):
    length = arrays[0].shape[0]
    height = 4 * length + (FLAG_ROWS if chunk == 0 else 0)
    return pl.pallas_call(
        functools.partial(pack_kernel, chunk == 0),
        grid=(1,),
        out_shape=jax.ShapeDtypeStruct((height, width), jnp.bfloat16),
        in_specs=[whole(pltpu.SMEM)] + [pl.BlockSpec((length, width), lambda i: (0, chunk))] * 4,
        out_specs=pl.BlockSpec((height, width), lambda i: (0, 0)),
        name="pack_heads",
    )(links, *arrays)


def attention_kernel(scaling, role, place_ref, *refs):
    sources, openers, out_ref = refs[:4], refs[4:8], refs[8]
    x, flags, kacc, vacc, out, sems = refs[9:]
    odd = place_ref[1]
    _, length, triple = out.shape
    width = triple // 3
    factor = scaling * LOG2E

    def rows(e, kind, head):
        return x[e, kind * length : (kind + 1) * length, lanes(head * HD, HD)]

    def one_head(head, carry):
        seen = set()
        here = lanes(head * HD, HD)
        for e in range(4):
            blocks = ((e + 3) % 4, e, (e + 1) % 4)
            gaps = flags[e].astype(jnp.float32) * 1e30
            before, after = gaps[0:1, :length], gaps[FLAG_ROWS // 2 : FLAG_ROWS // 2 + 1, :length]
            far_below = jnp.where(odd == 0, before, after)
            far_above = jnp.where(odd == 0, after, before)
            q = rows(e, 0, head)
            g = rows(e, 3, head)
            scores = [dot_last(rows(f, 1, head), q) for f in blocks]
            tops = [jnp.max(s, axis=0, keepdims=True) for s in scores]
            top = jnp.maximum(tops[1], jnp.maximum(tops[0] - far_below, tops[2] - far_above))
            offsets = (top + far_below, top, top + far_above)
            powers = [jnp.exp2((s - o) * factor) for s, o in zip(scores, offsets)]
            inverse = 1.0 / sum(jnp.sum(p, axis=0, keepdims=True) for p in powers)
            prob_grads = [dot_last(rows(f, 2, head), g) for f in blocks]
            delta = inverse * sum(
                jnp.sum(p * d, axis=0, keepdims=True) for p, d in zip(powers, prob_grads)
            )
            query_grad = None
            for f, p, d in zip(blocks, powers, prob_grads):
                probs = p * inverse
                score_grad = (probs * scaling * (d - delta)).astype(jnp.bfloat16)
                part = dot_first(score_grad, rows(f, 1, head))
                query_grad = part if query_grad is None else query_grad + part
                key_part = dot(score_grad, q)
                value_part = dot(probs.astype(jnp.bfloat16), g)
                if f in seen:
                    kacc[f] += key_part
                    vacc[f] += value_part
                else:
                    seen.add(f)
                    kacc[f] = key_part
                    vacc[f] = value_part
            out[e, :, here] = query_grad.astype(out.dtype)
        for f in range(4):
            out[f, :, lanes(width + head * HD, HD)] = kacc[f].astype(out.dtype)
            out[f, :, lanes(2 * width + head * HD, HD)] = vacc[f].astype(out.dtype)
        return carry

    @pl.when(place_ref[0] == role)
    def _():
        run_copies(
            [
                pltpu.make_async_copy(source.at[0 : 4 * length], x.at[e], sems.at[e])
                for e, source in enumerate(sources)
            ]
            + [
                pltpu.make_async_copy(
                    opener.at[4 * length : 4 * length + FLAG_ROWS], flags.at[e], sems.at[4 + e]
                )
                for e, opener in enumerate(openers)
            ]
        )
        lax.fori_loop(0, width // HD, one_head, 0)
        run_copies([pltpu.make_async_copy(out, out_ref, sems.at[8])])


def attention(place, role, sources, openers, length):
    width = sources[0].shape[1]
    out = jax.ShapeDtypeStruct((4, length, 3 * width), jnp.bfloat16)
    return pl.pallas_call(
        functools.partial(attention_kernel, HD ** (-0.5), role),
        out_shape=out,
        in_specs=[whole(pltpu.SMEM)] + [whole(pltpu.HBM)] * 8,
        out_specs=whole(pltpu.HBM),
        scratch_shapes=[
            pltpu.VMEM((4, 4 * length, width), jnp.bfloat16),
            pltpu.VMEM((4, FLAG_ROWS, width), jnp.bfloat16),
            pltpu.VMEM((4, length, HD), jnp.float32),
            pltpu.VMEM((4, length, HD), jnp.float32),
            pltpu.VMEM(out.shape, out.dtype),
            pltpu.SemaphoreType.DMA((9,)),
        ],
        compiler_params=pltpu.CompilerParams(vmem_limit_bytes=32 * MIB),
        cost_estimate=pl.CostEstimate(
            flops=4 * 5 * 2 * length * 3 * length * width * 2,
            bytes_accessed=2 * length * 7 * width * 4,
            transcendentals=12 * length * length * (width // HD),
        ),
        name="attention_gradients",
    )(place, *sources, *openers)


def input_kernel(role, chunks, place_ref, *refs):
    grad_refs, weight_refs, out_refs = refs[:chunks], refs[chunks : chunks + 2], refs[chunks + 2 : -4]
    grads, weights, outs, sems = refs[-4:]
    core, plane = place_ref[0], place_ref[2]
    rows = weights.shape[2]
    width = grads.shape[3] // 3
    slots = len(out_refs)
    order = list(range(1, slots)) + [0]

    @pl.when(core == role)
    def _():
        fetches = [
            pltpu.make_async_copy(ref, weights.at[side], sems.at[side])
            for side, ref in enumerate(weight_refs)
        ]
        loads = {
            s: [
                pltpu.make_async_copy(
                    ref.at[jnp.bitwise_xor(plane, s)], grads.at[s, chunk], sems.at[2 + s * chunks + chunk]
                )
                for chunk, ref in enumerate(grad_refs)
            ]
            for s in order
        }
        stores = [
            pltpu.make_async_copy(outs.at[s], out, sems.at[2 + slots * chunks + s])
            for s, out in enumerate(out_refs)
        ]
        for copy in fetches + [load for s in order for load in loads[s]]:
            copy.start()
        for copy in fetches:
            copy.wait()
        for s in order:
            for load in loads[s]:
                load.wait()
            for side, at in ((0, core), (1, 1 - core)):
                total = None
                for chunk in range(chunks):
                    right = jnp.concatenate(
                        [
                            weights[side, kind, :, chunk * width : (chunk + 1) * width]
                            for kind in range(3)
                        ],
                        axis=1,
                    )
                    part = dot_last(grads[s, chunk], right)
                    total = part if total is None else total + part
                outs[s, :, lanes(at * rows, rows)] = total.astype(outs.dtype)
            stores[s].start()
        for store in stores:
            store.wait()


def input_product(place, role, grads, own_weights, mate_weights):
    blocks, length, triple = grads[0].shape
    _, rows, cols = own_weights.shape
    chunks = len(grads)
    out = jax.ShapeDtypeStruct((length, 2 * rows), jnp.bfloat16)
    return pl.pallas_call(
        functools.partial(input_kernel, role, chunks),
        out_shape=[out] * blocks,
        in_specs=[whole(pltpu.SMEM)] + [whole(pltpu.HBM)] * (chunks + 2),
        out_specs=[whole(pltpu.HBM)] * blocks,
        scratch_shapes=[
            pltpu.VMEM((blocks, chunks, length, triple), jnp.bfloat16),
            pltpu.VMEM((2, 3, rows, cols), jnp.bfloat16),
            pltpu.VMEM((blocks, length, 2 * rows), jnp.bfloat16),
            pltpu.SemaphoreType.DMA((2 + blocks * (chunks + 1),)),
        ],
        compiler_params=pltpu.CompilerParams(vmem_limit_bytes=32 * MIB),
        cost_estimate=pl.CostEstimate(
            flops=2 * blocks * length * 2 * rows * 3 * cols,
            bytes_accessed=2 * (blocks * length * (2 * rows + 3 * cols) + 6 * rows * cols),
            transcendentals=0,
        ),
        name="input_gradient",
    )(place, *grads, own_weights, mate_weights)


def weight_kernel(mine, mean_scale, chunks, place_ref, *refs):
    sources, refs = refs[:6], refs[6:]
    grad_refs, refs = (refs[:chunks], refs[chunks : 2 * chunks]), refs[2 * chunks :]
    received, refs = (refs[:3], refs[3:]) if mine else ((), refs)
    out_refs = refs[:3]
    tokens, turned, grads, sems = refs[3:]
    core = place_ref[0]
    rows = out_refs[0].shape[0]
    _, blocks, length, triple = grads.shape
    width = triple // 3
    start = (core if mine else 1 - core) * rows
    own, mate_in, first, second, corner, corner_far = sources
    chosen = ((own, mate_in, first, second), (first, second, corner, corner_far))

    def copies(which):
        return [
            pltpu.make_async_copy(source.at[:, lanes(start, rows)], tokens.at[e], sems.at[e])
            for e, source in enumerate(chosen[which])
        ] + [
            pltpu.make_async_copy(ref, grads.at[chunk], sems.at[blocks + chunk])
            for chunk, ref in enumerate(grad_refs[which])
        ]

    for which in range(2):

        @pl.when(core == which)
        def _():
            for copy in copies(which):
                copy.start()

    waits = copies(0)
    for e in range(blocks):
        waits[e].wait()
        turned[:, e * length : (e + 1) * length] = tokens[e].T
    for chunk in range(chunks):
        waits[blocks + chunk].wait()
        for kind, out in enumerate(out_refs):
            right = grads[chunk, :, :, kind * width : (kind + 1) * width]
            here = slice(chunk * width, (chunk + 1) * width)
            total = dot(turned[...], right.reshape(blocks * length, width))
            if mine:
                total = (total + received[kind][:, here]) * mean_scale
            out[:, here] = total


def weight_product(place, mine, mean_scale, tokens, grads, received=()):
    chunks = len(grads[0])
    blocks, length, triple = grads[0][0].shape
    rows = tokens[0].shape[1] // 2
    cols = triple // 3 * chunks
    return pl.pallas_call(
        functools.partial(weight_kernel, mine, mean_scale, chunks),
        out_shape=[jax.ShapeDtypeStruct((rows, cols), jnp.float32)] * 3,
        in_specs=[whole(pltpu.SMEM)]
        + [whole(pltpu.HBM)] * (6 + 2 * chunks)
        + [whole()] * len(received),
        out_specs=[whole()] * 3,
        scratch_shapes=[
            pltpu.VMEM((blocks, length, rows), jnp.bfloat16),
            pltpu.VMEM((rows, blocks * length), jnp.bfloat16),
            pltpu.VMEM((chunks, blocks, length, triple), jnp.bfloat16),
            pltpu.SemaphoreType.DMA((blocks + chunks,)),
        ],
        compiler_params=pltpu.CompilerParams(vmem_limit_bytes=40 * MIB),
        cost_estimate=pl.CostEstimate(
            flops=2 * rows * 3 * cols * blocks * length,
            bytes_accessed=2 * blocks * length * (rows + 3 * cols) + 12 * rows * cols,
            transcendentals=0,
        ),
        name="weight_gradient_own" if mine else "weight_gradient_mate",
    )(place, *tokens, *grads[0], *grads[1], *received)


def after(values, *earlier):
    return lax.optimization_barrier((tuple(values), tuple(earlier)))[0]


def gather_body(
    normed,
    queries,
    saved_keys,
    saved_values,
    output_grad,
    view_links,
    query_weight,
    key_weight,
    value_weight,
):
    length, cols = queries.shape[2:]
    model_width = normed.shape[-1]
    rows = query_weight.shape[0]
    prompts, views, groups = (lax.axis_size(name) for name in ("dp", "view", "head"))
    mean_scale = 1.0 / (prompts * views)
    width = cols // 2
    view = lax.axis_index("view")
    core = lax.rem(view, 2)
    chip = lax.axis_index("dp") * (views // 2) + view // 2
    place = jnp.stack([core, core, lax.axis_index("head")]).astype(jnp.int32)

    arrays = tuple(a.reshape(length, cols) for a in (queries, saved_keys, saved_values, output_grad))
    packs, straights, crosseds, mates = [], [], [], []
    for chunk in range(cols // width):
        packs.append(pack(chunk, width, view_links, after(arrays, *mates[-1:])))
        straights.append(moved(packs[-1], straight))
        crosseds.append(moved(packs[-1], crossed))
        (sent,) = after((packs[-1],), *mates[-1:])
        mates.append(moved(sent, inwards))
    relays_x, relays_y = [], []
    for chunk, sent in enumerate(straights):
        (sent,) = after((sent,), *straights[chunk + 1 :], *crosseds[chunk + 1 :], *relays_x[-1:])
        relays_x.append(moved(sent, relay_x))
        relays_y.append(moved(sent, relay_y))
    sets = (
        list(zip(packs, mates, straights, crosseds)),
        list(zip(straights, crosseds, relays_x, relays_y)),
    )

    own_weights = jnp.stack(after((query_weight, key_weight, value_weight), mates[0]))
    mate_weights = moved(own_weights, mate)

    def exchange(role, slots):
        total = slots[0].astype(jnp.float32)
        for s in range(1, groups):
            pairs = [
                ((y * views + v) * groups + z, (y * views + v) * groups + (z ^ s))
                for y in range(prompts)
                for v in range(role, views, 2)
                for z in range(groups)
            ]
            total += lax.ppermute(slots[s], ("dp", "view", "head"), pairs).astype(jnp.float32)
        return total.astype(jnp.bfloat16)

    def deliver(role, total):
        pairs = [
            (
                (y * views + v) * groups + z,
                ((y ^ role) * views + (v ^ z)) * groups + y * (views // 2) + v // 2,
            )
            for y in range(prompts)
            for v in range(role, views, 2)
            for z in range(groups)
        ]
        return lax.ppermute(total, ("dp", "view", "head"), pairs)

    def attend_all(role, turn):
        results = []
        for sources in sets[role]:
            results.append(attention(turn, role, sources, sets[role][0], length))
            (turn,) = after((turn,), results[-1])
        return results

    first = attend_all(0, place)
    first_slots = input_product(place, 0, first, own_weights, mate_weights)
    (turn,) = after((place,), *first_slots)
    second = attend_all(1, turn)
    gate = (relays_x[-1], relays_y[-1], second[0])
    first_total = exchange(0, after(first_slots, *gate))
    (turn,) = after((place,), first_total)
    second_slots = input_product(turn, 1, second, own_weights, mate_weights)
    second_total = exchange(1, second_slots)
    grads = (first, second)
    landed = (deliver(0, first_total), deliver(1, second_total))
    from_first = lax.axis_index("head") // (views // 2) == lax.axis_index("dp")
    input_grad = jnp.where(from_first, landed[0], landed[1])

    flat = normed.reshape(length, model_width)

    def columns(of_chip):
        return lax.dynamic_slice_in_dim(flat, of_chip * (2 * rows), 2 * rows, axis=1)

    toward_x, toward_y = jnp.bitwise_xor(chip, 1), jnp.bitwise_xor(chip, 2)
    here = columns(chip)
    to_straight = columns(jnp.where(core == 0, toward_x, toward_y))
    to_crossed = columns(jnp.where(core == 0, toward_y, toward_x))
    to_corner = columns(jnp.bitwise_xor(chip, 3))
    (sent,) = after((here,), mates[0])
    (to_corner,) = after((to_corner,), *gate)
    to_straight, to_crossed = after((to_straight, to_crossed), first_total)
    tokens = (
        here,
        moved(sent, inwards),
        moved(to_straight, straight),
        moved(to_crossed, crossed),
        moved(to_corner, corner_same),
        moved(to_corner, corner_cross),
    )
    for_mate = weight_product(place, False, mean_scale, tokens, grads)
    from_mate = [moved(w, mate) for w in for_mate]
    weight_grads = weight_product(place, True, mean_scale, tokens, grads, from_mate)
    return (
        input_grad.reshape(1, 1, length, model_width // groups),
        *weight_grads,
    )


def solution(mesh):
    prompts, views, groups = (mesh.shape[name] for name in ("dp", "view", "head"))
    loop_of_four = prompts * 2 == views and prompts * views == 2 * groups and views == groups

    def choose(*arrays):
        batch, held, length, cols = arrays[1].shape
        if loop_of_four and batch == held == 1 and cols % (2 * HD) == 0 and cols >= 2 * length:
            return gather_body(*arrays)
        return halo_body(*arrays)

    placed = (
        P("dp", "view", None, None),
        P("dp", "view", None, "head"),
        P("dp", "view", None, "head"),
        P("dp", "view", None, "head"),
        P("dp", "view", None, "head"),
        P("view", None),
        P(("dp", "view"), "head"),
        P(("dp", "view"), "head"),
        P(("dp", "view"), "head"),
    )
    return jax.shard_map(
        choose,
        mesh=mesh,
        in_specs=placed,
        out_specs=(
            P("dp", "view", None, "head"),
            P(("dp", "view"), "head"),
            P(("dp", "view"), "head"),
            P(("dp", "view"), "head"),
        ),
        check_vma=False,
    )
```

```python
import functools

import jax
import jax.numpy as jnp
from jax import lax
from jax.experimental import pallas as pl
from jax.experimental.pallas import tpu as pltpu
from jax.sharding import PartitionSpec as P

HD = 128
LOG2E = 1.4426950408889634
MIB = 1024 * 1024


def shifted(value, axis, steps):
    count = lax.axis_size(axis)
    pairs = [(source, (source + steps) % count) for source in range(count)]
    return lax.ppermute(value, axis, pairs)


def attend(query_rows, grad_rows, blocks, usable, scaling):
    batch_size, length, col_count = query_rows.shape
    heads_here = col_count // HD
    key_heads = blocks[..., :col_count].reshape(batch_size, 3 * length, heads_here, HD)
    value_heads = blocks[..., col_count:].reshape(batch_size, 3 * length, heads_here, HD)
    query_heads = query_rows.reshape(batch_size, length, heads_here, HD)
    grad_heads = grad_rows.reshape(batch_size, length, heads_here, HD)
    scores = (
        jnp.einsum("bshd,bthd->bhst", query_heads, key_heads, preferred_element_type=jnp.float32)
        * scaling
    )
    scores = jnp.where(usable, scores, -1e30)
    largest = jnp.max(scores, axis=-1, keepdims=True)
    powers = jnp.exp(scores - largest)
    attn_probs = powers / jnp.sum(powers, axis=-1, keepdims=True)
    probs_half = attn_probs.astype(jnp.bfloat16)
    prob_grad = jnp.einsum(
        "bshd,bthd->bhst", grad_heads, value_heads, preferred_element_type=jnp.float32
    )
    row_delta = jnp.sum(attn_probs * prob_grad, axis=-1, keepdims=True)
    score_grad = (scaling * attn_probs * (prob_grad - row_delta)).astype(jnp.bfloat16)
    query_grad = jnp.einsum(
        "bhst,bthd->bshd", score_grad, key_heads, preferred_element_type=jnp.float32
    )
    key_grad = jnp.einsum(
        "bhst,bshd->bthd", score_grad, query_heads, preferred_element_type=jnp.float32
    )
    value_grad = jnp.einsum(
        "bhst,bshd->bthd", probs_half, grad_heads, preferred_element_type=jnp.float32
    )
    query_grad = query_grad.reshape(batch_size, length, col_count)
    key_grad = key_grad.reshape(batch_size, 3, length, col_count)
    value_grad = value_grad.reshape(batch_size, 3, length, col_count)
    return (query_grad, jnp.concatenate([key_grad, value_grad], axis=-1))


def halo_body(
    normed,
    queries,
    saved_keys,
    saved_values,
    output_grad,
    view_links,
    query_weight,
    key_weight,
    value_weight,
):
    scaling = HD ** (-0.5)
    batch_size, view_count, length, col_count = queries.shape
    model_width = normed.shape[-1]
    pairs = jnp.concatenate([saved_keys, saved_values], axis=-1)
    from_lower = shifted(pairs, "view", 1)
    from_upper = shifted(pairs, "view", -1)
    extended = jnp.concatenate([from_lower, pairs, from_upper], axis=1)
    block_index = jnp.arange(3 * length) // length
    pair_grads = jnp.zeros(extended.shape, jnp.float32)
    link_flags = view_links[0] >= 0
    usable = jnp.where(
        block_index == 0, link_flags[0], jnp.where(block_index == 2, link_flags[1], True)
    )
    query_grad, block_grad = attend(queries[:, 0], output_grad[:, 0], extended, usable, scaling)
    query_grads = [query_grad]
    pair_grads = pair_grads.at[:, 0:3].add(block_grad)
    row_count = batch_size * view_count * length
    query_half = jnp.stack(query_grads, axis=1).astype(jnp.bfloat16).reshape(row_count, col_count)
    flat_input = normed.reshape(row_count, model_width)
    mean_scale = 1.0 / (lax.axis_size("dp") * batch_size * lax.axis_size("view") * view_count)
    from_lower_grads = shifted(pair_grads[:, -1:], "view", 1)
    from_upper_grads = shifted(pair_grads[:, :1], "view", -1)
    own_grads = pair_grads[:, 1 : view_count + 1]
    own_grads = own_grads.at[:, :1].add(from_lower_grads)
    own_grads = own_grads.at[:, -1:].add(from_upper_grads)
    key_half = own_grads[..., :col_count].astype(jnp.bfloat16).reshape(row_count, col_count)
    value_half = own_grads[..., col_count:].astype(jnp.bfloat16).reshape(row_count, col_count)
    all_grads = jnp.concatenate([query_half, key_half, value_half], axis=-1)
    grads_three = all_grads.reshape(row_count, 3, col_count)
    stacked = jnp.stack([query_weight, key_weight, value_weight])
    partial_input = jnp.einsum(
        "ric,ipc->rp",
        grads_three,
        lax.all_gather(stacked, ("dp", "view"), axis=1, tiled=True),
        preferred_element_type=jnp.float32,
    )
    summed_input = lax.psum_scatter(partial_input, "head", scatter_dimension=1, tiled=True)
    input_grad = summed_input.astype(jnp.bfloat16).reshape(
        batch_size, view_count, length, model_width // lax.axis_size("head")
    )
    product = lax.dot_general(
        flat_input, all_grads, (((0,), (0,)), ((), ())), preferred_element_type=jnp.float32
    )
    together = lax.psum_scatter(
        product * mean_scale, ("dp", "view"), scatter_dimension=0, tiled=True
    )
    grad_query = together[:, :col_count]
    grad_key = together[:, col_count : 2 * col_count]
    grad_value = together[:, 2 * col_count :]
    return (input_grad, grad_query, grad_key, grad_value)


def moved(value, target):
    prompts, views = lax.axis_size("dp"), lax.axis_size("view")
    pairs = []
    for y in range(prompts):
        for v in range(views):
            goal = target(y, v)
            if goal is not None:
                pairs.append((y * views + v, goal[0] * views + goal[1]))
    return lax.ppermute(value, ("dp", "view"), pairs)


def mate(y, v):
    return (y, v ^ 1)


def along_x(y, v):
    return (y, v ^ 2)


def across_x(y, v):
    return (y, v ^ 3)


def only(core, target):
    return lambda y, v: target(y, v) if v % 2 == core else None


def along_y(y, v):
    return (y ^ 1, v)


def across_y(y, v):
    return (y ^ 1, v ^ 1)


def straight(y, v):
    return along_x(y, v) if v % 2 == 0 else along_y(y, v)


def crossed(y, v):
    return across_y(y, v) if v % 2 == 0 else across_x(y, v)


def corner_same(y, v):
    return None if v % 2 == 0 else (y ^ 1, v ^ 2)


def corner_cross(y, v):
    return (y ^ 1, v ^ 3) if v % 2 == 0 else None


def lanes(start, size):
    return pl.ds(pl.multiple_of(start, HD), size)


def whole(space=pltpu.VMEM):
    return pl.BlockSpec(memory_space=space)


def dot_last(a, b):
    return lax.dot_general(a, b, (((1,), (1,)), ((), ())), preferred_element_type=jnp.float32)


def dot_first(a, b):
    return lax.dot_general(a, b, (((0,), (0,)), ((), ())), preferred_element_type=jnp.float32)


def dot(a, b):
    return jnp.dot(a, b, preferred_element_type=jnp.float32)


def after(values, *earlier):
    return lax.optimization_barrier((tuple(values), tuple(earlier)))[0]


CORE, PLANE, HERE, BESIDE = range(4)
FLAG_ROWS = 16


def pack_kernel(picks, place_ref, links_ref, q_ref, k_ref, v_ref, g_ref, *out_refs):
    length = q_ref.shape[0]
    core = place_ref[CORE]
    for pick, out_ref in zip(picks, out_refs):
        start = pick(core, place_ref[HERE], place_ref[BESIDE]) * HD
        for kind, source in enumerate((q_ref, k_ref, v_ref, g_ref)):
            out_ref[kind * length : (kind + 1) * length] = source[:, lanes(start, HD)]
        row = lax.broadcasted_iota(jnp.int32, (FLAG_ROWS, HD), 0)
        gaps = [
            jnp.where(links_ref[0, side] >= 0, 0.0, 1.0).astype(jnp.float32) for side in range(2)
        ]
        flags = jnp.where(row < FLAG_ROWS // 2, gaps[0], gaps[1])
        out_ref[4 * length : 4 * length + FLAG_ROWS] = flags.astype(out_ref.dtype)


def pack(picks, place, links, arrays):
    length = arrays[0].shape[0]
    out = jax.ShapeDtypeStruct((4 * length + FLAG_ROWS, HD), jnp.bfloat16)
    return pl.pallas_call(
        functools.partial(pack_kernel, picks),
        out_shape=[out] * len(picks),
        in_specs=[whole(pltpu.SMEM)] * 2 + [whole()] * 4,
        out_specs=[whole()] * len(picks),
        name="pack_heads",
    )(place, links, *arrays)


def attention_kernel(scaling, both, place_ref, x0, x1, x2, x3, out_ref, kacc, vacc):
    xs = (x0, x1, x2, x3)
    core = place_ref[CORE]
    length = out_ref.shape[1]
    factor = scaling * LOG2E

    def rows(e, kind):
        return xs[e][kind * length : (kind + 1) * length]

    def gap(e, side):
        at = 4 * length + side * (FLAG_ROWS // 2)
        flags = xs[e][at : at + FLAG_ROWS // 2].astype(jnp.float32)[0:1]
        return jnp.concatenate([flags] * (length // HD), axis=1) * 1e30

    def compute():
        seen = set()
        for e in range(4):
            blocks = ((e + 3) % 4, e, (e + 1) % 4)
            before, behind = gap(e, 0), gap(e, 1)
            far_below = jnp.where(core == 0, before, behind)
            far_above = jnp.where(core == 0, behind, before)
            q, g = rows(e, 0), rows(e, 3)
            scores = [dot_last(rows(f, 1), q) for f in blocks]
            tops = [jnp.max(s, axis=0, keepdims=True) for s in scores]
            top = jnp.maximum(tops[1], jnp.maximum(tops[0] - far_below, tops[2] - far_above))
            offsets = (top + far_below, top, top + far_above)
            powers = [jnp.exp2((s - o) * factor) for s, o in zip(scores, offsets)]
            inverse = 1.0 / sum(jnp.sum(p, axis=0, keepdims=True) for p in powers)
            prob_grads = [dot_last(rows(f, 2), g) for f in blocks]
            delta = inverse * sum(
                jnp.sum(p * d, axis=0, keepdims=True) for p, d in zip(powers, prob_grads)
            )
            query_grad = None
            for f, p, d in zip(blocks, powers, prob_grads):
                probs = p * inverse
                score_grad = (probs * scaling * (d - delta)).astype(jnp.bfloat16)
                part = dot_first(score_grad, rows(f, 1))
                query_grad = part if query_grad is None else query_grad + part
                key_part = dot(score_grad, q)
                value_part = dot(probs.astype(jnp.bfloat16), g)
                if f in seen:
                    kacc[f] += key_part
                    vacc[f] += value_part
                else:
                    seen.add(f)
                    kacc[f] = key_part
                    vacc[f] = value_part
            out_ref[e, :, 0:HD] = query_grad.astype(out_ref.dtype)
        out_ref[:, :, HD : 2 * HD] = kacc[...].astype(out_ref.dtype)
        out_ref[:, :, 2 * HD : 3 * HD] = vacc[...].astype(out_ref.dtype)

    if both:
        compute()
    else:
        pl.when(core == 0)(compute)


def attention(place, both, sources):
    length = (sources[0].shape[0] - FLAG_ROWS) // 4
    return pl.pallas_call(
        functools.partial(attention_kernel, HD ** (-0.5), both),
        out_shape=jax.ShapeDtypeStruct((4, length, 3 * HD), jnp.bfloat16),
        in_specs=[whole(pltpu.SMEM)] + [whole()] * 4,
        out_specs=whole(),
        scratch_shapes=[pltpu.VMEM((4, length, HD), jnp.float32)] * 2,
        compiler_params=pltpu.CompilerParams(vmem_limit_bytes=32 * MIB),
        cost_estimate=pl.CostEstimate(
            flops=4 * 5 * 2 * length * 3 * length * HD * 2,
            bytes_accessed=2 * length * 7 * HD * 4,
            transcendentals=12 * length * length,
        ),
        name="attention_gradients",
    )(place, *sources)


def turn_kernel(q_ref, k_ref, v_ref, out_ref):
    for head in range(q_ref.shape[1] // HD):
        for kind, source in enumerate((q_ref, k_ref, v_ref)):
            at = (head * 3 + kind) * HD
            out_ref[at : at + HD] = source[:, head * HD : (head + 1) * HD].T


def turned_weights(weights):
    rows, cols = weights[0].shape
    return pl.pallas_call(
        turn_kernel,
        out_shape=jax.ShapeDtypeStruct((3 * cols, rows), jnp.bfloat16),
        in_specs=[whole()] * 3,
        out_specs=whole(),
        compiler_params=pltpu.CompilerParams(vmem_limit_bytes=16 * MIB),
        name="turn_weights",
    )(*weights)


def input_kernel(role, marks, place_ref, *refs):
    count = len(marks)
    grad_refs, weight_refs, out_refs = refs[:count], refs[count : count + 2], refs[count + 2 : -4]
    grads, weights, outs, sems = refs[-4:]
    core, plane = place_ref[CORE], place_ref[PLANE]
    rows = weights.shape[2]
    triple = grad_refs[0].shape[2]
    slots = len(out_refs)
    order = list(range(1, slots)) + [0]

    @pl.when(core == role)
    def _():
        fetches = [
            pltpu.make_async_copy(ref, weights.at[side], sems.at[side])
            for side, ref in enumerate(weight_refs)
        ]
        loads = {
            s: [
                pltpu.make_async_copy(
                    ref.at[jnp.bitwise_xor(plane, s ^ flip)],
                    grads.at[s, :, lanes((place_ref[base] + step) * triple, triple)],
                    sems.at[2 + s * count + at],
                )
                for at, (ref, (base, step, flip)) in enumerate(zip(grad_refs, marks))
            ]
            for s in order
        }
        stores = [
            pltpu.make_async_copy(outs.at[s], out, sems.at[2 + slots * count + s])
            for s, out in enumerate(out_refs)
        ]
        for copy in loads[order[0]] + fetches + [load for s in order[1:] for load in loads[s]]:
            copy.start()
        for copy in fetches:
            copy.wait()
        for s in order:
            for load in loads[s]:
                load.wait()
            for side, at in ((0, core), (1, 1 - core)):
                total = dot(grads[s], weights[side])
                outs[s, :, lanes(at * rows, rows)] = total.astype(outs.dtype)
            stores[s].start()
        for store in stores:
            store.wait()


def input_product(place, role, grads, own_weights, mate_weights):
    blocks, length, triple = grads[0][0].shape
    depth, rows = own_weights.shape
    count = len(grads)
    out = jax.ShapeDtypeStruct((length, 2 * rows), jnp.bfloat16)
    return pl.pallas_call(
        functools.partial(input_kernel, role, [mark for _, mark in grads]),
        out_shape=[out] * blocks,
        in_specs=[whole(pltpu.SMEM)] + [whole(pltpu.HBM)] * (count + 2),
        out_specs=[whole(pltpu.HBM)] * blocks,
        scratch_shapes=[
            pltpu.VMEM((blocks, length, depth), jnp.bfloat16),
            pltpu.VMEM((2, depth, rows), jnp.bfloat16),
            pltpu.VMEM((blocks, length, 2 * rows), jnp.bfloat16),
            pltpu.SemaphoreType.DMA((2 + blocks * (count + 1),)),
        ],
        compiler_params=pltpu.CompilerParams(vmem_limit_bytes=32 * MIB),
        cost_estimate=pl.CostEstimate(
            flops=2 * blocks * length * 2 * rows * depth,
            bytes_accessed=2 * (blocks * length * (2 * rows + depth) + 2 * rows * depth),
            transcendentals=0,
        ),
        name="input_gradient",
    )(place, *[array for array, _ in grads], own_weights, mate_weights)


def weight_kernel(mine, mean_scale, marks, place_ref, *refs):
    sources, refs = refs[:6], refs[6:]
    count = len(marks[0])
    grad_refs, refs = (refs[:count], refs[count : 2 * count]), refs[2 * count :]
    received, refs = (refs[:3], refs[3:]) if mine else ((), refs)
    out_refs = refs[:3]
    if mine:
        tokens, turned, grads, sums, sems = refs[3:]
    else:
        tokens, turned, grads, sems = refs[3:]
    core = place_ref[CORE]
    rows = out_refs[0].shape[0]
    blocks, length, triple = grad_refs[0][0].shape
    start = (core if mine else 1 - core) * rows
    own, mate_in, first, second, corner, corner_far = sources
    chosen = ((own, mate_in, first, second), (first, second, corner, corner_far))

    def copies(which):
        return [
            pltpu.make_async_copy(source.at[:, lanes(start, rows)], tokens.at[e], sems.at[e])
            for e, source in enumerate(chosen[which])
        ] + [
            pltpu.make_async_copy(
                ref.at[e ^ flip],
                grads.at[
                    e * length : (e + 1) * length,
                    lanes((place_ref[base] + step) * triple, triple),
                ],
                sems.at[blocks + at * blocks + e],
            )
            for at, (ref, (base, step, flip)) in enumerate(zip(grad_refs[which], marks[which]))
            for e in range(blocks)
        ]

    for which in range(2):

        @pl.when(core == which)
        def _():
            for copy in copies(which):
                copy.start()

    arrivals = [
        pltpu.make_async_copy(ref, sums.at[kind], sems.at[blocks * (count + 1) + kind])
        for kind, ref in enumerate(received)
    ]
    for copy in arrivals:
        copy.start()
    waits = copies(0)
    for e in range(blocks):
        waits[e].wait()
        turned[:, e * length : (e + 1) * length] = tokens[e].T
    for copy in waits[blocks:] + arrivals:
        copy.wait()
    for pair in range(count // 2):
        total = dot(turned[...], grads[:, pair * 2 * triple : (pair + 1) * 2 * triple])
        for head in range(2):
            here = slice((2 * pair + head) * HD, (2 * pair + head + 1) * HD)
            for kind, out in enumerate(out_refs):
                at = (head * 3 + kind) * HD
                part = total[:, at : at + HD]
                if mine:
                    part = (part + sums[kind, :, here]) * mean_scale
                out[:, here] = part


def weight_product(place, mine, mean_scale, tokens, grads, received=()):
    blocks, length, triple = grads[0][0][0].shape
    count = len(grads[0])
    rows = tokens[0].shape[1] // 2
    cols = HD * count
    return pl.pallas_call(
        functools.partial(
            weight_kernel, mine, mean_scale, [[mark for _, mark in part] for part in grads]
        ),
        out_shape=[jax.ShapeDtypeStruct((rows, cols), jnp.float32)] * 3,
        in_specs=[whole(pltpu.SMEM)] + [whole(pltpu.HBM)] * (6 + 2 * count + len(received)),
        out_specs=[whole()] * 3,
        scratch_shapes=[
            pltpu.VMEM((blocks, length, rows), jnp.bfloat16),
            pltpu.VMEM((rows, blocks * length), jnp.bfloat16),
            pltpu.VMEM((blocks * length, count * triple), jnp.bfloat16),
        ]
        + ([pltpu.VMEM((3, rows, cols), jnp.float32)] if mine else [])
        + [pltpu.SemaphoreType.DMA((blocks * (count + 1) + 3,))],
        compiler_params=pltpu.CompilerParams(vmem_limit_bytes=40 * MIB),
        cost_estimate=pl.CostEstimate(
            flops=2 * rows * 3 * cols * blocks * length,
            bytes_accessed=2 * blocks * length * (rows + 3 * cols) + 12 * rows * cols,
            transcendentals=0,
        ),
        name="weight_gradient_own" if mine else "weight_gradient_mate",
    )(place, *tokens, *[array for part in grads for array, _ in part], *received)


def gather_body(
    normed,
    queries,
    saved_keys,
    saved_values,
    output_grad,
    view_links,
    query_weight,
    key_weight,
    value_weight,
):
    length, cols = queries.shape[2:]
    model_width = normed.shape[-1]
    rows = query_weight.shape[0]
    prompts, views, groups = (lax.axis_size(name) for name in ("dp", "view", "head"))
    mean_scale = 1.0 / (prompts * views)
    half = cols // HD // 2
    view = lax.axis_index("view")
    core = lax.rem(view, 2)
    side = view // 2
    chip = lax.axis_index("dp") * (views // 2) + side
    place = jnp.stack([core, lax.axis_index("head"), side * half, (1 - side) * half])
    place = place.astype(jnp.int32)
    arrays = tuple(a.reshape(length, cols) for a in (queries, saved_keys, saved_values, output_grad))

    ready = []
    for step in range(0, half, 2):
        if step + 1 < half:
            picks = (
                lambda c, here, beside, step=step: here + step + c,
                lambda c, here, beside, step=step: here + step + 1 - c,
                lambda c, here, beside, step=step: beside + step + c,
                lambda c, here, beside, step=step: beside + step + 1 - c,
            )
            own, to_mate, to_x, to_cross = pack(picks, place, view_links, arrays)
            sources = (own, moved(to_mate, mate), moved(to_x, along_x), moved(to_cross, across_x))
        else:
            picks = (
                lambda c, here, beside, step=step: here + step,
                lambda c, here, beside, step=step: beside + step,
            )
            own, to_x = pack(picks, place, view_links, arrays)
            sources = (
                own,
                moved(own, only(1, mate)),
                moved(to_x, only(0, along_x)),
                moved(to_x, only(1, across_x)),
            )
        arrays = after(arrays, own)
        ready.append((step, step + 1 < half, sources))

    own_weights = turned_weights(after((query_weight, key_weight, value_weight), arrays[0]))
    mate_weights = moved(own_weights, mate)

    first, second = [], []
    turn = place
    for step, both, sources in ready:
        made = attention(turn, both, sources)
        (turn,) = after((place,), made)
        if both:
            inward = moved(made, only(1, mate))
            ahead = moved(made, straight)
            aside = moved(made, crossed)
            first += [
                (made, (HERE, step, 0)),
                (inward, (HERE, step + 1, 1)),
                (ahead, (BESIDE, step, 2)),
                (aside, (BESIDE, step + 1, 3)),
            ]
            second += [
                (ahead, (HERE, step + 1, 0)),
                (aside, (HERE, step, 1)),
                (moved(ahead, only(1, along_x)), (BESIDE, step + 1, 2)),
                (moved(ahead, only(0, across_y)), (BESIDE, step, 3)),
            ]
        else:
            ahead = moved(made, only(0, along_x))
            aside = moved(made, only(0, across_y))
            first += [(made, (HERE, step, 0)), (ahead, (BESIDE, step, 2))]
            second += [
                (aside, (HERE, step, 1)),
                (moved(ahead, only(0, across_y)), (BESIDE, step, 3)),
            ]

    def exchange(role, slots):
        total = slots[0].astype(jnp.float32)
        for s in range(1, groups):
            pairs = [
                ((y * views + v) * groups + z, (y * views + v) * groups + (z ^ s))
                for y in range(prompts)
                for v in range(role, views, 2)
                for z in range(groups)
            ]
            total += lax.ppermute(slots[s], ("dp", "view", "head"), pairs).astype(jnp.float32)
        return total.astype(jnp.bfloat16)

    def deliver(role, total):
        pairs = [
            (
                (y * views + v) * groups + z,
                ((y ^ role) * views + (v ^ z)) * groups + y * (views // 2) + v // 2,
            )
            for y in range(prompts)
            for v in range(role, views, 2)
            for z in range(groups)
        ]
        return lax.ppermute(total, ("dp", "view", "head"), pairs)

    first_slots = input_product(turn, 0, first, own_weights, mate_weights)
    first_total = exchange(0, first_slots)
    (turn,) = after((place,), first_total)
    second_slots = input_product(turn, 1, second, own_weights, mate_weights)
    second_total = exchange(1, second_slots)
    landed = (deliver(0, first_total), deliver(1, second_total))
    from_first = lax.axis_index("head") // (views // 2) == lax.axis_index("dp")
    input_grad = jnp.where(from_first, landed[0], landed[1])

    flat = normed.reshape(length, model_width)

    def columns(of_chip):
        return lax.dynamic_slice_in_dim(flat, of_chip * (2 * rows), 2 * rows, axis=1)

    toward_x, toward_y = jnp.bitwise_xor(chip, 1), jnp.bitwise_xor(chip, 2)
    here = columns(chip)
    to_straight = columns(jnp.where(core == 0, toward_x, toward_y))
    to_crossed = columns(jnp.where(core == 0, toward_y, toward_x))
    to_corner = columns(jnp.bitwise_xor(chip, 3))
    (sent,) = after((here,), ready[0][2][1])
    to_straight, to_crossed, to_corner = after(
        (to_straight, to_crossed, to_corner), second[2][0], second[3][0]
    )
    tokens = (
        here,
        moved(sent, only(1, mate)),
        moved(to_straight, straight),
        moved(to_crossed, crossed),
        moved(to_corner, corner_same),
        moved(to_corner, corner_cross),
    )
    for_mate = weight_product(place, False, mean_scale, tokens, (first, second))
    from_mate = [moved(w, mate) for w in for_mate]
    weight_grads = weight_product(place, True, mean_scale, tokens, (first, second), from_mate)
    return (
        input_grad.reshape(1, 1, length, model_width // groups),
        *weight_grads,
    )


def solution(mesh):
    prompts, views, groups = (mesh.shape[name] for name in ("dp", "view", "head"))
    loop_of_four = prompts * 2 == views and prompts * views == 2 * groups and views == groups

    def choose(*arrays):
        batch, held, length, cols = arrays[1].shape
        if loop_of_four and batch == held == 1 and length % HD == 0 and cols % (2 * HD) == 0:
            return gather_body(*arrays)
        return halo_body(*arrays)

    placed = (
        P("dp", "view", None, None),
        P("dp", "view", None, "head"),
        P("dp", "view", None, "head"),
        P("dp", "view", None, "head"),
        P("dp", "view", None, "head"),
        P("view", None),
        P(("dp", "view"), "head"),
        P(("dp", "view"), "head"),
        P(("dp", "view"), "head"),
    )
    return jax.shard_map(
        choose,
        mesh=mesh,
        in_specs=placed,
        out_specs=(
            P("dp", "view", None, "head"),
            P(("dp", "view"), "head"),
            P(("dp", "view"), "head"),
            P(("dp", "view"), "head"),
        ),
        check_vma=False,
    )
```

```python
import functools

import jax
import jax.numpy as jnp
from jax import lax
from jax.experimental import pallas as pl
from jax.experimental.pallas import tpu as pltpu
from jax.sharding import PartitionSpec as P

HD = 128
LOG2E = 1.4426950408889634
MIB = 1024 * 1024


def shifted(value, axis, steps):
    count = lax.axis_size(axis)
    pairs = [(source, (source + steps) % count) for source in range(count)]
    return lax.ppermute(value, axis, pairs)


def attend(query_rows, grad_rows, blocks, usable, scaling):
    batch_size, length, col_count = query_rows.shape
    heads_here = col_count // HD
    key_heads = blocks[..., :col_count].reshape(batch_size, 3 * length, heads_here, HD)
    value_heads = blocks[..., col_count:].reshape(batch_size, 3 * length, heads_here, HD)
    query_heads = query_rows.reshape(batch_size, length, heads_here, HD)
    grad_heads = grad_rows.reshape(batch_size, length, heads_here, HD)
    scores = (
        jnp.einsum("bshd,bthd->bhst", query_heads, key_heads, preferred_element_type=jnp.float32)
        * scaling
    )
    scores = jnp.where(usable, scores, -1e30)
    largest = jnp.max(scores, axis=-1, keepdims=True)
    powers = jnp.exp(scores - largest)
    attn_probs = powers / jnp.sum(powers, axis=-1, keepdims=True)
    probs_half = attn_probs.astype(jnp.bfloat16)
    prob_grad = jnp.einsum(
        "bshd,bthd->bhst", grad_heads, value_heads, preferred_element_type=jnp.float32
    )
    row_delta = jnp.sum(attn_probs * prob_grad, axis=-1, keepdims=True)
    score_grad = (scaling * attn_probs * (prob_grad - row_delta)).astype(jnp.bfloat16)
    query_grad = jnp.einsum(
        "bhst,bthd->bshd", score_grad, key_heads, preferred_element_type=jnp.float32
    )
    key_grad = jnp.einsum(
        "bhst,bshd->bthd", score_grad, query_heads, preferred_element_type=jnp.float32
    )
    value_grad = jnp.einsum(
        "bhst,bshd->bthd", probs_half, grad_heads, preferred_element_type=jnp.float32
    )
    query_grad = query_grad.reshape(batch_size, length, col_count)
    key_grad = key_grad.reshape(batch_size, 3, length, col_count)
    value_grad = value_grad.reshape(batch_size, 3, length, col_count)
    return (query_grad, jnp.concatenate([key_grad, value_grad], axis=-1))


def halo_body(
    normed,
    queries,
    saved_keys,
    saved_values,
    output_grad,
    view_links,
    query_weight,
    key_weight,
    value_weight,
):
    scaling = HD ** (-0.5)
    batch_size, view_count, length, col_count = queries.shape
    model_width = normed.shape[-1]
    pairs = jnp.concatenate([saved_keys, saved_values], axis=-1)
    from_lower = shifted(pairs, "view", 1)
    from_upper = shifted(pairs, "view", -1)
    extended = jnp.concatenate([from_lower, pairs, from_upper], axis=1)
    block_index = jnp.arange(3 * length) // length
    pair_grads = jnp.zeros(extended.shape, jnp.float32)
    link_flags = view_links[0] >= 0
    usable = jnp.where(
        block_index == 0, link_flags[0], jnp.where(block_index == 2, link_flags[1], True)
    )
    query_grad, block_grad = attend(queries[:, 0], output_grad[:, 0], extended, usable, scaling)
    query_grads = [query_grad]
    pair_grads = pair_grads.at[:, 0:3].add(block_grad)
    row_count = batch_size * view_count * length
    query_half = jnp.stack(query_grads, axis=1).astype(jnp.bfloat16).reshape(row_count, col_count)
    flat_input = normed.reshape(row_count, model_width)
    mean_scale = 1.0 / (lax.axis_size("dp") * batch_size * lax.axis_size("view") * view_count)
    from_lower_grads = shifted(pair_grads[:, -1:], "view", 1)
    from_upper_grads = shifted(pair_grads[:, :1], "view", -1)
    own_grads = pair_grads[:, 1 : view_count + 1]
    own_grads = own_grads.at[:, :1].add(from_lower_grads)
    own_grads = own_grads.at[:, -1:].add(from_upper_grads)
    key_half = own_grads[..., :col_count].astype(jnp.bfloat16).reshape(row_count, col_count)
    value_half = own_grads[..., col_count:].astype(jnp.bfloat16).reshape(row_count, col_count)
    all_grads = jnp.concatenate([query_half, key_half, value_half], axis=-1)
    grads_three = all_grads.reshape(row_count, 3, col_count)
    stacked = jnp.stack([query_weight, key_weight, value_weight])
    partial_input = jnp.einsum(
        "ric,ipc->rp",
        grads_three,
        lax.all_gather(stacked, ("dp", "view"), axis=1, tiled=True),
        preferred_element_type=jnp.float32,
    )
    summed_input = lax.psum_scatter(partial_input, "head", scatter_dimension=1, tiled=True)
    input_grad = summed_input.astype(jnp.bfloat16).reshape(
        batch_size, view_count, length, model_width // lax.axis_size("head")
    )
    product = lax.dot_general(
        flat_input, all_grads, (((0,), (0,)), ((), ())), preferred_element_type=jnp.float32
    )
    together = lax.psum_scatter(
        product * mean_scale, ("dp", "view"), scatter_dimension=0, tiled=True
    )
    grad_query = together[:, :col_count]
    grad_key = together[:, col_count : 2 * col_count]
    grad_value = together[:, 2 * col_count :]
    return (input_grad, grad_query, grad_key, grad_value)


def moved(value, target):
    prompts, views = lax.axis_size("dp"), lax.axis_size("view")
    pairs = []
    for y in range(prompts):
        for v in range(views):
            goal = target(y, v)
            if goal is not None:
                pairs.append((y * views + v, goal[0] * views + goal[1]))
    return lax.ppermute(value, ("dp", "view"), pairs)


def mate(y, v):
    return (y, v ^ 1)


def along_x(y, v):
    return (y, v ^ 2)


def across_x(y, v):
    return (y, v ^ 3)


def only(core, target):
    return lambda y, v: target(y, v) if v % 2 == core else None


def along_y(y, v):
    return (y ^ 1, v)


def across_y(y, v):
    return (y ^ 1, v ^ 1)


def straight(y, v):
    return along_x(y, v) if v % 2 == 0 else along_y(y, v)


def crossed(y, v):
    return across_y(y, v) if v % 2 == 0 else across_x(y, v)


def corner_same(y, v):
    return None if v % 2 == 0 else (y ^ 1, v ^ 2)


def corner_cross(y, v):
    return (y ^ 1, v ^ 3) if v % 2 == 0 else None


def lanes(start, size):
    return pl.ds(pl.multiple_of(start, HD), size)


def whole(space=pltpu.VMEM):
    return pl.BlockSpec(memory_space=space)


def dot_last(a, b):
    return lax.dot_general(a, b, (((1,), (1,)), ((), ())), preferred_element_type=jnp.float32)


def dot_first(a, b):
    return lax.dot_general(a, b, (((0,), (0,)), ((), ())), preferred_element_type=jnp.float32)


def dot(a, b):
    return jnp.dot(a, b, preferred_element_type=jnp.float32)


def after(values, *earlier):
    return lax.optimization_barrier((tuple(values), tuple(earlier)))[0]


CORE, PLANE, HERE, BESIDE = range(4)
FLAG_ROWS = 16


def pack_kernel(count, place_ref, links_ref, *refs):
    del place_ref
    sources, out_refs = refs[: 4 * count], refs[4 * count :]
    length = sources[0].shape[0]
    row = lax.broadcasted_iota(jnp.int32, (FLAG_ROWS, HD), 0)
    gaps = [jnp.where(links_ref[0, side] >= 0, 0.0, 1.0).astype(jnp.float32) for side in range(2)]
    flags = jnp.where(row < FLAG_ROWS // 2, gaps[0], gaps[1])
    for at, out_ref in enumerate(out_refs):
        for kind in range(4):
            out_ref[kind * length : (kind + 1) * length] = sources[4 * at + kind][...]
        out_ref[4 * length : 4 * length + FLAG_ROWS] = flags.astype(out_ref.dtype)


def pack(picks, place, links, arrays):
    length = arrays[0].shape[0]
    height = 4 * length + FLAG_ROWS
    return pl.pallas_call(
        functools.partial(pack_kernel, len(picks)),
        grid_spec=pltpu.PrefetchScalarGridSpec(
            num_scalar_prefetch=1,
            grid=(1,),
            in_specs=[whole(pltpu.SMEM)]
            + [
                pl.BlockSpec(
                    (length, HD),
                    lambda i, place, pick=pick: (0, pick(place[CORE], place[HERE], place[BESIDE])),
                )
                for pick in picks
                for _ in arrays
            ],
            out_specs=[pl.BlockSpec((height, HD), lambda i, place: (0, 0))] * len(picks),
        ),
        out_shape=[jax.ShapeDtypeStruct((height, HD), jnp.bfloat16)] * len(picks),
        name="pack_heads",
    )(place, links, *(arrays * len(picks)))


def attention_kernel(scaling, both, place_ref, x0, x1, x2, x3, out_ref, kacc, vacc):
    xs = (x0, x1, x2, x3)
    core = place_ref[CORE]
    length = out_ref.shape[1]
    factor = scaling * LOG2E

    def rows(e, kind):
        return xs[e][kind * length : (kind + 1) * length]

    def gap(e, side):
        at = 4 * length + side * (FLAG_ROWS // 2)
        flags = xs[e][at : at + FLAG_ROWS // 2].astype(jnp.float32)[0:1]
        return jnp.concatenate([flags] * (length // HD), axis=1) * 1e30

    def compute():
        seen = set()
        for e in range(4):
            blocks = ((e + 3) % 4, e, (e + 1) % 4)
            before, behind = gap(e, 0), gap(e, 1)
            far_below = jnp.where(core == 0, before, behind)
            far_above = jnp.where(core == 0, behind, before)
            q, g = rows(e, 0), rows(e, 3)
            scores = [dot_last(rows(f, 1), q) for f in blocks]
            tops = [jnp.max(s, axis=0, keepdims=True) for s in scores]
            top = jnp.maximum(tops[1], jnp.maximum(tops[0] - far_below, tops[2] - far_above))
            offsets = (top + far_below, top, top + far_above)
            powers = [jnp.exp2((s - o) * factor) for s, o in zip(scores, offsets)]
            inverse = 1.0 / sum(jnp.sum(p, axis=0, keepdims=True) for p in powers)
            prob_grads = [dot_last(rows(f, 2), g) for f in blocks]
            delta = inverse * sum(
                jnp.sum(p * d, axis=0, keepdims=True) for p, d in zip(powers, prob_grads)
            )
            query_grad = None
            for f, p, d in zip(blocks, powers, prob_grads):
                probs = p * inverse
                score_grad = (probs * scaling * (d - delta)).astype(jnp.bfloat16)
                part = dot_first(score_grad, rows(f, 1))
                query_grad = part if query_grad is None else query_grad + part
                key_part = dot(score_grad, q)
                value_part = dot(probs.astype(jnp.bfloat16), g)
                if f in seen:
                    kacc[f] += key_part
                    vacc[f] += value_part
                else:
                    seen.add(f)
                    kacc[f] = key_part
                    vacc[f] = value_part
            out_ref[e, :, 0:HD] = query_grad.astype(out_ref.dtype)
        out_ref[:, :, HD : 2 * HD] = kacc[...].astype(out_ref.dtype)
        out_ref[:, :, 2 * HD : 3 * HD] = vacc[...].astype(out_ref.dtype)

    if both:
        compute()
    else:
        pl.when(core == 0)(compute)


def attention(place, both, sources):
    length = (sources[0].shape[0] - FLAG_ROWS) // 4
    return pl.pallas_call(
        functools.partial(attention_kernel, HD ** (-0.5), both),
        out_shape=jax.ShapeDtypeStruct((4, length, 3 * HD), jnp.bfloat16),
        in_specs=[whole(pltpu.SMEM)] + [whole()] * 4,
        out_specs=whole(),
        scratch_shapes=[pltpu.VMEM((4, length, HD), jnp.float32)] * 2,
        compiler_params=pltpu.CompilerParams(vmem_limit_bytes=12 * MIB),
        cost_estimate=pl.CostEstimate(
            flops=4 * 5 * 2 * length * 3 * length * HD * 2,
            bytes_accessed=2 * length * 7 * HD * 4,
            transcendentals=12 * length * length,
        ),
        name="attention_gradients",
    )(place, *sources)


def turn_kernel(q_ref, k_ref, v_ref, out_ref):
    for head in range(q_ref.shape[1] // HD):
        for kind, source in enumerate((q_ref, k_ref, v_ref)):
            at = (head * 3 + kind) * HD
            out_ref[at : at + HD] = source[:, head * HD : (head + 1) * HD].T


def turned_weights(weights):
    rows, cols = weights[0].shape
    return pl.pallas_call(
        turn_kernel,
        out_shape=jax.ShapeDtypeStruct((3 * cols, rows), jnp.bfloat16),
        in_specs=[whole()] * 3,
        out_specs=whole(),
        compiler_params=pltpu.CompilerParams(vmem_limit_bytes=8 * MIB),
        name="turn_weights",
    )(*weights)


def input_kernel(role, marks, place_ref, *refs):
    count = len(marks)
    grad_refs, weight_refs, out_refs = refs[:count], refs[count : count + 2], refs[count + 2 : -3]
    grads, outs, sems = refs[-3:]
    core, plane = place_ref[CORE], place_ref[PLANE]
    rows = weight_refs[0].shape[1]
    triple = grad_refs[0].shape[2]
    slots = len(out_refs)
    order = list(range(1, slots)) + [0]

    @pl.when(core == role)
    def _():
        loads = {
            s: [
                pltpu.make_async_copy(
                    ref.at[jnp.bitwise_xor(plane, s ^ flip)],
                    grads.at[s, place_ref[base] + step],
                    sems.at[s * count + at],
                )
                for at, (ref, (base, step, flip)) in enumerate(zip(grad_refs, marks))
            ]
            for s in order
        }
        stores = [
            pltpu.make_async_copy(outs.at[s], out, sems.at[slots * count + s])
            for s, out in enumerate(out_refs)
        ]
        for s in order:
            for load in loads[s]:
                load.start()
        for s in order:
            for load in loads[s]:
                load.wait()
            left = jnp.concatenate([grads[s, head] for head in range(count)], axis=1)
            for weights, at in zip(weight_refs, (core, 1 - core)):
                outs[s, :, lanes(at * rows, rows)] = dot(left, weights[...]).astype(outs.dtype)
            stores[s].start()
        for store in stores:
            store.wait()


def input_product(place, role, grads, own_weights, mate_weights):
    blocks, length, triple = grads[0][0].shape
    depth, rows = own_weights.shape
    count = len(grads)
    out = jax.ShapeDtypeStruct((length, 2 * rows), jnp.bfloat16)
    return pl.pallas_call(
        functools.partial(input_kernel, role, [mark for _, mark in grads]),
        out_shape=[out] * blocks,
        in_specs=[whole(pltpu.SMEM)] + [whole(pltpu.HBM)] * count + [whole()] * 2,
        out_specs=[whole(pltpu.HBM)] * blocks,
        scratch_shapes=[
            pltpu.VMEM((blocks, count, length, triple), jnp.bfloat16),
            pltpu.VMEM((blocks, length, 2 * rows), jnp.bfloat16),
            pltpu.SemaphoreType.DMA((blocks * (count + 1),)),
        ],
        compiler_params=pltpu.CompilerParams(vmem_limit_bytes=12 * MIB),
        cost_estimate=pl.CostEstimate(
            flops=2 * blocks * length * 2 * rows * depth,
            bytes_accessed=2 * (blocks * length * (2 * rows + depth) + 2 * rows * depth),
            transcendentals=0,
        ),
        name="input_gradient",
    )(place, *[array for array, _ in grads], own_weights, mate_weights)


def weight_kernel(mine, mean_scale, marks, place_ref, *refs):
    sources, refs = refs[:6], refs[6:]
    count = len(marks[0])
    grad_refs, refs = (refs[:count], refs[count : 2 * count]), refs[2 * count :]
    received, refs = (refs[:3], refs[3:]) if mine else ((), refs)
    out_refs = refs[:3]
    if mine:
        tokens, turned, grads, sums, sems = refs[3:]
    else:
        tokens, turned, grads, sems = refs[3:]
    core = place_ref[CORE]
    rows = out_refs[0].shape[0]
    blocks, length, triple = grad_refs[0][0].shape
    part = core if mine else 1 - core
    own, mate_in, first, second, corner, corner_far = sources
    chosen = ((own, mate_in, first, second), (first, second, corner, corner_far))

    def copies(which):
        return [
            pltpu.make_async_copy(source.at[part], tokens.at[e], sems.at[e])
            for e, source in enumerate(chosen[which])
        ] + [
            pltpu.make_async_copy(
                ref.at[e ^ flip],
                grads.at[place_ref[base] + step, e],
                sems.at[blocks + at * blocks + e],
            )
            for at, (ref, (base, step, flip)) in enumerate(zip(grad_refs[which], marks[which]))
            for e in range(blocks)
        ]

    for which in range(2):

        @pl.when(core == which)
        def _():
            for copy in copies(which):
                copy.start()

    arrivals = [
        pltpu.make_async_copy(ref, sums.at[kind], sems.at[blocks * (count + 1) + kind])
        for kind, ref in enumerate(received)
    ]
    for copy in arrivals:
        copy.start()
    waits = copies(0)
    for e in range(blocks):
        waits[e].wait()
        turned[:, e * length : (e + 1) * length] = tokens[e].T
    for copy in waits[blocks:] + arrivals:
        copy.wait()
    for pair in range(count // 2):
        right = [grads[2 * pair + head].reshape(blocks * length, triple) for head in range(2)]
        total = dot(turned[...], jnp.concatenate(right, axis=1))
        for head in range(2):
            here = slice((2 * pair + head) * HD, (2 * pair + head + 1) * HD)
            for kind, out in enumerate(out_refs):
                at = (head * 3 + kind) * HD
                value = total[:, at : at + HD]
                if mine:
                    value = (value + sums[kind, :, here]) * mean_scale
                out[:, here] = value


def weight_product(place, mine, mean_scale, tokens, grads, received=()):
    blocks, length, triple = grads[0][0][0].shape
    count = len(grads[0])
    rows = tokens[0].shape[2]
    cols = HD * count
    return pl.pallas_call(
        functools.partial(
            weight_kernel, mine, mean_scale, [[mark for _, mark in part] for part in grads]
        ),
        out_shape=[jax.ShapeDtypeStruct((rows, cols), jnp.float32)] * 3,
        in_specs=[whole(pltpu.SMEM)] + [whole(pltpu.HBM)] * (6 + 2 * count + len(received)),
        out_specs=[whole()] * 3,
        scratch_shapes=[
            pltpu.VMEM((blocks, length, rows), jnp.bfloat16),
            pltpu.VMEM((rows, blocks * length), jnp.bfloat16),
            pltpu.VMEM((count, blocks, length, triple), jnp.bfloat16),
        ]
        + ([pltpu.VMEM((3, rows, cols), jnp.float32)] if mine else [])
        + [pltpu.SemaphoreType.DMA((blocks * (count + 1) + 3,))],
        compiler_params=pltpu.CompilerParams(vmem_limit_bytes=20 * MIB),
        cost_estimate=pl.CostEstimate(
            flops=2 * rows * 3 * cols * blocks * length,
            bytes_accessed=2 * blocks * length * (rows + 3 * cols) + 12 * rows * cols,
            transcendentals=0,
        ),
        name="weight_gradient_own" if mine else "weight_gradient_mate",
    )(place, *tokens, *[array for part in grads for array, _ in part], *received)


def choose_kernel(which_ref, first_ref, second_ref, out_ref, sem):
    for which, ref in enumerate((first_ref, second_ref)):

        @pl.when(which_ref[0] == which)
        def _():
            copy = pltpu.make_async_copy(ref, out_ref, sem)
            copy.start()
            copy.wait()


def chosen_of(which, first, second):
    return pl.pallas_call(
        choose_kernel,
        out_shape=jax.ShapeDtypeStruct(first.shape, first.dtype),
        in_specs=[whole(pltpu.SMEM)] + [whole(pltpu.HBM)] * 2,
        out_specs=whole(),
        scratch_shapes=[pltpu.SemaphoreType.DMA],
        name="choose_block",
    )(which, first, second)


def gather_body(
    normed,
    queries,
    saved_keys,
    saved_values,
    output_grad,
    view_links,
    query_weight,
    key_weight,
    value_weight,
):
    length, cols = queries.shape[2:]
    model_width = normed.shape[-1]
    rows = query_weight.shape[0]
    prompts, views, groups = (lax.axis_size(name) for name in ("dp", "view", "head"))
    mean_scale = 1.0 / (prompts * views)
    half = cols // HD // 2
    view = lax.axis_index("view")
    core = lax.rem(view, 2)
    side = view // 2
    chip = lax.axis_index("dp") * (views // 2) + side
    place = jnp.stack([core, lax.axis_index("head"), side * half, (1 - side) * half])
    place = place.astype(jnp.int32)
    arrays = tuple(a.reshape(length, cols) for a in (queries, saved_keys, saved_values, output_grad))

    ready = []
    for step in sorted(range(0, half, 2), key=lambda step: step + 1 < half):
        if step + 1 < half:
            picks = (
                lambda c, here, beside, step=step: beside + step + c,
                lambda c, here, beside, step=step: beside + step + 1 - c,
                lambda c, here, beside, step=step: here + step + c,
                lambda c, here, beside, step=step: here + step + 1 - c,
            )
            to_x, to_cross, own, to_mate = pack(picks, place, view_links, arrays)
            sources = (own, moved(to_mate, mate), moved(to_x, along_x), moved(to_cross, across_x))
        else:
            picks = (
                lambda c, here, beside, step=step: beside + step,
                lambda c, here, beside, step=step: here + step,
            )
            to_x, own = pack(picks, place, view_links, arrays)
            sources = (
                own,
                moved(own, only(1, mate)),
                moved(to_x, only(0, along_x)),
                moved(to_x, only(1, across_x)),
            )
        arrays = after(arrays, own)
        ready.append((step, step + 1 < half, sources))

    own_weights = turned_weights(after((query_weight, key_weight, value_weight), arrays[0]))
    mate_weights = moved(own_weights, mate)

    first, second = [], []
    turn = place
    for step, both, sources in ready:
        made = attention(turn, both, sources)
        (turn,) = after((place,), made)
        if both:
            inward = moved(made, only(1, mate))
            ahead = moved(made, straight)
            aside = moved(made, crossed)
            first += [
                (made, (HERE, step, 0)),
                (inward, (HERE, step + 1, 1)),
                (ahead, (BESIDE, step, 2)),
                (aside, (BESIDE, step + 1, 3)),
            ]
            second += [
                (ahead, (HERE, step + 1, 0)),
                (aside, (HERE, step, 1)),
                (moved(ahead, only(1, along_x)), (BESIDE, step + 1, 2)),
                (moved(ahead, only(0, across_y)), (BESIDE, step, 3)),
            ]
        else:
            ahead = moved(made, only(0, along_x))
            aside = moved(made, only(0, across_y))
            first += [(made, (HERE, step, 0)), (ahead, (BESIDE, step, 2))]
            second += [
                (aside, (HERE, step, 1)),
                (moved(ahead, only(0, across_y)), (BESIDE, step, 3)),
            ]

    def exchange(role, slots):
        total = slots[0].astype(jnp.float32)
        for s in range(1, groups):
            pairs = [
                ((y * views + v) * groups + z, (y * views + v) * groups + (z ^ s))
                for y in range(prompts)
                for v in range(role, views, 2)
                for z in range(groups)
            ]
            total += lax.ppermute(slots[s], ("dp", "view", "head"), pairs).astype(jnp.float32)
        return total.astype(jnp.bfloat16)

    def deliver(role, total, *earlier):
        def spot(y, v, z):
            return (y * views + v) * groups + z

        corners = [
            (y, v, z) for y in range(prompts) for v in range(role, views, 2) for z in range(groups)
        ]
        pairs = [(spot(y, v, z), spot(y ^ role, v ^ z, z)) for y, v, z in corners]
        beside = lax.ppermute(total, ("dp", "view", "head"), pairs)
        pairs = [
            (spot(y ^ role, v ^ z, z), spot(y ^ role, v ^ z, y * (views // 2) + v // 2))
            for y, v, z in corners
        ]
        (beside,) = after((beside,), *earlier)
        return lax.ppermute(beside, ("dp", "view", "head"), pairs)

    first_slots = input_product(turn, 0, first, own_weights, mate_weights)
    first_total = exchange(0, first_slots)
    (turn,) = after((place,), first_total)
    second_slots = input_product(turn, 1, second, own_weights, mate_weights)
    second_total = exchange(1, second_slots)
    flat = normed.reshape(length, model_width)

    def columns(of_chip):
        parts = [
            lax.dynamic_slice_in_dim(flat, (2 * of_chip + part) * rows, rows, axis=1)
            for part in range(2)
        ]
        return jnp.stack(parts)

    toward_x, toward_y = jnp.bitwise_xor(chip, 1), jnp.bitwise_xor(chip, 2)
    here = columns(chip)
    to_straight = columns(jnp.where(core == 0, toward_x, toward_y))
    to_crossed = columns(jnp.where(core == 0, toward_y, toward_x))
    to_corner = columns(jnp.bitwise_xor(chip, 3))
    (sent,) = after((here,), ready[0][2][1])
    to_straight, to_crossed, to_corner = after(
        (to_straight, to_crossed, to_corner), *[array for array, _ in second]
    )
    tokens = (
        here,
        moved(sent, only(1, mate)),
        moved(to_straight, straight),
        moved(to_crossed, crossed),
        moved(to_corner, corner_same),
        moved(to_corner, corner_cross),
    )
    for_mate = weight_product(place, False, mean_scale, tokens, (first, second))
    from_mate = [moved(w, mate) for w in for_mate]
    weight_grads = weight_product(place, True, mean_scale, tokens, (first, second), from_mate)
    landed = (deliver(0, first_total), deliver(1, second_total, *weight_grads))
    which = jnp.bitwise_xor(lax.axis_index("head") // (views // 2), lax.axis_index("dp"))
    input_grad = chosen_of(which.reshape(1).astype(jnp.int32), *landed)
    return (
        input_grad.reshape(1, 1, length, model_width // groups),
        *weight_grads,
    )


def solution(mesh):
    prompts, views, groups = (mesh.shape[name] for name in ("dp", "view", "head"))
    loop_of_four = prompts * 2 == views and prompts * views == 2 * groups and views == groups

    def choose(*arrays):
        batch, held, length, cols = arrays[1].shape
        if loop_of_four and batch == held == 1 and length % HD == 0 and cols % (2 * HD) == 0:
            return gather_body(*arrays)
        return halo_body(*arrays)

    placed = (
        P("dp", "view", None, None),
        P("dp", "view", None, "head"),
        P("dp", "view", None, "head"),
        P("dp", "view", None, "head"),
        P("dp", "view", None, "head"),
        P("view", None),
        P(("dp", "view"), "head"),
        P(("dp", "view"), "head"),
        P(("dp", "view"), "head"),
    )
    return jax.shard_map(
        choose,
        mesh=mesh,
        in_specs=placed,
        out_specs=(
            P("dp", "view", None, "head"),
            P(("dp", "view"), "head"),
            P(("dp", "view"), "head"),
            P(("dp", "view"), "head"),
        ),
        check_vma=False,
    )
```

```python
import functools

import jax
import jax.numpy as jnp
from jax import lax
from jax.experimental import pallas as pl
from jax.experimental.pallas import tpu as pltpu
from jax.sharding import PartitionSpec as P

HD = 128
LOG2E = 1.4426950408889634
MIB = 1024 * 1024


def shifted(value, axis, steps):
    count = lax.axis_size(axis)
    pairs = [(source, (source + steps) % count) for source in range(count)]
    return lax.ppermute(value, axis, pairs)


def attend(query_rows, grad_rows, blocks, usable, scaling):
    batch_size, length, col_count = query_rows.shape
    heads_here = col_count // HD
    key_heads = blocks[..., :col_count].reshape(batch_size, 3 * length, heads_here, HD)
    value_heads = blocks[..., col_count:].reshape(batch_size, 3 * length, heads_here, HD)
    query_heads = query_rows.reshape(batch_size, length, heads_here, HD)
    grad_heads = grad_rows.reshape(batch_size, length, heads_here, HD)
    scores = (
        jnp.einsum("bshd,bthd->bhst", query_heads, key_heads, preferred_element_type=jnp.float32)
        * scaling
    )
    scores = jnp.where(usable, scores, -1e30)
    largest = jnp.max(scores, axis=-1, keepdims=True)
    powers = jnp.exp(scores - largest)
    attn_probs = powers / jnp.sum(powers, axis=-1, keepdims=True)
    probs_half = attn_probs.astype(jnp.bfloat16)
    prob_grad = jnp.einsum(
        "bshd,bthd->bhst", grad_heads, value_heads, preferred_element_type=jnp.float32
    )
    row_delta = jnp.sum(attn_probs * prob_grad, axis=-1, keepdims=True)
    score_grad = (scaling * attn_probs * (prob_grad - row_delta)).astype(jnp.bfloat16)
    query_grad = jnp.einsum(
        "bhst,bthd->bshd", score_grad, key_heads, preferred_element_type=jnp.float32
    )
    key_grad = jnp.einsum(
        "bhst,bshd->bthd", score_grad, query_heads, preferred_element_type=jnp.float32
    )
    value_grad = jnp.einsum(
        "bhst,bshd->bthd", probs_half, grad_heads, preferred_element_type=jnp.float32
    )
    query_grad = query_grad.reshape(batch_size, length, col_count)
    key_grad = key_grad.reshape(batch_size, 3, length, col_count)
    value_grad = value_grad.reshape(batch_size, 3, length, col_count)
    return (query_grad, jnp.concatenate([key_grad, value_grad], axis=-1))


def halo_body(
    normed,
    queries,
    saved_keys,
    saved_values,
    output_grad,
    view_links,
    query_weight,
    key_weight,
    value_weight,
):
    scaling = HD ** (-0.5)
    batch_size, view_count, length, col_count = queries.shape
    model_width = normed.shape[-1]
    pairs = jnp.concatenate([saved_keys, saved_values], axis=-1)
    from_lower = shifted(pairs, "view", 1)
    from_upper = shifted(pairs, "view", -1)
    extended = jnp.concatenate([from_lower, pairs, from_upper], axis=1)
    block_index = jnp.arange(3 * length) // length
    pair_grads = jnp.zeros(extended.shape, jnp.float32)
    link_flags = view_links[0] >= 0
    usable = jnp.where(
        block_index == 0, link_flags[0], jnp.where(block_index == 2, link_flags[1], True)
    )
    query_grad, block_grad = attend(queries[:, 0], output_grad[:, 0], extended, usable, scaling)
    query_grads = [query_grad]
    pair_grads = pair_grads.at[:, 0:3].add(block_grad)
    row_count = batch_size * view_count * length
    query_half = jnp.stack(query_grads, axis=1).astype(jnp.bfloat16).reshape(row_count, col_count)
    flat_input = normed.reshape(row_count, model_width)
    mean_scale = 1.0 / (lax.axis_size("dp") * batch_size * lax.axis_size("view") * view_count)
    from_lower_grads = shifted(pair_grads[:, -1:], "view", 1)
    from_upper_grads = shifted(pair_grads[:, :1], "view", -1)
    own_grads = pair_grads[:, 1 : view_count + 1]
    own_grads = own_grads.at[:, :1].add(from_lower_grads)
    own_grads = own_grads.at[:, -1:].add(from_upper_grads)
    key_half = own_grads[..., :col_count].astype(jnp.bfloat16).reshape(row_count, col_count)
    value_half = own_grads[..., col_count:].astype(jnp.bfloat16).reshape(row_count, col_count)
    all_grads = jnp.concatenate([query_half, key_half, value_half], axis=-1)
    grads_three = all_grads.reshape(row_count, 3, col_count)
    stacked = jnp.stack([query_weight, key_weight, value_weight])
    partial_input = jnp.einsum(
        "ric,ipc->rp",
        grads_three,
        lax.all_gather(stacked, ("dp", "view"), axis=1, tiled=True),
        preferred_element_type=jnp.float32,
    )
    summed_input = lax.psum_scatter(partial_input, "head", scatter_dimension=1, tiled=True)
    input_grad = summed_input.astype(jnp.bfloat16).reshape(
        batch_size, view_count, length, model_width // lax.axis_size("head")
    )
    product = lax.dot_general(
        flat_input, all_grads, (((0,), (0,)), ((), ())), preferred_element_type=jnp.float32
    )
    together = lax.psum_scatter(
        product * mean_scale, ("dp", "view"), scatter_dimension=0, tiled=True
    )
    grad_query = together[:, :col_count]
    grad_key = together[:, col_count : 2 * col_count]
    grad_value = together[:, 2 * col_count :]
    return (input_grad, grad_query, grad_key, grad_value)


def moved(value, target):
    prompts, views = lax.axis_size("dp"), lax.axis_size("view")
    pairs = []
    for y in range(prompts):
        for v in range(views):
            goal = target(y, v)
            if goal is not None:
                pairs.append((y * views + v, goal[0] * views + goal[1]))
    return lax.ppermute(value, ("dp", "view"), pairs)


def mate(y, v):
    return (y, v ^ 1)


def along_x(y, v):
    return (y, v ^ 2)


def across_x(y, v):
    return (y, v ^ 3)


def only(core, target):
    return lambda y, v: target(y, v) if v % 2 == core else None


def along_y(y, v):
    return (y ^ 1, v)


def across_y(y, v):
    return (y ^ 1, v ^ 1)


def straight(y, v):
    return along_x(y, v) if v % 2 == 0 else along_y(y, v)


def crossed(y, v):
    return across_y(y, v) if v % 2 == 0 else across_x(y, v)


def corner_same(y, v):
    return None if v % 2 == 0 else (y ^ 1, v ^ 2)


def corner_cross(y, v):
    return (y ^ 1, v ^ 3) if v % 2 == 0 else None


def lanes(start, size):
    return pl.ds(pl.multiple_of(start, HD), size)


def whole(space=pltpu.VMEM):
    return pl.BlockSpec(memory_space=space)


def dot_last(a, b):
    return lax.dot_general(a, b, (((1,), (1,)), ((), ())), preferred_element_type=jnp.float32)


def dot_first(a, b):
    return lax.dot_general(a, b, (((0,), (0,)), ((), ())), preferred_element_type=jnp.float32)


def dot(a, b):
    return jnp.dot(a, b, preferred_element_type=jnp.float32)


def after(values, *earlier):
    return lax.optimization_barrier((tuple(values), tuple(earlier)))[0]


CORE, PLANE, HERE, BESIDE = range(4)
FLAG_ROWS = 16


def pack_kernel(picks, place_ref, links_ref, q_ref, k_ref, v_ref, g_ref, *out_refs):
    length = q_ref.shape[0]
    row = lax.broadcasted_iota(jnp.int32, (FLAG_ROWS, HD), 0)
    gaps = [jnp.where(links_ref[0, side] >= 0, 0.0, 1.0).astype(jnp.float32) for side in range(2)]
    flags = jnp.where(row < FLAG_ROWS // 2, gaps[0], gaps[1])
    for heads, out_ref in zip(picks, out_refs):
        for at, (base, step, sign) in enumerate(heads):
            head = place_ref[base] + step + sign * place_ref[CORE]
            for kind, source in enumerate((q_ref, k_ref, v_ref, g_ref)):
                out_ref[at, kind * length : (kind + 1) * length] = source[:, lanes(head * HD, HD)]
            out_ref[at, 4 * length : 4 * length + FLAG_ROWS] = flags.astype(out_ref.dtype)


def pack(picks, place, links, arrays):
    length = arrays[0].shape[0]
    height = 4 * length + FLAG_ROWS
    return pl.pallas_call(
        functools.partial(pack_kernel, picks),
        out_shape=[
            jax.ShapeDtypeStruct((len(heads), height, HD), jnp.bfloat16) for heads in picks
        ],
        in_specs=[whole(pltpu.SMEM)] * 2 + [whole()] * 4,
        out_specs=[whole()] * len(picks),
        compiler_params=pltpu.CompilerParams(vmem_limit_bytes=12 * MIB),
        name="pack_heads",
    )(place, links, *arrays)


def one_head(scaling, core, xs, length, keys, values, key_sums, value_sums):
    factor = scaling * LOG2E

    def rows(e, kind):
        return xs[e][kind * length : (kind + 1) * length]

    def gap(e, side):
        at = 4 * length + side * (FLAG_ROWS // 2)
        flags = xs[e][at : at + FLAG_ROWS // 2].astype(jnp.float32)[0:1]
        return jnp.concatenate([flags] * (length // HD), axis=1) * 1e30

    for at in range(6):
        keys[at * length : (at + 1) * length] = rows((at + 3) % 4, 1)
        values[at * length : (at + 1) * length] = rows((at + 3) % 4, 2)
    query_grads = []
    for e in range(4):
        blocks = slice(e * length, (e + 3) * length)
        before, behind = gap(e, 0), gap(e, 1)
        far_below = jnp.where(core == 0, before, behind)
        far_above = jnp.where(core == 0, behind, before)
        q, g = rows(e, 0), rows(e, 3)
        near = keys[blocks]
        scores = dot_last(near, q)
        scores = [scores[at * length : (at + 1) * length] for at in range(3)]
        tops = [jnp.max(part, axis=0, keepdims=True) for part in scores]
        top = jnp.maximum(tops[1], jnp.maximum(tops[0] - far_below, tops[2] - far_above))
        offsets = (top + far_below, top, top + far_above)
        powers = [jnp.exp2((part - o) * factor) for part, o in zip(scores, offsets)]
        inverse = 1.0 / sum(jnp.sum(p, axis=0, keepdims=True) for p in powers)
        prob_grads = dot_last(values[blocks], g)
        prob_grads = [prob_grads[at * length : (at + 1) * length] for at in range(3)]
        delta = inverse * sum(
            jnp.sum(p * d, axis=0, keepdims=True) for p, d in zip(powers, prob_grads)
        )
        probs = [p * inverse for p in powers]
        score_grad = jnp.concatenate(
            [
                (p * scaling * (d - delta)).astype(jnp.bfloat16)
                for p, d in zip(probs, prob_grads)
            ],
            axis=0,
        )
        probs_half = jnp.concatenate([p.astype(jnp.bfloat16) for p in probs], axis=0)
        query_grads.append(dot_first(score_grad, near))
        for sums, part in ((key_sums, dot(score_grad, q)), (value_sums, dot(probs_half, g))):
            if e == 0:
                sums[blocks] = part
            else:
                held = slice(e * length, (e + 2) * length)
                sums[held] += part[: 2 * length]
                sums[(e + 2) * length : (e + 3) * length] = part[2 * length :]

    def by_view(sums):
        parts = [sums[at * length : (at + 1) * length] for at in range(6)]
        return (parts[1] + parts[5], parts[2], parts[3], parts[0] + parts[4])

    return query_grads, by_view(key_sums), by_view(value_sums)


def attention_kernel(scaling, own_heads, place_ref, *refs):
    own, mate_in, x_in, cross_in, mate_x_in = refs[:5]
    out_ref, keys, values, key_sums, value_sums = refs[5:]
    length = out_ref.shape[1]
    heads = own.shape[0]
    for head in range(heads):
        shared = head >= own_heads
        far = mate_x_in if shared else cross_in
        xs = [own.at[head], mate_in.at[head], x_in.at[head], far.at[head]]
        grads = one_head(
            scaling, place_ref[CORE], xs, length, keys, values, key_sums, value_sums
        )
        for e in range(4):
            if shared and e % 2 == 1:
                continue
            at = 4 * own_heads + e // 2 if shared else 4 * head + e
            for kind in range(3):
                out_ref[at, :, kind * HD : (kind + 1) * HD] = grads[kind][e].astype(out_ref.dtype)


def attention(place, own_heads, sources):
    heads, height, _ = sources[0].shape
    length = (height - FLAG_ROWS) // 4
    held = 4 * own_heads + 2 * (heads - own_heads)
    return pl.pallas_call(
        functools.partial(attention_kernel, HD ** (-0.5), own_heads),
        out_shape=jax.ShapeDtypeStruct((held, length, 3 * HD), jnp.bfloat16),
        in_specs=[whole(pltpu.SMEM)] + [whole()] * 5,
        out_specs=whole(),
        scratch_shapes=[pltpu.VMEM((6 * length, HD), jnp.bfloat16)] * 2
        + [pltpu.VMEM((6 * length, HD), jnp.float32)] * 2,
        compiler_params=pltpu.CompilerParams(vmem_limit_bytes=20 * MIB),
        cost_estimate=pl.CostEstimate(
            flops=heads * 4 * 5 * 2 * length * 3 * length * HD * 2,
            bytes_accessed=heads * 2 * length * 7 * HD * 4,
            transcendentals=heads * 12 * length * length,
        ),
        name="attention_gradients",
    )(place, *sources)


def turn_kernel(q_ref, k_ref, v_ref, out_ref):
    for head in range(q_ref.shape[1] // HD):
        for kind, source in enumerate((q_ref, k_ref, v_ref)):
            at = (head * 3 + kind) * HD
            out_ref[at : at + HD] = source[:, head * HD : (head + 1) * HD].T


def turned_weights(weights):
    rows, cols = weights[0].shape
    return pl.pallas_call(
        turn_kernel,
        out_shape=jax.ShapeDtypeStruct((3 * cols, rows), jnp.bfloat16),
        in_specs=[whole()] * 3,
        out_specs=whole(),
        compiler_params=pltpu.CompilerParams(vmem_limit_bytes=8 * MIB),
        name="turn_weights",
    )(*weights)


def gathered(role, own_heads, shared, refs):
    sides = []
    for side in range(2):
        pieces = []
        for head in range(own_heads):
            for maker in range(2):
                k = 2 * side + (maker ^ role)
                pieces.append([refs[k][4 * head + (e ^ k)] for e in range(4)])
        for at in range(shared):
            rows = []
            for e in range(4):
                k = 2 * side + e % 2
                rows.append(refs[k][4 * own_heads + 2 * at + (e // 2 ^ side)])
            pieces.append(rows)
        sides.append(
            jnp.concatenate([jnp.concatenate(rows, axis=0) for rows in pieces], axis=1)
        )
    return sides


def input_kernel(role, own_heads, shared, place_ref, *refs):
    grad_refs, weight_refs, out_refs, total = refs[:4], refs[4:6], refs[6:-1], refs[-1]
    core, plane = place_ref[CORE], place_ref[PLANE]
    rows = weight_refs[0].shape[1]
    length = out_refs[0].shape[0]

    @pl.when(core == role)
    def _():
        lefts = gathered(role, own_heads, shared, grad_refs)
        depth = lefts[0].shape[1]
        for weights, at in zip(weight_refs, (core, 1 - core)):
            parts = []
            for base, left in zip((HERE, BESIDE), lefts):
                start = pl.multiple_of(place_ref[base] * (3 * HD), HD)
                parts.append(dot(left, weights[pl.ds(start, depth)]))
            product = (parts[0] + parts[1]).astype(total.dtype)
            for e in range(4):
                total[e, :, lanes(at * rows, rows)] = product[e * length : (e + 1) * length]
        for s, out_ref in enumerate(out_refs):
            out_ref[...] = total[jnp.bitwise_xor(plane, s)]


def input_product(place, role, own_heads, shared, grads, own_weights, mate_weights):
    _, length, _ = grads[0].shape
    depth, rows = own_weights.shape
    out = jax.ShapeDtypeStruct((length, 2 * rows), jnp.bfloat16)
    return pl.pallas_call(
        functools.partial(input_kernel, role, own_heads, shared),
        out_shape=[out] * 4,
        in_specs=[whole(pltpu.SMEM)] + [whole()] * 6,
        out_specs=[whole()] * 4,
        scratch_shapes=[pltpu.VMEM((4, length, 2 * rows), jnp.bfloat16)],
        compiler_params=pltpu.CompilerParams(vmem_limit_bytes=28 * MIB),
        cost_estimate=pl.CostEstimate(
            flops=8 * length * 2 * rows * depth,
            bytes_accessed=8 * length * (2 * rows + depth) + 4 * rows * depth,
            transcendentals=0,
        ),
        name="input_gradient",
    )(place, *grads, own_weights, mate_weights)


def weight_kernel(mine, mean_scale, own_heads, shared, place_ref, *refs):
    own, mate_in, first, second, corner, corner_far = refs[:6]
    made, inward, ahead, aside, relay_x, relay_y = refs[6:12]
    if mine:
        received, out_refs, turned = refs[12], refs[13:16], refs[16]
    else:
        received, out_refs, turned = None, [refs[12].at[kind] for kind in range(3)], refs[13]
    core = place_ref[CORE]
    length = own.shape[1]
    part = core if mine else 1 - core
    tokens = ((own, mate_in, first, second), (first, second, corner, corner_far))
    grads = ((made, inward, ahead, aside), (ahead, aside, relay_x, relay_y))
    for role in range(2):

        @pl.when(core == role)
        def _():
            for e, source in enumerate(tokens[role]):
                turned[:, e * length : (e + 1) * length] = source[part].T
            sides = gathered(role, own_heads, shared, grads[role])
            for base, side in zip((HERE, BESIDE), sides):
                total = dot(turned[...], side)
                for head in range(side.shape[1] // (3 * HD)):
                    here = lanes((place_ref[base] + head) * HD, HD)
                    for kind, out in enumerate(out_refs):
                        at = (head * 3 + kind) * HD
                        value = total[:, at : at + HD]
                        if mine:
                            value = (value + received[kind, :, here]) * mean_scale
                        out[:, here] = value


def weight_product(place, mine, mean_scale, own_heads, shared, tokens, grads, received=()):
    _, length, triple = grads[0].shape
    rows = tokens[0].shape[2]
    cols = 2 * (2 * own_heads + shared) * HD
    out = jax.ShapeDtypeStruct((rows, cols), jnp.float32)
    both = jax.ShapeDtypeStruct((3, rows, cols), jnp.float32)
    return pl.pallas_call(
        functools.partial(weight_kernel, mine, mean_scale, own_heads, shared),
        out_shape=[out] * 3 if mine else both,
        in_specs=[whole(pltpu.SMEM)] + [whole()] * (12 + len(received)),
        out_specs=[whole()] * 3 if mine else whole(),
        scratch_shapes=[pltpu.VMEM((rows, 4 * length), jnp.bfloat16)],
        compiler_params=pltpu.CompilerParams(vmem_limit_bytes=36 * MIB),
        cost_estimate=pl.CostEstimate(
            flops=8 * rows * 3 * cols * length,
            bytes_accessed=8 * length * (rows + 3 * cols) + 12 * rows * cols,
            transcendentals=0,
        ),
        name="weight_gradient_own" if mine else "weight_gradient_mate",
    )(place, *tokens, *grads, *received)


def choose_kernel(which_ref, first_ref, second_ref, out_ref):
    for which, ref in enumerate((first_ref, second_ref)):

        @pl.when(which_ref[0] == which)
        def _():
            out_ref[...] = ref[...]


def chosen_of(which, first, second):
    return pl.pallas_call(
        choose_kernel,
        out_shape=jax.ShapeDtypeStruct(first.shape, first.dtype),
        in_specs=[whole(pltpu.SMEM)] + [whole()] * 2,
        out_specs=whole(),
        compiler_params=pltpu.CompilerParams(vmem_limit_bytes=8 * MIB),
        name="choose_block",
    )(which, first, second)


def gather_body(
    normed,
    queries,
    saved_keys,
    saved_values,
    output_grad,
    view_links,
    query_weight,
    key_weight,
    value_weight,
):
    length, cols = queries.shape[2:]
    model_width = normed.shape[-1]
    rows = query_weight.shape[0]
    prompts, views, groups = (lax.axis_size(name) for name in ("dp", "view", "head"))
    mean_scale = 1.0 / (prompts * views)
    half = cols // HD // 2
    view = lax.axis_index("view")
    core = lax.rem(view, 2)
    side = view // 2
    chip = lax.axis_index("dp") * (views // 2) + side
    place = jnp.stack([core, lax.axis_index("head"), side * half, (1 - side) * half])
    place = place.astype(jnp.int32)
    arrays = tuple(a.reshape(length, cols) for a in (queries, saved_keys, saved_values, output_grad))

    own_heads, shared = half // 2, half % 2
    both = [2 * own_heads + at for at in range(shared)]
    each = [2 * step for step in range(own_heads)]
    to_x, to_cross, to_mate, own = pack(
        (
            [(BESIDE, step, 1) for step in each] + [(BESIDE, step, 0) for step in both],
            [(BESIDE, step + 1, -1) for step in each],
            [(HERE, step + 1, -1) for step in each] + [(HERE, step, 0) for step in both],
            [(HERE, step, 1) for step in each] + [(HERE, step, 0) for step in both],
        ),
        place,
        view_links,
        arrays,
    )
    x_in = moved(to_x, along_x)
    cross_in = moved(to_cross, across_x)
    mate_in = moved(to_mate, mate)
    mate_x_in = moved(x_in, mate)

    own_weights = turned_weights(after((query_weight, key_weight, value_weight), own))
    mate_weights = moved(own_weights, mate)

    flat = normed.reshape(length, model_width)

    def columns(of_chip):
        parts = [
            lax.dynamic_slice_in_dim(flat, (2 * of_chip + part) * rows, rows, axis=1)
            for part in range(2)
        ]
        return jnp.stack(parts)

    toward_x, toward_y = jnp.bitwise_xor(chip, 1), jnp.bitwise_xor(chip, 2)
    here = columns(chip)
    to_straight = columns(jnp.where(core == 0, toward_x, toward_y))
    to_crossed = columns(jnp.where(core == 0, toward_y, toward_x))
    to_corner = columns(jnp.bitwise_xor(chip, 3))
    (sent,) = after((here,), mate_in)
    mate_here = moved(sent, only(1, mate))
    to_straight, to_crossed = after((to_straight, to_crossed), cross_in)
    normed_ahead = moved(to_straight, straight)
    normed_aside = moved(to_crossed, crossed)

    made = attention(place, own_heads, (own, mate_in, x_in, cross_in, mate_x_in))
    (made,) = after((made,), mate_here, normed_ahead, normed_aside)
    ahead = moved(made, straight)
    aside = moved(made, crossed)
    inward = moved(made, only(1, mate))
    relay_x = moved(ahead, only(1, along_x))
    relay_y = moved(ahead, only(0, across_y))
    first = (made, inward, ahead, aside)
    second = (ahead, aside, relay_x, relay_y)

    def exchange(role, slots):
        arrived = []
        for s in range(1, groups):
            pairs = [
                ((y * views + v) * groups + z, (y * views + v) * groups + (z ^ s))
                for y in range(prompts)
                for v in range(role, views, 2)
                for z in range(groups)
            ]
            arrived.append(lax.ppermute(slots[s], ("dp", "view", "head"), pairs))
        total = sum(array.astype(jnp.float32) for array in (slots[0], *arrived))
        return total.astype(jnp.bfloat16), arrived

    def deliver(role, total, *earlier):
        def spot(y, v, z):
            return (y * views + v) * groups + z

        corners = [
            (y, v, z) for y in range(prompts) for v in range(role, views, 2) for z in range(groups)
        ]
        pairs = [(spot(y, v, z), spot(y ^ role, v ^ z, z)) for y, v, z in corners]
        beside = lax.ppermute(total, ("dp", "view", "head"), pairs)
        pairs = [
            (spot(y ^ role, v ^ z, z), spot(y ^ role, v ^ z, y * (views // 2) + v // 2))
            for y, v, z in corners
        ]
        (beside,) = after((beside,), *earlier)
        return lax.ppermute(beside, ("dp", "view", "head"), pairs)

    first_slots = input_product(place, 0, own_heads, shared, first, own_weights, mate_weights)
    first_total, _ = exchange(0, first_slots)
    (turn,) = after((place,), first_total)
    second_slots = input_product(turn, 1, own_heads, shared, second, own_weights, mate_weights)
    second_total, arrived = exchange(1, second_slots)
    (to_corner,) = after((to_corner,), *second_slots)
    tokens = (
        here,
        mate_here,
        normed_ahead,
        normed_aside,
        moved(to_corner, corner_same),
        moved(to_corner, corner_cross),
    )
    grads = (made, inward, ahead, aside, relay_x, relay_y)
    (turn,) = after((place,), arrived[1])
    for_mate = weight_product(turn, False, mean_scale, own_heads, shared, tokens, grads)
    from_mate = moved(for_mate, mate)
    weight_grads = weight_product(
        place, True, mean_scale, own_heads, shared, tokens, grads, (from_mate,)
    )
    landed = (deliver(0, first_total), deliver(1, second_total, *weight_grads))
    which = jnp.bitwise_xor(lax.axis_index("head") // (views // 2), lax.axis_index("dp"))
    input_grad = chosen_of(which.reshape(1).astype(jnp.int32), *landed)
    return (
        input_grad.reshape(1, 1, length, model_width // groups),
        *weight_grads,
    )


def solution(mesh):
    prompts, views, groups = (mesh.shape[name] for name in ("dp", "view", "head"))
    loop_of_four = prompts * 2 == views and prompts * views == 2 * groups and views == groups

    def choose(*arrays):
        batch, held, length, cols = arrays[1].shape
        if loop_of_four and batch == held == 1 and length % HD == 0 and cols % (2 * HD) == 0:
            return gather_body(*arrays)
        return halo_body(*arrays)

    placed = (
        P("dp", "view", None, None),
        P("dp", "view", None, "head"),
        P("dp", "view", None, "head"),
        P("dp", "view", None, "head"),
        P("dp", "view", None, "head"),
        P("view", None),
        P(("dp", "view"), "head"),
        P(("dp", "view"), "head"),
        P(("dp", "view"), "head"),
    )
    return jax.shard_map(
        choose,
        mesh=mesh,
        in_specs=placed,
        out_specs=(
            P("dp", "view", None, "head"),
            P(("dp", "view"), "head"),
            P(("dp", "view"), "head"),
            P(("dp", "view"), "head"),
        ),
        check_vma=False,
    )
```

```python
import functools

import jax
import jax.numpy as jnp
from jax import lax
from jax.experimental import pallas as pl
from jax.experimental.pallas import tpu as pltpu
from jax.sharding import PartitionSpec as P

HD = 128
LOG2E = 1.4426950408889634
MIB = 1024 * 1024


def shifted(value, axis, steps):
    count = lax.axis_size(axis)
    pairs = [(source, (source + steps) % count) for source in range(count)]
    return lax.ppermute(value, axis, pairs)


def attend(query_rows, grad_rows, blocks, usable, scaling):
    batch_size, length, col_count = query_rows.shape
    heads_here = col_count // HD
    key_heads = blocks[..., :col_count].reshape(batch_size, 3 * length, heads_here, HD)
    value_heads = blocks[..., col_count:].reshape(batch_size, 3 * length, heads_here, HD)
    query_heads = query_rows.reshape(batch_size, length, heads_here, HD)
    grad_heads = grad_rows.reshape(batch_size, length, heads_here, HD)
    scores = (
        jnp.einsum("bshd,bthd->bhst", query_heads, key_heads, preferred_element_type=jnp.float32)
        * scaling
    )
    scores = jnp.where(usable, scores, -1e30)
    largest = jnp.max(scores, axis=-1, keepdims=True)
    powers = jnp.exp(scores - largest)
    attn_probs = powers / jnp.sum(powers, axis=-1, keepdims=True)
    probs_half = attn_probs.astype(jnp.bfloat16)
    prob_grad = jnp.einsum(
        "bshd,bthd->bhst", grad_heads, value_heads, preferred_element_type=jnp.float32
    )
    row_delta = jnp.sum(attn_probs * prob_grad, axis=-1, keepdims=True)
    score_grad = (scaling * attn_probs * (prob_grad - row_delta)).astype(jnp.bfloat16)
    query_grad = jnp.einsum(
        "bhst,bthd->bshd", score_grad, key_heads, preferred_element_type=jnp.float32
    )
    key_grad = jnp.einsum(
        "bhst,bshd->bthd", score_grad, query_heads, preferred_element_type=jnp.float32
    )
    value_grad = jnp.einsum(
        "bhst,bshd->bthd", probs_half, grad_heads, preferred_element_type=jnp.float32
    )
    query_grad = query_grad.reshape(batch_size, length, col_count)
    key_grad = key_grad.reshape(batch_size, 3, length, col_count)
    value_grad = value_grad.reshape(batch_size, 3, length, col_count)
    return (query_grad, jnp.concatenate([key_grad, value_grad], axis=-1))


def halo_body(
    normed,
    queries,
    saved_keys,
    saved_values,
    output_grad,
    view_links,
    query_weight,
    key_weight,
    value_weight,
):
    scaling = HD ** (-0.5)
    batch_size, view_count, length, col_count = queries.shape
    model_width = normed.shape[-1]
    pairs = jnp.concatenate([saved_keys, saved_values], axis=-1)
    from_lower = shifted(pairs, "view", 1)
    from_upper = shifted(pairs, "view", -1)
    extended = jnp.concatenate([from_lower, pairs, from_upper], axis=1)
    block_index = jnp.arange(3 * length) // length
    pair_grads = jnp.zeros(extended.shape, jnp.float32)
    link_flags = view_links[0] >= 0
    usable = jnp.where(
        block_index == 0, link_flags[0], jnp.where(block_index == 2, link_flags[1], True)
    )
    query_grad, block_grad = attend(queries[:, 0], output_grad[:, 0], extended, usable, scaling)
    query_grads = [query_grad]
    pair_grads = pair_grads.at[:, 0:3].add(block_grad)
    row_count = batch_size * view_count * length
    query_half = jnp.stack(query_grads, axis=1).astype(jnp.bfloat16).reshape(row_count, col_count)
    flat_input = normed.reshape(row_count, model_width)
    mean_scale = 1.0 / (lax.axis_size("dp") * batch_size * lax.axis_size("view") * view_count)
    from_lower_grads = shifted(pair_grads[:, -1:], "view", 1)
    from_upper_grads = shifted(pair_grads[:, :1], "view", -1)
    own_grads = pair_grads[:, 1 : view_count + 1]
    own_grads = own_grads.at[:, :1].add(from_lower_grads)
    own_grads = own_grads.at[:, -1:].add(from_upper_grads)
    key_half = own_grads[..., :col_count].astype(jnp.bfloat16).reshape(row_count, col_count)
    value_half = own_grads[..., col_count:].astype(jnp.bfloat16).reshape(row_count, col_count)
    all_grads = jnp.concatenate([query_half, key_half, value_half], axis=-1)
    grads_three = all_grads.reshape(row_count, 3, col_count)
    stacked = jnp.stack([query_weight, key_weight, value_weight])
    partial_input = jnp.einsum(
        "ric,ipc->rp",
        grads_three,
        lax.all_gather(stacked, ("dp", "view"), axis=1, tiled=True),
        preferred_element_type=jnp.float32,
    )
    summed_input = lax.psum_scatter(partial_input, "head", scatter_dimension=1, tiled=True)
    input_grad = summed_input.astype(jnp.bfloat16).reshape(
        batch_size, view_count, length, model_width // lax.axis_size("head")
    )
    product = lax.dot_general(
        flat_input, all_grads, (((0,), (0,)), ((), ())), preferred_element_type=jnp.float32
    )
    together = lax.psum_scatter(
        product * mean_scale, ("dp", "view"), scatter_dimension=0, tiled=True
    )
    grad_query = together[:, :col_count]
    grad_key = together[:, col_count : 2 * col_count]
    grad_value = together[:, 2 * col_count :]
    return (input_grad, grad_query, grad_key, grad_value)


def moved(value, target):
    prompts, views = lax.axis_size("dp"), lax.axis_size("view")
    pairs = []
    for y in range(prompts):
        for v in range(views):
            goal = target(y, v)
            if goal is not None:
                pairs.append((y * views + v, goal[0] * views + goal[1]))
    return lax.ppermute(value, ("dp", "view"), pairs)


def mate(y, v):
    return (y, v ^ 1)


def along_x(y, v):
    return (y, v ^ 2)


def across_x(y, v):
    return (y, v ^ 3)


def only(core, target):
    return lambda y, v: target(y, v) if v % 2 == core else None


def along_y(y, v):
    return (y ^ 1, v)


def across_y(y, v):
    return (y ^ 1, v ^ 1)


def straight(y, v):
    return along_x(y, v) if v % 2 == 0 else along_y(y, v)


def crossed(y, v):
    return across_y(y, v) if v % 2 == 0 else across_x(y, v)


def corner_same(y, v):
    return None if v % 2 == 0 else (y ^ 1, v ^ 2)


def corner_cross(y, v):
    return (y ^ 1, v ^ 3) if v % 2 == 0 else None


def lanes(start, size):
    return pl.ds(pl.multiple_of(start, HD), size)


def whole(space=pltpu.VMEM):
    return pl.BlockSpec(memory_space=space)


def dot_last(a, b):
    return lax.dot_general(a, b, (((1,), (1,)), ((), ())), preferred_element_type=jnp.float32)


def dot_first(a, b):
    return lax.dot_general(a, b, (((0,), (0,)), ((), ())), preferred_element_type=jnp.float32)


def dot(a, b):
    return jnp.dot(a, b, preferred_element_type=jnp.float32)


def after(values, *earlier):
    return lax.optimization_barrier((tuple(values), tuple(earlier)))[0]


CORE, PLANE, HERE, BESIDE = range(4)
FLAG_ROWS = 16


def pack_kernel(picks, place_ref, links_ref, q_ref, k_ref, v_ref, g_ref, *out_refs):
    length = q_ref.shape[0]
    row = lax.broadcasted_iota(jnp.int32, (FLAG_ROWS, HD), 0)
    gaps = [jnp.where(links_ref[0, side] >= 0, 0.0, 1.0).astype(jnp.float32) for side in range(2)]
    flags = jnp.where(row < FLAG_ROWS // 2, gaps[0], gaps[1])
    for heads, out_ref in zip(picks, out_refs):
        for at, (base, step, sign) in enumerate(heads):
            head = place_ref[base] + step + sign * place_ref[CORE]
            for kind, source in enumerate((q_ref, k_ref, v_ref, g_ref)):
                out_ref[at, kind * length : (kind + 1) * length] = source[:, lanes(head * HD, HD)]
            out_ref[at, 4 * length : 4 * length + FLAG_ROWS] = flags.astype(out_ref.dtype)


def pack(picks, place, links, arrays):
    length = arrays[0].shape[0]
    height = 4 * length + FLAG_ROWS
    return pl.pallas_call(
        functools.partial(pack_kernel, picks),
        out_shape=[
            jax.ShapeDtypeStruct((len(heads), height, HD), jnp.bfloat16) for heads in picks
        ],
        in_specs=[whole(pltpu.SMEM)] * 2 + [whole()] * 4,
        out_specs=[whole()] * len(picks),
        name="pack_heads",
    )(place, links, *arrays)


def one_head(scaling, core, xs, length, keys, values, key_sums, value_sums):
    factor = scaling * LOG2E

    def rows(e, kind):
        return xs[e][kind * length : (kind + 1) * length]

    def gap(e, side):
        at = 4 * length + side * (FLAG_ROWS // 2)
        flags = xs[e][at : at + FLAG_ROWS // 2].astype(jnp.float32)[0:1]
        return jnp.concatenate([flags] * (length // HD), axis=1) * 1e30

    for at in range(6):
        keys[at * length : (at + 1) * length] = rows((at + 3) % 4, 1)
        values[at * length : (at + 1) * length] = rows((at + 3) % 4, 2)
    query_grads = []
    for e in range(4):
        blocks = slice(e * length, (e + 3) * length)
        before, behind = gap(e, 0), gap(e, 1)
        far_below = jnp.where(core == 0, before, behind)
        far_above = jnp.where(core == 0, behind, before)
        q, g = rows(e, 0), rows(e, 3)
        near = keys[blocks]
        scores = dot_last(near, q)
        scores = [scores[at * length : (at + 1) * length] for at in range(3)]
        tops = [jnp.max(part, axis=0, keepdims=True) for part in scores]
        top = jnp.maximum(tops[1], jnp.maximum(tops[0] - far_below, tops[2] - far_above))
        offsets = (top + far_below, top, top + far_above)
        powers = [jnp.exp2((part - o) * factor) for part, o in zip(scores, offsets)]
        inverse = 1.0 / sum(jnp.sum(p, axis=0, keepdims=True) for p in powers)
        prob_grads = dot_last(values[blocks], g)
        prob_grads = [prob_grads[at * length : (at + 1) * length] for at in range(3)]
        delta = inverse * sum(
            jnp.sum(p * d, axis=0, keepdims=True) for p, d in zip(powers, prob_grads)
        )
        probs = [p * inverse for p in powers]
        score_grad = jnp.concatenate(
            [
                (p * scaling * (d - delta)).astype(jnp.bfloat16)
                for p, d in zip(probs, prob_grads)
            ],
            axis=0,
        )
        probs_half = jnp.concatenate([p.astype(jnp.bfloat16) for p in probs], axis=0)
        query_grads.append(dot_first(score_grad, near))
        for sums, part in ((key_sums, dot(score_grad, q)), (value_sums, dot(probs_half, g))):
            if e == 0:
                sums[blocks] = part
            else:
                held = slice(e * length, (e + 2) * length)
                sums[held] += part[: 2 * length]
                sums[(e + 2) * length : (e + 3) * length] = part[2 * length :]

    def by_view(sums):
        parts = [sums[at * length : (at + 1) * length] for at in range(6)]
        return (parts[1] + parts[5], parts[2], parts[3], parts[0] + parts[4])

    return query_grads, by_view(key_sums), by_view(value_sums)


def attention_kernel(scaling, own_heads, place_ref, *refs):
    own, mate_in, x_in, cross_in, mate_x_in = refs[:5]
    out_ref, keys, values, key_sums, value_sums = refs[5:]
    length = out_ref.shape[1]
    heads = own.shape[0]
    for head in range(heads):
        shared = head >= own_heads
        far = mate_x_in if shared else cross_in
        xs = [own.at[head], mate_in.at[head], x_in.at[head], far.at[head]]
        grads = one_head(
            scaling, place_ref[CORE], xs, length, keys, values, key_sums, value_sums
        )
        for e in range(4):
            if shared and e % 2 == 1:
                continue
            at = 4 * own_heads + e // 2 if shared else 4 * head + e
            for kind in range(3):
                out_ref[at, :, kind * HD : (kind + 1) * HD] = grads[kind][e].astype(out_ref.dtype)


def attention(place, own_heads, sources):
    heads, height, _ = sources[0].shape
    length = (height - FLAG_ROWS) // 4
    held = 4 * own_heads + 2 * (heads - own_heads)
    return pl.pallas_call(
        functools.partial(attention_kernel, HD ** (-0.5), own_heads),
        out_shape=jax.ShapeDtypeStruct((held, length, 3 * HD), jnp.bfloat16),
        in_specs=[whole(pltpu.SMEM)] + [whole()] * 5,
        out_specs=whole(),
        scratch_shapes=[pltpu.VMEM((6 * length, HD), jnp.bfloat16)] * 2
        + [pltpu.VMEM((6 * length, HD), jnp.float32)] * 2,
        compiler_params=pltpu.CompilerParams(vmem_limit_bytes=20 * MIB),
        cost_estimate=pl.CostEstimate(
            flops=heads * 4 * 5 * 2 * length * 3 * length * HD * 2,
            bytes_accessed=heads * 2 * length * 7 * HD * 4,
            transcendentals=heads * 12 * length * length,
        ),
        name="attention_gradients",
    )(place, *sources)


def turn_kernel(place_ref, q_ref, k_ref, v_ref, out_ref):
    half = q_ref.shape[1] // HD // 2
    for side, base in enumerate((HERE, BESIDE)):
        for head in range(half):
            for kind, source in enumerate((q_ref, k_ref, v_ref)):
                at = ((side * half + head) * 3 + kind) * HD
                out_ref[at : at + HD] = source[:, lanes((place_ref[base] + head) * HD, HD)].T


def turned_weights(place, weights):
    rows, cols = weights[0].shape
    return pl.pallas_call(
        turn_kernel,
        out_shape=jax.ShapeDtypeStruct((3 * cols, rows), jnp.bfloat16),
        in_specs=[whole(pltpu.SMEM)] + [whole()] * 3,
        out_specs=whole(),
        compiler_params=pltpu.CompilerParams(vmem_limit_bytes=8 * MIB),
        name="turn_weights",
    )(place, *weights)


def join_kernel(place_ref, own_ref, mate_ref, out_ref):
    core = place_ref[CORE]
    rows = own_ref.shape[1]
    out_ref[:, lanes(core * rows, rows)] = own_ref[...]
    out_ref[:, lanes((1 - core) * rows, rows)] = mate_ref[...]


def joined_weights(place, own_weights, mate_weights):
    depth, rows = own_weights.shape
    return pl.pallas_call(
        join_kernel,
        out_shape=jax.ShapeDtypeStruct((depth, 2 * rows), jnp.bfloat16),
        in_specs=[whole(pltpu.SMEM)] + [whole()] * 2,
        out_specs=whole(),
        compiler_params=pltpu.CompilerParams(vmem_limit_bytes=12 * MIB),
        name="join_weights",
    )(place, own_weights, mate_weights)


def gathered(role, own_heads, shared, refs):
    sides = []
    for side in range(2):
        pieces = []
        for head in range(own_heads):
            for maker in range(2):
                k = 2 * side + (maker ^ role)
                pieces.append([refs[k][4 * head + (e ^ k)] for e in range(4)])
        for at in range(shared):
            rows = []
            for e in range(4):
                k = 2 * side + e % 2
                rows.append(refs[k][4 * own_heads + 2 * at + (e // 2 ^ side)])
            pieces.append(rows)
        sides.append(
            jnp.concatenate([jnp.concatenate(rows, axis=0) for rows in pieces], axis=1)
        )
    return sides


def input_kernel(role, own_heads, shared, place_ref, *refs):
    grad_refs, weights, out_refs, total = refs[:4], refs[4], refs[5:-1], refs[-1]
    length = out_refs[0].shape[0]

    @pl.when(place_ref[CORE] == role)
    def _():
        left = jnp.concatenate(gathered(role, own_heads, shared, grad_refs), axis=1)
        for e in range(4):
            product = dot(left[e * length : (e + 1) * length], weights[...])
            total[e] = product.astype(total.dtype)
        for s, out_ref in enumerate(out_refs):
            out_ref[...] = total[jnp.bitwise_xor(place_ref[PLANE], s)]


def input_product(place, role, own_heads, shared, grads, weights):
    _, length, _ = grads[0].shape
    depth, rows = weights.shape
    out = jax.ShapeDtypeStruct((length, rows), jnp.bfloat16)
    return pl.pallas_call(
        functools.partial(input_kernel, role, own_heads, shared),
        out_shape=[out] * 4,
        in_specs=[whole(pltpu.SMEM)] + [whole()] * 5,
        out_specs=[whole()] * 4,
        scratch_shapes=[pltpu.VMEM((4, length, rows), jnp.bfloat16)],
        compiler_params=pltpu.CompilerParams(vmem_limit_bytes=28 * MIB),
        cost_estimate=pl.CostEstimate(
            flops=8 * length * rows * depth,
            bytes_accessed=8 * length * (rows + depth) + 2 * rows * depth,
            transcendentals=0,
        ),
        name="input_gradient",
    )(place, *grads, weights)


def weight_kernel(mine, mean_scale, own_heads, shared, place_ref, *refs):
    own, mate_in, first, second, corner, corner_far = refs[:6]
    made, inward, ahead, aside, relay_x, relay_y = refs[6:12]
    if mine:
        received, out_refs, turned = refs[12], refs[13:16], refs[16]
    else:
        received, out_refs, turned = None, [refs[12].at[kind] for kind in range(3)], refs[13]
    core = place_ref[CORE]
    length = own.shape[1]
    part = core if mine else 1 - core
    tokens = ((own, mate_in, first, second), (first, second, corner, corner_far))
    grads = ((made, inward, ahead, aside), (ahead, aside, relay_x, relay_y))
    for role in range(2):

        @pl.when(core == role)
        def _():
            for e, source in enumerate(tokens[role]):
                turned[:, e * length : (e + 1) * length] = source[part].T
            sides = gathered(role, own_heads, shared, grads[role])
            for base, side in zip((HERE, BESIDE), sides):
                total = dot(turned[...], side)
                for head in range(side.shape[1] // (3 * HD)):
                    here = lanes((place_ref[base] + head) * HD, HD)
                    for kind, out in enumerate(out_refs):
                        at = (head * 3 + kind) * HD
                        value = total[:, at : at + HD]
                        if mine:
                            value = (value + received[kind, :, here]) * mean_scale
                        out[:, here] = value


def weight_product(place, mine, mean_scale, own_heads, shared, tokens, grads, received=()):
    _, length, triple = grads[0].shape
    rows = tokens[0].shape[2]
    cols = 2 * (2 * own_heads + shared) * HD
    out = jax.ShapeDtypeStruct((rows, cols), jnp.float32)
    both = jax.ShapeDtypeStruct((3, rows, cols), jnp.float32)
    return pl.pallas_call(
        functools.partial(weight_kernel, mine, mean_scale, own_heads, shared),
        out_shape=[out] * 3 if mine else both,
        in_specs=[whole(pltpu.SMEM)] + [whole()] * (12 + len(received)),
        out_specs=[whole()] * 3 if mine else whole(),
        scratch_shapes=[pltpu.VMEM((rows, 4 * length), jnp.bfloat16)],
        compiler_params=pltpu.CompilerParams(vmem_limit_bytes=36 * MIB),
        cost_estimate=pl.CostEstimate(
            flops=8 * rows * 3 * cols * length,
            bytes_accessed=8 * length * (rows + 3 * cols) + 12 * rows * cols,
            transcendentals=0,
        ),
        name="weight_gradient_own" if mine else "weight_gradient_mate",
    )(place, *tokens, *grads, *received)


def choose_kernel(which_ref, first_ref, second_ref, out_ref):
    for which, ref in enumerate((first_ref, second_ref)):

        @pl.when(which_ref[0] == which)
        def _():
            out_ref[...] = ref[...]


def chosen_of(which, first, second):
    return pl.pallas_call(
        choose_kernel,
        out_shape=jax.ShapeDtypeStruct(first.shape, first.dtype),
        in_specs=[whole(pltpu.SMEM)] + [whole()] * 2,
        out_specs=whole(),
        compiler_params=pltpu.CompilerParams(vmem_limit_bytes=8 * MIB),
        name="choose_block",
    )(which, first, second)


def gather_body(
    normed,
    queries,
    saved_keys,
    saved_values,
    output_grad,
    view_links,
    query_weight,
    key_weight,
    value_weight,
):
    length, cols = queries.shape[2:]
    model_width = normed.shape[-1]
    rows = query_weight.shape[0]
    prompts, views, groups = (lax.axis_size(name) for name in ("dp", "view", "head"))
    mean_scale = 1.0 / (prompts * views)
    half = cols // HD // 2
    view = lax.axis_index("view")
    core = lax.rem(view, 2)
    side = view // 2
    chip = lax.axis_index("dp") * (views // 2) + side
    place = jnp.stack([core, lax.axis_index("head"), side * half, (1 - side) * half])
    place = place.astype(jnp.int32)
    arrays = tuple(a.reshape(length, cols) for a in (queries, saved_keys, saved_values, output_grad))

    own_heads, shared = half // 2, half % 2
    both = [2 * own_heads + at for at in range(shared)]
    each = [2 * step for step in range(own_heads)]
    to_x, to_cross, to_mate, own = pack(
        (
            [(BESIDE, step, 1) for step in each] + [(BESIDE, step, 0) for step in both],
            [(BESIDE, step + 1, -1) for step in each],
            [(HERE, step + 1, -1) for step in each] + [(HERE, step, 0) for step in both],
            [(HERE, step, 1) for step in each] + [(HERE, step, 0) for step in both],
        ),
        place,
        view_links,
        arrays,
    )
    x_in = moved(to_x, along_x)
    cross_in = moved(to_cross, across_x)
    mate_in = moved(to_mate, mate)
    (sent,) = after((x_in,), cross_in)
    mate_x_in = moved(sent, mate)


    flat = normed.reshape(length, model_width)

    def columns(of_chip):
        parts = [
            lax.dynamic_slice_in_dim(flat, (2 * of_chip + part) * rows, rows, axis=1)
            for part in range(2)
        ]
        return jnp.stack(parts)

    toward_x, toward_y = jnp.bitwise_xor(chip, 1), jnp.bitwise_xor(chip, 2)
    here = columns(chip)
    to_straight = columns(jnp.where(core == 0, toward_x, toward_y))
    to_crossed = columns(jnp.where(core == 0, toward_y, toward_x))
    to_corner = columns(jnp.bitwise_xor(chip, 3))
    mate_here = moved(here, only(1, mate))
    to_straight, to_crossed = after((to_straight, to_crossed), cross_in)
    normed_ahead = moved(to_straight, straight)
    normed_aside = moved(to_crossed, crossed)

    own_weights = turned_weights(place, after((query_weight, key_weight, value_weight), x_in))
    (turn,) = after((place,), own_weights)
    made = attention(turn, own_heads, (own, mate_in, x_in, cross_in, mate_x_in))
    (made,) = after((made,), normed_ahead, normed_aside)
    weights = joined_weights(place, own_weights, moved(own_weights, mate))
    ahead = moved(made, straight)
    aside = moved(made, crossed)
    inward = moved(made, only(1, mate))
    (sent,) = after((ahead,), mate_here)
    relay_x = moved(sent, only(1, along_x))
    relay_y = moved(sent, only(0, across_y))
    first = (made, inward, ahead, aside)
    second = (ahead, aside, relay_x, relay_y)

    def exchange(role, slots):
        arrived = []
        for s in range(1, groups):
            pairs = [
                ((y * views + v) * groups + z, (y * views + v) * groups + (z ^ s))
                for y in range(prompts)
                for v in range(role, views, 2)
                for z in range(groups)
            ]
            arrived.append(lax.ppermute(slots[s], ("dp", "view", "head"), pairs))
        total = sum(array.astype(jnp.float32) for array in (slots[0], *arrived))
        return total.astype(jnp.bfloat16), arrived

    def deliver(role, total, *earlier):
        def spot(y, v, z):
            return (y * views + v) * groups + z

        corners = [
            (y, v, z) for y in range(prompts) for v in range(role, views, 2) for z in range(groups)
        ]
        pairs = [(spot(y, v, z), spot(y ^ role, v ^ z, z)) for y, v, z in corners]
        beside = lax.ppermute(total, ("dp", "view", "head"), pairs)
        pairs = [
            (spot(y ^ role, v ^ z, z), spot(y ^ role, v ^ z, y * (views // 2) + v // 2))
            for y, v, z in corners
        ]
        (beside,) = after((beside,), *earlier)
        return lax.ppermute(beside, ("dp", "view", "head"), pairs)

    first_slots = input_product(place, 0, own_heads, shared, first, weights)
    first_total, _ = exchange(0, first_slots)
    (turn,) = after((place,), first_total)
    second_slots = input_product(turn, 1, own_heads, shared, second, weights)
    second_total, arrived = exchange(1, second_slots)
    (to_corner,) = after((to_corner,), *second_slots)
    tokens = (
        here,
        mate_here,
        normed_ahead,
        normed_aside,
        moved(to_corner, corner_same),
        moved(to_corner, corner_cross),
    )
    grads = (made, inward, ahead, aside, relay_x, relay_y)
    (turn,) = after((place,), second_total)
    for_mate = weight_product(turn, False, mean_scale, own_heads, shared, tokens, grads)
    from_mate = moved(for_mate, mate)
    weight_grads = weight_product(
        place, True, mean_scale, own_heads, shared, tokens, grads, (from_mate,)
    )
    landed = (deliver(0, first_total), deliver(1, second_total))
    which = jnp.bitwise_xor(lax.axis_index("head") // (views // 2), lax.axis_index("dp"))
    input_grad = chosen_of(which.reshape(1).astype(jnp.int32), *landed)
    return (
        input_grad.reshape(1, 1, length, model_width // groups),
        *weight_grads,
    )


def solution(mesh):
    prompts, views, groups = (mesh.shape[name] for name in ("dp", "view", "head"))
    loop_of_four = prompts * 2 == views and prompts * views == 2 * groups and views == groups

    def choose(*arrays):
        batch, held, length, cols = arrays[1].shape
        if loop_of_four and batch == held == 1 and length % HD == 0 and cols % (2 * HD) == 0:
            return gather_body(*arrays)
        return halo_body(*arrays)

    placed = (
        P("dp", "view", None, None),
        P("dp", "view", None, "head"),
        P("dp", "view", None, "head"),
        P("dp", "view", None, "head"),
        P("dp", "view", None, "head"),
        P("view", None),
        P(("dp", "view"), "head"),
        P(("dp", "view"), "head"),
        P(("dp", "view"), "head"),
    )
    return jax.shard_map(
        choose,
        mesh=mesh,
        in_specs=placed,
        out_specs=(
            P("dp", "view", None, "head"),
            P(("dp", "view"), "head"),
            P(("dp", "view"), "head"),
            P(("dp", "view"), "head"),
        ),
        check_vma=False,
    )
```

```python
import functools

import jax
import jax.numpy as jnp
from jax import lax
from jax.experimental import pallas as pl
from jax.experimental.pallas import tpu as pltpu
from jax.sharding import PartitionSpec as P

HD = 128
LOG2E = 1.4426950408889634
MIB = 1024 * 1024


def shifted(value, axis, steps):
    count = lax.axis_size(axis)
    pairs = [(source, (source + steps) % count) for source in range(count)]
    return lax.ppermute(value, axis, pairs)


def attend(query_rows, grad_rows, blocks, usable, scaling):
    batch_size, length, col_count = query_rows.shape
    heads_here = col_count // HD
    key_heads = blocks[..., :col_count].reshape(batch_size, 3 * length, heads_here, HD)
    value_heads = blocks[..., col_count:].reshape(batch_size, 3 * length, heads_here, HD)
    query_heads = query_rows.reshape(batch_size, length, heads_here, HD)
    grad_heads = grad_rows.reshape(batch_size, length, heads_here, HD)
    scores = (
        jnp.einsum("bshd,bthd->bhst", query_heads, key_heads, preferred_element_type=jnp.float32)
        * scaling
    )
    scores = jnp.where(usable, scores, -1e30)
    largest = jnp.max(scores, axis=-1, keepdims=True)
    powers = jnp.exp(scores - largest)
    attn_probs = powers / jnp.sum(powers, axis=-1, keepdims=True)
    probs_half = attn_probs.astype(jnp.bfloat16)
    prob_grad = jnp.einsum(
        "bshd,bthd->bhst", grad_heads, value_heads, preferred_element_type=jnp.float32
    )
    row_delta = jnp.sum(attn_probs * prob_grad, axis=-1, keepdims=True)
    score_grad = (scaling * attn_probs * (prob_grad - row_delta)).astype(jnp.bfloat16)
    query_grad = jnp.einsum(
        "bhst,bthd->bshd", score_grad, key_heads, preferred_element_type=jnp.float32
    )
    key_grad = jnp.einsum(
        "bhst,bshd->bthd", score_grad, query_heads, preferred_element_type=jnp.float32
    )
    value_grad = jnp.einsum(
        "bhst,bshd->bthd", probs_half, grad_heads, preferred_element_type=jnp.float32
    )
    query_grad = query_grad.reshape(batch_size, length, col_count)
    key_grad = key_grad.reshape(batch_size, 3, length, col_count)
    value_grad = value_grad.reshape(batch_size, 3, length, col_count)
    return (query_grad, jnp.concatenate([key_grad, value_grad], axis=-1))


def halo_body(
    normed,
    queries,
    saved_keys,
    saved_values,
    output_grad,
    view_links,
    query_weight,
    key_weight,
    value_weight,
):
    scaling = HD ** (-0.5)
    batch_size, view_count, length, col_count = queries.shape
    model_width = normed.shape[-1]
    pairs = jnp.concatenate([saved_keys, saved_values], axis=-1)
    from_lower = shifted(pairs, "view", 1)
    from_upper = shifted(pairs, "view", -1)
    extended = jnp.concatenate([from_lower, pairs, from_upper], axis=1)
    block_index = jnp.arange(3 * length) // length
    pair_grads = jnp.zeros(extended.shape, jnp.float32)
    link_flags = view_links[0] >= 0
    usable = jnp.where(
        block_index == 0, link_flags[0], jnp.where(block_index == 2, link_flags[1], True)
    )
    query_grad, block_grad = attend(queries[:, 0], output_grad[:, 0], extended, usable, scaling)
    query_grads = [query_grad]
    pair_grads = pair_grads.at[:, 0:3].add(block_grad)
    row_count = batch_size * view_count * length
    query_half = jnp.stack(query_grads, axis=1).astype(jnp.bfloat16).reshape(row_count, col_count)
    flat_input = normed.reshape(row_count, model_width)
    mean_scale = 1.0 / (lax.axis_size("dp") * batch_size * lax.axis_size("view") * view_count)
    from_lower_grads = shifted(pair_grads[:, -1:], "view", 1)
    from_upper_grads = shifted(pair_grads[:, :1], "view", -1)
    own_grads = pair_grads[:, 1 : view_count + 1]
    own_grads = own_grads.at[:, :1].add(from_lower_grads)
    own_grads = own_grads.at[:, -1:].add(from_upper_grads)
    key_half = own_grads[..., :col_count].astype(jnp.bfloat16).reshape(row_count, col_count)
    value_half = own_grads[..., col_count:].astype(jnp.bfloat16).reshape(row_count, col_count)
    all_grads = jnp.concatenate([query_half, key_half, value_half], axis=-1)
    grads_three = all_grads.reshape(row_count, 3, col_count)
    stacked = jnp.stack([query_weight, key_weight, value_weight])
    partial_input = jnp.einsum(
        "ric,ipc->rp",
        grads_three,
        lax.all_gather(stacked, ("dp", "view"), axis=1, tiled=True),
        preferred_element_type=jnp.float32,
    )
    summed_input = lax.psum_scatter(partial_input, "head", scatter_dimension=1, tiled=True)
    input_grad = summed_input.astype(jnp.bfloat16).reshape(
        batch_size, view_count, length, model_width // lax.axis_size("head")
    )
    product = lax.dot_general(
        flat_input, all_grads, (((0,), (0,)), ((), ())), preferred_element_type=jnp.float32
    )
    together = lax.psum_scatter(
        product * mean_scale, ("dp", "view"), scatter_dimension=0, tiled=True
    )
    grad_query = together[:, :col_count]
    grad_key = together[:, col_count : 2 * col_count]
    grad_value = together[:, 2 * col_count :]
    return (input_grad, grad_query, grad_key, grad_value)


def moved(value, target):
    prompts, views = lax.axis_size("dp"), lax.axis_size("view")
    pairs = []
    for y in range(prompts):
        for v in range(views):
            goal = target(y, v)
            if goal is not None:
                pairs.append((y * views + v, goal[0] * views + goal[1]))
    return lax.ppermute(value, ("dp", "view"), pairs)


def mate(y, v):
    return (y, v ^ 1)


def along_x(y, v):
    return (y, v ^ 2)


def across_x(y, v):
    return (y, v ^ 3)


def only(core, target):
    return lambda y, v: target(y, v) if v % 2 == core else None


def along_y(y, v):
    return (y ^ 1, v)


def across_y(y, v):
    return (y ^ 1, v ^ 1)


def straight(y, v):
    return along_x(y, v) if v % 2 == 0 else along_y(y, v)


def crossed(y, v):
    return across_y(y, v) if v % 2 == 0 else across_x(y, v)


def corner_same(y, v):
    return None if v % 2 == 0 else (y ^ 1, v ^ 2)


def corner_cross(y, v):
    return (y ^ 1, v ^ 3) if v % 2 == 0 else None


def lanes(start, size):
    return pl.ds(pl.multiple_of(start, HD), size)


def whole(space=pltpu.VMEM):
    return pl.BlockSpec(memory_space=space)


def dot_last(a, b):
    return lax.dot_general(a, b, (((1,), (1,)), ((), ())), preferred_element_type=jnp.float32)


def dot_first(a, b):
    return lax.dot_general(a, b, (((0,), (0,)), ((), ())), preferred_element_type=jnp.float32)


def dot(a, b):
    return jnp.dot(a, b, preferred_element_type=jnp.float32)


def after(values, *earlier):
    return lax.optimization_barrier((tuple(values), tuple(earlier)))[0]


CORE, PLANE, HERE, BESIDE = range(4)
FLAG_ROWS = 16


def pack_kernel(picks, place_ref, links_ref, q_ref, k_ref, v_ref, g_ref, *out_refs):
    length = q_ref.shape[0]
    row = lax.broadcasted_iota(jnp.int32, (FLAG_ROWS, HD), 0)
    gaps = [jnp.where(links_ref[0, side] >= 0, 0.0, 1.0).astype(jnp.float32) for side in range(2)]
    flags = jnp.where(row < FLAG_ROWS // 2, gaps[0], gaps[1])
    for heads, out_ref in zip(picks, out_refs):
        for at, (base, step, sign) in enumerate(heads):
            head = place_ref[base] + step + sign * place_ref[CORE]
            for kind, source in enumerate((q_ref, k_ref, v_ref, g_ref)):
                out_ref[at, kind * length : (kind + 1) * length] = source[:, lanes(head * HD, HD)]
            out_ref[at, 4 * length : 4 * length + FLAG_ROWS] = flags.astype(out_ref.dtype)


def pack(picks, place, links, arrays):
    length = arrays[0].shape[0]
    height = 4 * length + FLAG_ROWS
    return pl.pallas_call(
        functools.partial(pack_kernel, picks),
        out_shape=[
            jax.ShapeDtypeStruct((len(heads), height, HD), jnp.bfloat16) for heads in picks
        ],
        in_specs=[whole(pltpu.SMEM)] * 2 + [whole()] * 4,
        out_specs=[whole()] * len(picks),
        name="pack_heads",
    )(place, links, *arrays)


def one_head(scaling, core, xs, length, keys, values, key_sums, value_sums):
    factor = scaling * LOG2E

    def rows(e, kind):
        return xs[e][kind * length : (kind + 1) * length]

    def gap(e, side):
        at = 4 * length + side * (FLAG_ROWS // 2)
        flags = xs[e][at : at + FLAG_ROWS // 2].astype(jnp.float32)[0:1]
        return jnp.concatenate([flags] * (length // HD), axis=1) * 1e30

    for at in range(6):
        keys[at * length : (at + 1) * length] = rows((at + 3) % 4, 1)
        values[at * length : (at + 1) * length] = rows((at + 3) % 4, 2)
    query_grads = []
    for e in range(4):
        blocks = slice(e * length, (e + 3) * length)
        before, behind = gap(e, 0), gap(e, 1)
        far_below = jnp.where(core == 0, before, behind)
        far_above = jnp.where(core == 0, behind, before)
        q, g = rows(e, 0), rows(e, 3)
        near = keys[blocks]
        scores = dot_last(near, q)
        scores = [scores[at * length : (at + 1) * length] for at in range(3)]
        tops = [jnp.max(part, axis=0, keepdims=True) for part in scores]
        top = jnp.maximum(tops[1], jnp.maximum(tops[0] - far_below, tops[2] - far_above))
        offsets = (top + far_below, top, top + far_above)
        powers = [jnp.exp2((part - o) * factor) for part, o in zip(scores, offsets)]
        inverse = 1.0 / sum(jnp.sum(p, axis=0, keepdims=True) for p in powers)
        prob_grads = dot_last(values[blocks], g)
        prob_grads = [prob_grads[at * length : (at + 1) * length] for at in range(3)]
        delta = inverse * sum(
            jnp.sum(p * d, axis=0, keepdims=True) for p, d in zip(powers, prob_grads)
        )
        probs = [p * inverse for p in powers]
        score_grad = jnp.concatenate(
            [
                (p * scaling * (d - delta)).astype(jnp.bfloat16)
                for p, d in zip(probs, prob_grads)
            ],
            axis=0,
        )
        probs_half = jnp.concatenate([p.astype(jnp.bfloat16) for p in probs], axis=0)
        query_grads.append(dot_first(score_grad, near))
        for sums, part in ((key_sums, dot(score_grad, q)), (value_sums, dot(probs_half, g))):
            if e == 0:
                sums[blocks] = part
            else:
                held = slice(e * length, (e + 2) * length)
                sums[held] += part[: 2 * length]
                sums[(e + 2) * length : (e + 3) * length] = part[2 * length :]

    def by_view(sums):
        parts = [sums[at * length : (at + 1) * length] for at in range(6)]
        return (parts[1] + parts[5], parts[2], parts[3], parts[0] + parts[4])

    return query_grads, by_view(key_sums), by_view(value_sums)


def attention_kernel(scaling, own_heads, place_ref, *refs):
    own, mate_in, x_in, cross_in, mate_x_in = refs[:5]
    out_ref, keys, values, key_sums, value_sums = refs[5:]
    length = out_ref.shape[1]
    heads = own.shape[0]
    for head in range(heads):
        shared = head >= own_heads
        far = mate_x_in if shared else cross_in
        xs = [own.at[head], mate_in.at[head], x_in.at[head], far.at[head]]
        grads = one_head(
            scaling, place_ref[CORE], xs, length, keys, values, key_sums, value_sums
        )
        for e in range(4):
            if shared and e % 2 == 1:
                continue
            at = 4 * own_heads + e // 2 if shared else 4 * head + e
            for kind in range(3):
                out_ref[at, :, kind * HD : (kind + 1) * HD] = grads[kind][e].astype(out_ref.dtype)


def attention(place, own_heads, sources):
    heads, height, _ = sources[0].shape
    length = (height - FLAG_ROWS) // 4
    held = 4 * own_heads + 2 * (heads - own_heads)
    return pl.pallas_call(
        functools.partial(attention_kernel, HD ** (-0.5), own_heads),
        out_shape=jax.ShapeDtypeStruct((held, length, 3 * HD), jnp.bfloat16),
        in_specs=[whole(pltpu.SMEM)] + [whole()] * 5,
        out_specs=whole(),
        scratch_shapes=[pltpu.VMEM((6 * length, HD), jnp.bfloat16)] * 2
        + [pltpu.VMEM((6 * length, HD), jnp.float32)] * 2,
        compiler_params=pltpu.CompilerParams(vmem_limit_bytes=12 * MIB),
        cost_estimate=pl.CostEstimate(
            flops=heads * 4 * 5 * 2 * length * 3 * length * HD * 2,
            bytes_accessed=heads * 2 * length * 7 * HD * 4,
            transcendentals=heads * 12 * length * length,
        ),
        name="attention_gradients",
    )(place, *sources)


def turn_kernel(place_ref, q_ref, k_ref, v_ref, out_ref):
    half = q_ref.shape[1] // HD // 2
    for side, base in enumerate((HERE, BESIDE)):
        for head in range(half):
            for kind, source in enumerate((q_ref, k_ref, v_ref)):
                at = ((side * half + head) * 3 + kind) * HD
                out_ref[at : at + HD] = source[:, lanes((place_ref[base] + head) * HD, HD)].T


def turned_weights(place, weights):
    rows, cols = weights[0].shape
    return pl.pallas_call(
        turn_kernel,
        out_shape=jax.ShapeDtypeStruct((3 * cols, rows), jnp.bfloat16),
        in_specs=[whole(pltpu.SMEM)] + [whole()] * 3,
        out_specs=whole(),
        compiler_params=pltpu.CompilerParams(vmem_limit_bytes=8 * MIB),
        name="turn_weights",
    )(place, *weights)


def join_kernel(place_ref, own_ref, mate_ref, out_ref):
    core = place_ref[CORE]
    rows = own_ref.shape[1]
    out_ref[:, lanes(core * rows, rows)] = own_ref[...]
    out_ref[:, lanes((1 - core) * rows, rows)] = mate_ref[...]


def joined_weights(place, own_weights, mate_weights):
    depth, rows = own_weights.shape
    return pl.pallas_call(
        join_kernel,
        out_shape=jax.ShapeDtypeStruct((depth, 2 * rows), jnp.bfloat16),
        in_specs=[whole(pltpu.SMEM)] + [whole()] * 2,
        out_specs=whole(),
        compiler_params=pltpu.CompilerParams(vmem_limit_bytes=12 * MIB),
        name="join_weights",
    )(place, own_weights, mate_weights)


def gathered(role, own_heads, shared, refs):
    sides = []
    for side in range(2):
        pieces = []
        for head in range(own_heads):
            for maker in range(2):
                k = 2 * side + (maker ^ role)
                pieces.append([refs[k][4 * head + (e ^ k)] for e in range(4)])
        for at in range(shared):
            rows = []
            for e in range(4):
                k = 2 * side + e % 2
                rows.append(refs[k][4 * own_heads + 2 * at + (e // 2 ^ side)])
            pieces.append(rows)
        sides.append(
            jnp.concatenate([jnp.concatenate(rows, axis=0) for rows in pieces], axis=1)
        )
    return sides


def input_kernel(own_heads, shared, place_ref, *refs):
    grad_refs, weights, out_refs, total = refs[:6], refs[6], refs[7:-1], refs[-1]
    made, inward, ahead, aside, relay_x, relay_y = grad_refs
    grads = ((made, inward, ahead, aside), (ahead, aside, relay_x, relay_y))
    length = out_refs[0].shape[0]
    for role in range(2):

        @pl.when(place_ref[CORE] == role)
        def _():
            left = jnp.concatenate(gathered(role, own_heads, shared, grads[role]), axis=1)
            for e in range(4):
                product = dot(left[e * length : (e + 1) * length], weights[...])
                total[e] = product.astype(total.dtype)

    for s, out_ref in enumerate(out_refs):
        out_ref[...] = total[jnp.bitwise_xor(place_ref[PLANE], s)]


def input_product(place, own_heads, shared, grads, weights):
    _, length, _ = grads[0].shape
    depth, rows = weights.shape
    out = jax.ShapeDtypeStruct((length, rows), jnp.bfloat16)
    return pl.pallas_call(
        functools.partial(input_kernel, own_heads, shared),
        out_shape=[out] * 4,
        in_specs=[whole(pltpu.SMEM)] + [whole()] * 7,
        out_specs=[whole()] * 4,
        scratch_shapes=[pltpu.VMEM((4, length, rows), jnp.bfloat16)],
        compiler_params=pltpu.CompilerParams(vmem_limit_bytes=24 * MIB),
        cost_estimate=pl.CostEstimate(
            flops=8 * length * rows * depth,
            bytes_accessed=8 * length * (rows + depth) + 2 * rows * depth,
            transcendentals=0,
        ),
        name="input_gradient",
    )(place, *grads, weights)


def weight_kernel(mine, mean_scale, own_heads, shared, place_ref, *refs):
    own, mate_in, first, second, corner, corner_far = refs[:6]
    made, inward, ahead, aside, relay_x, relay_y = refs[6:12]
    if mine:
        received, out_refs, turned = refs[12], refs[13:16], refs[16]
    else:
        received, out_refs, turned = None, [refs[12].at[kind] for kind in range(3)], refs[13]
    core = place_ref[CORE]
    length = own.shape[1]
    part = core if mine else 1 - core
    tokens = ((own, mate_in, first, second), (first, second, corner, corner_far))
    grads = ((made, inward, ahead, aside), (ahead, aside, relay_x, relay_y))
    for role in range(2):

        @pl.when(core == role)
        def _():
            for e, source in enumerate(tokens[role]):
                turned[:, e * length : (e + 1) * length] = source[part].T
            sides = gathered(role, own_heads, shared, grads[role])
            for base, side in zip((HERE, BESIDE), sides):
                total = dot(turned[...], side)
                for head in range(side.shape[1] // (3 * HD)):
                    here = lanes((place_ref[base] + head) * HD, HD)
                    for kind, out in enumerate(out_refs):
                        at = (head * 3 + kind) * HD
                        value = total[:, at : at + HD]
                        if mine:
                            value = (value + received[kind, :, here]) * mean_scale
                        out[:, here] = value


def weight_product(place, mine, mean_scale, own_heads, shared, tokens, grads, received=()):
    _, length, triple = grads[0].shape
    rows = tokens[0].shape[2]
    cols = 2 * (2 * own_heads + shared) * HD
    out = jax.ShapeDtypeStruct((rows, cols), jnp.float32)
    both = jax.ShapeDtypeStruct((3, rows, cols), jnp.float32)
    return pl.pallas_call(
        functools.partial(weight_kernel, mine, mean_scale, own_heads, shared),
        out_shape=[out] * 3 if mine else both,
        in_specs=[whole(pltpu.SMEM)] + [whole()] * (12 + len(received)),
        out_specs=[whole()] * 3 if mine else whole(),
        scratch_shapes=[pltpu.VMEM((rows, 4 * length), jnp.bfloat16)],
        compiler_params=pltpu.CompilerParams(vmem_limit_bytes=24 * MIB),
        cost_estimate=pl.CostEstimate(
            flops=8 * rows * 3 * cols * length,
            bytes_accessed=8 * length * (rows + 3 * cols) + 12 * rows * cols,
            transcendentals=0,
        ),
        name="weight_gradient_own" if mine else "weight_gradient_mate",
    )(place, *tokens, *grads, *received)


def gather_body(
    normed,
    queries,
    saved_keys,
    saved_values,
    output_grad,
    view_links,
    query_weight,
    key_weight,
    value_weight,
):
    length, cols = queries.shape[2:]
    model_width = normed.shape[-1]
    rows = query_weight.shape[0]
    prompts, views, groups = (lax.axis_size(name) for name in ("dp", "view", "head"))
    mean_scale = 1.0 / (prompts * views)
    half = cols // HD // 2
    view = lax.axis_index("view")
    core = lax.rem(view, 2)
    side = view // 2
    chip = lax.axis_index("dp") * (views // 2) + side
    place = jnp.stack([core, lax.axis_index("head"), side * half, (1 - side) * half])
    place = place.astype(jnp.int32)
    arrays = tuple(a.reshape(length, cols) for a in (queries, saved_keys, saved_values, output_grad))

    own_heads, shared = half // 2, half % 2
    both = [2 * own_heads + at for at in range(shared)]
    each = [2 * step for step in range(own_heads)]
    to_x, to_cross, to_mate, own = pack(
        (
            [(BESIDE, step, 1) for step in each] + [(BESIDE, step, 0) for step in both],
            [(BESIDE, step + 1, -1) for step in each],
            [(HERE, step + 1, -1) for step in each] + [(HERE, step, 0) for step in both],
            [(HERE, step, 1) for step in each] + [(HERE, step, 0) for step in both],
        ),
        place,
        view_links,
        arrays,
    )
    x_in = moved(to_x, along_x)
    cross_in = moved(to_cross, across_x)
    mate_in = moved(to_mate, mate)
    (sent,) = after((x_in,), cross_in)
    mate_x_in = moved(sent, mate)


    flat = normed.reshape(length, model_width)

    def columns(of_chip):
        parts = [
            lax.dynamic_slice_in_dim(flat, (2 * of_chip + part) * rows, rows, axis=1)
            for part in range(2)
        ]
        return jnp.stack(parts)

    toward_x, toward_y = jnp.bitwise_xor(chip, 1), jnp.bitwise_xor(chip, 2)
    here = columns(chip)
    to_straight = columns(jnp.where(core == 0, toward_x, toward_y))
    to_crossed = columns(jnp.where(core == 0, toward_y, toward_x))
    to_corner = columns(jnp.bitwise_xor(chip, 3))
    mate_here = moved(here, only(1, mate))
    to_straight, to_crossed = after((to_straight, to_crossed), cross_in)
    normed_ahead = moved(to_straight, straight)
    normed_aside = moved(to_crossed, crossed)

    own_weights = turned_weights(place, after((query_weight, key_weight, value_weight), x_in))
    (turn,) = after((place,), own_weights)
    made = attention(turn, own_heads, (own, mate_in, x_in, cross_in, mate_x_in))
    (made,) = after((made,), normed_ahead, normed_aside)
    ahead = moved(made, straight)
    inward = moved(made, only(1, mate))
    (sent,) = after((made,), ahead)
    aside = moved(sent, crossed)
    relay_x = moved(ahead, only(1, along_x))
    relay_y = moved(ahead, only(0, across_y))
    weights = joined_weights(place, own_weights, moved(own_weights, mate))
    grads = (made, inward, ahead, aside, relay_x, relay_y)

    slots = input_product(place, own_heads, shared, grads, weights)
    arrived = [
        lax.ppermute(slots[s], "head", [(z, z ^ s) for z in range(groups)])
        for s in range(1, groups)
    ]
    (to_corner,) = after((to_corner,), *slots)
    tokens = (
        here,
        mate_here,
        normed_ahead,
        normed_aside,
        moved(to_corner, corner_same),
        moved(to_corner, corner_cross),
    )
    (turn,) = after((place,), arrived[1])
    for_mate = weight_product(turn, False, mean_scale, own_heads, shared, tokens, grads)
    from_mate = moved(for_mate, mate)
    weight_grads = weight_product(
        place, True, mean_scale, own_heads, shared, tokens, grads, (from_mate,)
    )
    (kept,) = after((slots[0],), weight_grads[0])
    total = sum(array.astype(jnp.float32) for array in (kept, *arrived))
    total = total.astype(jnp.bfloat16)

    def spot(y, v, z):
        return (y * views + v) * groups + z

    corners = [(y, v, z) for y in range(prompts) for v in range(views) for z in range(groups)]
    beside = lax.ppermute(
        total,
        ("dp", "view", "head"),
        [(spot(y, v, z), spot(y ^ (v % 2), v ^ z, z)) for y, v, z in corners],
    )
    input_grad = lax.ppermute(
        beside,
        ("dp", "view", "head"),
        [
            (
                spot(y ^ (v % 2), v ^ z, z),
                spot(y ^ (v % 2), v ^ z, y * (views // 2) + v // 2),
            )
            for y, v, z in corners
        ],
    )

    return (
        input_grad.reshape(1, 1, length, model_width // groups),
        *weight_grads,
    )


def solution(mesh):
    prompts, views, groups = (mesh.shape[name] for name in ("dp", "view", "head"))
    loop_of_four = prompts * 2 == views and prompts * views == 2 * groups and views == groups

    def choose(*arrays):
        batch, held, length, cols = arrays[1].shape
        if loop_of_four and batch == held == 1 and length % HD == 0 and cols % (2 * HD) == 0:
            return gather_body(*arrays)
        return halo_body(*arrays)

    placed = (
        P("dp", "view", None, None),
        P("dp", "view", None, "head"),
        P("dp", "view", None, "head"),
        P("dp", "view", None, "head"),
        P("dp", "view", None, "head"),
        P("view", None),
        P(("dp", "view"), "head"),
        P(("dp", "view"), "head"),
        P(("dp", "view"), "head"),
    )
    return jax.shard_map(
        choose,
        mesh=mesh,
        in_specs=placed,
        out_specs=(
            P("dp", "view", None, "head"),
            P(("dp", "view"), "head"),
            P(("dp", "view"), "head"),
            P(("dp", "view"), "head"),
        ),
        check_vma=False,
    )
```

```python
import functools

import jax
import jax.numpy as jnp
from jax import lax
from jax.experimental import pallas as pl
from jax.experimental.pallas import tpu as pltpu
from jax.sharding import PartitionSpec as P

HD = 128
LOG2E = 1.4426950408889634
MIB = 1024 * 1024


def shifted(value, axis, steps):
    count = lax.axis_size(axis)
    pairs = [(source, (source + steps) % count) for source in range(count)]
    return lax.ppermute(value, axis, pairs)


def attend(query_rows, grad_rows, blocks, usable, scaling):
    batch_size, length, col_count = query_rows.shape
    heads_here = col_count // HD
    key_heads = blocks[..., :col_count].reshape(batch_size, 3 * length, heads_here, HD)
    value_heads = blocks[..., col_count:].reshape(batch_size, 3 * length, heads_here, HD)
    query_heads = query_rows.reshape(batch_size, length, heads_here, HD)
    grad_heads = grad_rows.reshape(batch_size, length, heads_here, HD)
    scores = (
        jnp.einsum("bshd,bthd->bhst", query_heads, key_heads, preferred_element_type=jnp.float32)
        * scaling
    )
    scores = jnp.where(usable, scores, -1e30)
    largest = jnp.max(scores, axis=-1, keepdims=True)
    powers = jnp.exp(scores - largest)
    attn_probs = powers / jnp.sum(powers, axis=-1, keepdims=True)
    probs_half = attn_probs.astype(jnp.bfloat16)
    prob_grad = jnp.einsum(
        "bshd,bthd->bhst", grad_heads, value_heads, preferred_element_type=jnp.float32
    )
    row_delta = jnp.sum(attn_probs * prob_grad, axis=-1, keepdims=True)
    score_grad = (scaling * attn_probs * (prob_grad - row_delta)).astype(jnp.bfloat16)
    query_grad = jnp.einsum(
        "bhst,bthd->bshd", score_grad, key_heads, preferred_element_type=jnp.float32
    )
    key_grad = jnp.einsum(
        "bhst,bshd->bthd", score_grad, query_heads, preferred_element_type=jnp.float32
    )
    value_grad = jnp.einsum(
        "bhst,bshd->bthd", probs_half, grad_heads, preferred_element_type=jnp.float32
    )
    query_grad = query_grad.reshape(batch_size, length, col_count)
    key_grad = key_grad.reshape(batch_size, 3, length, col_count)
    value_grad = value_grad.reshape(batch_size, 3, length, col_count)
    return (query_grad, jnp.concatenate([key_grad, value_grad], axis=-1))


def halo_body(
    normed,
    queries,
    saved_keys,
    saved_values,
    output_grad,
    view_links,
    query_weight,
    key_weight,
    value_weight,
):
    scaling = HD ** (-0.5)
    batch_size, view_count, length, col_count = queries.shape
    model_width = normed.shape[-1]
    pairs = jnp.concatenate([saved_keys, saved_values], axis=-1)
    from_lower = shifted(pairs, "view", 1)
    from_upper = shifted(pairs, "view", -1)
    extended = jnp.concatenate([from_lower, pairs, from_upper], axis=1)
    block_index = jnp.arange(3 * length) // length
    pair_grads = jnp.zeros(extended.shape, jnp.float32)
    link_flags = view_links[0] >= 0
    usable = jnp.where(
        block_index == 0, link_flags[0], jnp.where(block_index == 2, link_flags[1], True)
    )
    query_grad, block_grad = attend(queries[:, 0], output_grad[:, 0], extended, usable, scaling)
    query_grads = [query_grad]
    pair_grads = pair_grads.at[:, 0:3].add(block_grad)
    row_count = batch_size * view_count * length
    query_half = jnp.stack(query_grads, axis=1).astype(jnp.bfloat16).reshape(row_count, col_count)
    flat_input = normed.reshape(row_count, model_width)
    mean_scale = 1.0 / (lax.axis_size("dp") * batch_size * lax.axis_size("view") * view_count)
    from_lower_grads = shifted(pair_grads[:, -1:], "view", 1)
    from_upper_grads = shifted(pair_grads[:, :1], "view", -1)
    own_grads = pair_grads[:, 1 : view_count + 1]
    own_grads = own_grads.at[:, :1].add(from_lower_grads)
    own_grads = own_grads.at[:, -1:].add(from_upper_grads)
    key_half = own_grads[..., :col_count].astype(jnp.bfloat16).reshape(row_count, col_count)
    value_half = own_grads[..., col_count:].astype(jnp.bfloat16).reshape(row_count, col_count)
    all_grads = jnp.concatenate([query_half, key_half, value_half], axis=-1)
    grads_three = all_grads.reshape(row_count, 3, col_count)
    stacked = jnp.stack([query_weight, key_weight, value_weight])
    partial_input = jnp.einsum(
        "ric,ipc->rp",
        grads_three,
        lax.all_gather(stacked, ("dp", "view"), axis=1, tiled=True),
        preferred_element_type=jnp.float32,
    )
    summed_input = lax.psum_scatter(partial_input, "head", scatter_dimension=1, tiled=True)
    input_grad = summed_input.astype(jnp.bfloat16).reshape(
        batch_size, view_count, length, model_width // lax.axis_size("head")
    )
    product = lax.dot_general(
        flat_input, all_grads, (((0,), (0,)), ((), ())), preferred_element_type=jnp.float32
    )
    together = lax.psum_scatter(
        product * mean_scale, ("dp", "view"), scatter_dimension=0, tiled=True
    )
    grad_query = together[:, :col_count]
    grad_key = together[:, col_count : 2 * col_count]
    grad_value = together[:, 2 * col_count :]
    return (input_grad, grad_query, grad_key, grad_value)


def moved(value, target):
    prompts, views = lax.axis_size("dp"), lax.axis_size("view")
    pairs = []
    for y in range(prompts):
        for v in range(views):
            goal = target(y, v)
            if goal is not None:
                pairs.append((y * views + v, goal[0] * views + goal[1]))
    return lax.ppermute(value, ("dp", "view"), pairs)


def mate(y, v):
    return (y, v ^ 1)


def along_x(y, v):
    return (y, v ^ 2)


def across_x(y, v):
    return (y, v ^ 3)


def only(core, target):
    return lambda y, v: target(y, v) if v % 2 == core else None


def along_y(y, v):
    return (y ^ 1, v)


def across_y(y, v):
    return (y ^ 1, v ^ 1)


def straight(y, v):
    return along_x(y, v) if v % 2 == 0 else along_y(y, v)


def crossed(y, v):
    return across_y(y, v) if v % 2 == 0 else across_x(y, v)


def corner_same(y, v):
    return None if v % 2 == 0 else (y ^ 1, v ^ 2)


def corner_cross(y, v):
    return (y ^ 1, v ^ 3) if v % 2 == 0 else None


def lanes(start, size):
    return pl.ds(pl.multiple_of(start, HD), size)


def whole(space=pltpu.VMEM):
    return pl.BlockSpec(memory_space=space)


def dot_last(a, b):
    return lax.dot_general(a, b, (((1,), (1,)), ((), ())), preferred_element_type=jnp.float32)


def dot_first(a, b):
    return lax.dot_general(a, b, (((0,), (0,)), ((), ())), preferred_element_type=jnp.float32)


def dot(a, b):
    return jnp.dot(a, b, preferred_element_type=jnp.float32)


def after(values, *earlier):
    return lax.optimization_barrier((tuple(values), tuple(earlier)))[0]


CORE, PLANE, HERE, BESIDE = range(4)
FLAG_ROWS = 16


def pack_kernel(picks, place_ref, links_ref, q_ref, k_ref, v_ref, g_ref, *out_refs):
    length = q_ref.shape[0]
    row = lax.broadcasted_iota(jnp.int32, (FLAG_ROWS, HD), 0)
    gaps = [jnp.where(links_ref[0, side] >= 0, 0.0, 1.0).astype(jnp.float32) for side in range(2)]
    flags = jnp.where(row < FLAG_ROWS // 2, gaps[0], gaps[1])
    for heads, out_ref in zip(picks, out_refs):
        for at, (base, step, sign) in enumerate(heads):
            head = place_ref[base] + step + sign * place_ref[CORE]
            for kind, source in enumerate((q_ref, k_ref, v_ref, g_ref)):
                out_ref[at, kind * length : (kind + 1) * length] = source[:, lanes(head * HD, HD)]
            out_ref[at, 4 * length : 4 * length + FLAG_ROWS] = flags.astype(out_ref.dtype)


def pack(picks, place, links, arrays):
    length = arrays[0].shape[0]
    height = 4 * length + FLAG_ROWS
    return pl.pallas_call(
        functools.partial(pack_kernel, picks),
        out_shape=[
            jax.ShapeDtypeStruct((len(heads), height, HD), jnp.bfloat16) for heads in picks
        ],
        in_specs=[whole(pltpu.SMEM)] * 2 + [whole()] * 4,
        out_specs=[whole()] * len(picks),
        name="pack_heads",
    )(place, links, *arrays)


def one_head(scaling, core, xs, length, keys, values, key_sums, value_sums):
    factor = scaling * LOG2E

    def rows(e, kind):
        return xs[e][kind * length : (kind + 1) * length]

    def gap(e, side):
        at = 4 * length + side * (FLAG_ROWS // 2)
        flags = xs[e][at : at + FLAG_ROWS // 2].astype(jnp.float32)[0:1]
        return jnp.concatenate([flags] * (length // HD), axis=1) * 1e30

    for at in range(6):
        keys[at * length : (at + 1) * length] = rows((at + 3) % 4, 1)
        values[at * length : (at + 1) * length] = rows((at + 3) % 4, 2)
    query_grads = []
    for e in range(4):
        blocks = slice(e * length, (e + 3) * length)
        before, behind = gap(e, 0), gap(e, 1)
        far_below = jnp.where(core == 0, before, behind)
        far_above = jnp.where(core == 0, behind, before)
        q, g = rows(e, 0), rows(e, 3)
        near = keys[blocks]
        scores = dot_last(near, q)
        scores = [scores[at * length : (at + 1) * length] for at in range(3)]
        tops = [jnp.max(part, axis=0, keepdims=True) for part in scores]
        top = jnp.maximum(tops[1], jnp.maximum(tops[0] - far_below, tops[2] - far_above))
        offsets = (top + far_below, top, top + far_above)
        powers = [jnp.exp2((part - o) * factor) for part, o in zip(scores, offsets)]
        inverse = 1.0 / sum(jnp.sum(p, axis=0, keepdims=True) for p in powers)
        prob_grads = dot_last(values[blocks], g)
        prob_grads = [prob_grads[at * length : (at + 1) * length] for at in range(3)]
        delta = inverse * sum(
            jnp.sum(p * d, axis=0, keepdims=True) for p, d in zip(powers, prob_grads)
        )
        probs = [p * inverse for p in powers]
        score_grad = jnp.concatenate(
            [
                (p * scaling * (d - delta)).astype(jnp.bfloat16)
                for p, d in zip(probs, prob_grads)
            ],
            axis=0,
        )
        probs_half = jnp.concatenate([p.astype(jnp.bfloat16) for p in probs], axis=0)
        query_grads.append(dot_first(score_grad, near))
        for sums, part in ((key_sums, dot(score_grad, q)), (value_sums, dot(probs_half, g))):
            if e == 0:
                sums[blocks] = part
            else:
                held = slice(e * length, (e + 2) * length)
                sums[held] += part[: 2 * length]
                sums[(e + 2) * length : (e + 3) * length] = part[2 * length :]

    def by_view(sums):
        parts = [sums[at * length : (at + 1) * length] for at in range(6)]
        return (parts[1] + parts[5], parts[2], parts[3], parts[0] + parts[4])

    return query_grads, by_view(key_sums), by_view(value_sums)


def attention_kernel(scaling, kept, place_ref, own, mate_in, x_in, far_in, *refs):
    out_ref, keys, values, key_sums, value_sums = refs
    length = out_ref.shape[1]
    heads = own.shape[0]
    for head in range(heads):
        xs = [own.at[head], mate_in.at[head], x_in.at[head], far_in.at[head]]
        grads = one_head(
            scaling, place_ref[CORE], xs, length, keys, values, key_sums, value_sums
        )
        for at, e in enumerate(kept):
            for kind in range(3):
                out_ref[len(kept) * head + at, :, kind * HD : (kind + 1) * HD] = grads[kind][
                    e
                ].astype(out_ref.dtype)


def attention(place, kept, sources):
    heads, height, _ = sources[0].shape
    length = (height - FLAG_ROWS) // 4
    return pl.pallas_call(
        functools.partial(attention_kernel, HD ** (-0.5), kept),
        out_shape=jax.ShapeDtypeStruct((len(kept) * heads, length, 3 * HD), jnp.bfloat16),
        in_specs=[whole(pltpu.SMEM)] + [whole()] * 4,
        out_specs=whole(),
        scratch_shapes=[pltpu.VMEM((6 * length, HD), jnp.bfloat16)] * 2
        + [pltpu.VMEM((6 * length, HD), jnp.float32)] * 2,
        compiler_params=pltpu.CompilerParams(vmem_limit_bytes=12 * MIB),
        cost_estimate=pl.CostEstimate(
            flops=heads * 4 * 5 * 2 * length * 3 * length * HD * 2,
            bytes_accessed=heads * 2 * length * 7 * HD * 4,
            transcendentals=heads * 12 * length * length,
        ),
        name="attention_gradients",
    )(place, *sources)


def turn_kernel(place_ref, q_ref, k_ref, v_ref, out_ref):
    half = q_ref.shape[1] // HD // 2
    for side, base in enumerate((HERE, BESIDE)):
        for head in range(half):
            for kind, source in enumerate((q_ref, k_ref, v_ref)):
                at = ((side * half + head) * 3 + kind) * HD
                out_ref[at : at + HD] = source[:, lanes((place_ref[base] + head) * HD, HD)].T


def turned_weights(place, weights):
    rows, cols = weights[0].shape
    return pl.pallas_call(
        turn_kernel,
        out_shape=jax.ShapeDtypeStruct((3 * cols, rows), jnp.bfloat16),
        in_specs=[whole(pltpu.SMEM)] + [whole()] * 3,
        out_specs=whole(),
        compiler_params=pltpu.CompilerParams(vmem_limit_bytes=8 * MIB),
        name="turn_weights",
    )(place, *weights)


def join_kernel(place_ref, own_ref, mate_ref, out_ref):
    core = place_ref[CORE]
    rows = own_ref.shape[1]
    out_ref[:, lanes(core * rows, rows)] = own_ref[...]
    out_ref[:, lanes((1 - core) * rows, rows)] = mate_ref[...]


def joined_weights(place, own_weights, mate_weights):
    depth, rows = own_weights.shape
    return pl.pallas_call(
        join_kernel,
        out_shape=jax.ShapeDtypeStruct((depth, 2 * rows), jnp.bfloat16),
        in_specs=[whole(pltpu.SMEM)] + [whole()] * 2,
        out_specs=whole(),
        compiler_params=pltpu.CompilerParams(vmem_limit_bytes=12 * MIB),
        name="join_weights",
    )(place, own_weights, mate_weights)


def gathered(role, refs):
    sides = []
    for side in range(2):
        pieces = []
        for head in range(refs[0][0].shape[0] // 4):
            for maker in range(2):
                k = 2 * side + (maker ^ role)
                pieces.append([refs[k][0][4 * head + (e ^ k)] for e in range(4)])
        for at in range(refs[0][1].shape[0] // 2 if len(refs[0]) > 1 else 0):
            rows = []
            for e in range(4):
                k = 2 * side + e % 2
                rows.append(refs[k][1][2 * at + (e // 2 ^ side)])
            pieces.append(rows)
        sides.append(
            jnp.concatenate([jnp.concatenate(rows, axis=0) for rows in pieces], axis=1)
        )
    return sides


def by_role(refs, parts):
    made, inward, ahead, aside, relay_x, relay_y = [
        refs[at * parts : (at + 1) * parts] for at in range(6)
    ]
    return ((made, inward, ahead, aside), (ahead, aside, relay_x, relay_y))


def input_kernel(parts, place_ref, *refs):
    weights, out_refs, total = refs[6 * parts], refs[6 * parts + 1 : -1], refs[-1]
    length = out_refs[0].shape[0]
    for role, grads in enumerate(by_role(refs, parts)):

        @pl.when(place_ref[CORE] == role)
        def _():
            left = jnp.concatenate(gathered(role, grads), axis=1)
            for e in range(4):
                product = dot(left[e * length : (e + 1) * length], weights[...])
                total[e] = product.astype(total.dtype)

    for s, out_ref in enumerate(out_refs):
        out_ref[...] = total[jnp.bitwise_xor(place_ref[PLANE], s)]


def input_product(place, grads, weights):
    _, length, _ = grads[0].shape
    depth, rows = weights.shape
    out = jax.ShapeDtypeStruct((length, rows), jnp.bfloat16)
    return pl.pallas_call(
        functools.partial(input_kernel, len(grads) // 6),
        out_shape=[out] * 4,
        in_specs=[whole(pltpu.SMEM)] + [whole()] * (len(grads) + 1),
        out_specs=[whole()] * 4,
        scratch_shapes=[pltpu.VMEM((4, length, rows), jnp.bfloat16)],
        compiler_params=pltpu.CompilerParams(vmem_limit_bytes=24 * MIB),
        cost_estimate=pl.CostEstimate(
            flops=8 * length * rows * depth,
            bytes_accessed=8 * length * (rows + depth) + 2 * rows * depth,
            transcendentals=0,
        ),
        name="input_gradient",
    )(place, *grads, weights)


def weight_kernel(mine, mean_scale, parts, place_ref, *refs):
    own, mate_in, first, second, corner, corner_far = refs[:6]
    grad_refs, refs = refs[6 : 6 + 6 * parts], refs[6 + 6 * parts :]
    if mine:
        received, out_refs, turned = refs[0], refs[1:4], refs[4]
    else:
        received, out_refs, turned = None, [refs[0].at[kind] for kind in range(3)], refs[1]
    core = place_ref[CORE]
    length = own.shape[1]
    part = core if mine else 1 - core
    tokens = ((own, mate_in, first, second), (first, second, corner, corner_far))
    for role, grads in enumerate(by_role(grad_refs, parts)):

        @pl.when(core == role)
        def _():
            for e, source in enumerate(tokens[role]):
                turned[:, e * length : (e + 1) * length] = source[part].T
            for base, side in zip((HERE, BESIDE), gathered(role, grads)):
                total = dot(turned[...], side)
                for head in range(side.shape[1] // (3 * HD)):
                    here = lanes((place_ref[base] + head) * HD, HD)
                    for kind, out in enumerate(out_refs):
                        at = (head * 3 + kind) * HD
                        value = total[:, at : at + HD]
                        if mine:
                            value = (value + received[kind, :, here]) * mean_scale
                        out[:, here] = value


def weight_product(place, mine, mean_scale, cols, tokens, grads, received=()):
    _, length, _ = grads[0].shape
    rows = tokens[0].shape[2]
    out = jax.ShapeDtypeStruct((rows, cols), jnp.float32)
    both = jax.ShapeDtypeStruct((3, rows, cols), jnp.float32)
    return pl.pallas_call(
        functools.partial(weight_kernel, mine, mean_scale, len(grads) // 6),
        out_shape=[out] * 3 if mine else both,
        in_specs=[whole(pltpu.SMEM)] + [whole()] * (6 + len(grads) + len(received)),
        out_specs=[whole()] * 3 if mine else whole(),
        scratch_shapes=[pltpu.VMEM((rows, 4 * length), jnp.bfloat16)],
        compiler_params=pltpu.CompilerParams(vmem_limit_bytes=24 * MIB),
        cost_estimate=pl.CostEstimate(
            flops=8 * rows * 3 * cols * length,
            bytes_accessed=8 * length * (rows + 3 * cols) + 12 * rows * cols,
            transcendentals=0,
        ),
        name="weight_gradient_own" if mine else "weight_gradient_mate",
    )(place, *tokens, *grads, *received)


def gather_body(
    normed,
    queries,
    saved_keys,
    saved_values,
    output_grad,
    view_links,
    query_weight,
    key_weight,
    value_weight,
):
    length, cols = queries.shape[2:]
    model_width = normed.shape[-1]
    rows = query_weight.shape[0]
    prompts, views, groups = (lax.axis_size(name) for name in ("dp", "view", "head"))
    mean_scale = 1.0 / (prompts * views)
    half = cols // HD // 2
    view = lax.axis_index("view")
    core = lax.rem(view, 2)
    side = view // 2
    chip = lax.axis_index("dp") * (views // 2) + side
    place = jnp.stack([core, lax.axis_index("head"), side * half, (1 - side) * half])
    place = place.astype(jnp.int32)
    arrays = tuple(a.reshape(length, cols) for a in (queries, saved_keys, saved_values, output_grad))

    own_heads, shared = half // 2, half % 2
    each = [2 * step for step in range(own_heads)]
    picks = [
        [(BESIDE, step, 1) for step in each],
        [(BESIDE, step + 1, -1) for step in each],
        [(HERE, step + 1, -1) for step in each],
        [(HERE, step, 1) for step in each],
    ]
    if shared:
        picks += [[(BESIDE, 2 * own_heads, 0)], [(HERE, 2 * own_heads, 0)]]
    packed = pack(picks, place, view_links, arrays)
    to_x, to_cross, to_mate, own = packed[:4]
    x_in = moved(to_x, along_x)
    cross_in = moved(to_cross, across_x)
    mate_in = moved(to_mate, mate)
    sets = [((0, 1, 2, 3), (own, mate_in, x_in, cross_in))]
    if shared:
        to_x, own = packed[4:]
        (to_x,) = after((to_x,), x_in)
        x_in = moved(to_x, along_x)
        sets.append(((0, 2), (own, moved(own, mate), x_in, moved(x_in, mate))))

    own_weights, turn = None, place
    parts = []
    for kept, sources in sets:
        made = attention(turn, kept, sources)
        if own_weights is None:
            ready = after((query_weight, key_weight, value_weight), made)
            own_weights = turned_weights(place, ready)
        (turn,) = after((place,), made, own_weights)
        ahead = moved(made, straight)
        aside = moved(made, crossed)
        inward = moved(made, only(1, mate))
        (sent,) = after((ahead,), aside, inward)
        relay_x = moved(sent, only(1, along_x))
        relay_y = moved(sent, only(0, across_y))
        parts.append((made, inward, ahead, aside, relay_x, relay_y))
    grads = [array for kind in zip(*parts) for array in kind]
    weights = joined_weights(place, own_weights, moved(own_weights, mate))

    slots = input_product(place, grads, weights)
    arrived = [
        lax.ppermute(slots[s], "head", [(z, z ^ s) for z in range(groups)])
        for s in range(1, groups)
    ]
    total = sum(array.astype(jnp.float32) for array in (slots[0], *arrived))
    total = total.astype(jnp.bfloat16)

    (flat,) = after((normed.reshape(length, model_width),), *slots)

    def columns(of_chip):
        columns = [
            lax.dynamic_slice_in_dim(flat, (2 * of_chip + part) * rows, rows, axis=1)
            for part in range(2)
        ]
        return jnp.stack(columns)

    toward_x, toward_y = jnp.bitwise_xor(chip, 1), jnp.bitwise_xor(chip, 2)
    here = columns(chip)
    to_straight = columns(jnp.where(core == 0, toward_x, toward_y))
    to_crossed = columns(jnp.where(core == 0, toward_y, toward_x))
    to_corner = columns(jnp.bitwise_xor(chip, 3))
    tokens = (
        here,
        moved(here, only(1, mate)),
        moved(to_straight, straight),
        moved(to_crossed, crossed),
        moved(to_corner, corner_same),
        moved(to_corner, corner_cross),
    )
    (turn,) = after((place,), total)
    for_mate = weight_product(turn, False, mean_scale, cols, tokens, grads)
    from_mate = moved(for_mate, mate)
    weight_grads = weight_product(place, True, mean_scale, cols, tokens, grads, (from_mate,))
    def spot(y, v, z):
        return (y * views + v) * groups + z

    corners = [(y, v, z) for y in range(prompts) for v in range(views) for z in range(groups)]
    beside = lax.ppermute(
        total,
        ("dp", "view", "head"),
        [(spot(y, v, z), spot(y ^ (v % 2), v ^ z, z)) for y, v, z in corners],
    )
    (beside,) = after((beside,), weight_grads[0])
    input_grad = lax.ppermute(
        beside,
        ("dp", "view", "head"),
        [
            (
                spot(y ^ (v % 2), v ^ z, z),
                spot(y ^ (v % 2), v ^ z, y * (views // 2) + v // 2),
            )
            for y, v, z in corners
        ],
    )

    return (
        input_grad.reshape(1, 1, length, model_width // groups),
        *weight_grads,
    )


def solution(mesh):
    prompts, views, groups = (mesh.shape[name] for name in ("dp", "view", "head"))
    loop_of_four = prompts * 2 == views and prompts * views == 2 * groups and views == groups

    def choose(*arrays):
        batch, held, length, cols = arrays[1].shape
        if loop_of_four and batch == held == 1 and length % HD == 0 and cols % (2 * HD) == 0:
            return gather_body(*arrays)
        return halo_body(*arrays)

    placed = (
        P("dp", "view", None, None),
        P("dp", "view", None, "head"),
        P("dp", "view", None, "head"),
        P("dp", "view", None, "head"),
        P("dp", "view", None, "head"),
        P("view", None),
        P(("dp", "view"), "head"),
        P(("dp", "view"), "head"),
        P(("dp", "view"), "head"),
    )
    return jax.shard_map(
        choose,
        mesh=mesh,
        in_specs=placed,
        out_specs=(
            P("dp", "view", None, "head"),
            P(("dp", "view"), "head"),
            P(("dp", "view"), "head"),
            P(("dp", "view"), "head"),
        ),
        check_vma=False,
    )
```

```python
import functools

import jax
import jax.numpy as jnp
from jax import lax
from jax.experimental import pallas as pl
from jax.experimental.pallas import tpu as pltpu
from jax.sharding import PartitionSpec as P

HD = 128
LOG2E = 1.4426950408889634
MIB = 1024 * 1024


def shifted(value, axis, steps):
    count = lax.axis_size(axis)
    pairs = [(source, (source + steps) % count) for source in range(count)]
    return lax.ppermute(value, axis, pairs)


def attend(query_rows, grad_rows, blocks, usable, scaling):
    batch_size, length, col_count = query_rows.shape
    heads_here = col_count // HD
    key_heads = blocks[..., :col_count].reshape(batch_size, 3 * length, heads_here, HD)
    value_heads = blocks[..., col_count:].reshape(batch_size, 3 * length, heads_here, HD)
    query_heads = query_rows.reshape(batch_size, length, heads_here, HD)
    grad_heads = grad_rows.reshape(batch_size, length, heads_here, HD)
    scores = (
        jnp.einsum("bshd,bthd->bhst", query_heads, key_heads, preferred_element_type=jnp.float32)
        * scaling
    )
    scores = jnp.where(usable, scores, -1e30)
    largest = jnp.max(scores, axis=-1, keepdims=True)
    powers = jnp.exp(scores - largest)
    attn_probs = powers / jnp.sum(powers, axis=-1, keepdims=True)
    probs_half = attn_probs.astype(jnp.bfloat16)
    prob_grad = jnp.einsum(
        "bshd,bthd->bhst", grad_heads, value_heads, preferred_element_type=jnp.float32
    )
    row_delta = jnp.sum(attn_probs * prob_grad, axis=-1, keepdims=True)
    score_grad = (scaling * attn_probs * (prob_grad - row_delta)).astype(jnp.bfloat16)
    query_grad = jnp.einsum(
        "bhst,bthd->bshd", score_grad, key_heads, preferred_element_type=jnp.float32
    )
    key_grad = jnp.einsum(
        "bhst,bshd->bthd", score_grad, query_heads, preferred_element_type=jnp.float32
    )
    value_grad = jnp.einsum(
        "bhst,bshd->bthd", probs_half, grad_heads, preferred_element_type=jnp.float32
    )
    query_grad = query_grad.reshape(batch_size, length, col_count)
    key_grad = key_grad.reshape(batch_size, 3, length, col_count)
    value_grad = value_grad.reshape(batch_size, 3, length, col_count)
    return (query_grad, jnp.concatenate([key_grad, value_grad], axis=-1))


def halo_body(
    normed,
    queries,
    saved_keys,
    saved_values,
    output_grad,
    view_links,
    query_weight,
    key_weight,
    value_weight,
):
    scaling = HD ** (-0.5)
    batch_size, view_count, length, col_count = queries.shape
    model_width = normed.shape[-1]
    pairs = jnp.concatenate([saved_keys, saved_values], axis=-1)
    from_lower = shifted(pairs, "view", 1)
    from_upper = shifted(pairs, "view", -1)
    extended = jnp.concatenate([from_lower, pairs, from_upper], axis=1)
    block_index = jnp.arange(3 * length) // length
    pair_grads = jnp.zeros(extended.shape, jnp.float32)
    link_flags = view_links[0] >= 0
    usable = jnp.where(
        block_index == 0, link_flags[0], jnp.where(block_index == 2, link_flags[1], True)
    )
    query_grad, block_grad = attend(queries[:, 0], output_grad[:, 0], extended, usable, scaling)
    query_grads = [query_grad]
    pair_grads = pair_grads.at[:, 0:3].add(block_grad)
    row_count = batch_size * view_count * length
    query_half = jnp.stack(query_grads, axis=1).astype(jnp.bfloat16).reshape(row_count, col_count)
    flat_input = normed.reshape(row_count, model_width)
    mean_scale = 1.0 / (lax.axis_size("dp") * batch_size * lax.axis_size("view") * view_count)
    from_lower_grads = shifted(pair_grads[:, -1:], "view", 1)
    from_upper_grads = shifted(pair_grads[:, :1], "view", -1)
    own_grads = pair_grads[:, 1 : view_count + 1]
    own_grads = own_grads.at[:, :1].add(from_lower_grads)
    own_grads = own_grads.at[:, -1:].add(from_upper_grads)
    key_half = own_grads[..., :col_count].astype(jnp.bfloat16).reshape(row_count, col_count)
    value_half = own_grads[..., col_count:].astype(jnp.bfloat16).reshape(row_count, col_count)
    all_grads = jnp.concatenate([query_half, key_half, value_half], axis=-1)
    grads_three = all_grads.reshape(row_count, 3, col_count)
    stacked = jnp.stack([query_weight, key_weight, value_weight])
    partial_input = jnp.einsum(
        "ric,ipc->rp",
        grads_three,
        lax.all_gather(stacked, ("dp", "view"), axis=1, tiled=True),
        preferred_element_type=jnp.float32,
    )
    summed_input = lax.psum_scatter(partial_input, "head", scatter_dimension=1, tiled=True)
    input_grad = summed_input.astype(jnp.bfloat16).reshape(
        batch_size, view_count, length, model_width // lax.axis_size("head")
    )
    product = lax.dot_general(
        flat_input, all_grads, (((0,), (0,)), ((), ())), preferred_element_type=jnp.float32
    )
    together = lax.psum_scatter(
        product * mean_scale, ("dp", "view"), scatter_dimension=0, tiled=True
    )
    grad_query = together[:, :col_count]
    grad_key = together[:, col_count : 2 * col_count]
    grad_value = together[:, 2 * col_count :]
    return (input_grad, grad_query, grad_key, grad_value)


def moved(value, target):
    prompts, views = lax.axis_size("dp"), lax.axis_size("view")
    pairs = []
    for y in range(prompts):
        for v in range(views):
            goal = target(y, v)
            if goal is not None:
                pairs.append((y * views + v, goal[0] * views + goal[1]))
    return lax.ppermute(value, ("dp", "view"), pairs)


def mate(y, v):
    return (y, v ^ 1)


def along_x(y, v):
    return (y, v ^ 2)


def across_x(y, v):
    return (y, v ^ 3)


def only(core, target):
    return lambda y, v: target(y, v) if v % 2 == core else None


def along_y(y, v):
    return (y ^ 1, v)


def across_y(y, v):
    return (y ^ 1, v ^ 1)


def straight(y, v):
    return along_x(y, v) if v % 2 == 0 else along_y(y, v)


def crossed(y, v):
    return across_y(y, v) if v % 2 == 0 else across_x(y, v)


def corner_same(y, v):
    return None if v % 2 == 0 else (y ^ 1, v ^ 2)


def corner_cross(y, v):
    return (y ^ 1, v ^ 3) if v % 2 == 0 else None


def lanes(start, size):
    return pl.ds(pl.multiple_of(start, HD), size)


def whole(space=pltpu.VMEM):
    return pl.BlockSpec(memory_space=space)


def dot_last(a, b):
    return lax.dot_general(a, b, (((1,), (1,)), ((), ())), preferred_element_type=jnp.float32)


def dot_first(a, b):
    return lax.dot_general(a, b, (((0,), (0,)), ((), ())), preferred_element_type=jnp.float32)


def dot(a, b):
    return jnp.dot(a, b, preferred_element_type=jnp.float32)


def after(values, *earlier):
    return lax.optimization_barrier((tuple(values), tuple(earlier)))[0]


CORE, PLANE, HERE, BESIDE = range(4)
FLAG_ROWS = 16


def pack_kernel(picks, place_ref, links_ref, q_ref, k_ref, v_ref, g_ref, *out_refs):
    length = q_ref.shape[0]
    row = lax.broadcasted_iota(jnp.int32, (FLAG_ROWS, HD), 0)
    gaps = [jnp.where(links_ref[0, side] >= 0, 0.0, 1.0).astype(jnp.float32) for side in range(2)]
    flags = jnp.where(row < FLAG_ROWS // 2, gaps[0], gaps[1])
    for heads, out_ref in zip(picks, out_refs):
        for at, (base, step, sign) in enumerate(heads):
            head = place_ref[base] + step + sign * place_ref[CORE]
            for kind, source in enumerate((q_ref, k_ref, v_ref, g_ref)):
                out_ref[at, kind * length : (kind + 1) * length] = source[:, lanes(head * HD, HD)]
            out_ref[at, 4 * length : 4 * length + FLAG_ROWS] = flags.astype(out_ref.dtype)


def pack(picks, place, links, arrays):
    length = arrays[0].shape[0]
    height = 4 * length + FLAG_ROWS
    return pl.pallas_call(
        functools.partial(pack_kernel, picks),
        out_shape=[
            jax.ShapeDtypeStruct((len(heads), height, HD), jnp.bfloat16) for heads in picks
        ],
        in_specs=[whole(pltpu.SMEM)] * 2 + [whole()] * 4,
        out_specs=[whole()] * len(picks),
        name="pack_heads",
    )(place, links, *arrays)


def one_head(scaling, core, xs, length, keys, values, key_sums, value_sums):
    factor = scaling * LOG2E

    def rows(e, kind):
        return xs[e][kind * length : (kind + 1) * length]

    def gap(e, side):
        at = 4 * length + side * (FLAG_ROWS // 2)
        flags = xs[e][at : at + FLAG_ROWS // 2].astype(jnp.float32)[0:1]
        return jnp.concatenate([flags] * (length // HD), axis=1) * 1e30

    for at in range(6):
        keys[at * length : (at + 1) * length] = rows((at + 3) % 4, 1)
        values[at * length : (at + 1) * length] = rows((at + 3) % 4, 2)
    query_grads = []
    for e in range(4):
        blocks = slice(e * length, (e + 3) * length)
        before, behind = gap(e, 0), gap(e, 1)
        far_below = jnp.where(core == 0, before, behind)
        far_above = jnp.where(core == 0, behind, before)
        q, g = rows(e, 0), rows(e, 3)
        near = keys[blocks]
        scores = dot_last(near, q)
        scores = [scores[at * length : (at + 1) * length] for at in range(3)]
        tops = [jnp.max(part, axis=0, keepdims=True) for part in scores]
        top = jnp.maximum(tops[1], jnp.maximum(tops[0] - far_below, tops[2] - far_above))
        offsets = (top + far_below, top, top + far_above)
        powers = [jnp.exp2((part - o) * factor) for part, o in zip(scores, offsets)]
        inverse = 1.0 / sum(jnp.sum(p, axis=0, keepdims=True) for p in powers)
        prob_grads = dot_last(values[blocks], g)
        prob_grads = [prob_grads[at * length : (at + 1) * length] for at in range(3)]
        delta = inverse * sum(
            jnp.sum(p * d, axis=0, keepdims=True) for p, d in zip(powers, prob_grads)
        )
        probs = [p * inverse for p in powers]
        score_grad = jnp.concatenate(
            [
                (p * scaling * (d - delta)).astype(jnp.bfloat16)
                for p, d in zip(probs, prob_grads)
            ],
            axis=0,
        )
        probs_half = jnp.concatenate([p.astype(jnp.bfloat16) for p in probs], axis=0)
        query_grads.append(dot_first(score_grad, near))
        for sums, part in ((key_sums, dot(score_grad, q)), (value_sums, dot(probs_half, g))):
            if e == 0:
                sums[blocks] = part
            else:
                held = slice(e * length, (e + 2) * length)
                sums[held] += part[: 2 * length]
                sums[(e + 2) * length : (e + 3) * length] = part[2 * length :]

    def by_view(sums):
        parts = [sums[at * length : (at + 1) * length] for at in range(6)]
        return (parts[1] + parts[5], parts[2], parts[3], parts[0] + parts[4])

    return query_grads, by_view(key_sums), by_view(value_sums)


def attention_kernel(scaling, kept, place_ref, own, mate_in, x_in, far_in, *refs):
    out_ref, keys, values, key_sums, value_sums = refs
    length = out_ref.shape[1]
    heads = own.shape[0]
    for head in range(heads):
        xs = [own.at[head], mate_in.at[head], x_in.at[head], far_in.at[head]]
        grads = one_head(
            scaling, place_ref[CORE], xs, length, keys, values, key_sums, value_sums
        )
        for at, e in enumerate(kept):
            for kind in range(3):
                out_ref[len(kept) * head + at, :, kind * HD : (kind + 1) * HD] = grads[kind][
                    e
                ].astype(out_ref.dtype)


def attention(place, kept, sources):
    heads, height, _ = sources[0].shape
    length = (height - FLAG_ROWS) // 4
    return pl.pallas_call(
        functools.partial(attention_kernel, HD ** (-0.5), kept),
        out_shape=jax.ShapeDtypeStruct((len(kept) * heads, length, 3 * HD), jnp.bfloat16),
        in_specs=[whole(pltpu.SMEM)] + [whole()] * 4,
        out_specs=whole(),
        scratch_shapes=[pltpu.VMEM((6 * length, HD), jnp.bfloat16)] * 2
        + [pltpu.VMEM((6 * length, HD), jnp.float32)] * 2,
        compiler_params=pltpu.CompilerParams(vmem_limit_bytes=12 * MIB),
        cost_estimate=pl.CostEstimate(
            flops=heads * 4 * 5 * 2 * length * 3 * length * HD * 2,
            bytes_accessed=heads * 2 * length * 7 * HD * 4,
            transcendentals=heads * 12 * length * length,
        ),
        name="attention_gradients",
    )(place, *sources)


def turn_kernel(place_ref, q_ref, k_ref, v_ref, out_ref):
    half = q_ref.shape[1] // HD // 2
    for side, base in enumerate((HERE, BESIDE)):
        for head in range(half):
            for kind, source in enumerate((q_ref, k_ref, v_ref)):
                at = ((side * half + head) * 3 + kind) * HD
                out_ref[at : at + HD] = source[:, lanes((place_ref[base] + head) * HD, HD)].T


def turned_weights(place, weights):
    rows, cols = weights[0].shape
    return pl.pallas_call(
        turn_kernel,
        out_shape=jax.ShapeDtypeStruct((3 * cols, rows), jnp.bfloat16),
        in_specs=[whole(pltpu.SMEM)] + [whole()] * 3,
        out_specs=whole(),
        compiler_params=pltpu.CompilerParams(vmem_limit_bytes=8 * MIB),
        name="turn_weights",
    )(place, *weights)


def join_kernel(place_ref, own_ref, mate_ref, out_ref):
    core = place_ref[CORE]
    rows = own_ref.shape[1]
    out_ref[:, lanes(core * rows, rows)] = own_ref[...]
    out_ref[:, lanes((1 - core) * rows, rows)] = mate_ref[...]


def joined_weights(place, own_weights, mate_weights):
    depth, rows = own_weights.shape
    return pl.pallas_call(
        join_kernel,
        out_shape=jax.ShapeDtypeStruct((depth, 2 * rows), jnp.bfloat16),
        in_specs=[whole(pltpu.SMEM)] + [whole()] * 2,
        out_specs=whole(),
        compiler_params=pltpu.CompilerParams(vmem_limit_bytes=12 * MIB),
        name="join_weights",
    )(place, own_weights, mate_weights)


def gathered(role, refs):
    sides = []
    for side in range(2):
        pieces = []
        for head in range(refs[0][0].shape[0] // 4):
            for maker in range(2):
                k = 2 * side + (maker ^ role)
                pieces.append([refs[k][0][4 * head + (e ^ k)] for e in range(4)])
        for at in range(refs[0][1].shape[0] // 2 if len(refs[0]) > 1 else 0):
            rows = []
            for e in range(4):
                k = 2 * side + e % 2
                rows.append(refs[k][1][2 * at + (e // 2 ^ side)])
            pieces.append(rows)
        sides.append(
            jnp.concatenate([jnp.concatenate(rows, axis=0) for rows in pieces], axis=1)
        )
    return sides


def by_role(refs, parts):
    made, inward, ahead, aside, relay_x, relay_y = [
        refs[at * parts : (at + 1) * parts] for at in range(6)
    ]
    return ((made, inward, ahead, aside), (ahead, aside, relay_x, relay_y))


def input_kernel(parts, place_ref, *refs):
    weights, out_refs, total = refs[6 * parts], refs[6 * parts + 1 : -1], refs[-1]
    length = out_refs[0].shape[0]
    for role, grads in enumerate(by_role(refs, parts)):

        @pl.when(place_ref[CORE] == role)
        def _():
            left = jnp.concatenate(gathered(role, grads), axis=1)
            for e in range(4):
                product = dot(left[e * length : (e + 1) * length], weights[...])
                total[e] = product.astype(total.dtype)

    for s, out_ref in enumerate(out_refs):
        out_ref[...] = total[jnp.bitwise_xor(place_ref[PLANE], s)]


def input_product(place, grads, weights):
    _, length, _ = grads[0].shape
    depth, rows = weights.shape
    out = jax.ShapeDtypeStruct((length, rows), jnp.bfloat16)
    return pl.pallas_call(
        functools.partial(input_kernel, len(grads) // 6),
        out_shape=[out] * 4,
        in_specs=[whole(pltpu.SMEM)] + [whole()] * (len(grads) + 1),
        out_specs=[whole()] * 4,
        scratch_shapes=[pltpu.VMEM((4, length, rows), jnp.bfloat16)],
        compiler_params=pltpu.CompilerParams(vmem_limit_bytes=16 * MIB),
        cost_estimate=pl.CostEstimate(
            flops=8 * length * rows * depth,
            bytes_accessed=8 * length * (rows + depth) + 2 * rows * depth,
            transcendentals=0,
        ),
        name="input_gradient",
    )(place, *grads, weights)


def weight_kernel(mine, mean_scale, parts, place_ref, *refs):
    own, mate_in, first, second, corner, corner_far = refs[:6]
    grad_refs, refs = refs[6 : 6 + 6 * parts], refs[6 + 6 * parts :]
    if mine:
        received, out_refs, turned = refs[0], refs[1:4], refs[4]
    else:
        received, out_refs, turned = None, [refs[0].at[kind] for kind in range(3)], refs[1]
    core = place_ref[CORE]
    length = own.shape[1]
    part = core if mine else 1 - core
    tokens = ((own, mate_in, first, second), (first, second, corner, corner_far))
    for role, grads in enumerate(by_role(grad_refs, parts)):

        @pl.when(core == role)
        def _():
            for e, source in enumerate(tokens[role]):
                turned[:, e * length : (e + 1) * length] = source[part].T
            for base, side in zip((HERE, BESIDE), gathered(role, grads)):
                total = dot(turned[...], side)
                for head in range(side.shape[1] // (3 * HD)):
                    here = lanes((place_ref[base] + head) * HD, HD)
                    for kind, out in enumerate(out_refs):
                        at = (head * 3 + kind) * HD
                        value = total[:, at : at + HD]
                        if mine:
                            value = (value + received[kind, :, here]) * mean_scale
                        out[:, here] = value


def weight_product(place, mine, mean_scale, cols, tokens, grads, received=()):
    _, length, _ = grads[0].shape
    rows = tokens[0].shape[2]
    out = jax.ShapeDtypeStruct((rows, cols), jnp.float32)
    both = jax.ShapeDtypeStruct((3, rows, cols), jnp.float32)
    return pl.pallas_call(
        functools.partial(weight_kernel, mine, mean_scale, len(grads) // 6),
        out_shape=[out] * 3 if mine else both,
        in_specs=[whole(pltpu.SMEM)] + [whole()] * (6 + len(grads) + len(received)),
        out_specs=[whole()] * 3 if mine else whole(),
        scratch_shapes=[pltpu.VMEM((rows, 4 * length), jnp.bfloat16)],
        compiler_params=pltpu.CompilerParams(vmem_limit_bytes=16 * MIB),
        cost_estimate=pl.CostEstimate(
            flops=8 * rows * 3 * cols * length,
            bytes_accessed=8 * length * (rows + 3 * cols) + 12 * rows * cols,
            transcendentals=0,
        ),
        name="weight_gradient_own" if mine else "weight_gradient_mate",
    )(place, *tokens, *grads, *received)


def gather_body(
    normed,
    queries,
    saved_keys,
    saved_values,
    output_grad,
    view_links,
    query_weight,
    key_weight,
    value_weight,
):
    length, cols = queries.shape[2:]
    model_width = normed.shape[-1]
    rows = query_weight.shape[0]
    prompts, views, groups = (lax.axis_size(name) for name in ("dp", "view", "head"))
    mean_scale = 1.0 / (prompts * views)
    half = cols // HD // 2
    view = lax.axis_index("view")
    core = lax.rem(view, 2)
    side = view // 2
    chip = lax.axis_index("dp") * (views // 2) + side
    place = jnp.stack([core, lax.axis_index("head"), side * half, (1 - side) * half])
    place = place.astype(jnp.int32)
    arrays = tuple(a.reshape(length, cols) for a in (queries, saved_keys, saved_values, output_grad))

    own_heads, shared = half // 2, half % 2
    each = [2 * step for step in range(own_heads)]
    picks = [
        [(BESIDE, step, 1) for step in each],
        [(BESIDE, step + 1, -1) for step in each],
        [(HERE, step + 1, -1) for step in each],
        [(HERE, step, 1) for step in each],
    ]
    if shared:
        picks += [[(BESIDE, 2 * own_heads, 0)], [(HERE, 2 * own_heads, 0)]]
    packed = pack(picks, place, view_links, arrays)
    to_x, to_cross, to_mate, own = packed[:4]
    x_in = moved(to_x, along_x)
    cross_in = moved(to_cross, across_x)
    mate_in = moved(to_mate, mate)
    sets = [((0, 1, 2, 3), (own, mate_in, x_in, cross_in))]
    if shared:
        to_x, own = packed[4:]
        (to_x,) = after((to_x,), x_in)
        x_in = moved(to_x, along_x)
        sets.append(((0, 2), (own, moved(own, mate), x_in, moved(x_in, mate))))

    flat = normed.reshape(length, model_width)

    def columns(of_chip):
        columns = [
            lax.dynamic_slice_in_dim(flat, (2 * of_chip + part) * rows, rows, axis=1)
            for part in range(2)
        ]
        return jnp.stack(columns)

    toward_x, toward_y = jnp.bitwise_xor(chip, 1), jnp.bitwise_xor(chip, 2)
    here = columns(chip)
    to_straight = columns(jnp.where(core == 0, toward_x, toward_y))
    to_crossed = columns(jnp.where(core == 0, toward_y, toward_x))
    to_corner = columns(jnp.bitwise_xor(chip, 3))
    mate_here = moved(here, only(1, mate))

    own_weights, turn = None, place
    parts = []
    for kept, sources in sets:
        made = attention(turn, kept, sources)
        if own_weights is None:
            ready = after((query_weight, key_weight, value_weight), made)
            own_weights = turned_weights(place, ready)
        (turn,) = after((place,), made, own_weights)
        ahead = moved(made, straight)
        aside = moved(made, crossed)
        inward = moved(made, only(1, mate))
        (sent,) = after((ahead,), aside, inward, mate_here, to_straight, to_crossed, to_corner)
        relay_x = moved(sent, only(1, along_x))
        relay_y = moved(sent, only(0, across_y))
        parts.append((made, inward, ahead, aside, relay_x, relay_y))
    grads = [array for kind in zip(*parts) for array in kind]
    weights = joined_weights(place, own_weights, moved(own_weights, mate))

    slots = input_product(place, grads, weights)
    arrived = [
        lax.ppermute(slots[s], "head", [(z, z ^ s) for z in range(groups)])
        for s in range(1, groups)
    ]
    total = sum(array.astype(jnp.float32) for array in (slots[0], *arrived))
    total = total.astype(jnp.bfloat16)

    to_straight, to_crossed = after((to_straight, to_crossed), *slots)
    normed_ahead = moved(to_straight, straight)
    normed_aside = moved(to_crossed, crossed)
    (to_corner,) = after((to_corner,), normed_ahead, normed_aside)
    tokens = (
        here,
        mate_here,
        normed_ahead,
        normed_aside,
        moved(to_corner, corner_same),
        moved(to_corner, corner_cross),
    )
    (turn,) = after((place,), total)
    for_mate = weight_product(turn, False, mean_scale, cols, tokens, grads)
    from_mate = moved(for_mate, mate)
    weight_grads = weight_product(place, True, mean_scale, cols, tokens, grads, (from_mate,))
    def spot(y, v, z):
        return (y * views + v) * groups + z

    corners = [(y, v, z) for y in range(prompts) for v in range(views) for z in range(groups)]
    beside = lax.ppermute(
        total,
        ("dp", "view", "head"),
        [(spot(y, v, z), spot(y ^ (v % 2), v ^ z, z)) for y, v, z in corners],
    )
    (beside,) = after((beside,), for_mate)
    input_grad = lax.ppermute(
        beside,
        ("dp", "view", "head"),
        [
            (
                spot(y ^ (v % 2), v ^ z, z),
                spot(y ^ (v % 2), v ^ z, y * (views // 2) + v // 2),
            )
            for y, v, z in corners
        ],
    )

    (input_grad,) = after((input_grad,), *weight_grads)
    return (
        input_grad.reshape(1, 1, length, model_width // groups),
        *weight_grads,
    )


def solution(mesh):
    prompts, views, groups = (mesh.shape[name] for name in ("dp", "view", "head"))
    loop_of_four = prompts * 2 == views and prompts * views == 2 * groups and views == groups

    def choose(*arrays):
        batch, held, length, cols = arrays[1].shape
        if loop_of_four and batch == held == 1 and length % HD == 0 and cols % (2 * HD) == 0:
            return gather_body(*arrays)
        return halo_body(*arrays)

    placed = (
        P("dp", "view", None, None),
        P("dp", "view", None, "head"),
        P("dp", "view", None, "head"),
        P("dp", "view", None, "head"),
        P("dp", "view", None, "head"),
        P("view", None),
        P(("dp", "view"), "head"),
        P(("dp", "view"), "head"),
        P(("dp", "view"), "head"),
    )
    return jax.shard_map(
        choose,
        mesh=mesh,
        in_specs=placed,
        out_specs=(
            P("dp", "view", None, "head"),
            P(("dp", "view"), "head"),
            P(("dp", "view"), "head"),
            P(("dp", "view"), "head"),
        ),
        check_vma=False,
    )
```

```python
import functools

import jax
import jax.numpy as jnp
from jax import lax
from jax.experimental import pallas as pl
from jax.experimental.pallas import tpu as pltpu
from jax.sharding import PartitionSpec as P

HD = 128
LOG2E = 1.4426950408889634
MIB = 1024 * 1024


def shifted(value, axis, steps):
    count = lax.axis_size(axis)
    pairs = [(source, (source + steps) % count) for source in range(count)]
    return lax.ppermute(value, axis, pairs)


def attend(query_rows, grad_rows, blocks, usable, scaling):
    batch_size, length, col_count = query_rows.shape
    heads_here = col_count // HD
    key_heads = blocks[..., :col_count].reshape(batch_size, 3 * length, heads_here, HD)
    value_heads = blocks[..., col_count:].reshape(batch_size, 3 * length, heads_here, HD)
    query_heads = query_rows.reshape(batch_size, length, heads_here, HD)
    grad_heads = grad_rows.reshape(batch_size, length, heads_here, HD)
    scores = (
        jnp.einsum("bshd,bthd->bhst", query_heads, key_heads, preferred_element_type=jnp.float32)
        * scaling
    )
    scores = jnp.where(usable, scores, -1e30)
    largest = jnp.max(scores, axis=-1, keepdims=True)
    powers = jnp.exp(scores - largest)
    attn_probs = powers / jnp.sum(powers, axis=-1, keepdims=True)
    probs_half = attn_probs.astype(jnp.bfloat16)
    prob_grad = jnp.einsum(
        "bshd,bthd->bhst", grad_heads, value_heads, preferred_element_type=jnp.float32
    )
    row_delta = jnp.sum(attn_probs * prob_grad, axis=-1, keepdims=True)
    score_grad = (scaling * attn_probs * (prob_grad - row_delta)).astype(jnp.bfloat16)
    query_grad = jnp.einsum(
        "bhst,bthd->bshd", score_grad, key_heads, preferred_element_type=jnp.float32
    )
    key_grad = jnp.einsum(
        "bhst,bshd->bthd", score_grad, query_heads, preferred_element_type=jnp.float32
    )
    value_grad = jnp.einsum(
        "bhst,bshd->bthd", probs_half, grad_heads, preferred_element_type=jnp.float32
    )
    query_grad = query_grad.reshape(batch_size, length, col_count)
    key_grad = key_grad.reshape(batch_size, 3, length, col_count)
    value_grad = value_grad.reshape(batch_size, 3, length, col_count)
    return (query_grad, jnp.concatenate([key_grad, value_grad], axis=-1))


def halo_body(
    normed,
    queries,
    saved_keys,
    saved_values,
    output_grad,
    view_links,
    query_weight,
    key_weight,
    value_weight,
):
    scaling = HD ** (-0.5)
    batch_size, view_count, length, col_count = queries.shape
    model_width = normed.shape[-1]
    pairs = jnp.concatenate([saved_keys, saved_values], axis=-1)
    from_lower = shifted(pairs, "view", 1)
    from_upper = shifted(pairs, "view", -1)
    extended = jnp.concatenate([from_lower, pairs, from_upper], axis=1)
    block_index = jnp.arange(3 * length) // length
    pair_grads = jnp.zeros(extended.shape, jnp.float32)
    link_flags = view_links[0] >= 0
    usable = jnp.where(
        block_index == 0, link_flags[0], jnp.where(block_index == 2, link_flags[1], True)
    )
    query_grad, block_grad = attend(queries[:, 0], output_grad[:, 0], extended, usable, scaling)
    query_grads = [query_grad]
    pair_grads = pair_grads.at[:, 0:3].add(block_grad)
    row_count = batch_size * view_count * length
    query_half = jnp.stack(query_grads, axis=1).astype(jnp.bfloat16).reshape(row_count, col_count)
    flat_input = normed.reshape(row_count, model_width)
    mean_scale = 1.0 / (lax.axis_size("dp") * batch_size * lax.axis_size("view") * view_count)
    from_lower_grads = shifted(pair_grads[:, -1:], "view", 1)
    from_upper_grads = shifted(pair_grads[:, :1], "view", -1)
    own_grads = pair_grads[:, 1 : view_count + 1]
    own_grads = own_grads.at[:, :1].add(from_lower_grads)
    own_grads = own_grads.at[:, -1:].add(from_upper_grads)
    key_half = own_grads[..., :col_count].astype(jnp.bfloat16).reshape(row_count, col_count)
    value_half = own_grads[..., col_count:].astype(jnp.bfloat16).reshape(row_count, col_count)
    all_grads = jnp.concatenate([query_half, key_half, value_half], axis=-1)
    grads_three = all_grads.reshape(row_count, 3, col_count)
    stacked = jnp.stack([query_weight, key_weight, value_weight])
    partial_input = jnp.einsum(
        "ric,ipc->rp",
        grads_three,
        lax.all_gather(stacked, ("dp", "view"), axis=1, tiled=True),
        preferred_element_type=jnp.float32,
    )
    summed_input = lax.psum_scatter(partial_input, "head", scatter_dimension=1, tiled=True)
    input_grad = summed_input.astype(jnp.bfloat16).reshape(
        batch_size, view_count, length, model_width // lax.axis_size("head")
    )
    product = lax.dot_general(
        flat_input, all_grads, (((0,), (0,)), ((), ())), preferred_element_type=jnp.float32
    )
    together = lax.psum_scatter(
        product * mean_scale, ("dp", "view"), scatter_dimension=0, tiled=True
    )
    grad_query = together[:, :col_count]
    grad_key = together[:, col_count : 2 * col_count]
    grad_value = together[:, 2 * col_count :]
    return (input_grad, grad_query, grad_key, grad_value)


def moved(value, target):
    prompts, views = lax.axis_size("dp"), lax.axis_size("view")
    pairs = []
    for y in range(prompts):
        for v in range(views):
            goal = target(y, v)
            if goal is not None:
                pairs.append((y * views + v, goal[0] * views + goal[1]))
    return lax.ppermute(value, ("dp", "view"), pairs)


def mate(y, v):
    return (y, v ^ 1)


def along_x(y, v):
    return (y, v ^ 2)


def across_x(y, v):
    return (y, v ^ 3)


def only(core, target):
    return lambda y, v: target(y, v) if v % 2 == core else None


def along_y(y, v):
    return (y ^ 1, v)


def across_y(y, v):
    return (y ^ 1, v ^ 1)


def straight(y, v):
    return along_x(y, v) if v % 2 == 0 else along_y(y, v)


def crossed(y, v):
    return across_y(y, v) if v % 2 == 0 else across_x(y, v)


def corner_same(y, v):
    return None if v % 2 == 0 else (y ^ 1, v ^ 2)


def corner_cross(y, v):
    return (y ^ 1, v ^ 3) if v % 2 == 0 else None


def lanes(start, size):
    return pl.ds(pl.multiple_of(start, HD), size)


def whole(space=pltpu.VMEM):
    return pl.BlockSpec(memory_space=space)


def dot_last(a, b):
    return lax.dot_general(a, b, (((1,), (1,)), ((), ())), preferred_element_type=jnp.float32)


def dot_first(a, b):
    return lax.dot_general(a, b, (((0,), (0,)), ((), ())), preferred_element_type=jnp.float32)


def dot(a, b):
    return jnp.dot(a, b, preferred_element_type=jnp.float32)


def after(values, *earlier):
    return lax.optimization_barrier((tuple(values), tuple(earlier)))[0]


CORE, PLANE, HERE, BESIDE = range(4)
FLAG_ROWS = 16


def pack_kernel(picks, place_ref, links_ref, q_ref, k_ref, v_ref, g_ref, *out_refs):
    length = q_ref.shape[0]
    row = lax.broadcasted_iota(jnp.int32, (FLAG_ROWS, HD), 0)
    gaps = [jnp.where(links_ref[0, side] >= 0, 0.0, 1.0).astype(jnp.float32) for side in range(2)]
    flags = jnp.where(row < FLAG_ROWS // 2, gaps[0], gaps[1])
    for heads, out_ref in zip(picks, out_refs):
        for at, (base, step, sign) in enumerate(heads):
            head = place_ref[base] + step + sign * place_ref[CORE]
            for kind, source in enumerate((q_ref, k_ref, v_ref, g_ref)):
                out_ref[at, kind * length : (kind + 1) * length] = source[:, lanes(head * HD, HD)]
            out_ref[at, 4 * length : 4 * length + FLAG_ROWS] = flags.astype(out_ref.dtype)


def pack(picks, place, links, arrays):
    length = arrays[0].shape[0]
    height = 4 * length + FLAG_ROWS
    return pl.pallas_call(
        functools.partial(pack_kernel, picks),
        out_shape=[
            jax.ShapeDtypeStruct((len(heads), height, HD), jnp.bfloat16) for heads in picks
        ],
        in_specs=[whole(pltpu.SMEM)] * 2 + [whole()] * 4,
        out_specs=[whole()] * len(picks),
        name="pack_heads",
    )(place, links, *arrays)


def one_head(scaling, core, xs, length, keys, values, key_sums, value_sums):
    factor = scaling * LOG2E

    def rows(e, kind):
        return xs[e][kind * length : (kind + 1) * length]

    def gap(e, side):
        at = 4 * length + side * (FLAG_ROWS // 2)
        flags = xs[e][at : at + FLAG_ROWS // 2].astype(jnp.float32)[0:1]
        return jnp.concatenate([flags] * (length // HD), axis=1) * 1e30

    for at in range(6):
        keys[at * length : (at + 1) * length] = rows((at + 3) % 4, 1)
        values[at * length : (at + 1) * length] = rows((at + 3) % 4, 2)
    query_grads = []
    for e in range(4):
        blocks = slice(e * length, (e + 3) * length)
        before, behind = gap(e, 0), gap(e, 1)
        far_below = jnp.where(core == 0, before, behind)
        far_above = jnp.where(core == 0, behind, before)
        q, g = rows(e, 0), rows(e, 3)
        near = keys[blocks]
        scores = dot_last(near, q)
        scores = [scores[at * length : (at + 1) * length] for at in range(3)]
        tops = [jnp.max(part, axis=0, keepdims=True) for part in scores]
        top = jnp.maximum(tops[1], jnp.maximum(tops[0] - far_below, tops[2] - far_above))
        offsets = (top + far_below, top, top + far_above)
        powers = [jnp.exp2((part - o) * factor) for part, o in zip(scores, offsets)]
        inverse = 1.0 / sum(jnp.sum(p, axis=0, keepdims=True) for p in powers)
        prob_grads = dot_last(values[blocks], g)
        prob_grads = [prob_grads[at * length : (at + 1) * length] for at in range(3)]
        delta = inverse * sum(
            jnp.sum(p * d, axis=0, keepdims=True) for p, d in zip(powers, prob_grads)
        )
        probs = [p * inverse for p in powers]
        score_grad = jnp.concatenate(
            [
                (p * scaling * (d - delta)).astype(jnp.bfloat16)
                for p, d in zip(probs, prob_grads)
            ],
            axis=0,
        )
        probs_half = jnp.concatenate([p.astype(jnp.bfloat16) for p in probs], axis=0)
        query_grads.append(dot_first(score_grad, near))
        for sums, part in ((key_sums, dot(score_grad, q)), (value_sums, dot(probs_half, g))):
            if e == 0:
                sums[blocks] = part
            else:
                held = slice(e * length, (e + 2) * length)
                sums[held] += part[: 2 * length]
                sums[(e + 2) * length : (e + 3) * length] = part[2 * length :]

    def by_view(sums):
        parts = [sums[at * length : (at + 1) * length] for at in range(6)]
        return (parts[1] + parts[5], parts[2], parts[3], parts[0] + parts[4])

    return query_grads, by_view(key_sums), by_view(value_sums)


def attention_kernel(scaling, kept, place_ref, own, mate_in, x_in, far_in, *refs):
    out_ref, keys, values, key_sums, value_sums = refs
    length = out_ref.shape[1]
    heads = own.shape[0]
    for head in range(heads):
        xs = [own.at[head], mate_in.at[head], x_in.at[head], far_in.at[head]]
        grads = one_head(
            scaling, place_ref[CORE], xs, length, keys, values, key_sums, value_sums
        )
        for at, e in enumerate(kept):
            for kind in range(3):
                out_ref[len(kept) * head + at, :, kind * HD : (kind + 1) * HD] = grads[kind][
                    e
                ].astype(out_ref.dtype)


def attention(place, kept, sources):
    heads, height, _ = sources[0].shape
    length = (height - FLAG_ROWS) // 4
    return pl.pallas_call(
        functools.partial(attention_kernel, HD ** (-0.5), kept),
        out_shape=jax.ShapeDtypeStruct((len(kept) * heads, length, 3 * HD), jnp.bfloat16),
        in_specs=[whole(pltpu.SMEM)] + [whole()] * 4,
        out_specs=whole(),
        scratch_shapes=[pltpu.VMEM((6 * length, HD), jnp.bfloat16)] * 2
        + [pltpu.VMEM((6 * length, HD), jnp.float32)] * 2,
        compiler_params=pltpu.CompilerParams(vmem_limit_bytes=12 * MIB),
        cost_estimate=pl.CostEstimate(
            flops=heads * 4 * 5 * 2 * length * 3 * length * HD * 2,
            bytes_accessed=heads * 2 * length * 7 * HD * 4,
            transcendentals=heads * 12 * length * length,
        ),
        name="attention_gradients",
    )(place, *sources)


def turn_kernel(place_ref, q_ref, k_ref, v_ref, out_ref):
    half = q_ref.shape[1] // HD // 2
    for side, base in enumerate((HERE, BESIDE)):
        for head in range(half):
            for kind, source in enumerate((q_ref, k_ref, v_ref)):
                at = ((side * half + head) * 3 + kind) * HD
                out_ref[at : at + HD] = source[:, lanes((place_ref[base] + head) * HD, HD)].T


def turned_weights(place, weights):
    rows, cols = weights[0].shape
    return pl.pallas_call(
        turn_kernel,
        out_shape=jax.ShapeDtypeStruct((3 * cols, rows), jnp.bfloat16),
        in_specs=[whole(pltpu.SMEM)] + [whole()] * 3,
        out_specs=whole(),
        compiler_params=pltpu.CompilerParams(vmem_limit_bytes=8 * MIB),
        name="turn_weights",
    )(place, *weights)


def join_kernel(place_ref, own_ref, mate_ref, out_ref):
    core = place_ref[CORE]
    rows = own_ref.shape[1]
    out_ref[:, lanes(core * rows, rows)] = own_ref[...]
    out_ref[:, lanes((1 - core) * rows, rows)] = mate_ref[...]


def joined_weights(place, own_weights, mate_weights):
    depth, rows = own_weights.shape
    return pl.pallas_call(
        join_kernel,
        out_shape=jax.ShapeDtypeStruct((depth, 2 * rows), jnp.bfloat16),
        in_specs=[whole(pltpu.SMEM)] + [whole()] * 2,
        out_specs=whole(),
        compiler_params=pltpu.CompilerParams(vmem_limit_bytes=12 * MIB),
        name="join_weights",
    )(place, own_weights, mate_weights)


def gathered(role, refs):
    sides = []
    for side in range(2):
        pieces = []
        for head in range(refs[0][0].shape[0] // 4):
            for maker in range(2):
                k = 2 * side + (maker ^ role)
                pieces.append([refs[k][0][4 * head + (e ^ k)] for e in range(4)])
        for at in range(refs[0][1].shape[0] // 2 if len(refs[0]) > 1 else 0):
            rows = []
            for e in range(4):
                k = 2 * side + e % 2
                rows.append(refs[k][1][2 * at + (e // 2 ^ side)])
            pieces.append(rows)
        sides.append(
            jnp.concatenate([jnp.concatenate(rows, axis=0) for rows in pieces], axis=1)
        )
    return sides


def by_role(refs, parts):
    made, inward, ahead, aside, relay_x, relay_y = [
        refs[at * parts : (at + 1) * parts] for at in range(6)
    ]
    return ((made, inward, ahead, aside), (ahead, aside, relay_x, relay_y))


def input_kernel(parts, place_ref, *refs):
    weights, out_refs, total = refs[6 * parts], refs[6 * parts + 1 : -1], refs[-1]
    length = out_refs[0].shape[0]
    for role, grads in enumerate(by_role(refs, parts)):

        @pl.when(place_ref[CORE] == role)
        def _():
            left = jnp.concatenate(gathered(role, grads), axis=1)
            for e in range(4):
                product = dot(left[e * length : (e + 1) * length], weights[...])
                total[e] = product.astype(total.dtype)

    for s, out_ref in enumerate(out_refs):
        out_ref[...] = total[jnp.bitwise_xor(place_ref[PLANE], s)]


def input_product(place, grads, weights):
    _, length, _ = grads[0].shape
    depth, rows = weights.shape
    out = jax.ShapeDtypeStruct((length, rows), jnp.bfloat16)
    return pl.pallas_call(
        functools.partial(input_kernel, len(grads) // 6),
        out_shape=[out] * 4,
        in_specs=[whole(pltpu.SMEM)] + [whole()] * (len(grads) + 1),
        out_specs=[whole()] * 4,
        scratch_shapes=[pltpu.VMEM((4, length, rows), jnp.bfloat16)],
        compiler_params=pltpu.CompilerParams(vmem_limit_bytes=16 * MIB),
        cost_estimate=pl.CostEstimate(
            flops=8 * length * rows * depth,
            bytes_accessed=8 * length * (rows + depth) + 2 * rows * depth,
            transcendentals=0,
        ),
        name="input_gradient",
    )(place, *grads, weights)


def weight_kernel(mine, mean_scale, parts, place_ref, *refs):
    own, mate_in, first, second, corner, corner_far = refs[:6]
    grad_refs, refs = refs[6 : 6 + 6 * parts], refs[6 + 6 * parts :]
    if mine:
        received, out_refs, turned = refs[0], refs[1:4], refs[4]
    else:
        received, out_refs, turned = None, [refs[0].at[kind] for kind in range(3)], refs[1]
    core = place_ref[CORE]
    length = own.shape[1]
    part = core if mine else 1 - core
    tokens = ((own, mate_in, first, second), (first, second, corner, corner_far))
    for role, grads in enumerate(by_role(grad_refs, parts)):

        @pl.when(core == role)
        def _():
            for e, source in enumerate(tokens[role]):
                turned[:, e * length : (e + 1) * length] = source[part].T
            for base, side in zip((HERE, BESIDE), gathered(role, grads)):
                total = dot(turned[...], side)
                for head in range(side.shape[1] // (3 * HD)):
                    here = lanes((place_ref[base] + head) * HD, HD)
                    for kind, out in enumerate(out_refs):
                        at = (head * 3 + kind) * HD
                        value = total[:, at : at + HD]
                        if mine:
                            value = (value + received[kind, :, here]) * mean_scale
                        out[:, here] = value.astype(out.dtype)


def weight_product(place, mine, mean_scale, cols, tokens, grads, received=()):
    _, length, _ = grads[0].shape
    rows = tokens[0].shape[2]
    out = jax.ShapeDtypeStruct((rows, cols), jnp.float32)
    both = jax.ShapeDtypeStruct((3, rows, cols), jnp.bfloat16)
    return pl.pallas_call(
        functools.partial(weight_kernel, mine, mean_scale, len(grads) // 6),
        out_shape=[out] * 3 if mine else both,
        in_specs=[whole(pltpu.SMEM)] + [whole()] * (6 + len(grads) + len(received)),
        out_specs=[whole()] * 3 if mine else whole(),
        scratch_shapes=[pltpu.VMEM((rows, 4 * length), jnp.bfloat16)],
        compiler_params=pltpu.CompilerParams(vmem_limit_bytes=16 * MIB),
        cost_estimate=pl.CostEstimate(
            flops=8 * rows * 3 * cols * length,
            bytes_accessed=8 * length * (rows + 3 * cols) + 12 * rows * cols,
            transcendentals=0,
        ),
        name="weight_gradient_own" if mine else "weight_gradient_mate",
    )(place, *tokens, *grads, *received)


def gather_body(
    normed,
    queries,
    saved_keys,
    saved_values,
    output_grad,
    view_links,
    query_weight,
    key_weight,
    value_weight,
):
    length, cols = queries.shape[2:]
    model_width = normed.shape[-1]
    rows = query_weight.shape[0]
    prompts, views, groups = (lax.axis_size(name) for name in ("dp", "view", "head"))
    mean_scale = 1.0 / (prompts * views)
    half = cols // HD // 2
    view = lax.axis_index("view")
    core = lax.rem(view, 2)
    side = view // 2
    chip = lax.axis_index("dp") * (views // 2) + side
    place = jnp.stack([core, lax.axis_index("head"), side * half, (1 - side) * half])
    place = place.astype(jnp.int32)
    arrays = tuple(a.reshape(length, cols) for a in (queries, saved_keys, saved_values, output_grad))

    own_heads, shared = half // 2, half % 2
    each = [2 * step for step in range(own_heads)]
    picks = [
        [(BESIDE, step, 1) for step in each],
        [(BESIDE, step + 1, -1) for step in each],
        [(HERE, step + 1, -1) for step in each],
        [(HERE, step, 1) for step in each],
    ]
    if shared:
        picks += [[(BESIDE, 2 * own_heads, 0)], [(HERE, 2 * own_heads, 0)]]
    packed = pack(picks, place, view_links, arrays)
    to_x, to_cross, to_mate, own = packed[:4]
    x_in = moved(to_x, along_x)
    cross_in = moved(to_cross, across_x)
    mate_in = moved(to_mate, mate)
    sets = [((0, 1, 2, 3), (own, mate_in, x_in, cross_in))]
    if shared:
        to_x, own = packed[4:]
        (to_x,) = after((to_x,), x_in)
        x_in = moved(to_x, along_x)
        sets.append(((0, 2), (own, moved(own, mate), x_in, moved(x_in, mate))))

    flat = normed.reshape(length, model_width)

    def columns(of_chip):
        columns = [
            lax.dynamic_slice_in_dim(flat, (2 * of_chip + part) * rows, rows, axis=1)
            for part in range(2)
        ]
        return jnp.stack(columns)

    toward_x, toward_y = jnp.bitwise_xor(chip, 1), jnp.bitwise_xor(chip, 2)
    here = columns(chip)
    to_straight = columns(jnp.where(core == 0, toward_x, toward_y))
    to_crossed = columns(jnp.where(core == 0, toward_y, toward_x))
    to_corner = columns(jnp.bitwise_xor(chip, 3))
    mate_here = moved(here, only(1, mate))

    own_weights, turn = None, place
    parts = []
    for kept, sources in sets:
        made = attention(turn, kept, sources)
        if own_weights is None:
            ready = after((query_weight, key_weight, value_weight), made)
            own_weights = turned_weights(place, ready)
        (turn,) = after((place,), made, own_weights)
        ahead = moved(made, straight)
        aside = moved(made, crossed)
        inward = moved(made, only(1, mate))
        (sent,) = after((ahead,), aside, inward, mate_here, to_straight, to_crossed, to_corner)
        relay_x = moved(sent, only(1, along_x))
        relay_y = moved(sent, only(0, across_y))
        parts.append((made, inward, ahead, aside, relay_x, relay_y))
    grads = [array for kind in zip(*parts) for array in kind]
    weights = joined_weights(place, own_weights, moved(own_weights, mate))

    slots = input_product(place, grads, weights)
    arrived = [
        lax.ppermute(slots[s], "head", [(z, z ^ s) for z in range(groups)])
        for s in range(1, groups)
    ]
    total = sum(array.astype(jnp.float32) for array in (slots[0], *arrived))
    total = total.astype(jnp.bfloat16)

    to_straight, to_crossed = after((to_straight, to_crossed), *slots)
    normed_ahead = moved(to_straight, straight)
    normed_aside = moved(to_crossed, crossed)
    (to_corner,) = after((to_corner,), normed_ahead, normed_aside)
    tokens = (
        here,
        mate_here,
        normed_ahead,
        normed_aside,
        moved(to_corner, corner_same),
        moved(to_corner, corner_cross),
    )
    (total,) = after((total,), tokens[4], tokens[5])

    def spot(y, v, z):
        return (y * views + v) * groups + z

    corners = [(y, v, z) for y in range(prompts) for v in range(views) for z in range(groups)]
    beside = lax.ppermute(
        total,
        ("dp", "view", "head"),
        [(spot(y, v, z), spot(y ^ (v % 2), v ^ z, z)) for y, v, z in corners],
    )
    (turn,) = after((place,), beside)
    for_mate = weight_product(turn, False, mean_scale, cols, tokens, grads)
    from_mate = moved(for_mate, mate)
    weight_grads = weight_product(place, True, mean_scale, cols, tokens, grads, (from_mate,))
    (beside,) = after((beside,), for_mate)
    input_grad = lax.ppermute(
        beside,
        ("dp", "view", "head"),
        [
            (
                spot(y ^ (v % 2), v ^ z, z),
                spot(y ^ (v % 2), v ^ z, y * (views // 2) + v // 2),
            )
            for y, v, z in corners
        ],
    )

    (input_grad,) = after((input_grad,), *weight_grads)
    return (
        input_grad.reshape(1, 1, length, model_width // groups),
        *weight_grads,
    )


def solution(mesh):
    prompts, views, groups = (mesh.shape[name] for name in ("dp", "view", "head"))
    loop_of_four = prompts * 2 == views and prompts * views == 2 * groups and views == groups

    def choose(*arrays):
        batch, held, length, cols = arrays[1].shape
        if loop_of_four and batch == held == 1 and length % HD == 0 and cols % (2 * HD) == 0:
            return gather_body(*arrays)
        return halo_body(*arrays)

    placed = (
        P("dp", "view", None, None),
        P("dp", "view", None, "head"),
        P("dp", "view", None, "head"),
        P("dp", "view", None, "head"),
        P("dp", "view", None, "head"),
        P("view", None),
        P(("dp", "view"), "head"),
        P(("dp", "view"), "head"),
        P(("dp", "view"), "head"),
    )
    return jax.shard_map(
        choose,
        mesh=mesh,
        in_specs=placed,
        out_specs=(
            P("dp", "view", None, "head"),
            P(("dp", "view"), "head"),
            P(("dp", "view"), "head"),
            P(("dp", "view"), "head"),
        ),
        check_vma=False,
    )
```

```python
import functools

import jax
import jax.numpy as jnp
from jax import lax
from jax.experimental import pallas as pl
from jax.experimental.pallas import tpu as pltpu
from jax.sharding import PartitionSpec as P

HD = 128
LOG2E = 1.4426950408889634
MIB = 1024 * 1024


def shifted(value, axis, steps):
    count = lax.axis_size(axis)
    pairs = [(source, (source + steps) % count) for source in range(count)]
    return lax.ppermute(value, axis, pairs)


def attend(query_rows, grad_rows, blocks, usable, scaling):
    batch_size, length, col_count = query_rows.shape
    heads_here = col_count // HD
    key_heads = blocks[..., :col_count].reshape(batch_size, 3 * length, heads_here, HD)
    value_heads = blocks[..., col_count:].reshape(batch_size, 3 * length, heads_here, HD)
    query_heads = query_rows.reshape(batch_size, length, heads_here, HD)
    grad_heads = grad_rows.reshape(batch_size, length, heads_here, HD)
    scores = (
        jnp.einsum("bshd,bthd->bhst", query_heads, key_heads, preferred_element_type=jnp.float32)
        * scaling
    )
    scores = jnp.where(usable, scores, -1e30)
    largest = jnp.max(scores, axis=-1, keepdims=True)
    powers = jnp.exp(scores - largest)
    attn_probs = powers / jnp.sum(powers, axis=-1, keepdims=True)
    probs_half = attn_probs.astype(jnp.bfloat16)
    prob_grad = jnp.einsum(
        "bshd,bthd->bhst", grad_heads, value_heads, preferred_element_type=jnp.float32
    )
    row_delta = jnp.sum(attn_probs * prob_grad, axis=-1, keepdims=True)
    score_grad = (scaling * attn_probs * (prob_grad - row_delta)).astype(jnp.bfloat16)
    query_grad = jnp.einsum(
        "bhst,bthd->bshd", score_grad, key_heads, preferred_element_type=jnp.float32
    )
    key_grad = jnp.einsum(
        "bhst,bshd->bthd", score_grad, query_heads, preferred_element_type=jnp.float32
    )
    value_grad = jnp.einsum(
        "bhst,bshd->bthd", probs_half, grad_heads, preferred_element_type=jnp.float32
    )
    query_grad = query_grad.reshape(batch_size, length, col_count)
    key_grad = key_grad.reshape(batch_size, 3, length, col_count)
    value_grad = value_grad.reshape(batch_size, 3, length, col_count)
    return (query_grad, jnp.concatenate([key_grad, value_grad], axis=-1))


def halo_body(
    normed,
    queries,
    saved_keys,
    saved_values,
    output_grad,
    view_links,
    query_weight,
    key_weight,
    value_weight,
):
    scaling = HD ** (-0.5)
    batch_size, view_count, length, col_count = queries.shape
    model_width = normed.shape[-1]
    pairs = jnp.concatenate([saved_keys, saved_values], axis=-1)
    from_lower = shifted(pairs, "view", 1)
    from_upper = shifted(pairs, "view", -1)
    extended = jnp.concatenate([from_lower, pairs, from_upper], axis=1)
    block_index = jnp.arange(3 * length) // length
    pair_grads = jnp.zeros(extended.shape, jnp.float32)
    link_flags = view_links[0] >= 0
    usable = jnp.where(
        block_index == 0, link_flags[0], jnp.where(block_index == 2, link_flags[1], True)
    )
    query_grad, block_grad = attend(queries[:, 0], output_grad[:, 0], extended, usable, scaling)
    query_grads = [query_grad]
    pair_grads = pair_grads.at[:, 0:3].add(block_grad)
    row_count = batch_size * view_count * length
    query_half = jnp.stack(query_grads, axis=1).astype(jnp.bfloat16).reshape(row_count, col_count)
    flat_input = normed.reshape(row_count, model_width)
    mean_scale = 1.0 / (lax.axis_size("dp") * batch_size * lax.axis_size("view") * view_count)
    from_lower_grads = shifted(pair_grads[:, -1:], "view", 1)
    from_upper_grads = shifted(pair_grads[:, :1], "view", -1)
    own_grads = pair_grads[:, 1 : view_count + 1]
    own_grads = own_grads.at[:, :1].add(from_lower_grads)
    own_grads = own_grads.at[:, -1:].add(from_upper_grads)
    key_half = own_grads[..., :col_count].astype(jnp.bfloat16).reshape(row_count, col_count)
    value_half = own_grads[..., col_count:].astype(jnp.bfloat16).reshape(row_count, col_count)
    all_grads = jnp.concatenate([query_half, key_half, value_half], axis=-1)
    grads_three = all_grads.reshape(row_count, 3, col_count)
    stacked = jnp.stack([query_weight, key_weight, value_weight])
    partial_input = jnp.einsum(
        "ric,ipc->rp",
        grads_three,
        lax.all_gather(stacked, ("dp", "view"), axis=1, tiled=True),
        preferred_element_type=jnp.float32,
    )
    summed_input = lax.psum_scatter(partial_input, "head", scatter_dimension=1, tiled=True)
    input_grad = summed_input.astype(jnp.bfloat16).reshape(
        batch_size, view_count, length, model_width // lax.axis_size("head")
    )
    product = lax.dot_general(
        flat_input, all_grads, (((0,), (0,)), ((), ())), preferred_element_type=jnp.float32
    )
    together = lax.psum_scatter(
        product * mean_scale, ("dp", "view"), scatter_dimension=0, tiled=True
    )
    grad_query = together[:, :col_count]
    grad_key = together[:, col_count : 2 * col_count]
    grad_value = together[:, 2 * col_count :]
    return (input_grad, grad_query, grad_key, grad_value)


def moved(value, target):
    prompts, views = lax.axis_size("dp"), lax.axis_size("view")
    pairs = []
    for y in range(prompts):
        for v in range(views):
            goal = target(y, v)
            if goal is not None:
                pairs.append((y * views + v, goal[0] * views + goal[1]))
    return lax.ppermute(value, ("dp", "view"), pairs)


def mate(y, v):
    return (y, v ^ 1)


def along_x(y, v):
    return (y, v ^ 2)


def across_x(y, v):
    return (y, v ^ 3)


def only(core, target):
    return lambda y, v: target(y, v) if v % 2 == core else None


def along_y(y, v):
    return (y ^ 1, v)


def across_y(y, v):
    return (y ^ 1, v ^ 1)


def straight(y, v):
    return along_x(y, v) if v % 2 == 0 else along_y(y, v)


def crossed(y, v):
    return across_y(y, v) if v % 2 == 0 else across_x(y, v)


def corner_same(y, v):
    return None if v % 2 == 0 else (y ^ 1, v ^ 2)


def corner_cross(y, v):
    return (y ^ 1, v ^ 3) if v % 2 == 0 else None


def lanes(start, size):
    return pl.ds(pl.multiple_of(start, HD), size)


def whole(space=pltpu.VMEM):
    return pl.BlockSpec(memory_space=space)


def dot_last(a, b):
    return lax.dot_general(a, b, (((1,), (1,)), ((), ())), preferred_element_type=jnp.float32)


def dot_first(a, b):
    return lax.dot_general(a, b, (((0,), (0,)), ((), ())), preferred_element_type=jnp.float32)


def dot(a, b):
    return jnp.dot(a, b, preferred_element_type=jnp.float32)


def after(values, *earlier):
    return lax.optimization_barrier((tuple(values), tuple(earlier)))[0]


CORE, PLANE, HERE, BESIDE = range(4)
FLAG_ROWS = 16


def pack_kernel(picks, place_ref, links_ref, q_ref, k_ref, v_ref, g_ref, *out_refs):
    length = q_ref.shape[0]
    row = lax.broadcasted_iota(jnp.int32, (FLAG_ROWS, HD), 0)
    gaps = [jnp.where(links_ref[0, side] >= 0, 0.0, 1.0).astype(jnp.float32) for side in range(2)]
    flags = jnp.where(row < FLAG_ROWS // 2, gaps[0], gaps[1])
    for heads, out_ref in zip(picks, out_refs):
        for at, (base, step, sign) in enumerate(heads):
            head = place_ref[base] + step + sign * place_ref[CORE]
            for kind, source in enumerate((q_ref, k_ref, v_ref, g_ref)):
                out_ref[at, kind * length : (kind + 1) * length] = source[:, lanes(head * HD, HD)]
            out_ref[at, 4 * length : 4 * length + FLAG_ROWS] = flags.astype(out_ref.dtype)


def pack(picks, place, links, arrays):
    length = arrays[0].shape[0]
    height = 4 * length + FLAG_ROWS
    return pl.pallas_call(
        functools.partial(pack_kernel, picks),
        out_shape=[
            jax.ShapeDtypeStruct((len(heads), height, HD), jnp.bfloat16) for heads in picks
        ],
        in_specs=[whole(pltpu.SMEM)] * 2 + [whole()] * 4,
        out_specs=[whole()] * len(picks),
        name="pack_heads",
    )(place, links, *arrays)


def one_head(scaling, core, xs, length, keys, values, key_sums, value_sums):
    factor = scaling * LOG2E

    def rows(e, kind):
        return xs[e][kind * length : (kind + 1) * length]

    def gap(e, side):
        at = 4 * length + side * (FLAG_ROWS // 2)
        flags = xs[e][at : at + FLAG_ROWS // 2].astype(jnp.float32)[0:1]
        return jnp.concatenate([flags] * (length // HD), axis=1) * 1e30

    for at in range(6):
        keys[at * length : (at + 1) * length] = rows((at + 3) % 4, 1)
        values[at * length : (at + 1) * length] = rows((at + 3) % 4, 2)
    query_grads = []
    for e in range(4):
        blocks = slice(e * length, (e + 3) * length)
        before, behind = gap(e, 0), gap(e, 1)
        far_below = jnp.where(core == 0, before, behind)
        far_above = jnp.where(core == 0, behind, before)
        q, g = rows(e, 0), rows(e, 3)
        near = keys[blocks]
        scores = dot_last(near, q)
        scores = [scores[at * length : (at + 1) * length] for at in range(3)]
        tops = [jnp.max(part, axis=0, keepdims=True) for part in scores]
        top = jnp.maximum(tops[1], jnp.maximum(tops[0] - far_below, tops[2] - far_above))
        offsets = (top + far_below, top, top + far_above)
        powers = [jnp.exp2((part - o) * factor) for part, o in zip(scores, offsets)]
        inverse = 1.0 / sum(jnp.sum(p, axis=0, keepdims=True) for p in powers)
        prob_grads = dot_last(values[blocks], g)
        prob_grads = [prob_grads[at * length : (at + 1) * length] for at in range(3)]
        delta = inverse * sum(
            jnp.sum(p * d, axis=0, keepdims=True) for p, d in zip(powers, prob_grads)
        )
        probs = [p * inverse for p in powers]
        score_grad = jnp.concatenate(
            [
                (p * scaling * (d - delta)).astype(jnp.bfloat16)
                for p, d in zip(probs, prob_grads)
            ],
            axis=0,
        )
        probs_half = jnp.concatenate([p.astype(jnp.bfloat16) for p in probs], axis=0)
        query_grads.append(dot_first(score_grad, near))
        for sums, part in ((key_sums, dot(score_grad, q)), (value_sums, dot(probs_half, g))):
            if e == 0:
                sums[blocks] = part
            else:
                held = slice(e * length, (e + 2) * length)
                sums[held] += part[: 2 * length]
                sums[(e + 2) * length : (e + 3) * length] = part[2 * length :]

    def by_view(sums):
        parts = [sums[at * length : (at + 1) * length] for at in range(6)]
        return (parts[1] + parts[5], parts[2], parts[3], parts[0] + parts[4])

    return query_grads, by_view(key_sums), by_view(value_sums)


def attention_kernel(scaling, kept, place_ref, own, mate_in, x_in, far_in, *refs):
    out_ref, keys, values, key_sums, value_sums = refs
    length = out_ref.shape[1]
    heads = own.shape[0]
    for head in range(heads):
        xs = [own.at[head], mate_in.at[head], x_in.at[head], far_in.at[head]]
        grads = one_head(
            scaling, place_ref[CORE], xs, length, keys, values, key_sums, value_sums
        )
        for at, e in enumerate(kept):
            for kind in range(3):
                out_ref[len(kept) * head + at, :, kind * HD : (kind + 1) * HD] = grads[kind][
                    e
                ].astype(out_ref.dtype)


def attention(place, kept, sources):
    heads, height, _ = sources[0].shape
    length = (height - FLAG_ROWS) // 4
    return pl.pallas_call(
        functools.partial(attention_kernel, HD ** (-0.5), kept),
        out_shape=jax.ShapeDtypeStruct((len(kept) * heads, length, 3 * HD), jnp.bfloat16),
        in_specs=[whole(pltpu.SMEM)] + [whole()] * 4,
        out_specs=whole(),
        scratch_shapes=[pltpu.VMEM((6 * length, HD), jnp.bfloat16)] * 2
        + [pltpu.VMEM((6 * length, HD), jnp.float32)] * 2,
        compiler_params=pltpu.CompilerParams(vmem_limit_bytes=40 * MIB),
        cost_estimate=pl.CostEstimate(
            flops=heads * 4 * 5 * 2 * length * 3 * length * HD * 2,
            bytes_accessed=heads * 2 * length * 7 * HD * 4,
            transcendentals=heads * 12 * length * length,
        ),
        name="attention_gradients",
    )(place, *sources)


def turn_kernel(place_ref, q_ref, k_ref, v_ref, out_ref):
    half = q_ref.shape[1] // HD // 2
    for side, base in enumerate((HERE, BESIDE)):
        for head in range(half):
            for kind, source in enumerate((q_ref, k_ref, v_ref)):
                at = ((side * half + head) * 3 + kind) * HD
                out_ref[at : at + HD] = source[:, lanes((place_ref[base] + head) * HD, HD)].T


def turned_weights(place, weights):
    rows, cols = weights[0].shape
    return pl.pallas_call(
        turn_kernel,
        out_shape=jax.ShapeDtypeStruct((3 * cols, rows), jnp.bfloat16),
        in_specs=[whole(pltpu.SMEM)] + [whole()] * 3,
        out_specs=whole(),
        compiler_params=pltpu.CompilerParams(vmem_limit_bytes=8 * MIB),
        name="turn_weights",
    )(place, *weights)


def join_kernel(place_ref, own_ref, mate_ref, out_ref):
    core = place_ref[CORE]
    rows = own_ref.shape[1]
    out_ref[:, lanes(core * rows, rows)] = own_ref[...]
    out_ref[:, lanes((1 - core) * rows, rows)] = mate_ref[...]


def joined_weights(place, own_weights, mate_weights):
    depth, rows = own_weights.shape
    return pl.pallas_call(
        join_kernel,
        out_shape=jax.ShapeDtypeStruct((depth, 2 * rows), jnp.bfloat16),
        in_specs=[whole(pltpu.SMEM)] + [whole()] * 2,
        out_specs=whole(),
        compiler_params=pltpu.CompilerParams(vmem_limit_bytes=12 * MIB),
        name="join_weights",
    )(place, own_weights, mate_weights)


def gathered(role, refs):
    sides = []
    for side in range(2):
        pieces = []
        for head in range(refs[0][0].shape[0] // 4):
            for maker in range(2):
                k = 2 * side + (maker ^ role)
                pieces.append([refs[k][0][4 * head + (e ^ k)] for e in range(4)])
        for at in range(refs[0][1].shape[0] // 2 if len(refs[0]) > 1 else 0):
            rows = []
            for e in range(4):
                k = 2 * side + e % 2
                rows.append(refs[k][1][2 * at + (e // 2 ^ side)])
            pieces.append(rows)
        sides.append(
            jnp.concatenate([jnp.concatenate(rows, axis=0) for rows in pieces], axis=1)
        )
    return sides


def by_role(refs, parts):
    made, inward, ahead, aside, relay_x, relay_y = [
        refs[at * parts : (at + 1) * parts] for at in range(6)
    ]
    return ((made, inward, ahead, aside), (ahead, aside, relay_x, relay_y))


def input_kernel(parts, place_ref, *refs):
    weights, out_refs, total = refs[6 * parts], refs[6 * parts + 1 : -1], refs[-1]
    length = out_refs[0].shape[0]
    for role, grads in enumerate(by_role(refs, parts)):

        @pl.when(place_ref[CORE] == role)
        def _():
            left = jnp.concatenate(gathered(role, grads), axis=1)
            for e in range(4):
                product = dot(left[e * length : (e + 1) * length], weights[...])
                total[e] = product.astype(total.dtype)

    for s, out_ref in enumerate(out_refs):
        out_ref[...] = total[jnp.bitwise_xor(place_ref[PLANE], s)]


def input_product(place, grads, weights):
    _, length, _ = grads[0].shape
    depth, rows = weights.shape
    out = jax.ShapeDtypeStruct((length, rows), jnp.bfloat16)
    return pl.pallas_call(
        functools.partial(input_kernel, len(grads) // 6),
        out_shape=[out] * 4,
        in_specs=[whole(pltpu.SMEM)] + [whole()] * (len(grads) + 1),
        out_specs=[whole()] * 4,
        scratch_shapes=[pltpu.VMEM((4, length, rows), jnp.bfloat16)],
        compiler_params=pltpu.CompilerParams(vmem_limit_bytes=16 * MIB),
        cost_estimate=pl.CostEstimate(
            flops=8 * length * rows * depth,
            bytes_accessed=8 * length * (rows + depth) + 2 * rows * depth,
            transcendentals=0,
        ),
        name="input_gradient",
    )(place, *grads, weights)


def weight_kernel(mine, mean_scale, parts, place_ref, *refs):
    own, mate_in, first, second, corner, corner_far = refs[:6]
    grad_refs, refs = refs[6 : 6 + 6 * parts], refs[6 + 6 * parts :]
    if mine:
        received, out_refs, turned = refs[0], refs[1:4], refs[4]
    else:
        received, out_refs, turned = None, [refs[0].at[kind] for kind in range(3)], refs[1]
    core = place_ref[CORE]
    length = own.shape[1]
    part = core if mine else 1 - core
    tokens = ((own, mate_in, first, second), (first, second, corner, corner_far))
    for role, grads in enumerate(by_role(grad_refs, parts)):

        @pl.when(core == role)
        def _():
            for e, source in enumerate(tokens[role]):
                turned[:, e * length : (e + 1) * length] = source[part].T
            for base, side in zip((HERE, BESIDE), gathered(role, grads)):
                total = dot(turned[...], side)
                for head in range(side.shape[1] // (3 * HD)):
                    here = lanes((place_ref[base] + head) * HD, HD)
                    for kind, out in enumerate(out_refs):
                        at = (head * 3 + kind) * HD
                        value = total[:, at : at + HD]
                        if mine:
                            value = (value + received[kind, :, here]) * mean_scale
                        out[:, here] = value.astype(out.dtype)


def weight_product(place, mine, mean_scale, cols, tokens, grads, received=()):
    _, length, _ = grads[0].shape
    rows = tokens[0].shape[2]
    out = jax.ShapeDtypeStruct((rows, cols), jnp.float32)
    both = jax.ShapeDtypeStruct((3, rows, cols), jnp.bfloat16)
    return pl.pallas_call(
        functools.partial(weight_kernel, mine, mean_scale, len(grads) // 6),
        out_shape=[out] * 3 if mine else both,
        in_specs=[whole(pltpu.SMEM)] + [whole()] * (6 + len(grads) + len(received)),
        out_specs=[whole()] * 3 if mine else whole(),
        scratch_shapes=[pltpu.VMEM((rows, 4 * length), jnp.bfloat16)],
        compiler_params=pltpu.CompilerParams(vmem_limit_bytes=16 * MIB),
        cost_estimate=pl.CostEstimate(
            flops=8 * rows * 3 * cols * length,
            bytes_accessed=8 * length * (rows + 3 * cols) + 12 * rows * cols,
            transcendentals=0,
        ),
        name="weight_gradient_own" if mine else "weight_gradient_mate",
    )(place, *tokens, *grads, *received)


def gather_body(
    normed,
    queries,
    saved_keys,
    saved_values,
    output_grad,
    view_links,
    query_weight,
    key_weight,
    value_weight,
):
    length, cols = queries.shape[2:]
    model_width = normed.shape[-1]
    rows = query_weight.shape[0]
    prompts, views, groups = (lax.axis_size(name) for name in ("dp", "view", "head"))
    mean_scale = 1.0 / (prompts * views)
    half = cols // HD // 2
    view = lax.axis_index("view")
    core = lax.rem(view, 2)
    side = view // 2
    chip = lax.axis_index("dp") * (views // 2) + side
    place = jnp.stack([core, lax.axis_index("head"), side * half, (1 - side) * half])
    place = place.astype(jnp.int32)
    arrays = tuple(a.reshape(length, cols) for a in (queries, saved_keys, saved_values, output_grad))

    own_heads, shared = half // 2, half % 2
    each = [2 * step for step in range(own_heads)]
    picks = [
        [(BESIDE, step, 1) for step in each],
        [(BESIDE, step + 1, -1) for step in each],
        [(HERE, step + 1, -1) for step in each],
        [(HERE, step, 1) for step in each],
    ]
    if shared:
        picks += [[(BESIDE, 2 * own_heads, 0)], [(HERE, 2 * own_heads, 0)]]
    packed = pack(picks, place, view_links, arrays)
    to_x, to_cross, to_mate, own = packed[:4]
    x_in = moved(to_x, along_x)
    cross_in = moved(to_cross, across_x)
    mate_in = moved(to_mate, mate)
    sets = [((0, 1, 2, 3), (own, mate_in, x_in, cross_in))]
    if shared:
        to_x, own = packed[4:]
        (to_x,) = after((to_x,), x_in)
        x_in = moved(to_x, along_x)
        sets.append(((0, 2), (own, moved(own, mate), x_in, moved(x_in, mate))))

    flat = normed.reshape(length, model_width)

    def columns(of_chip):
        columns = [
            lax.dynamic_slice_in_dim(flat, (2 * of_chip + part) * rows, rows, axis=1)
            for part in range(2)
        ]
        return jnp.stack(columns)

    toward_x, toward_y = jnp.bitwise_xor(chip, 1), jnp.bitwise_xor(chip, 2)
    here = columns(chip)
    to_straight = columns(jnp.where(core == 0, toward_x, toward_y))
    to_crossed = columns(jnp.where(core == 0, toward_y, toward_x))
    to_corner = columns(jnp.bitwise_xor(chip, 3))
    own_weights, turn = None, place
    parts = []
    for kept, sources in sets:
        made = attention(turn, kept, sources)
        if own_weights is None:
            ready = after((query_weight, key_weight, value_weight), made)
            own_weights = turned_weights(place, ready)
        ahead = moved(made, straight)
        aside = moved(made, crossed)
        inward = moved(made, only(1, mate))
        (turn,) = after((place,), made, own_weights)
        (sent,) = after((ahead,), aside, inward, here, to_straight, to_crossed, to_corner)
        relay_x = moved(sent, only(1, along_x))
        relay_y = moved(sent, only(0, across_y))
        parts.append((made, inward, ahead, aside, relay_x, relay_y))
    grads = [array for kind in zip(*parts) for array in kind]
    weights = joined_weights(place, own_weights, moved(own_weights, mate))

    slots = input_product(place, grads, weights)
    arrived = [
        lax.ppermute(slots[s], "head", [(z, z ^ s) for z in range(groups)])
        for s in range(1, groups)
    ]
    total = sum(array.astype(jnp.float32) for array in (slots[0], *arrived))
    total = total.astype(jnp.bfloat16)

    to_straight, to_crossed = after((to_straight, to_crossed), *slots)
    normed_ahead = moved(to_straight, straight)
    normed_aside = moved(to_crossed, crossed)
    to_corner, sent = after((to_corner, here), normed_ahead, normed_aside)
    mate_here = moved(sent, only(1, mate))
    tokens = (
        here,
        mate_here,
        normed_ahead,
        normed_aside,
        moved(to_corner, corner_same),
        moved(to_corner, corner_cross),
    )
    (total,) = after((total,), tokens[4], tokens[5])

    def spot(y, v, z):
        return (y * views + v) * groups + z

    corners = [(y, v, z) for y in range(prompts) for v in range(views) for z in range(groups)]
    beside = lax.ppermute(
        total,
        ("dp", "view", "head"),
        [(spot(y, v, z), spot(y ^ (v % 2), v ^ z, z)) for y, v, z in corners],
    )
    (turn,) = after((place,), beside)
    for_mate = weight_product(turn, False, mean_scale, cols, tokens, grads)
    from_mate = moved(for_mate, mate)
    weight_grads = weight_product(place, True, mean_scale, cols, tokens, grads, (from_mate,))
    (beside,) = after((beside,), for_mate)
    input_grad = lax.ppermute(
        beside,
        ("dp", "view", "head"),
        [
            (
                spot(y ^ (v % 2), v ^ z, z),
                spot(y ^ (v % 2), v ^ z, y * (views // 2) + v // 2),
            )
            for y, v, z in corners
        ],
    )

    (input_grad,) = after((input_grad,), *weight_grads)
    return (
        input_grad.reshape(1, 1, length, model_width // groups),
        *weight_grads,
    )


def solution(mesh):
    prompts, views, groups = (mesh.shape[name] for name in ("dp", "view", "head"))
    loop_of_four = prompts * 2 == views and prompts * views == 2 * groups and views == groups

    def choose(*arrays):
        batch, held, length, cols = arrays[1].shape
        if loop_of_four and batch == held == 1 and length % HD == 0 and cols % (2 * HD) == 0:
            return gather_body(*arrays)
        return halo_body(*arrays)

    placed = (
        P("dp", "view", None, None),
        P("dp", "view", None, "head"),
        P("dp", "view", None, "head"),
        P("dp", "view", None, "head"),
        P("dp", "view", None, "head"),
        P("view", None),
        P(("dp", "view"), "head"),
        P(("dp", "view"), "head"),
        P(("dp", "view"), "head"),
    )
    return jax.shard_map(
        choose,
        mesh=mesh,
        in_specs=placed,
        out_specs=(
            P("dp", "view", None, "head"),
            P(("dp", "view"), "head"),
            P(("dp", "view"), "head"),
            P(("dp", "view"), "head"),
        ),
        check_vma=False,
    )
```

```python
import functools

import jax
import jax.numpy as jnp
from jax import lax
from jax.experimental import pallas as pl
from jax.experimental.pallas import tpu as pltpu
from jax.sharding import PartitionSpec as P

HD = 128
LOG2E = 1.4426950408889634
MIB = 1024 * 1024


def shifted(value, axis, steps):
    count = lax.axis_size(axis)
    pairs = [(source, (source + steps) % count) for source in range(count)]
    return lax.ppermute(value, axis, pairs)


def attend(query_rows, grad_rows, blocks, usable, scaling):
    batch_size, length, col_count = query_rows.shape
    heads_here = col_count // HD
    key_heads = blocks[..., :col_count].reshape(batch_size, 3 * length, heads_here, HD)
    value_heads = blocks[..., col_count:].reshape(batch_size, 3 * length, heads_here, HD)
    query_heads = query_rows.reshape(batch_size, length, heads_here, HD)
    grad_heads = grad_rows.reshape(batch_size, length, heads_here, HD)
    scores = (
        jnp.einsum("bshd,bthd->bhst", query_heads, key_heads, preferred_element_type=jnp.float32)
        * scaling
    )
    scores = jnp.where(usable, scores, -1e30)
    largest = jnp.max(scores, axis=-1, keepdims=True)
    powers = jnp.exp(scores - largest)
    attn_probs = powers / jnp.sum(powers, axis=-1, keepdims=True)
    probs_half = attn_probs.astype(jnp.bfloat16)
    prob_grad = jnp.einsum(
        "bshd,bthd->bhst", grad_heads, value_heads, preferred_element_type=jnp.float32
    )
    row_delta = jnp.sum(attn_probs * prob_grad, axis=-1, keepdims=True)
    score_grad = (scaling * attn_probs * (prob_grad - row_delta)).astype(jnp.bfloat16)
    query_grad = jnp.einsum(
        "bhst,bthd->bshd", score_grad, key_heads, preferred_element_type=jnp.float32
    )
    key_grad = jnp.einsum(
        "bhst,bshd->bthd", score_grad, query_heads, preferred_element_type=jnp.float32
    )
    value_grad = jnp.einsum(
        "bhst,bshd->bthd", probs_half, grad_heads, preferred_element_type=jnp.float32
    )
    query_grad = query_grad.reshape(batch_size, length, col_count)
    key_grad = key_grad.reshape(batch_size, 3, length, col_count)
    value_grad = value_grad.reshape(batch_size, 3, length, col_count)
    return (query_grad, jnp.concatenate([key_grad, value_grad], axis=-1))


def halo_body(
    normed,
    queries,
    saved_keys,
    saved_values,
    output_grad,
    view_links,
    query_weight,
    key_weight,
    value_weight,
):
    scaling = HD ** (-0.5)
    batch_size, view_count, length, col_count = queries.shape
    model_width = normed.shape[-1]
    pairs = jnp.concatenate([saved_keys, saved_values], axis=-1)
    from_lower = shifted(pairs, "view", 1)
    from_upper = shifted(pairs, "view", -1)
    extended = jnp.concatenate([from_lower, pairs, from_upper], axis=1)
    block_index = jnp.arange(3 * length) // length
    pair_grads = jnp.zeros(extended.shape, jnp.float32)
    link_flags = view_links[0] >= 0
    usable = jnp.where(
        block_index == 0, link_flags[0], jnp.where(block_index == 2, link_flags[1], True)
    )
    query_grad, block_grad = attend(queries[:, 0], output_grad[:, 0], extended, usable, scaling)
    query_grads = [query_grad]
    pair_grads = pair_grads.at[:, 0:3].add(block_grad)
    row_count = batch_size * view_count * length
    query_half = jnp.stack(query_grads, axis=1).astype(jnp.bfloat16).reshape(row_count, col_count)
    flat_input = normed.reshape(row_count, model_width)
    mean_scale = 1.0 / (lax.axis_size("dp") * batch_size * lax.axis_size("view") * view_count)
    from_lower_grads = shifted(pair_grads[:, -1:], "view", 1)
    from_upper_grads = shifted(pair_grads[:, :1], "view", -1)
    own_grads = pair_grads[:, 1 : view_count + 1]
    own_grads = own_grads.at[:, :1].add(from_lower_grads)
    own_grads = own_grads.at[:, -1:].add(from_upper_grads)
    key_half = own_grads[..., :col_count].astype(jnp.bfloat16).reshape(row_count, col_count)
    value_half = own_grads[..., col_count:].astype(jnp.bfloat16).reshape(row_count, col_count)
    all_grads = jnp.concatenate([query_half, key_half, value_half], axis=-1)
    grads_three = all_grads.reshape(row_count, 3, col_count)
    stacked = jnp.stack([query_weight, key_weight, value_weight])
    partial_input = jnp.einsum(
        "ric,ipc->rp",
        grads_three,
        lax.all_gather(stacked, ("dp", "view"), axis=1, tiled=True),
        preferred_element_type=jnp.float32,
    )
    summed_input = lax.psum_scatter(partial_input, "head", scatter_dimension=1, tiled=True)
    input_grad = summed_input.astype(jnp.bfloat16).reshape(
        batch_size, view_count, length, model_width // lax.axis_size("head")
    )
    product = lax.dot_general(
        flat_input, all_grads, (((0,), (0,)), ((), ())), preferred_element_type=jnp.float32
    )
    together = lax.psum_scatter(
        product * mean_scale, ("dp", "view"), scatter_dimension=0, tiled=True
    )
    grad_query = together[:, :col_count]
    grad_key = together[:, col_count : 2 * col_count]
    grad_value = together[:, 2 * col_count :]
    return (input_grad, grad_query, grad_key, grad_value)


def moved(value, target):
    prompts, views = lax.axis_size("dp"), lax.axis_size("view")
    pairs = []
    for y in range(prompts):
        for v in range(views):
            goal = target(y, v)
            if goal is not None:
                pairs.append((y * views + v, goal[0] * views + goal[1]))
    return lax.ppermute(value, ("dp", "view"), pairs)


def mate(y, v):
    return (y, v ^ 1)


def along_x(y, v):
    return (y, v ^ 2)


def across_x(y, v):
    return (y, v ^ 3)


def only(core, target):
    return lambda y, v: target(y, v) if v % 2 == core else None


def along_y(y, v):
    return (y ^ 1, v)


def across_y(y, v):
    return (y ^ 1, v ^ 1)


def straight(y, v):
    return along_x(y, v) if v % 2 == 0 else along_y(y, v)


def crossed(y, v):
    return across_y(y, v) if v % 2 == 0 else across_x(y, v)


def corner_same(y, v):
    return None if v % 2 == 0 else (y ^ 1, v ^ 2)


def corner_cross(y, v):
    return (y ^ 1, v ^ 3) if v % 2 == 0 else None


def lanes(start, size):
    return pl.ds(pl.multiple_of(start, HD), size)


def whole(space=pltpu.VMEM):
    return pl.BlockSpec(memory_space=space)


def dot_last(a, b):
    return lax.dot_general(a, b, (((1,), (1,)), ((), ())), preferred_element_type=jnp.float32)


def dot_first(a, b):
    return lax.dot_general(a, b, (((0,), (0,)), ((), ())), preferred_element_type=jnp.float32)


def dot(a, b):
    return jnp.dot(a, b, preferred_element_type=jnp.float32)


def after(values, *earlier):
    return lax.optimization_barrier((tuple(values), tuple(earlier)))[0]


CORE, PLANE, HERE, BESIDE = range(4)
FLAG_ROWS = 16


def pack_kernel(picks, place_ref, links_ref, q_ref, k_ref, v_ref, g_ref, *out_refs):
    length = q_ref.shape[0]
    row = lax.broadcasted_iota(jnp.int32, (FLAG_ROWS, HD), 0)
    gaps = [jnp.where(links_ref[0, side] >= 0, 0.0, 1.0).astype(jnp.float32) for side in range(2)]
    flags = jnp.where(row < FLAG_ROWS // 2, gaps[0], gaps[1])
    for heads, out_ref in zip(picks, out_refs):
        for at, (base, step, sign) in enumerate(heads):
            head = place_ref[base] + step + sign * place_ref[CORE]
            for kind, source in enumerate((q_ref, k_ref, v_ref, g_ref)):
                out_ref[at, kind * length : (kind + 1) * length] = source[:, lanes(head * HD, HD)]
            out_ref[at, 4 * length : 4 * length + FLAG_ROWS] = flags.astype(out_ref.dtype)


def pack(picks, place, links, arrays):
    length = arrays[0].shape[0]
    height = 4 * length + FLAG_ROWS
    return pl.pallas_call(
        functools.partial(pack_kernel, picks),
        out_shape=[
            jax.ShapeDtypeStruct((len(heads), height, HD), jnp.bfloat16) for heads in picks
        ],
        in_specs=[whole(pltpu.SMEM)] * 2 + [whole()] * 4,
        out_specs=[whole()] * len(picks),
        name="pack_heads",
    )(place, links, *arrays)


def one_head(scaling, core, xs, length, keys, values, key_sums, value_sums):
    factor = scaling * LOG2E

    def rows(e, kind):
        return xs[e][kind * length : (kind + 1) * length]

    def gap(e, side):
        at = 4 * length + side * (FLAG_ROWS // 2)
        flags = xs[e][at : at + FLAG_ROWS // 2].astype(jnp.float32)[0:1]
        return jnp.concatenate([flags] * (length // HD), axis=1) * 1e30

    for at in range(6):
        keys[at * length : (at + 1) * length] = rows((at + 3) % 4, 1)
        values[at * length : (at + 1) * length] = rows((at + 3) % 4, 2)
    query_grads = []
    for e in range(4):
        blocks = slice(e * length, (e + 3) * length)
        before, behind = gap(e, 0), gap(e, 1)
        far_below = jnp.where(core == 0, before, behind)
        far_above = jnp.where(core == 0, behind, before)
        q, g = rows(e, 0), rows(e, 3)
        near = keys[blocks]
        scores = dot_last(near, q)
        scores = [scores[at * length : (at + 1) * length] for at in range(3)]
        tops = [jnp.max(part, axis=0, keepdims=True) for part in scores]
        top = jnp.maximum(tops[1], jnp.maximum(tops[0] - far_below, tops[2] - far_above))
        offsets = (top + far_below, top, top + far_above)
        powers = [jnp.exp2((part - o) * factor) for part, o in zip(scores, offsets)]
        inverse = 1.0 / sum(jnp.sum(p, axis=0, keepdims=True) for p in powers)
        prob_grads = dot_last(values[blocks], g)
        prob_grads = [prob_grads[at * length : (at + 1) * length] for at in range(3)]
        delta = inverse * sum(
            jnp.sum(p * d, axis=0, keepdims=True) for p, d in zip(powers, prob_grads)
        )
        probs = [p * inverse for p in powers]
        score_grad = jnp.concatenate(
            [
                (p * scaling * (d - delta)).astype(jnp.bfloat16)
                for p, d in zip(probs, prob_grads)
            ],
            axis=0,
        )
        probs_half = jnp.concatenate([p.astype(jnp.bfloat16) for p in probs], axis=0)
        query_grads.append(dot_first(score_grad, near))
        for sums, part in ((key_sums, dot(score_grad, q)), (value_sums, dot(probs_half, g))):
            if e == 0:
                sums[blocks] = part
            else:
                held = slice(e * length, (e + 2) * length)
                sums[held] += part[: 2 * length]
                sums[(e + 2) * length : (e + 3) * length] = part[2 * length :]

    def by_view(sums):
        parts = [sums[at * length : (at + 1) * length] for at in range(6)]
        return (parts[1] + parts[5], parts[2], parts[3], parts[0] + parts[4])

    return query_grads, by_view(key_sums), by_view(value_sums)


def attention_kernel(scaling, kept, place_ref, own, mate_in, x_in, far_in, *refs):
    out_ref, keys, values, key_sums, value_sums = refs
    length = out_ref.shape[1]
    heads = own.shape[0]
    for head in range(heads):
        xs = [own.at[head], mate_in.at[head], x_in.at[head], far_in.at[head]]
        grads = one_head(
            scaling, place_ref[CORE], xs, length, keys, values, key_sums, value_sums
        )
        for at, e in enumerate(kept):
            for kind in range(3):
                out_ref[len(kept) * head + at, :, kind * HD : (kind + 1) * HD] = grads[kind][
                    e
                ].astype(out_ref.dtype)


def attention(place, kept, sources):
    heads, height, _ = sources[0].shape
    length = (height - FLAG_ROWS) // 4
    return pl.pallas_call(
        functools.partial(attention_kernel, HD ** (-0.5), kept),
        out_shape=jax.ShapeDtypeStruct((len(kept) * heads, length, 3 * HD), jnp.bfloat16),
        in_specs=[whole(pltpu.SMEM)] + [whole()] * 4,
        out_specs=whole(),
        scratch_shapes=[pltpu.VMEM((6 * length, HD), jnp.bfloat16)] * 2
        + [pltpu.VMEM((6 * length, HD), jnp.float32)] * 2,
        compiler_params=pltpu.CompilerParams(vmem_limit_bytes=12 * MIB),
        cost_estimate=pl.CostEstimate(
            flops=heads * 4 * 5 * 2 * length * 3 * length * HD * 2,
            bytes_accessed=heads * 2 * length * 7 * HD * 4,
            transcendentals=heads * 12 * length * length,
        ),
        name="attention_gradients",
    )(place, *sources)


def turn_kernel(place_ref, q_ref, k_ref, v_ref, out_ref):
    half = q_ref.shape[1] // HD // 2
    for side, base in enumerate((HERE, BESIDE)):
        for head in range(half):
            for kind, source in enumerate((q_ref, k_ref, v_ref)):
                at = ((side * half + head) * 3 + kind) * HD
                out_ref[at : at + HD] = source[:, lanes((place_ref[base] + head) * HD, HD)].T


def turned_weights(place, weights):
    rows, cols = weights[0].shape
    return pl.pallas_call(
        turn_kernel,
        out_shape=jax.ShapeDtypeStruct((3 * cols, rows), jnp.bfloat16),
        in_specs=[whole(pltpu.SMEM)] + [whole()] * 3,
        out_specs=whole(),
        compiler_params=pltpu.CompilerParams(vmem_limit_bytes=8 * MIB),
        name="turn_weights",
    )(place, *weights)


def join_kernel(place_ref, own_ref, mate_ref, out_ref):
    core = place_ref[CORE]
    rows = own_ref.shape[1]
    out_ref[:, lanes(core * rows, rows)] = own_ref[...]
    out_ref[:, lanes((1 - core) * rows, rows)] = mate_ref[...]


def joined_weights(place, own_weights, mate_weights):
    depth, rows = own_weights.shape
    return pl.pallas_call(
        join_kernel,
        out_shape=jax.ShapeDtypeStruct((depth, 2 * rows), jnp.bfloat16),
        in_specs=[whole(pltpu.SMEM)] + [whole()] * 2,
        out_specs=whole(),
        compiler_params=pltpu.CompilerParams(vmem_limit_bytes=12 * MIB),
        name="join_weights",
    )(place, own_weights, mate_weights)


def gathered(role, refs):
    sides = []
    for side in range(2):
        pieces = []
        for head in range(refs[0][0].shape[0] // 4):
            for maker in range(2):
                k = 2 * side + (maker ^ role)
                pieces.append([refs[k][0][4 * head + (e ^ k)] for e in range(4)])
        for at in range(refs[0][1].shape[0] // 2 if len(refs[0]) > 1 else 0):
            rows = []
            for e in range(4):
                k = 2 * side + e % 2
                rows.append(refs[k][1][2 * at + (e // 2 ^ side)])
            pieces.append(rows)
        sides.append(
            jnp.concatenate([jnp.concatenate(rows, axis=0) for rows in pieces], axis=1)
        )
    return sides


def by_role(refs, parts):
    made, inward, ahead, aside, relay_x, relay_y = [
        refs[at * parts : (at + 1) * parts] for at in range(6)
    ]
    return ((made, inward, ahead, aside), (ahead, aside, relay_x, relay_y))


def input_kernel(parts, place_ref, *refs):
    weights, out_refs, total = refs[6 * parts], refs[6 * parts + 1 : -1], refs[-1]
    length = out_refs[0].shape[0]
    for role, grads in enumerate(by_role(refs, parts)):

        @pl.when(place_ref[CORE] == role)
        def _():
            left = jnp.concatenate(gathered(role, grads), axis=1)
            for e in range(4):
                product = dot(left[e * length : (e + 1) * length], weights[...])
                total[e] = product.astype(total.dtype)

    for s, out_ref in enumerate(out_refs):
        out_ref[...] = total[jnp.bitwise_xor(place_ref[PLANE], s)]


def input_product(place, grads, weights):
    _, length, _ = grads[0].shape
    depth, rows = weights.shape
    out = jax.ShapeDtypeStruct((length, rows), jnp.bfloat16)
    return pl.pallas_call(
        functools.partial(input_kernel, len(grads) // 6),
        out_shape=[out] * 4,
        in_specs=[whole(pltpu.SMEM)] + [whole()] * (len(grads) + 1),
        out_specs=[whole()] * 4,
        scratch_shapes=[pltpu.VMEM((4, length, rows), jnp.bfloat16)],
        compiler_params=pltpu.CompilerParams(vmem_limit_bytes=16 * MIB),
        cost_estimate=pl.CostEstimate(
            flops=8 * length * rows * depth,
            bytes_accessed=8 * length * (rows + depth) + 2 * rows * depth,
            transcendentals=0,
        ),
        name="input_gradient",
    )(place, *grads, weights)


def weight_kernel(mine, mean_scale, parts, place_ref, *refs):
    own, mate_in, first, second, corner, corner_far = refs[:6]
    grad_refs, refs = refs[6 : 6 + 6 * parts], refs[6 + 6 * parts :]
    if mine:
        received, out_refs, turned = refs[:3], refs[3:6], refs[6]
    else:
        received, out_refs, turned = None, refs[:3], refs[3]
    core = place_ref[CORE]
    length = own.shape[1]
    part = core if mine else 1 - core
    tokens = ((own, mate_in, first, second), (first, second, corner, corner_far))
    for role, grads in enumerate(by_role(grad_refs, parts)):

        @pl.when(core == role)
        def _():
            for e, source in enumerate(tokens[role]):
                turned[:, e * length : (e + 1) * length] = source[part].T
            for base, side in zip((HERE, BESIDE), gathered(role, grads)):
                total = dot(turned[...], side)
                for head in range(side.shape[1] // (3 * HD)):
                    here = lanes((place_ref[base] + head) * HD, HD)
                    for kind, out in enumerate(out_refs):
                        at = (head * 3 + kind) * HD
                        value = total[:, at : at + HD]
                        if mine:
                            value = (value + received[kind][:, here]) * mean_scale
                        out[:, here] = value.astype(out.dtype)


def weight_product(place, mine, mean_scale, cols, tokens, grads, received=()):
    _, length, _ = grads[0].shape
    rows = tokens[0].shape[2]
    out = jax.ShapeDtypeStruct((rows, cols), jnp.float32 if mine else jnp.bfloat16)
    return pl.pallas_call(
        functools.partial(weight_kernel, mine, mean_scale, len(grads) // 6),
        out_shape=[out] * 3,
        in_specs=[whole(pltpu.SMEM)] + [whole()] * (6 + len(grads) + len(received)),
        out_specs=[whole()] * 3,
        scratch_shapes=[pltpu.VMEM((rows, 4 * length), jnp.bfloat16)],
        compiler_params=pltpu.CompilerParams(vmem_limit_bytes=16 * MIB),
        cost_estimate=pl.CostEstimate(
            flops=8 * rows * 3 * cols * length,
            bytes_accessed=8 * length * (rows + 3 * cols) + 12 * rows * cols,
            transcendentals=0,
        ),
        name="weight_gradient_own" if mine else "weight_gradient_mate",
    )(place, *tokens, *grads, *received)


def gather_body(
    normed,
    queries,
    saved_keys,
    saved_values,
    output_grad,
    view_links,
    query_weight,
    key_weight,
    value_weight,
):
    length, cols = queries.shape[2:]
    model_width = normed.shape[-1]
    rows = query_weight.shape[0]
    prompts, views, groups = (lax.axis_size(name) for name in ("dp", "view", "head"))
    mean_scale = 1.0 / (prompts * views)
    half = cols // HD // 2
    view = lax.axis_index("view")
    core = lax.rem(view, 2)
    side = view // 2
    chip = lax.axis_index("dp") * (views // 2) + side
    place = jnp.stack([core, lax.axis_index("head"), side * half, (1 - side) * half])
    place = place.astype(jnp.int32)
    arrays = tuple(a.reshape(length, cols) for a in (queries, saved_keys, saved_values, output_grad))

    own_heads, shared = half // 2, half % 2
    each = [2 * step for step in range(own_heads)]
    picks = [
        [(BESIDE, step, 1) for step in each],
        [(BESIDE, step + 1, -1) for step in each],
        [(HERE, step + 1, -1) for step in each],
        [(HERE, step, 1) for step in each],
    ]
    if shared:
        picks += [[(BESIDE, 2 * own_heads, 0)], [(HERE, 2 * own_heads, 0)]]
    packed = pack(picks, place, view_links, arrays)
    to_x, to_cross, to_mate, own = packed[:4]
    x_in = moved(to_x, along_x)
    cross_in = moved(to_cross, across_x)
    mate_in = moved(to_mate, mate)
    sets = [((0, 1, 2, 3), (own, mate_in, x_in, cross_in))]
    if shared:
        to_x, own = packed[4:]
        (to_x,) = after((to_x,), x_in)
        x_in = moved(to_x, along_x)
        sets.append(((0, 2), (own, moved(own, mate), x_in, moved(x_in, mate))))

    flat = normed.reshape(length, model_width)

    def columns(of_chip):
        columns = [
            lax.dynamic_slice_in_dim(flat, (2 * of_chip + part) * rows, rows, axis=1)
            for part in range(2)
        ]
        return jnp.stack(columns)

    toward_x, toward_y = jnp.bitwise_xor(chip, 1), jnp.bitwise_xor(chip, 2)
    here = columns(chip)
    to_straight = columns(jnp.where(core == 0, toward_x, toward_y))
    to_crossed = columns(jnp.where(core == 0, toward_y, toward_x))
    to_corner = columns(jnp.bitwise_xor(chip, 3))
    mate_here = moved(here, only(1, mate))

    own_weights, turn = None, place
    parts = []
    for kept, sources in sets:
        made = attention(turn, kept, sources)
        if own_weights is None:
            ready = after((query_weight, key_weight, value_weight), made)
            own_weights = turned_weights(place, ready)
        (turn,) = after((place,), made, own_weights)
        ahead = moved(made, straight)
        aside = moved(made, crossed)
        inward = moved(made, only(1, mate))
        (sent,) = after((ahead,), aside, inward, mate_here, to_straight, to_crossed, to_corner)
        relay_x = moved(sent, only(1, along_x))
        relay_y = moved(sent, only(0, across_y))
        parts.append((made, inward, ahead, aside, relay_x, relay_y))
    grads = [array for kind in zip(*parts) for array in kind]
    weights = joined_weights(place, own_weights, moved(own_weights, mate))

    slots = input_product(place, grads, weights)
    last = groups - 1
    far = lax.ppermute(slots[3], "head", [(0, 1), (last, last - 1)])
    nearest = lax.ppermute(slots[1], "head", [(z, z ^ 1) for z in range(groups)])
    inner = lax.ppermute(slots[3], "head", [(1, last - 1), (last - 1, 1)])
    joint = (slots[2].astype(jnp.float32) + far.astype(jnp.float32)).astype(jnp.bfloat16)
    across = lax.ppermute(joint, "head", [(z, z ^ 2) for z in range(groups)])
    arrived = [nearest, inner, across]
    total = sum(array.astype(jnp.float32) for array in (slots[0], *arrived))
    total = total.astype(jnp.bfloat16)

    to_straight, to_crossed = after((to_straight, to_crossed), *slots)
    normed_ahead = moved(to_straight, straight)
    normed_aside = moved(to_crossed, crossed)
    (to_corner,) = after((to_corner,), normed_ahead, normed_aside)
    tokens = (
        here,
        mate_here,
        normed_ahead,
        normed_aside,
        moved(to_corner, corner_same),
        moved(to_corner, corner_cross),
    )
    (total,) = after((total,), tokens[4], tokens[5])

    def spot(y, v, z):
        return (y * views + v) * groups + z

    corners = [(y, v, z) for y in range(prompts) for v in range(views) for z in range(groups)]
    beside = lax.ppermute(
        total,
        ("dp", "view", "head"),
        [(spot(y, v, z), spot(y ^ (v % 2), v ^ z, z)) for y, v, z in corners],
    )
    (turn,) = after((place,), arrived[0])
    for_mate = weight_product(turn, False, mean_scale, cols, tokens, grads)
    from_mate = [moved(part, mate) for part in for_mate]
    weight_grads = weight_product(place, True, mean_scale, cols, tokens, grads, from_mate)
    input_grad = lax.ppermute(
        beside,
        ("dp", "view", "head"),
        [
            (
                spot(y ^ (v % 2), v ^ z, z),
                spot(y ^ (v % 2), v ^ z, y * (views // 2) + v // 2),
            )
            for y, v, z in corners
        ],
    )

    (input_grad,) = after((input_grad,), *weight_grads)
    return (
        input_grad.reshape(1, 1, length, model_width // groups),
        *weight_grads,
    )


def solution(mesh):
    prompts, views, groups = (mesh.shape[name] for name in ("dp", "view", "head"))
    loop_of_four = prompts * 2 == views and prompts * views == 2 * groups and views == groups

    def choose(*arrays):
        batch, held, length, cols = arrays[1].shape
        if loop_of_four and batch == held == 1 and length % HD == 0 and cols % (2 * HD) == 0:
            return gather_body(*arrays)
        return halo_body(*arrays)

    placed = (
        P("dp", "view", None, None),
        P("dp", "view", None, "head"),
        P("dp", "view", None, "head"),
        P("dp", "view", None, "head"),
        P("dp", "view", None, "head"),
        P("view", None),
        P(("dp", "view"), "head"),
        P(("dp", "view"), "head"),
        P(("dp", "view"), "head"),
    )
    return jax.shard_map(
        choose,
        mesh=mesh,
        in_specs=placed,
        out_specs=(
            P("dp", "view", None, "head"),
            P(("dp", "view"), "head"),
            P(("dp", "view"), "head"),
            P(("dp", "view"), "head"),
        ),
        check_vma=False,
    )
```

```python
import functools

import jax
import jax.numpy as jnp
from jax import lax
from jax.experimental import pallas as pl
from jax.experimental.pallas import tpu as pltpu
from jax.sharding import PartitionSpec as P

HD = 128
LOG2E = 1.4426950408889634
MIB = 1024 * 1024


def shifted(value, axis, steps):
    count = lax.axis_size(axis)
    pairs = [(source, (source + steps) % count) for source in range(count)]
    return lax.ppermute(value, axis, pairs)


def attend(query_rows, grad_rows, blocks, usable, scaling):
    batch_size, length, col_count = query_rows.shape
    heads_here = col_count // HD
    key_heads = blocks[..., :col_count].reshape(batch_size, 3 * length, heads_here, HD)
    value_heads = blocks[..., col_count:].reshape(batch_size, 3 * length, heads_here, HD)
    query_heads = query_rows.reshape(batch_size, length, heads_here, HD)
    grad_heads = grad_rows.reshape(batch_size, length, heads_here, HD)
    scores = (
        jnp.einsum("bshd,bthd->bhst", query_heads, key_heads, preferred_element_type=jnp.float32)
        * scaling
    )
    scores = jnp.where(usable, scores, -1e30)
    largest = jnp.max(scores, axis=-1, keepdims=True)
    powers = jnp.exp(scores - largest)
    attn_probs = powers / jnp.sum(powers, axis=-1, keepdims=True)
    probs_half = attn_probs.astype(jnp.bfloat16)
    prob_grad = jnp.einsum(
        "bshd,bthd->bhst", grad_heads, value_heads, preferred_element_type=jnp.float32
    )
    row_delta = jnp.sum(attn_probs * prob_grad, axis=-1, keepdims=True)
    score_grad = (scaling * attn_probs * (prob_grad - row_delta)).astype(jnp.bfloat16)
    query_grad = jnp.einsum(
        "bhst,bthd->bshd", score_grad, key_heads, preferred_element_type=jnp.float32
    )
    key_grad = jnp.einsum(
        "bhst,bshd->bthd", score_grad, query_heads, preferred_element_type=jnp.float32
    )
    value_grad = jnp.einsum(
        "bhst,bshd->bthd", probs_half, grad_heads, preferred_element_type=jnp.float32
    )
    query_grad = query_grad.reshape(batch_size, length, col_count)
    key_grad = key_grad.reshape(batch_size, 3, length, col_count)
    value_grad = value_grad.reshape(batch_size, 3, length, col_count)
    return (query_grad, jnp.concatenate([key_grad, value_grad], axis=-1))


def halo_body(
    normed,
    queries,
    saved_keys,
    saved_values,
    output_grad,
    view_links,
    query_weight,
    key_weight,
    value_weight,
):
    scaling = HD ** (-0.5)
    batch_size, view_count, length, col_count = queries.shape
    model_width = normed.shape[-1]
    pairs = jnp.concatenate([saved_keys, saved_values], axis=-1)
    from_lower = shifted(pairs, "view", 1)
    from_upper = shifted(pairs, "view", -1)
    extended = jnp.concatenate([from_lower, pairs, from_upper], axis=1)
    block_index = jnp.arange(3 * length) // length
    pair_grads = jnp.zeros(extended.shape, jnp.float32)
    link_flags = view_links[0] >= 0
    usable = jnp.where(
        block_index == 0, link_flags[0], jnp.where(block_index == 2, link_flags[1], True)
    )
    query_grad, block_grad = attend(queries[:, 0], output_grad[:, 0], extended, usable, scaling)
    query_grads = [query_grad]
    pair_grads = pair_grads.at[:, 0:3].add(block_grad)
    row_count = batch_size * view_count * length
    query_half = jnp.stack(query_grads, axis=1).astype(jnp.bfloat16).reshape(row_count, col_count)
    flat_input = normed.reshape(row_count, model_width)
    mean_scale = 1.0 / (lax.axis_size("dp") * batch_size * lax.axis_size("view") * view_count)
    from_lower_grads = shifted(pair_grads[:, -1:], "view", 1)
    from_upper_grads = shifted(pair_grads[:, :1], "view", -1)
    own_grads = pair_grads[:, 1 : view_count + 1]
    own_grads = own_grads.at[:, :1].add(from_lower_grads)
    own_grads = own_grads.at[:, -1:].add(from_upper_grads)
    key_half = own_grads[..., :col_count].astype(jnp.bfloat16).reshape(row_count, col_count)
    value_half = own_grads[..., col_count:].astype(jnp.bfloat16).reshape(row_count, col_count)
    all_grads = jnp.concatenate([query_half, key_half, value_half], axis=-1)
    grads_three = all_grads.reshape(row_count, 3, col_count)
    stacked = jnp.stack([query_weight, key_weight, value_weight])
    partial_input = jnp.einsum(
        "ric,ipc->rp",
        grads_three,
        lax.all_gather(stacked, ("dp", "view"), axis=1, tiled=True),
        preferred_element_type=jnp.float32,
    )
    summed_input = lax.psum_scatter(partial_input, "head", scatter_dimension=1, tiled=True)
    input_grad = summed_input.astype(jnp.bfloat16).reshape(
        batch_size, view_count, length, model_width // lax.axis_size("head")
    )
    product = lax.dot_general(
        flat_input, all_grads, (((0,), (0,)), ((), ())), preferred_element_type=jnp.float32
    )
    together = lax.psum_scatter(
        product * mean_scale, ("dp", "view"), scatter_dimension=0, tiled=True
    )
    grad_query = together[:, :col_count]
    grad_key = together[:, col_count : 2 * col_count]
    grad_value = together[:, 2 * col_count :]
    return (input_grad, grad_query, grad_key, grad_value)


def moved(value, target):
    prompts, views = lax.axis_size("dp"), lax.axis_size("view")
    pairs = []
    for y in range(prompts):
        for v in range(views):
            goal = target(y, v)
            if goal is not None:
                pairs.append((y * views + v, goal[0] * views + goal[1]))
    return lax.ppermute(value, ("dp", "view"), pairs)


def mate(y, v):
    return (y, v ^ 1)


def along_x(y, v):
    return (y, v ^ 2)


def across_x(y, v):
    return (y, v ^ 3)


def only(core, target):
    return lambda y, v: target(y, v) if v % 2 == core else None


def along_y(y, v):
    return (y ^ 1, v)


def across_y(y, v):
    return (y ^ 1, v ^ 1)


def straight(y, v):
    return along_x(y, v) if v % 2 == 0 else along_y(y, v)


def crossed(y, v):
    return across_y(y, v) if v % 2 == 0 else across_x(y, v)


def corner_same(y, v):
    return None if v % 2 == 0 else (y ^ 1, v ^ 2)


def corner_cross(y, v):
    return (y ^ 1, v ^ 3) if v % 2 == 0 else None


def lanes(start, size):
    return pl.ds(pl.multiple_of(start, HD), size)


def whole(space=pltpu.VMEM):
    return pl.BlockSpec(memory_space=space)


def dot_last(a, b):
    return lax.dot_general(a, b, (((1,), (1,)), ((), ())), preferred_element_type=jnp.float32)


def dot_first(a, b):
    return lax.dot_general(a, b, (((0,), (0,)), ((), ())), preferred_element_type=jnp.float32)


def dot(a, b):
    return jnp.dot(a, b, preferred_element_type=jnp.float32)


def after(values, *earlier):
    return lax.optimization_barrier((tuple(values), tuple(earlier)))[0]


CORE, PLANE, HERE, BESIDE = range(4)
FLAG_ROWS = 16


def pack_kernel(picks, half, links_ref, q_ref, k_ref, v_ref, g_ref, *out_refs):
    length = q_ref.shape[0]
    row = lax.broadcasted_iota(jnp.int32, (FLAG_ROWS, HD), 0)
    gaps = [jnp.where(links_ref[0, side] >= 0, 0.0, 1.0).astype(jnp.float32) for side in range(2)]
    flags = jnp.where(row < FLAG_ROWS // 2, gaps[0], gaps[1])
    view = lax.axis_index("view")
    side = view // 2
    first = {HERE: side * half, BESIDE: (1 - side) * half}
    for heads, out_ref in zip(picks, out_refs):
        for at, (base, step, sign) in enumerate(heads):
            head = first[base] + step + sign * lax.rem(view, 2)
            for kind, source in enumerate((q_ref, k_ref, v_ref, g_ref)):
                out_ref[at, kind * length : (kind + 1) * length] = source[:, lanes(head * HD, HD)]
            out_ref[at, 4 * length : 4 * length + FLAG_ROWS] = flags.astype(out_ref.dtype)


def pack(picks, half, links, arrays):
    length = arrays[0].shape[0]
    height = 4 * length + FLAG_ROWS
    return pl.pallas_call(
        functools.partial(pack_kernel, picks, half),
        out_shape=[
            jax.ShapeDtypeStruct((len(heads), height, HD), jnp.bfloat16) for heads in picks
        ],
        in_specs=[whole(pltpu.SMEM)] + [whole()] * 4,
        out_specs=[whole()] * len(picks),
        name="pack_heads",
    )(links, *arrays)


def one_head(scaling, core, xs, length, keys, values, key_sums, value_sums):
    factor = scaling * LOG2E

    def rows(e, kind):
        return xs[e][kind * length : (kind + 1) * length]

    def gap(e, side):
        at = 4 * length + side * (FLAG_ROWS // 2)
        flags = xs[e][at : at + FLAG_ROWS // 2].astype(jnp.float32)[0:1]
        return jnp.concatenate([flags] * (length // HD), axis=1) * 1e30

    for at in range(6):
        keys[at * length : (at + 1) * length] = rows((at + 3) % 4, 1)
        values[at * length : (at + 1) * length] = rows((at + 3) % 4, 2)
    query_grads = []
    for e in range(4):
        blocks = slice(e * length, (e + 3) * length)
        before, behind = gap(e, 0), gap(e, 1)
        far_below = jnp.where(core == 0, before, behind)
        far_above = jnp.where(core == 0, behind, before)
        q, g = rows(e, 0), rows(e, 3)
        near = keys[blocks]
        scores = dot_last(near, q)
        scores = [scores[at * length : (at + 1) * length] for at in range(3)]
        tops = [jnp.max(part, axis=0, keepdims=True) for part in scores]
        top = jnp.maximum(tops[1], jnp.maximum(tops[0] - far_below, tops[2] - far_above))
        offsets = (top + far_below, top, top + far_above)
        powers = [jnp.exp2((part - o) * factor) for part, o in zip(scores, offsets)]
        inverse = 1.0 / sum(jnp.sum(p, axis=0, keepdims=True) for p in powers)
        prob_grads = dot_last(values[blocks], g)
        prob_grads = [prob_grads[at * length : (at + 1) * length] for at in range(3)]
        delta = inverse * sum(
            jnp.sum(p * d, axis=0, keepdims=True) for p, d in zip(powers, prob_grads)
        )
        probs = [p * inverse for p in powers]
        score_grad = jnp.concatenate(
            [
                (p * scaling * (d - delta)).astype(jnp.bfloat16)
                for p, d in zip(probs, prob_grads)
            ],
            axis=0,
        )
        probs_half = jnp.concatenate([p.astype(jnp.bfloat16) for p in probs], axis=0)
        query_grads.append(dot_first(score_grad, near))
        for sums, part in ((key_sums, dot(score_grad, q)), (value_sums, dot(probs_half, g))):
            if e == 0:
                sums[blocks] = part
            else:
                held = slice(e * length, (e + 2) * length)
                sums[held] += part[: 2 * length]
                sums[(e + 2) * length : (e + 3) * length] = part[2 * length :]

    def by_view(sums):
        parts = [sums[at * length : (at + 1) * length] for at in range(6)]
        return (parts[1] + parts[5], parts[2], parts[3], parts[0] + parts[4])

    return query_grads, by_view(key_sums), by_view(value_sums)


def attention_kernel(scaling, kept, place_ref, own, mate_in, x_in, far_in, *refs):
    out_ref, keys, values, key_sums, value_sums = refs
    length = out_ref.shape[1]
    heads = own.shape[0]
    for head in range(heads):
        xs = [own.at[head], mate_in.at[head], x_in.at[head], far_in.at[head]]
        grads = one_head(
            scaling, place_ref[CORE], xs, length, keys, values, key_sums, value_sums
        )
        for at, e in enumerate(kept):
            for kind in range(3):
                out_ref[len(kept) * head + at, :, kind * HD : (kind + 1) * HD] = grads[kind][
                    e
                ].astype(out_ref.dtype)


def attention(place, kept, sources):
    heads, height, _ = sources[0].shape
    length = (height - FLAG_ROWS) // 4
    return pl.pallas_call(
        functools.partial(attention_kernel, HD ** (-0.5), kept),
        out_shape=jax.ShapeDtypeStruct((len(kept) * heads, length, 3 * HD), jnp.bfloat16),
        in_specs=[whole(pltpu.SMEM)] + [whole()] * 4,
        out_specs=whole(),
        scratch_shapes=[pltpu.VMEM((6 * length, HD), jnp.bfloat16)] * 2
        + [pltpu.VMEM((6 * length, HD), jnp.float32)] * 2,
        compiler_params=pltpu.CompilerParams(vmem_limit_bytes=12 * MIB),
        cost_estimate=pl.CostEstimate(
            flops=heads * 4 * 5 * 2 * length * 3 * length * HD * 2,
            bytes_accessed=heads * 2 * length * 7 * HD * 4,
            transcendentals=heads * 12 * length * length,
        ),
        name="attention_gradients",
    )(place, *sources)


def turn_kernel(place_ref, q_ref, k_ref, v_ref, out_ref):
    half = q_ref.shape[1] // HD // 2
    for side, base in enumerate((HERE, BESIDE)):
        for head in range(half):
            for kind, source in enumerate((q_ref, k_ref, v_ref)):
                at = ((side * half + head) * 3 + kind) * HD
                out_ref[at : at + HD] = source[:, lanes((place_ref[base] + head) * HD, HD)].T


def turned_weights(place, weights):
    rows, cols = weights[0].shape
    return pl.pallas_call(
        turn_kernel,
        out_shape=jax.ShapeDtypeStruct((3 * cols, rows), jnp.bfloat16),
        in_specs=[whole(pltpu.SMEM)] + [whole()] * 3,
        out_specs=whole(),
        compiler_params=pltpu.CompilerParams(vmem_limit_bytes=8 * MIB),
        name="turn_weights",
    )(place, *weights)


def join_kernel(place_ref, own_ref, mate_ref, out_ref):
    core = place_ref[CORE]
    rows = own_ref.shape[1]
    out_ref[:, lanes(core * rows, rows)] = own_ref[...]
    out_ref[:, lanes((1 - core) * rows, rows)] = mate_ref[...]


def joined_weights(place, own_weights, mate_weights):
    depth, rows = own_weights.shape
    return pl.pallas_call(
        join_kernel,
        out_shape=jax.ShapeDtypeStruct((depth, 2 * rows), jnp.bfloat16),
        in_specs=[whole(pltpu.SMEM)] + [whole()] * 2,
        out_specs=whole(),
        compiler_params=pltpu.CompilerParams(vmem_limit_bytes=12 * MIB),
        name="join_weights",
    )(place, own_weights, mate_weights)


def gathered(role, side, refs):
    pieces = []
    for head in range(refs[0][0].shape[0] // 4):
        for maker in range(2):
            k = maker ^ role
            pieces.append([refs[k][0][4 * head + (e ^ (2 * side + k))] for e in range(4)])
    for at in range(refs[0][1].shape[0] // 2 if len(refs[0]) > 1 else 0):
        pieces.append([refs[e % 2][1][2 * at + (e // 2 ^ side)] for e in range(4)])
    return jnp.concatenate([jnp.concatenate(rows, axis=0) for rows in pieces], axis=1)


def by_role(refs, parts):
    made, inward, ahead, aside, relay_x, relay_y = [
        refs[at * parts : (at + 1) * parts] for at in range(6)
    ]
    return (((made, inward), (ahead, aside)), ((ahead, aside), (relay_x, relay_y)))


def input_kernel(side, parts, place_ref, *refs):
    pairs = [refs[at * parts : (at + 1) * parts] for at in range(4)]
    weights, refs = refs[4 * parts], refs[4 * parts + 1 :]
    if side == 0:
        total, before = refs[0], None
    else:
        before, out_refs, total = refs[0], refs[1:-1], refs[-1]
    length = total.shape[1]
    for role in range(2):

        @pl.when(place_ref[CORE] == role)
        def _():
            left = gathered(role, side, pairs[2 * role : 2 * role + 2])
            depth = left.shape[1]
            rows = weights[side * depth : (side + 1) * depth]
            for e in range(4):
                product = dot(left[e * length : (e + 1) * length], rows)
                if before is not None:
                    product += before[e]
                total[e] = product.astype(total.dtype)

    if before is not None:
        for s, out_ref in enumerate(out_refs):
            out_ref[...] = total[jnp.bitwise_xor(place_ref[PLANE], s)]


def input_product(place, side, grads, weights, before=()):
    _, length, _ = grads[0].shape
    depth, rows = weights.shape
    if side == 0:
        out = jax.ShapeDtypeStruct((4, length, rows), jnp.float32)
    else:
        out = [jax.ShapeDtypeStruct((length, rows), jnp.bfloat16)] * 4
    return pl.pallas_call(
        functools.partial(input_kernel, side, len(grads) // 4),
        out_shape=out,
        in_specs=[whole(pltpu.SMEM)] + [whole()] * (len(grads) + 1 + len(before)),
        out_specs=whole() if side == 0 else [whole()] * 4,
        scratch_shapes=[pltpu.VMEM((4, length, rows), jnp.bfloat16)] if side else [],
        compiler_params=pltpu.CompilerParams(vmem_limit_bytes=16 * MIB),
        cost_estimate=pl.CostEstimate(
            flops=4 * length * rows * depth,
            bytes_accessed=8 * length * (rows + depth) + rows * depth,
            transcendentals=0,
        ),
        name="input_gradient_next" if side else "input_gradient_here",
    )(place, *grads, weights, *before)


def weight_kernel(mine, mean_scale, parts, place_ref, *refs):
    own, mate_in, first, second, corner, corner_far = refs[:6]
    grad_refs, refs = refs[6 : 6 + 6 * parts], refs[6 + 6 * parts :]
    if mine:
        received, out_refs, turned = refs[:3], refs[3:6], refs[6]
    else:
        received, out_refs, turned = None, refs[:3], refs[3]
    core = place_ref[CORE]
    length = own.shape[1]
    part = core if mine else 1 - core
    tokens = ((own, mate_in, first, second), (first, second, corner, corner_far))
    for role, grads in enumerate(by_role(grad_refs, parts)):

        @pl.when(core == role)
        def _():
            for e, source in enumerate(tokens[role]):
                turned[:, e * length : (e + 1) * length] = source[part].T
            for side, base in enumerate((HERE, BESIDE)):
                total = dot(turned[...], gathered(role, side, grads[side]))
                for head in range(total.shape[1] // (3 * HD)):
                    here = lanes((place_ref[base] + head) * HD, HD)
                    for kind, out in enumerate(out_refs):
                        at = (head * 3 + kind) * HD
                        value = total[:, at : at + HD]
                        if mine:
                            value = (value + received[kind][:, here]) * mean_scale
                        out[:, here] = value.astype(out.dtype)


def weight_product(place, mine, mean_scale, cols, tokens, grads, received=()):
    _, length, _ = grads[0].shape
    rows = tokens[0].shape[2]
    out = jax.ShapeDtypeStruct((rows, cols), jnp.float32 if mine else jnp.bfloat16)
    return pl.pallas_call(
        functools.partial(weight_kernel, mine, mean_scale, len(grads) // 6),
        out_shape=[out] * 3,
        in_specs=[whole(pltpu.SMEM)] + [whole()] * (6 + len(grads) + len(received)),
        out_specs=[whole()] * 3,
        scratch_shapes=[pltpu.VMEM((rows, 4 * length), jnp.bfloat16)],
        compiler_params=pltpu.CompilerParams(vmem_limit_bytes=16 * MIB),
        cost_estimate=pl.CostEstimate(
            flops=8 * rows * 3 * cols * length,
            bytes_accessed=8 * length * (rows + 3 * cols) + 12 * rows * cols,
            transcendentals=0,
        ),
        name="weight_gradient_own" if mine else "weight_gradient_mate",
    )(place, *tokens, *grads, *received)


def gather_body(
    normed,
    queries,
    saved_keys,
    saved_values,
    output_grad,
    view_links,
    query_weight,
    key_weight,
    value_weight,
):
    length, cols = queries.shape[2:]
    model_width = normed.shape[-1]
    rows = query_weight.shape[0]
    prompts, views, groups = (lax.axis_size(name) for name in ("dp", "view", "head"))
    mean_scale = 1.0 / (prompts * views)
    half = cols // HD // 2
    view = lax.axis_index("view")
    core = lax.rem(view, 2)
    side = view // 2
    chip = lax.axis_index("dp") * (views // 2) + side
    place = jnp.stack([core, lax.axis_index("head"), side * half, (1 - side) * half])
    place = place.astype(jnp.int32)
    arrays = tuple(a.reshape(length, cols) for a in (queries, saved_keys, saved_values, output_grad))

    own_heads, shared = half // 2, half % 2
    each = [2 * step for step in range(own_heads)]
    picks = [
        [(BESIDE, step, 1) for step in each],
        [(BESIDE, step + 1, -1) for step in each],
        [(HERE, step + 1, -1) for step in each],
        [(HERE, step, 1) for step in each],
    ]
    if shared:
        picks += [[(BESIDE, 2 * own_heads, 0)], [(HERE, 2 * own_heads, 0)]]
    packed = pack(picks, half, view_links, arrays)
    to_x, to_cross, to_mate, own = packed[:4]
    x_in = moved(to_x, along_x)
    cross_in = moved(to_cross, across_x)
    mate_in = moved(to_mate, mate)
    sets = [((0, 1, 2, 3), (own, mate_in, x_in, cross_in))]
    if shared:
        to_x, own = packed[4:]
        (to_x,) = after((to_x,), x_in)
        x_in = moved(to_x, along_x)
        sets.append(((0, 2), (own, moved(own, mate), x_in, moved(x_in, mate))))

    flat = normed.reshape(length, model_width)

    def columns(of_chip):
        columns = [
            lax.dynamic_slice_in_dim(flat, (2 * of_chip + part) * rows, rows, axis=1)
            for part in range(2)
        ]
        return jnp.stack(columns)

    toward_x, toward_y = jnp.bitwise_xor(chip, 1), jnp.bitwise_xor(chip, 2)
    here = columns(chip)
    to_straight = columns(jnp.where(core == 0, toward_x, toward_y))
    to_crossed = columns(jnp.where(core == 0, toward_y, toward_x))
    to_corner = columns(jnp.bitwise_xor(chip, 3))
    mate_here = moved(here, only(1, mate))

    own_weights, turn = None, place
    parts, sents = [], []
    for kept, sources in sets:
        made = attention(turn, kept, sources)
        if own_weights is None:
            ready = after((query_weight, key_weight, value_weight), made)
            own_weights = turned_weights(place, ready)
        (turn,) = after((place,), made, own_weights)
        ahead = moved(made, straight)
        aside = moved(made, crossed)
        inward = moved(made, only(1, mate))
        (sent,) = after((ahead,), aside, inward, mate_here, to_straight, to_crossed, to_corner)
        relay_x = moved(sent, only(1, along_x))
        relay_y = moved(sent, only(0, across_y))
        sents.append(sent)
        parts.append((made, inward, ahead, aside, relay_x, relay_y))
    grads = [array for kind in zip(*parts) for array in kind]
    weights = joined_weights(place, own_weights, moved(own_weights, mate))

    count = 2 * len(parts)
    here_sum = input_product(place, 0, [*grads[:count], *sents, *grads[3 * len(parts) : 4 * len(parts)]], weights)
    slots = input_product(place, 1, grads[count:], weights, (here_sum,))
    last = groups - 1
    far = lax.ppermute(slots[3], "head", [(0, 1), (last, last - 1)])
    nearest = lax.ppermute(slots[1], "head", [(z, z ^ 1) for z in range(groups)])
    inner = lax.ppermute(slots[3], "head", [(1, last - 1), (last - 1, 1)])
    joint = (slots[2].astype(jnp.float32) + far.astype(jnp.float32)).astype(jnp.bfloat16)
    across = lax.ppermute(joint, "head", [(z, z ^ 2) for z in range(groups)])
    arrived = [nearest, inner, across]
    total = sum(array.astype(jnp.float32) for array in (slots[0], *arrived))
    total = total.astype(jnp.bfloat16)

    to_straight, to_crossed = after((to_straight, to_crossed), *slots)
    normed_ahead = moved(to_straight, straight)
    normed_aside = moved(to_crossed, crossed)
    (to_corner,) = after((to_corner,), normed_ahead, normed_aside)
    tokens = (
        here,
        mate_here,
        normed_ahead,
        normed_aside,
        moved(to_corner, corner_same),
        moved(to_corner, corner_cross),
    )
    (total,) = after((total,), tokens[4], tokens[5])

    def spot(y, v, z):
        return (y * views + v) * groups + z

    corners = [(y, v, z) for y in range(prompts) for v in range(views) for z in range(groups)]
    beside = lax.ppermute(
        total,
        ("dp", "view", "head"),
        [(spot(y, v, z), spot(y ^ (v % 2), v ^ z, z)) for y, v, z in corners],
    )
    (turn,) = after((place,), arrived[0])
    for_mate = weight_product(turn, False, mean_scale, cols, tokens, grads)
    from_mate = [moved(part, mate) for part in for_mate]
    weight_grads = weight_product(place, True, mean_scale, cols, tokens, grads, from_mate)
    input_grad = lax.ppermute(
        beside,
        ("dp", "view", "head"),
        [
            (
                spot(y ^ (v % 2), v ^ z, z),
                spot(y ^ (v % 2), v ^ z, y * (views // 2) + v // 2),
            )
            for y, v, z in corners
        ],
    )

    (input_grad,) = after((input_grad,), *weight_grads)
    return (
        input_grad.reshape(1, 1, length, model_width // groups),
        *weight_grads,
    )


def solution(mesh):
    prompts, views, groups = (mesh.shape[name] for name in ("dp", "view", "head"))
    loop_of_four = prompts * 2 == views and prompts * views == 2 * groups and views == groups

    def choose(*arrays):
        batch, held, length, cols = arrays[1].shape
        if loop_of_four and batch == held == 1 and length % HD == 0 and cols % (2 * HD) == 0:
            return gather_body(*arrays)
        return halo_body(*arrays)

    placed = (
        P("dp", "view", None, None),
        P("dp", "view", None, "head"),
        P("dp", "view", None, "head"),
        P("dp", "view", None, "head"),
        P("dp", "view", None, "head"),
        P("view", None),
        P(("dp", "view"), "head"),
        P(("dp", "view"), "head"),
        P(("dp", "view"), "head"),
    )
    return jax.shard_map(
        choose,
        mesh=mesh,
        in_specs=placed,
        out_specs=(
            P("dp", "view", None, "head"),
            P(("dp", "view"), "head"),
            P(("dp", "view"), "head"),
            P(("dp", "view"), "head"),
        ),
        check_vma=False,
    )
```

```python
import functools

import jax
import jax.numpy as jnp
from jax import lax
from jax.experimental import pallas as pl
from jax.experimental.pallas import tpu as pltpu
from jax.sharding import PartitionSpec as P

HD = 128
LOG2E = 1.4426950408889634
MIB = 1024 * 1024


def shifted(value, axis, steps):
    count = lax.axis_size(axis)
    pairs = [(source, (source + steps) % count) for source in range(count)]
    return lax.ppermute(value, axis, pairs)


def attend(query_rows, grad_rows, blocks, usable, scaling):
    batch_size, length, col_count = query_rows.shape
    heads_here = col_count // HD
    key_heads = blocks[..., :col_count].reshape(batch_size, 3 * length, heads_here, HD)
    value_heads = blocks[..., col_count:].reshape(batch_size, 3 * length, heads_here, HD)
    query_heads = query_rows.reshape(batch_size, length, heads_here, HD)
    grad_heads = grad_rows.reshape(batch_size, length, heads_here, HD)
    scores = (
        jnp.einsum("bshd,bthd->bhst", query_heads, key_heads, preferred_element_type=jnp.float32)
        * scaling
    )
    scores = jnp.where(usable, scores, -1e30)
    largest = jnp.max(scores, axis=-1, keepdims=True)
    powers = jnp.exp(scores - largest)
    attn_probs = powers / jnp.sum(powers, axis=-1, keepdims=True)
    probs_half = attn_probs.astype(jnp.bfloat16)
    prob_grad = jnp.einsum(
        "bshd,bthd->bhst", grad_heads, value_heads, preferred_element_type=jnp.float32
    )
    row_delta = jnp.sum(attn_probs * prob_grad, axis=-1, keepdims=True)
    score_grad = (scaling * attn_probs * (prob_grad - row_delta)).astype(jnp.bfloat16)
    query_grad = jnp.einsum(
        "bhst,bthd->bshd", score_grad, key_heads, preferred_element_type=jnp.float32
    )
    key_grad = jnp.einsum(
        "bhst,bshd->bthd", score_grad, query_heads, preferred_element_type=jnp.float32
    )
    value_grad = jnp.einsum(
        "bhst,bshd->bthd", probs_half, grad_heads, preferred_element_type=jnp.float32
    )
    query_grad = query_grad.reshape(batch_size, length, col_count)
    key_grad = key_grad.reshape(batch_size, 3, length, col_count)
    value_grad = value_grad.reshape(batch_size, 3, length, col_count)
    return (query_grad, jnp.concatenate([key_grad, value_grad], axis=-1))


def halo_body(
    normed,
    queries,
    saved_keys,
    saved_values,
    output_grad,
    view_links,
    query_weight,
    key_weight,
    value_weight,
):
    scaling = HD ** (-0.5)
    batch_size, view_count, length, col_count = queries.shape
    model_width = normed.shape[-1]
    pairs = jnp.concatenate([saved_keys, saved_values], axis=-1)
    from_lower = shifted(pairs, "view", 1)
    from_upper = shifted(pairs, "view", -1)
    extended = jnp.concatenate([from_lower, pairs, from_upper], axis=1)
    block_index = jnp.arange(3 * length) // length
    pair_grads = jnp.zeros(extended.shape, jnp.float32)
    link_flags = view_links[0] >= 0
    usable = jnp.where(
        block_index == 0, link_flags[0], jnp.where(block_index == 2, link_flags[1], True)
    )
    query_grad, block_grad = attend(queries[:, 0], output_grad[:, 0], extended, usable, scaling)
    query_grads = [query_grad]
    pair_grads = pair_grads.at[:, 0:3].add(block_grad)
    row_count = batch_size * view_count * length
    query_half = jnp.stack(query_grads, axis=1).astype(jnp.bfloat16).reshape(row_count, col_count)
    flat_input = normed.reshape(row_count, model_width)
    mean_scale = 1.0 / (lax.axis_size("dp") * batch_size * lax.axis_size("view") * view_count)
    from_lower_grads = shifted(pair_grads[:, -1:], "view", 1)
    from_upper_grads = shifted(pair_grads[:, :1], "view", -1)
    own_grads = pair_grads[:, 1 : view_count + 1]
    own_grads = own_grads.at[:, :1].add(from_lower_grads)
    own_grads = own_grads.at[:, -1:].add(from_upper_grads)
    key_half = own_grads[..., :col_count].astype(jnp.bfloat16).reshape(row_count, col_count)
    value_half = own_grads[..., col_count:].astype(jnp.bfloat16).reshape(row_count, col_count)
    all_grads = jnp.concatenate([query_half, key_half, value_half], axis=-1)
    grads_three = all_grads.reshape(row_count, 3, col_count)
    stacked = jnp.stack([query_weight, key_weight, value_weight])
    partial_input = jnp.einsum(
        "ric,ipc->rp",
        grads_three,
        lax.all_gather(stacked, ("dp", "view"), axis=1, tiled=True),
        preferred_element_type=jnp.float32,
    )
    summed_input = lax.psum_scatter(partial_input, "head", scatter_dimension=1, tiled=True)
    input_grad = summed_input.astype(jnp.bfloat16).reshape(
        batch_size, view_count, length, model_width // lax.axis_size("head")
    )
    product = lax.dot_general(
        flat_input, all_grads, (((0,), (0,)), ((), ())), preferred_element_type=jnp.float32
    )
    together = lax.psum_scatter(
        product * mean_scale, ("dp", "view"), scatter_dimension=0, tiled=True
    )
    grad_query = together[:, :col_count]
    grad_key = together[:, col_count : 2 * col_count]
    grad_value = together[:, 2 * col_count :]
    return (input_grad, grad_query, grad_key, grad_value)


def moved(value, target):
    prompts, views = lax.axis_size("dp"), lax.axis_size("view")
    pairs = []
    for y in range(prompts):
        for v in range(views):
            goal = target(y, v)
            if goal is not None:
                pairs.append((y * views + v, goal[0] * views + goal[1]))
    return lax.ppermute(value, ("dp", "view"), pairs)


def mate(y, v):
    return (y, v ^ 1)


def along_x(y, v):
    return (y, v ^ 2)


def across_x(y, v):
    return (y, v ^ 3)


def only(core, target):
    return lambda y, v: target(y, v) if v % 2 == core else None


def along_y(y, v):
    return (y ^ 1, v)


def across_y(y, v):
    return (y ^ 1, v ^ 1)


def straight(y, v):
    return along_x(y, v) if v % 2 == 0 else along_y(y, v)


def crossed(y, v):
    return across_y(y, v) if v % 2 == 0 else across_x(y, v)


def corner_same(y, v):
    return None if v % 2 == 0 else (y ^ 1, v ^ 2)


def corner_cross(y, v):
    return (y ^ 1, v ^ 3) if v % 2 == 0 else None


def lanes(start, size):
    return pl.ds(pl.multiple_of(start, HD), size)


def whole(space=pltpu.VMEM):
    return pl.BlockSpec(memory_space=space)


def dot_last(a, b):
    return lax.dot_general(a, b, (((1,), (1,)), ((), ())), preferred_element_type=jnp.float32)


def dot_first(a, b):
    return lax.dot_general(a, b, (((0,), (0,)), ((), ())), preferred_element_type=jnp.float32)


def dot(a, b):
    return jnp.dot(a, b, preferred_element_type=jnp.float32)


def after(values, *earlier):
    return lax.optimization_barrier((tuple(values), tuple(earlier)))[0]


CORE, PLANE, HERE, BESIDE = range(4)
FLAG_ROWS = 16


def pack_kernel(picks, place_ref, links_ref, q_ref, k_ref, v_ref, g_ref, *out_refs):
    length = q_ref.shape[0]
    row = lax.broadcasted_iota(jnp.int32, (FLAG_ROWS, HD), 0)
    gaps = [jnp.where(links_ref[0, side] >= 0, 0.0, 1.0).astype(jnp.float32) for side in range(2)]
    flags = jnp.where(row < FLAG_ROWS // 2, gaps[0], gaps[1])
    for heads, out_ref in zip(picks, out_refs):
        for at, (base, step, sign) in enumerate(heads):
            head = place_ref[base] + step + sign * place_ref[CORE]
            for kind, source in enumerate((q_ref, k_ref, v_ref, g_ref)):
                out_ref[at, kind * length : (kind + 1) * length] = source[:, lanes(head * HD, HD)]
            out_ref[at, 4 * length : 4 * length + FLAG_ROWS] = flags.astype(out_ref.dtype)


def pack(picks, place, links, arrays):
    length = arrays[0].shape[0]
    height = 4 * length + FLAG_ROWS
    return pl.pallas_call(
        functools.partial(pack_kernel, picks),
        out_shape=[
            jax.ShapeDtypeStruct((len(heads), height, HD), jnp.bfloat16) for heads in picks
        ],
        in_specs=[whole(pltpu.SMEM)] * 2 + [whole()] * 4,
        out_specs=[whole()] * len(picks),
        name="pack_heads",
    )(place, links, *arrays)


def one_head(scaling, core, xs, length, keys, values, key_sums, value_sums):
    factor = scaling * LOG2E

    def rows(e, kind):
        return xs[e][kind * length : (kind + 1) * length]

    def gap(e, side):
        at = 4 * length + side * (FLAG_ROWS // 2)
        flags = xs[e][at : at + FLAG_ROWS // 2].astype(jnp.float32)[0:1]
        return jnp.concatenate([flags] * (length // HD), axis=1) * 1e30

    for at in range(6):
        keys[at * length : (at + 1) * length] = rows((at + 3) % 4, 1)
        values[at * length : (at + 1) * length] = rows((at + 3) % 4, 2)
    query_grads = []
    for e in range(4):
        blocks = slice(e * length, (e + 3) * length)
        before, behind = gap(e, 0), gap(e, 1)
        far_below = jnp.where(core == 0, before, behind)
        far_above = jnp.where(core == 0, behind, before)
        q, g = rows(e, 0), rows(e, 3)
        near = keys[blocks]
        scores = dot_last(near, q)
        scores = [scores[at * length : (at + 1) * length] for at in range(3)]
        tops = [jnp.max(part, axis=0, keepdims=True) for part in scores]
        top = jnp.maximum(tops[1], jnp.maximum(tops[0] - far_below, tops[2] - far_above))
        offsets = (top + far_below, top, top + far_above)
        powers = [jnp.exp2((part - o) * factor) for part, o in zip(scores, offsets)]
        inverse = 1.0 / sum(jnp.sum(p, axis=0, keepdims=True) for p in powers)
        prob_grads = dot_last(values[blocks], g)
        prob_grads = [prob_grads[at * length : (at + 1) * length] for at in range(3)]
        delta = inverse * sum(
            jnp.sum(p * d, axis=0, keepdims=True) for p, d in zip(powers, prob_grads)
        )
        probs = [p * inverse for p in powers]
        score_grad = jnp.concatenate(
            [
                (p * scaling * (d - delta)).astype(jnp.bfloat16)
                for p, d in zip(probs, prob_grads)
            ],
            axis=0,
        )
        probs_half = jnp.concatenate([p.astype(jnp.bfloat16) for p in probs], axis=0)
        query_grads.append(dot_first(score_grad, near))
        for sums, part in ((key_sums, dot(score_grad, q)), (value_sums, dot(probs_half, g))):
            if e == 0:
                sums[blocks] = part
            else:
                held = slice(e * length, (e + 2) * length)
                sums[held] += part[: 2 * length]
                sums[(e + 2) * length : (e + 3) * length] = part[2 * length :]

    def by_view(sums):
        parts = [sums[at * length : (at + 1) * length] for at in range(6)]
        return (parts[1] + parts[5], parts[2], parts[3], parts[0] + parts[4])

    return query_grads, by_view(key_sums), by_view(value_sums)


def attention_kernel(scaling, kept, place_ref, own, mate_in, x_in, far_in, *refs):
    out_ref, keys, values, key_sums, value_sums = refs
    length = out_ref.shape[1]
    heads = own.shape[0]
    for head in range(heads):
        xs = [own.at[head], mate_in.at[head], x_in.at[head], far_in.at[head]]
        grads = one_head(
            scaling, place_ref[CORE], xs, length, keys, values, key_sums, value_sums
        )
        for at, e in enumerate(kept):
            for kind in range(3):
                out_ref[len(kept) * head + at, :, kind * HD : (kind + 1) * HD] = grads[kind][
                    e
                ].astype(out_ref.dtype)


def attention(place, kept, sources):
    heads, height, _ = sources[0].shape
    length = (height - FLAG_ROWS) // 4
    return pl.pallas_call(
        functools.partial(attention_kernel, HD ** (-0.5), kept),
        out_shape=jax.ShapeDtypeStruct((len(kept) * heads, length, 3 * HD), jnp.bfloat16),
        in_specs=[whole(pltpu.SMEM)] + [whole()] * 4,
        out_specs=whole(),
        scratch_shapes=[pltpu.VMEM((6 * length, HD), jnp.bfloat16)] * 2
        + [pltpu.VMEM((6 * length, HD), jnp.float32)] * 2,
        compiler_params=pltpu.CompilerParams(vmem_limit_bytes=12 * MIB),
        cost_estimate=pl.CostEstimate(
            flops=heads * 4 * 5 * 2 * length * 3 * length * HD * 2,
            bytes_accessed=heads * 2 * length * 7 * HD * 4,
            transcendentals=heads * 12 * length * length,
        ),
        name="attention_gradients",
    )(place, *sources)


def turn_kernel(place_ref, q_ref, k_ref, v_ref, out_ref):
    half = q_ref.shape[1] // HD // 2
    for side, base in enumerate((HERE, BESIDE)):
        for head in range(half):
            for kind, source in enumerate((q_ref, k_ref, v_ref)):
                at = ((side * half + head) * 3 + kind) * HD
                out_ref[at : at + HD] = source[:, lanes((place_ref[base] + head) * HD, HD)].T


def turned_weights(place, weights):
    rows, cols = weights[0].shape
    return pl.pallas_call(
        turn_kernel,
        out_shape=jax.ShapeDtypeStruct((3 * cols, rows), jnp.bfloat16),
        in_specs=[whole(pltpu.SMEM)] + [whole()] * 3,
        out_specs=whole(),
        compiler_params=pltpu.CompilerParams(vmem_limit_bytes=8 * MIB),
        name="turn_weights",
    )(place, *weights)


def join_kernel(place_ref, own_ref, mate_ref, out_ref):
    core = place_ref[CORE]
    rows = own_ref.shape[1]
    out_ref[:, lanes(core * rows, rows)] = own_ref[...]
    out_ref[:, lanes((1 - core) * rows, rows)] = mate_ref[...]


def joined_weights(place, own_weights, mate_weights):
    depth, rows = own_weights.shape
    return pl.pallas_call(
        join_kernel,
        out_shape=jax.ShapeDtypeStruct((depth, 2 * rows), jnp.bfloat16),
        in_specs=[whole(pltpu.SMEM)] + [whole()] * 2,
        out_specs=whole(),
        compiler_params=pltpu.CompilerParams(vmem_limit_bytes=12 * MIB),
        name="join_weights",
    )(place, own_weights, mate_weights)


def gathered(role, refs):
    sides = []
    for side in range(2):
        pieces = []
        for head in range(refs[0][0].shape[0] // 4):
            for maker in range(2):
                k = 2 * side + (maker ^ role)
                pieces.append([refs[k][0][4 * head + (e ^ k)] for e in range(4)])
        for at in range(refs[0][1].shape[0] // 2 if len(refs[0]) > 1 else 0):
            rows = []
            for e in range(4):
                k = 2 * side + e % 2
                rows.append(refs[k][1][2 * at + (e // 2 ^ side)])
            pieces.append(rows)
        sides.append(
            jnp.concatenate([jnp.concatenate(rows, axis=0) for rows in pieces], axis=1)
        )
    return sides


def by_role(refs, parts):
    made, inward, ahead, aside, relay_x, relay_y = [
        refs[at * parts : (at + 1) * parts] for at in range(6)
    ]
    return ((made, inward, ahead, aside), (ahead, aside, relay_x, relay_y))


def input_kernel(parts, place_ref, *refs):
    weights, out_refs, total = refs[6 * parts], refs[6 * parts + 1 : -1], refs[-1]
    length = out_refs[0].shape[0]
    for role, grads in enumerate(by_role(refs, parts)):

        @pl.when(place_ref[CORE] == role)
        def _():
            left = jnp.concatenate(gathered(role, grads), axis=1)
            for e in range(4):
                product = dot(left[e * length : (e + 1) * length], weights[...])
                total[e] = product.astype(total.dtype)

    for s, out_ref in enumerate(out_refs):
        out_ref[...] = total[jnp.bitwise_xor(place_ref[PLANE], s)]


def input_product(place, grads, weights):
    _, length, _ = grads[0].shape
    depth, rows = weights.shape
    out = jax.ShapeDtypeStruct((length, rows), jnp.bfloat16)
    return pl.pallas_call(
        functools.partial(input_kernel, len(grads) // 6),
        out_shape=[out] * 4,
        in_specs=[whole(pltpu.SMEM)] + [whole()] * (len(grads) + 1),
        out_specs=[whole()] * 4,
        scratch_shapes=[pltpu.VMEM((4, length, rows), jnp.bfloat16)],
        compiler_params=pltpu.CompilerParams(vmem_limit_bytes=16 * MIB),
        cost_estimate=pl.CostEstimate(
            flops=8 * length * rows * depth,
            bytes_accessed=8 * length * (rows + depth) + 2 * rows * depth,
            transcendentals=0,
        ),
        name="input_gradient",
    )(place, *grads, weights)


def weight_kernel(mine, mean_scale, parts, place_ref, *refs):
    own, mate_in, first, second, corner, corner_far = refs[:6]
    grad_refs, refs = refs[6 : 6 + 6 * parts], refs[6 + 6 * parts :]
    if mine:
        received, out_refs, turned = refs[:3], refs[3:6], refs[6]
    else:
        received, out_refs, turned = None, refs[:3], refs[3]
    core = place_ref[CORE]
    length = own.shape[1]
    part = core if mine else 1 - core
    tokens = ((own, mate_in, first, second), (first, second, corner, corner_far))
    for role, grads in enumerate(by_role(grad_refs, parts)):

        @pl.when(core == role)
        def _():
            for e, source in enumerate(tokens[role]):
                turned[:, e * length : (e + 1) * length] = source[part].T
            for base, side in zip((HERE, BESIDE), gathered(role, grads)):
                total = dot(turned[...], side)
                for head in range(side.shape[1] // (3 * HD)):
                    here = lanes((place_ref[base] + head) * HD, HD)
                    for kind, out in enumerate(out_refs):
                        at = (head * 3 + kind) * HD
                        value = total[:, at : at + HD]
                        if mine:
                            value = (value + received[kind][:, here]) * mean_scale
                        out[:, here] = value.astype(out.dtype)


def weight_product(place, mine, mean_scale, cols, tokens, grads, received=()):
    _, length, _ = grads[0].shape
    rows = tokens[0].shape[2]
    out = jax.ShapeDtypeStruct((rows, cols), jnp.float32 if mine else jnp.bfloat16)
    return pl.pallas_call(
        functools.partial(weight_kernel, mine, mean_scale, len(grads) // 6),
        out_shape=[out] * 3,
        in_specs=[whole(pltpu.SMEM)] + [whole()] * (6 + len(grads) + len(received)),
        out_specs=[whole()] * 3,
        scratch_shapes=[pltpu.VMEM((rows, 4 * length), jnp.bfloat16)],
        compiler_params=pltpu.CompilerParams(vmem_limit_bytes=16 * MIB),
        cost_estimate=pl.CostEstimate(
            flops=8 * rows * 3 * cols * length,
            bytes_accessed=8 * length * (rows + 3 * cols) + 12 * rows * cols,
            transcendentals=0,
        ),
        name="weight_gradient_own" if mine else "weight_gradient_mate",
    )(place, *tokens, *grads, *received)


def gather_body(
    normed,
    queries,
    saved_keys,
    saved_values,
    output_grad,
    view_links,
    query_weight,
    key_weight,
    value_weight,
):
    length, cols = queries.shape[2:]
    model_width = normed.shape[-1]
    rows = query_weight.shape[0]
    prompts, views, groups = (lax.axis_size(name) for name in ("dp", "view", "head"))
    mean_scale = 1.0 / (prompts * views)
    half = cols // HD // 2
    view = lax.axis_index("view")
    core = lax.rem(view, 2)
    side = view // 2
    chip = lax.axis_index("dp") * (views // 2) + side
    place = jnp.stack([core, lax.axis_index("head"), side * half, (1 - side) * half])
    place = place.astype(jnp.int32)
    arrays = tuple(a.reshape(length, cols) for a in (queries, saved_keys, saved_values, output_grad))

    own_heads, shared = half // 2, half % 2
    each = [2 * step for step in range(own_heads)]
    picks = [
        [(BESIDE, step, 1) for step in each],
        [(BESIDE, step + 1, -1) for step in each],
        [(HERE, step + 1, -1) for step in each],
        [(HERE, step, 1) for step in each],
    ]
    if shared:
        picks += [[(BESIDE, 2 * own_heads, 0)], [(HERE, 2 * own_heads, 0)]]
    packed = pack(picks, place, view_links, arrays)
    to_x, to_cross, to_mate, own = packed[:4]
    x_in = moved(to_x, along_x)
    cross_in = moved(to_cross, across_x)
    mate_in = moved(to_mate, mate)
    sets = [((0, 1, 2, 3), (own, mate_in, x_in, cross_in))]
    if shared:
        to_x, own = packed[4:]
        (to_x,) = after((to_x,), cross_in)
        x_in = moved(to_x, along_x)
        sets.append(((0, 2), (own, moved(own, mate), x_in, moved(x_in, mate))))

    flat = normed.reshape(length, model_width)

    def columns(of_chip):
        columns = [
            lax.dynamic_slice_in_dim(flat, (2 * of_chip + part) * rows, rows, axis=1)
            for part in range(2)
        ]
        return jnp.stack(columns)

    toward_x, toward_y = jnp.bitwise_xor(chip, 1), jnp.bitwise_xor(chip, 2)
    here = columns(chip)
    to_straight = columns(jnp.where(core == 0, toward_x, toward_y))
    to_crossed = columns(jnp.where(core == 0, toward_y, toward_x))
    to_corner = columns(jnp.bitwise_xor(chip, 3))
    mate_here = moved(here, only(1, mate))

    own_weights, turn = None, place
    parts = []
    for kept, sources in sets:
        made = attention(turn, kept, sources)
        if own_weights is None:
            ready = after((query_weight, key_weight, value_weight), sets[0][1][2])
            own_weights = turned_weights(place, ready)
        (turn,) = after((place,), made, own_weights)
        ahead = moved(made, straight)
        aside = moved(made, crossed)
        inward = moved(made, only(1, mate))
        (sent,) = after((ahead,), aside, inward, mate_here, to_straight, to_crossed, to_corner)
        relay_x = moved(sent, only(1, along_x))
        relay_y = moved(sent, only(0, across_y))
        parts.append((made, inward, ahead, aside, relay_x, relay_y))
    grads = [array for kind in zip(*parts) for array in kind]
    weights = joined_weights(place, own_weights, moved(own_weights, mate))

    slots = input_product(place, grads, weights)
    last = groups - 1
    far = lax.ppermute(slots[3], "head", [(0, 1), (last, last - 1)])
    nearest = lax.ppermute(slots[1], "head", [(z, z ^ 1) for z in range(groups)])
    inner = lax.ppermute(slots[3], "head", [(1, last - 1), (last - 1, 1)])
    joint = (slots[2].astype(jnp.float32) + far.astype(jnp.float32)).astype(jnp.bfloat16)
    across = lax.ppermute(joint, "head", [(z, z ^ 2) for z in range(groups)])
    arrived = [nearest, inner, across]
    total = sum(array.astype(jnp.float32) for array in (slots[0], *arrived))
    total = total.astype(jnp.bfloat16)

    to_straight, to_crossed = after((to_straight, to_crossed), *slots)
    normed_ahead = moved(to_straight, straight)
    normed_aside = moved(to_crossed, crossed)
    (to_corner,) = after((to_corner,), normed_ahead, normed_aside)
    tokens = (
        here,
        mate_here,
        normed_ahead,
        normed_aside,
        moved(to_corner, corner_same),
        moved(to_corner, corner_cross),
    )
    (total,) = after((total,), tokens[4], tokens[5])

    def spot(y, v, z):
        return (y * views + v) * groups + z

    corners = [(y, v, z) for y in range(prompts) for v in range(views) for z in range(groups)]
    beside = lax.ppermute(
        total,
        ("dp", "view", "head"),
        [(spot(y, v, z), spot(y ^ (v % 2), v ^ z, z)) for y, v, z in corners],
    )
    (turn,) = after((place,), arrived[0])
    for_mate = weight_product(turn, False, mean_scale, cols, tokens, grads)
    from_mate = [moved(part, mate) for part in for_mate]
    weight_grads = weight_product(place, True, mean_scale, cols, tokens, grads, from_mate)
    input_grad = lax.ppermute(
        beside,
        ("dp", "view", "head"),
        [
            (
                spot(y ^ (v % 2), v ^ z, z),
                spot(y ^ (v % 2), v ^ z, y * (views // 2) + v // 2),
            )
            for y, v, z in corners
        ],
    )

    (input_grad,) = after((input_grad,), *weight_grads)
    return (
        input_grad.reshape(1, 1, length, model_width // groups),
        *weight_grads,
    )


def solution(mesh):
    prompts, views, groups = (mesh.shape[name] for name in ("dp", "view", "head"))
    loop_of_four = prompts * 2 == views and prompts * views == 2 * groups and views == groups

    def choose(*arrays):
        batch, held, length, cols = arrays[1].shape
        if loop_of_four and batch == held == 1 and length % HD == 0 and cols % (2 * HD) == 0:
            return gather_body(*arrays)
        return halo_body(*arrays)

    placed = (
        P("dp", "view", None, None),
        P("dp", "view", None, "head"),
        P("dp", "view", None, "head"),
        P("dp", "view", None, "head"),
        P("dp", "view", None, "head"),
        P("view", None),
        P(("dp", "view"), "head"),
        P(("dp", "view"), "head"),
        P(("dp", "view"), "head"),
    )
    return jax.shard_map(
        choose,
        mesh=mesh,
        in_specs=placed,
        out_specs=(
            P("dp", "view", None, "head"),
            P(("dp", "view"), "head"),
            P(("dp", "view"), "head"),
            P(("dp", "view"), "head"),
        ),
        check_vma=False,
    )
```

```python
import functools

import jax
import jax.numpy as jnp
from jax import lax
from jax.experimental import pallas as pl
from jax.experimental.pallas import tpu as pltpu
from jax.sharding import PartitionSpec as P

HD = 128
LOG2E = 1.4426950408889634
MIB = 1024 * 1024


def shifted(value, axis, steps):
    count = lax.axis_size(axis)
    pairs = [(source, (source + steps) % count) for source in range(count)]
    return lax.ppermute(value, axis, pairs)


def attend(query_rows, grad_rows, blocks, usable, scaling):
    batch_size, length, col_count = query_rows.shape
    heads_here = col_count // HD
    key_heads = blocks[..., :col_count].reshape(batch_size, 3 * length, heads_here, HD)
    value_heads = blocks[..., col_count:].reshape(batch_size, 3 * length, heads_here, HD)
    query_heads = query_rows.reshape(batch_size, length, heads_here, HD)
    grad_heads = grad_rows.reshape(batch_size, length, heads_here, HD)
    scores = (
        jnp.einsum("bshd,bthd->bhst", query_heads, key_heads, preferred_element_type=jnp.float32)
        * scaling
    )
    scores = jnp.where(usable, scores, -1e30)
    largest = jnp.max(scores, axis=-1, keepdims=True)
    powers = jnp.exp(scores - largest)
    attn_probs = powers / jnp.sum(powers, axis=-1, keepdims=True)
    probs_half = attn_probs.astype(jnp.bfloat16)
    prob_grad = jnp.einsum(
        "bshd,bthd->bhst", grad_heads, value_heads, preferred_element_type=jnp.float32
    )
    row_delta = jnp.sum(attn_probs * prob_grad, axis=-1, keepdims=True)
    score_grad = (scaling * attn_probs * (prob_grad - row_delta)).astype(jnp.bfloat16)
    query_grad = jnp.einsum(
        "bhst,bthd->bshd", score_grad, key_heads, preferred_element_type=jnp.float32
    )
    key_grad = jnp.einsum(
        "bhst,bshd->bthd", score_grad, query_heads, preferred_element_type=jnp.float32
    )
    value_grad = jnp.einsum(
        "bhst,bshd->bthd", probs_half, grad_heads, preferred_element_type=jnp.float32
    )
    query_grad = query_grad.reshape(batch_size, length, col_count)
    key_grad = key_grad.reshape(batch_size, 3, length, col_count)
    value_grad = value_grad.reshape(batch_size, 3, length, col_count)
    return (query_grad, jnp.concatenate([key_grad, value_grad], axis=-1))


def halo_body(
    normed,
    queries,
    saved_keys,
    saved_values,
    output_grad,
    view_links,
    query_weight,
    key_weight,
    value_weight,
):
    scaling = HD ** (-0.5)
    batch_size, view_count, length, col_count = queries.shape
    model_width = normed.shape[-1]
    pairs = jnp.concatenate([saved_keys, saved_values], axis=-1)
    from_lower = shifted(pairs, "view", 1)
    from_upper = shifted(pairs, "view", -1)
    extended = jnp.concatenate([from_lower, pairs, from_upper], axis=1)
    block_index = jnp.arange(3 * length) // length
    pair_grads = jnp.zeros(extended.shape, jnp.float32)
    link_flags = view_links[0] >= 0
    usable = jnp.where(
        block_index == 0, link_flags[0], jnp.where(block_index == 2, link_flags[1], True)
    )
    query_grad, block_grad = attend(queries[:, 0], output_grad[:, 0], extended, usable, scaling)
    query_grads = [query_grad]
    pair_grads = pair_grads.at[:, 0:3].add(block_grad)
    row_count = batch_size * view_count * length
    query_half = jnp.stack(query_grads, axis=1).astype(jnp.bfloat16).reshape(row_count, col_count)
    flat_input = normed.reshape(row_count, model_width)
    mean_scale = 1.0 / (lax.axis_size("dp") * batch_size * lax.axis_size("view") * view_count)
    from_lower_grads = shifted(pair_grads[:, -1:], "view", 1)
    from_upper_grads = shifted(pair_grads[:, :1], "view", -1)
    own_grads = pair_grads[:, 1 : view_count + 1]
    own_grads = own_grads.at[:, :1].add(from_lower_grads)
    own_grads = own_grads.at[:, -1:].add(from_upper_grads)
    key_half = own_grads[..., :col_count].astype(jnp.bfloat16).reshape(row_count, col_count)
    value_half = own_grads[..., col_count:].astype(jnp.bfloat16).reshape(row_count, col_count)
    all_grads = jnp.concatenate([query_half, key_half, value_half], axis=-1)
    grads_three = all_grads.reshape(row_count, 3, col_count)
    stacked = jnp.stack([query_weight, key_weight, value_weight])
    partial_input = jnp.einsum(
        "ric,ipc->rp",
        grads_three,
        lax.all_gather(stacked, ("dp", "view"), axis=1, tiled=True),
        preferred_element_type=jnp.float32,
    )
    summed_input = lax.psum_scatter(partial_input, "head", scatter_dimension=1, tiled=True)
    input_grad = summed_input.astype(jnp.bfloat16).reshape(
        batch_size, view_count, length, model_width // lax.axis_size("head")
    )
    product = lax.dot_general(
        flat_input, all_grads, (((0,), (0,)), ((), ())), preferred_element_type=jnp.float32
    )
    together = lax.psum_scatter(
        product * mean_scale, ("dp", "view"), scatter_dimension=0, tiled=True
    )
    grad_query = together[:, :col_count]
    grad_key = together[:, col_count : 2 * col_count]
    grad_value = together[:, 2 * col_count :]
    return (input_grad, grad_query, grad_key, grad_value)


def moved(value, target):
    prompts, views = lax.axis_size("dp"), lax.axis_size("view")
    pairs = []
    for y in range(prompts):
        for v in range(views):
            goal = target(y, v)
            if goal is not None:
                pairs.append((y * views + v, goal[0] * views + goal[1]))
    return lax.ppermute(value, ("dp", "view"), pairs)


def mate(y, v):
    return (y, v ^ 1)


def along_x(y, v):
    return (y, v ^ 2)


def across_x(y, v):
    return (y, v ^ 3)


def only(core, target):
    return lambda y, v: target(y, v) if v % 2 == core else None


def along_y(y, v):
    return (y ^ 1, v)


def across_y(y, v):
    return (y ^ 1, v ^ 1)


def straight(y, v):
    return along_x(y, v) if v % 2 == 0 else along_y(y, v)


def crossed(y, v):
    return across_y(y, v) if v % 2 == 0 else across_x(y, v)


def corner_same(y, v):
    return None if v % 2 == 0 else (y ^ 1, v ^ 2)


def corner_cross(y, v):
    return (y ^ 1, v ^ 3) if v % 2 == 0 else None


def lanes(start, size):
    return pl.ds(pl.multiple_of(start, HD), size)


def whole(space=pltpu.VMEM):
    return pl.BlockSpec(memory_space=space)


def dot_last(a, b):
    return lax.dot_general(a, b, (((1,), (1,)), ((), ())), preferred_element_type=jnp.float32)


def dot_first(a, b):
    return lax.dot_general(a, b, (((0,), (0,)), ((), ())), preferred_element_type=jnp.float32)


def dot(a, b):
    return jnp.dot(a, b, preferred_element_type=jnp.float32)


def after(values, *earlier):
    return lax.optimization_barrier((tuple(values), tuple(earlier)))[0]


CORE, PLANE, HERE, BESIDE = range(4)
FLAG_ROWS = 16


def pack_kernel(picks, place_ref, links_ref, q_ref, k_ref, v_ref, g_ref, *out_refs):
    length = q_ref.shape[0]
    row = lax.broadcasted_iota(jnp.int32, (FLAG_ROWS, HD), 0)
    gaps = [jnp.where(links_ref[0, side] >= 0, 0.0, 1.0).astype(jnp.float32) for side in range(2)]
    flags = jnp.where(row < FLAG_ROWS // 2, gaps[0], gaps[1])
    for heads, out_ref in zip(picks, out_refs):
        for at, (base, step, sign) in enumerate(heads):
            head = place_ref[base] + step + sign * place_ref[CORE]
            for kind, source in enumerate((q_ref, k_ref, v_ref, g_ref)):
                out_ref[at, kind * length : (kind + 1) * length] = source[:, lanes(head * HD, HD)]
            out_ref[at, 4 * length : 4 * length + FLAG_ROWS] = flags.astype(out_ref.dtype)


def pack(picks, place, links, arrays):
    length = arrays[0].shape[0]
    height = 4 * length + FLAG_ROWS
    return pl.pallas_call(
        functools.partial(pack_kernel, picks),
        out_shape=[
            jax.ShapeDtypeStruct((len(heads), height, HD), jnp.bfloat16) for heads in picks
        ],
        in_specs=[whole(pltpu.SMEM)] * 2 + [whole()] * 4,
        out_specs=[whole()] * len(picks),
        name="pack_heads",
    )(place, links, *arrays)


def one_head(scaling, core, xs, length, keys, values, key_sums, value_sums):
    factor = scaling * LOG2E

    def rows(e, kind):
        return xs[e][kind * length : (kind + 1) * length]

    def gap(e, side):
        at = 4 * length + side * (FLAG_ROWS // 2)
        flags = xs[e][at : at + FLAG_ROWS // 2].astype(jnp.float32)[0:1]
        return jnp.concatenate([flags] * (length // HD), axis=1) * 1e30

    for at in range(6):
        keys[at * length : (at + 1) * length] = rows((at + 3) % 4, 1)
        values[at * length : (at + 1) * length] = rows((at + 3) % 4, 2)
    query_grads = []
    for e in range(4):
        blocks = slice(e * length, (e + 3) * length)
        before, behind = gap(e, 0), gap(e, 1)
        far_below = jnp.where(core == 0, before, behind)
        far_above = jnp.where(core == 0, behind, before)
        q, g = rows(e, 0), rows(e, 3)
        near = keys[blocks]
        scores = dot_last(near, q)
        scores = [scores[at * length : (at + 1) * length] for at in range(3)]
        tops = [jnp.max(part, axis=0, keepdims=True) for part in scores]
        top = jnp.maximum(tops[1], jnp.maximum(tops[0] - far_below, tops[2] - far_above))
        offsets = (top + far_below, top, top + far_above)
        powers = [jnp.exp2((part - o) * factor) for part, o in zip(scores, offsets)]
        inverse = 1.0 / sum(jnp.sum(p, axis=0, keepdims=True) for p in powers)
        prob_grads = dot_last(values[blocks], g)
        prob_grads = [prob_grads[at * length : (at + 1) * length] for at in range(3)]
        delta = inverse * sum(
            jnp.sum(p * d, axis=0, keepdims=True) for p, d in zip(powers, prob_grads)
        )
        probs = [p * inverse for p in powers]
        score_grad = jnp.concatenate(
            [
                (p * scaling * (d - delta)).astype(jnp.bfloat16)
                for p, d in zip(probs, prob_grads)
            ],
            axis=0,
        )
        probs_half = jnp.concatenate([p.astype(jnp.bfloat16) for p in probs], axis=0)
        query_grads.append(dot_first(score_grad, near))
        for sums, part in ((key_sums, dot(score_grad, q)), (value_sums, dot(probs_half, g))):
            if e == 0:
                sums[blocks] = part
            else:
                held = slice(e * length, (e + 2) * length)
                sums[held] += part[: 2 * length]
                sums[(e + 2) * length : (e + 3) * length] = part[2 * length :]

    def by_view(sums):
        parts = [sums[at * length : (at + 1) * length] for at in range(6)]
        return (parts[1] + parts[5], parts[2], parts[3], parts[0] + parts[4])

    return query_grads, by_view(key_sums), by_view(value_sums)


def attention_kernel(scaling, kept, place_ref, own, mate_in, x_in, far_in, *refs):
    out_ref, keys, values, key_sums, value_sums = refs
    length = out_ref.shape[1]
    heads = own.shape[0]
    for head in range(heads):
        xs = [own.at[head], mate_in.at[head], x_in.at[head], far_in.at[head]]
        grads = one_head(
            scaling, place_ref[CORE], xs, length, keys, values, key_sums, value_sums
        )
        for at, e in enumerate(kept):
            for kind in range(3):
                out_ref[len(kept) * head + at, :, kind * HD : (kind + 1) * HD] = grads[kind][
                    e
                ].astype(out_ref.dtype)


def attention(place, kept, sources):
    heads, height, _ = sources[0].shape
    length = (height - FLAG_ROWS) // 4
    return pl.pallas_call(
        functools.partial(attention_kernel, HD ** (-0.5), kept),
        out_shape=jax.ShapeDtypeStruct((len(kept) * heads, length, 3 * HD), jnp.bfloat16),
        in_specs=[whole(pltpu.SMEM)] + [whole()] * 4,
        out_specs=whole(),
        scratch_shapes=[pltpu.VMEM((6 * length, HD), jnp.bfloat16)] * 2
        + [pltpu.VMEM((6 * length, HD), jnp.float32)] * 2,
        compiler_params=pltpu.CompilerParams(vmem_limit_bytes=12 * MIB),
        cost_estimate=pl.CostEstimate(
            flops=heads * 4 * 5 * 2 * length * 3 * length * HD * 2,
            bytes_accessed=heads * 2 * length * 7 * HD * 4,
            transcendentals=heads * 12 * length * length,
        ),
        name="attention_gradients",
    )(place, *sources)


def turn_kernel(place_ref, q_ref, k_ref, v_ref, out_ref):
    half = q_ref.shape[1] // HD // 2
    for side, base in enumerate((HERE, BESIDE)):
        for head in range(half):
            for kind, source in enumerate((q_ref, k_ref, v_ref)):
                at = ((side * half + head) * 3 + kind) * HD
                out_ref[at : at + HD] = source[:, lanes((place_ref[base] + head) * HD, HD)].T


def turned_weights(place, weights):
    rows, cols = weights[0].shape
    return pl.pallas_call(
        turn_kernel,
        out_shape=jax.ShapeDtypeStruct((3 * cols, rows), jnp.bfloat16),
        in_specs=[whole(pltpu.SMEM)] + [whole()] * 3,
        out_specs=whole(),
        compiler_params=pltpu.CompilerParams(vmem_limit_bytes=8 * MIB),
        name="turn_weights",
    )(place, *weights)


def join_kernel(place_ref, own_ref, mate_ref, out_ref):
    core = place_ref[CORE]
    rows = own_ref.shape[1]
    out_ref[:, lanes(core * rows, rows)] = own_ref[...]
    out_ref[:, lanes((1 - core) * rows, rows)] = mate_ref[...]


def joined_weights(place, own_weights, mate_weights):
    depth, rows = own_weights.shape
    return pl.pallas_call(
        join_kernel,
        out_shape=jax.ShapeDtypeStruct((depth, 2 * rows), jnp.bfloat16),
        in_specs=[whole(pltpu.SMEM)] + [whole()] * 2,
        out_specs=whole(),
        compiler_params=pltpu.CompilerParams(vmem_limit_bytes=12 * MIB),
        name="join_weights",
    )(place, own_weights, mate_weights)


def gathered(role, refs):
    sides = []
    for side in range(2):
        pieces = []
        for head in range(refs[0][0].shape[0] // 4):
            for maker in range(2):
                k = 2 * side + (maker ^ role)
                pieces.append([refs[k][0][4 * head + (e ^ k)] for e in range(4)])
        for at in range(refs[0][1].shape[0] // 2 if len(refs[0]) > 1 else 0):
            rows = []
            for e in range(4):
                k = 2 * side + e % 2
                rows.append(refs[k][1][2 * at + (e // 2 ^ side)])
            pieces.append(rows)
        sides.append(
            jnp.concatenate([jnp.concatenate(rows, axis=0) for rows in pieces], axis=1)
        )
    return sides


def by_role(refs, parts):
    made, inward, ahead, aside, relay_x, relay_y = [
        refs[at * parts : (at + 1) * parts] for at in range(6)
    ]
    return ((made, inward, ahead, aside), (ahead, aside, relay_x, relay_y))


def input_kernel(parts, place_ref, *refs):
    weights, out_refs, total = refs[6 * parts], refs[6 * parts + 1 : -1], refs[-1]
    length = out_refs[0].shape[0]
    for role, grads in enumerate(by_role(refs, parts)):

        @pl.when(place_ref[CORE] == role)
        def _():
            left = jnp.concatenate(gathered(role, grads), axis=1)
            for e in range(4):
                product = dot(left[e * length : (e + 1) * length], weights[...])
                total[e] = product.astype(total.dtype)

    for s, out_ref in enumerate(out_refs):
        out_ref[...] = total[jnp.bitwise_xor(place_ref[PLANE], s)]


def input_product(place, grads, weights):
    _, length, _ = grads[0].shape
    depth, rows = weights.shape
    out = jax.ShapeDtypeStruct((length, rows), jnp.bfloat16)
    return pl.pallas_call(
        functools.partial(input_kernel, len(grads) // 6),
        out_shape=[out] * 4,
        in_specs=[whole(pltpu.SMEM)] + [whole()] * (len(grads) + 1),
        out_specs=[whole()] * 4,
        scratch_shapes=[pltpu.VMEM((4, length, rows), jnp.bfloat16)],
        compiler_params=pltpu.CompilerParams(vmem_limit_bytes=16 * MIB),
        cost_estimate=pl.CostEstimate(
            flops=8 * length * rows * depth,
            bytes_accessed=8 * length * (rows + depth) + 2 * rows * depth,
            transcendentals=0,
        ),
        name="input_gradient",
    )(place, *grads, weights)


def weight_kernel(mine, mean_scale, parts, place_ref, *refs):
    own, mate_in, first, second, corner, corner_far = refs[:6]
    grad_refs, refs = refs[6 : 6 + 6 * parts], refs[6 + 6 * parts :]
    if mine:
        received, out_refs, turned = refs[:3], refs[3:6], refs[6]
    else:
        received, out_refs, turned = None, refs[:3], refs[3]
    core = place_ref[CORE]
    length = own.shape[1]
    part = core if mine else 1 - core
    tokens = ((own, mate_in, first, second), (first, second, corner, corner_far))
    for role, grads in enumerate(by_role(grad_refs, parts)):

        @pl.when(core == role)
        def _():
            for e, source in enumerate(tokens[role]):
                turned[:, e * length : (e + 1) * length] = source[part].T
            for base, side in zip((HERE, BESIDE), gathered(role, grads)):
                total = dot(turned[...], side)
                for head in range(side.shape[1] // (3 * HD)):
                    here = lanes((place_ref[base] + head) * HD, HD)
                    for kind, out in enumerate(out_refs):
                        at = (head * 3 + kind) * HD
                        value = total[:, at : at + HD]
                        if mine:
                            value = (value + received[kind][:, here]) * mean_scale
                        out[:, here] = value.astype(out.dtype)


def weight_product(place, mine, mean_scale, cols, tokens, grads, received=()):
    _, length, _ = grads[0].shape
    rows = tokens[0].shape[2]
    out = jax.ShapeDtypeStruct((rows, cols), jnp.float32 if mine else jnp.bfloat16)
    return pl.pallas_call(
        functools.partial(weight_kernel, mine, mean_scale, len(grads) // 6),
        out_shape=[out] * 3,
        in_specs=[whole(pltpu.SMEM)] + [whole()] * (6 + len(grads) + len(received)),
        out_specs=[whole()] * 3,
        scratch_shapes=[pltpu.VMEM((rows, 4 * length), jnp.bfloat16)],
        compiler_params=pltpu.CompilerParams(vmem_limit_bytes=16 * MIB),
        cost_estimate=pl.CostEstimate(
            flops=8 * rows * 3 * cols * length,
            bytes_accessed=8 * length * (rows + 3 * cols) + 12 * rows * cols,
            transcendentals=0,
        ),
        name="weight_gradient_own" if mine else "weight_gradient_mate",
    )(place, *tokens, *grads, *received)


def gather_body(
    normed,
    queries,
    saved_keys,
    saved_values,
    output_grad,
    view_links,
    query_weight,
    key_weight,
    value_weight,
):
    length, cols = queries.shape[2:]
    model_width = normed.shape[-1]
    rows = query_weight.shape[0]
    prompts, views, groups = (lax.axis_size(name) for name in ("dp", "view", "head"))
    mean_scale = 1.0 / (prompts * views)
    half = cols // HD // 2
    view = lax.axis_index("view")
    core = lax.rem(view, 2)
    side = view // 2
    chip = lax.axis_index("dp") * (views // 2) + side
    place = jnp.stack([core, lax.axis_index("head"), side * half, (1 - side) * half])
    place = place.astype(jnp.int32)
    arrays = tuple(a.reshape(length, cols) for a in (queries, saved_keys, saved_values, output_grad))

    own_heads, shared = half // 2, half % 2
    each = [2 * step for step in range(own_heads)]
    picks = [
        [(BESIDE, step, 1) for step in each],
        [(BESIDE, step + 1, -1) for step in each],
        [(HERE, step + 1, -1) for step in each],
        [(HERE, step, 1) for step in each],
    ]
    if shared:
        picks += [[(BESIDE, 2 * own_heads, 0)], [(HERE, 2 * own_heads, 0)]]
    packed = pack(picks, place, view_links, arrays)
    to_x, to_cross, to_mate, own = packed[:4]
    x_in = moved(to_x, along_x)
    cross_in = moved(to_cross, across_x)
    mate_in = moved(to_mate, mate)
    sets = [((0, 1, 2, 3), (own, mate_in, x_in, cross_in))]
    if shared:
        to_x, own = packed[4:]
        (to_x,) = after((to_x,), x_in)
        x_in = moved(to_x, along_x)
        sets.append(((0, 2), (own, moved(own, mate), x_in, moved(x_in, mate))))

    flat = normed.reshape(length, model_width)

    def columns(of_chip):
        columns = [
            lax.dynamic_slice_in_dim(flat, (2 * of_chip + part) * rows, rows, axis=1)
            for part in range(2)
        ]
        return jnp.stack(columns)

    toward_x, toward_y = jnp.bitwise_xor(chip, 1), jnp.bitwise_xor(chip, 2)
    here = columns(chip)
    to_straight = columns(jnp.where(core == 0, toward_x, toward_y))
    to_crossed = columns(jnp.where(core == 0, toward_y, toward_x))
    to_corner = columns(jnp.bitwise_xor(chip, 3))
    own_weights, turn = None, place
    parts = []
    for kept, sources in sets:
        made = attention(turn, kept, sources)
        if own_weights is None:
            ready = after((query_weight, key_weight, value_weight), made)
            own_weights = turned_weights(place, ready)
        (turn,) = after((place,), made, own_weights)
        ahead = moved(made, straight)
        aside = moved(made, crossed)
        inward = moved(made, only(1, mate))
        (sent,) = after((ahead,), aside, inward, here, to_straight, to_crossed, to_corner)
        relay_x = moved(sent, only(1, along_x))
        relay_y = moved(sent, only(0, across_y))
        parts.append((made, inward, ahead, aside, relay_x, relay_y))
    grads = [array for kind in zip(*parts) for array in kind]
    weights = joined_weights(place, own_weights, moved(own_weights, mate))

    slots = input_product(place, grads, weights)
    last = groups - 1
    far = lax.ppermute(slots[3], "head", [(0, 1), (last, last - 1)])
    nearest = lax.ppermute(slots[1], "head", [(z, z ^ 1) for z in range(groups)])
    inner = lax.ppermute(slots[3], "head", [(1, last - 1), (last - 1, 1)])
    joint = (slots[2].astype(jnp.float32) + far.astype(jnp.float32)).astype(jnp.bfloat16)
    across = lax.ppermute(joint, "head", [(z, z ^ 2) for z in range(groups)])
    arrived = [nearest, inner, across]
    total = sum(array.astype(jnp.float32) for array in (slots[0], *arrived))
    total = total.astype(jnp.bfloat16)

    to_straight, to_crossed = after((to_straight, to_crossed), *slots)
    normed_ahead = moved(to_straight, straight)
    normed_aside = moved(to_crossed, crossed)
    to_corner, sent = after((to_corner, here), normed_ahead, normed_aside)
    mate_here = moved(sent, only(1, mate))
    tokens = (
        here,
        mate_here,
        normed_ahead,
        normed_aside,
        moved(to_corner, corner_same),
        moved(to_corner, corner_cross),
    )
    (total,) = after((total,), *tokens)

    def spot(y, v, z):
        return (y * views + v) * groups + z

    corners = [(y, v, z) for y in range(prompts) for v in range(views) for z in range(groups)]
    beside = lax.ppermute(
        total,
        ("dp", "view", "head"),
        [(spot(y, v, z), spot(y ^ (v % 2), v ^ z, z)) for y, v, z in corners],
    )
    (turn,) = after((place,), arrived[0])
    for_mate = weight_product(turn, False, mean_scale, cols, tokens, grads)
    from_mate = [moved(part, mate) for part in for_mate]
    weight_grads = weight_product(place, True, mean_scale, cols, tokens, grads, from_mate)
    input_grad = lax.ppermute(
        beside,
        ("dp", "view", "head"),
        [
            (
                spot(y ^ (v % 2), v ^ z, z),
                spot(y ^ (v % 2), v ^ z, y * (views // 2) + v // 2),
            )
            for y, v, z in corners
        ],
    )

    (input_grad,) = after((input_grad,), *weight_grads)
    return (
        input_grad.reshape(1, 1, length, model_width // groups),
        *weight_grads,
    )


def solution(mesh):
    prompts, views, groups = (mesh.shape[name] for name in ("dp", "view", "head"))
    loop_of_four = prompts * 2 == views and prompts * views == 2 * groups and views == groups

    def choose(*arrays):
        batch, held, length, cols = arrays[1].shape
        if loop_of_four and batch == held == 1 and length % HD == 0 and cols % (2 * HD) == 0:
            return gather_body(*arrays)
        return halo_body(*arrays)

    placed = (
        P("dp", "view", None, None),
        P("dp", "view", None, "head"),
        P("dp", "view", None, "head"),
        P("dp", "view", None, "head"),
        P("dp", "view", None, "head"),
        P("view", None),
        P(("dp", "view"), "head"),
        P(("dp", "view"), "head"),
        P(("dp", "view"), "head"),
    )
    return jax.shard_map(
        choose,
        mesh=mesh,
        in_specs=placed,
        out_specs=(
            P("dp", "view", None, "head"),
            P(("dp", "view"), "head"),
            P(("dp", "view"), "head"),
            P(("dp", "view"), "head"),
        ),
        check_vma=False,
    )
```

```python
import functools

import jax
import jax.numpy as jnp
from jax import lax
from jax.experimental import pallas as pl
from jax.experimental.pallas import tpu as pltpu
from jax.sharding import PartitionSpec as P

HD = 128
LOG2E = 1.4426950408889634
MIB = 1024 * 1024


def shifted(value, axis, steps):
    count = lax.axis_size(axis)
    pairs = [(source, (source + steps) % count) for source in range(count)]
    return lax.ppermute(value, axis, pairs)


def attend(query_rows, grad_rows, blocks, usable, scaling):
    batch_size, length, col_count = query_rows.shape
    heads_here = col_count // HD
    key_heads = blocks[..., :col_count].reshape(batch_size, 3 * length, heads_here, HD)
    value_heads = blocks[..., col_count:].reshape(batch_size, 3 * length, heads_here, HD)
    query_heads = query_rows.reshape(batch_size, length, heads_here, HD)
    grad_heads = grad_rows.reshape(batch_size, length, heads_here, HD)
    scores = (
        jnp.einsum("bshd,bthd->bhst", query_heads, key_heads, preferred_element_type=jnp.float32)
        * scaling
    )
    scores = jnp.where(usable, scores, -1e30)
    largest = jnp.max(scores, axis=-1, keepdims=True)
    powers = jnp.exp(scores - largest)
    attn_probs = powers / jnp.sum(powers, axis=-1, keepdims=True)
    probs_half = attn_probs.astype(jnp.bfloat16)
    prob_grad = jnp.einsum(
        "bshd,bthd->bhst", grad_heads, value_heads, preferred_element_type=jnp.float32
    )
    row_delta = jnp.sum(attn_probs * prob_grad, axis=-1, keepdims=True)
    score_grad = (scaling * attn_probs * (prob_grad - row_delta)).astype(jnp.bfloat16)
    query_grad = jnp.einsum(
        "bhst,bthd->bshd", score_grad, key_heads, preferred_element_type=jnp.float32
    )
    key_grad = jnp.einsum(
        "bhst,bshd->bthd", score_grad, query_heads, preferred_element_type=jnp.float32
    )
    value_grad = jnp.einsum(
        "bhst,bshd->bthd", probs_half, grad_heads, preferred_element_type=jnp.float32
    )
    query_grad = query_grad.reshape(batch_size, length, col_count)
    key_grad = key_grad.reshape(batch_size, 3, length, col_count)
    value_grad = value_grad.reshape(batch_size, 3, length, col_count)
    return (query_grad, jnp.concatenate([key_grad, value_grad], axis=-1))


def halo_body(
    normed,
    queries,
    saved_keys,
    saved_values,
    output_grad,
    view_links,
    query_weight,
    key_weight,
    value_weight,
):
    scaling = HD ** (-0.5)
    batch_size, view_count, length, col_count = queries.shape
    model_width = normed.shape[-1]
    pairs = jnp.concatenate([saved_keys, saved_values], axis=-1)
    from_lower = shifted(pairs, "view", 1)
    from_upper = shifted(pairs, "view", -1)
    extended = jnp.concatenate([from_lower, pairs, from_upper], axis=1)
    block_index = jnp.arange(3 * length) // length
    pair_grads = jnp.zeros(extended.shape, jnp.float32)
    link_flags = view_links[0] >= 0
    usable = jnp.where(
        block_index == 0, link_flags[0], jnp.where(block_index == 2, link_flags[1], True)
    )
    query_grad, block_grad = attend(queries[:, 0], output_grad[:, 0], extended, usable, scaling)
    query_grads = [query_grad]
    pair_grads = pair_grads.at[:, 0:3].add(block_grad)
    row_count = batch_size * view_count * length
    query_half = jnp.stack(query_grads, axis=1).astype(jnp.bfloat16).reshape(row_count, col_count)
    flat_input = normed.reshape(row_count, model_width)
    mean_scale = 1.0 / (lax.axis_size("dp") * batch_size * lax.axis_size("view") * view_count)
    from_lower_grads = shifted(pair_grads[:, -1:], "view", 1)
    from_upper_grads = shifted(pair_grads[:, :1], "view", -1)
    own_grads = pair_grads[:, 1 : view_count + 1]
    own_grads = own_grads.at[:, :1].add(from_lower_grads)
    own_grads = own_grads.at[:, -1:].add(from_upper_grads)
    key_half = own_grads[..., :col_count].astype(jnp.bfloat16).reshape(row_count, col_count)
    value_half = own_grads[..., col_count:].astype(jnp.bfloat16).reshape(row_count, col_count)
    all_grads = jnp.concatenate([query_half, key_half, value_half], axis=-1)
    grads_three = all_grads.reshape(row_count, 3, col_count)
    stacked = jnp.stack([query_weight, key_weight, value_weight])
    partial_input = jnp.einsum(
        "ric,ipc->rp",
        grads_three,
        lax.all_gather(stacked, ("dp", "view"), axis=1, tiled=True),
        preferred_element_type=jnp.float32,
    )
    summed_input = lax.psum_scatter(partial_input, "head", scatter_dimension=1, tiled=True)
    input_grad = summed_input.astype(jnp.bfloat16).reshape(
        batch_size, view_count, length, model_width // lax.axis_size("head")
    )
    product = lax.dot_general(
        flat_input, all_grads, (((0,), (0,)), ((), ())), preferred_element_type=jnp.float32
    )
    together = lax.psum_scatter(
        product * mean_scale, ("dp", "view"), scatter_dimension=0, tiled=True
    )
    grad_query = together[:, :col_count]
    grad_key = together[:, col_count : 2 * col_count]
    grad_value = together[:, 2 * col_count :]
    return (input_grad, grad_query, grad_key, grad_value)


def moved(value, target):
    prompts, views = lax.axis_size("dp"), lax.axis_size("view")
    pairs = []
    for y in range(prompts):
        for v in range(views):
            goal = target(y, v)
            if goal is not None:
                pairs.append((y * views + v, goal[0] * views + goal[1]))
    return lax.ppermute(value, ("dp", "view"), pairs)


def mate(y, v):
    return (y, v ^ 1)


def along_x(y, v):
    return (y, v ^ 2)


def across_x(y, v):
    return (y, v ^ 3)


def only(core, target):
    return lambda y, v: target(y, v) if v % 2 == core else None


def along_y(y, v):
    return (y ^ 1, v)


def across_y(y, v):
    return (y ^ 1, v ^ 1)


def straight(y, v):
    return along_x(y, v) if v % 2 == 0 else along_y(y, v)


def crossed(y, v):
    return across_y(y, v) if v % 2 == 0 else across_x(y, v)


def corner_same(y, v):
    return None if v % 2 == 0 else (y ^ 1, v ^ 2)


def corner_cross(y, v):
    return (y ^ 1, v ^ 3) if v % 2 == 0 else None


def lanes(start, size):
    return pl.ds(pl.multiple_of(start, HD), size)


def whole(space=pltpu.VMEM):
    return pl.BlockSpec(memory_space=space)


def dot_last(a, b):
    return lax.dot_general(a, b, (((1,), (1,)), ((), ())), preferred_element_type=jnp.float32)


def dot_first(a, b):
    return lax.dot_general(a, b, (((0,), (0,)), ((), ())), preferred_element_type=jnp.float32)


def dot(a, b):
    return jnp.dot(a, b, preferred_element_type=jnp.float32)


def after(values, *earlier):
    return lax.optimization_barrier((tuple(values), tuple(earlier)))[0]


CORE, PLANE, HERE, BESIDE = range(4)
FLAG_ROWS = 16


def pack_kernel(picks, place_ref, links_ref, q_ref, k_ref, v_ref, g_ref, *out_refs):
    length = q_ref.shape[0]
    row = lax.broadcasted_iota(jnp.int32, (FLAG_ROWS, HD), 0)
    gaps = [jnp.where(links_ref[0, side] >= 0, 0.0, 1.0).astype(jnp.float32) for side in range(2)]
    flags = jnp.where(row < FLAG_ROWS // 2, gaps[0], gaps[1])
    for heads, out_ref in zip(picks, out_refs):
        for at, (base, step, sign) in enumerate(heads):
            head = place_ref[base] + step + sign * place_ref[CORE]
            for kind, source in enumerate((q_ref, k_ref, v_ref, g_ref)):
                out_ref[at, kind * length : (kind + 1) * length] = source[:, lanes(head * HD, HD)]
            out_ref[at, 4 * length : 4 * length + FLAG_ROWS] = flags.astype(out_ref.dtype)


def pack(picks, place, links, arrays):
    length = arrays[0].shape[0]
    height = 4 * length + FLAG_ROWS
    return pl.pallas_call(
        functools.partial(pack_kernel, picks),
        out_shape=[
            jax.ShapeDtypeStruct((len(heads), height, HD), jnp.bfloat16) for heads in picks
        ],
        in_specs=[whole(pltpu.SMEM)] * 2 + [whole()] * 4,
        out_specs=[whole()] * len(picks),
        name="pack_heads",
    )(place, links, *arrays)


def one_head(scaling, core, xs, length, keys, values, key_sums, value_sums):
    factor = scaling * LOG2E

    def rows(e, kind):
        return xs[e][kind * length : (kind + 1) * length]

    def gap(e, side):
        at = 4 * length + side * (FLAG_ROWS // 2)
        flags = xs[e][at : at + FLAG_ROWS // 2].astype(jnp.float32)[0:1]
        return jnp.concatenate([flags] * (length // HD), axis=1) * 1e30

    for at in range(6):
        keys[at * length : (at + 1) * length] = rows((at + 3) % 4, 1)
        values[at * length : (at + 1) * length] = rows((at + 3) % 4, 2)
    query_grads = []
    for e in range(4):
        blocks = slice(e * length, (e + 3) * length)
        before, behind = gap(e, 0), gap(e, 1)
        far_below = jnp.where(core == 0, before, behind)
        far_above = jnp.where(core == 0, behind, before)
        q, g = rows(e, 0), rows(e, 3)
        near = keys[blocks]
        scores = dot_last(near, q)
        scores = [scores[at * length : (at + 1) * length] for at in range(3)]
        tops = [jnp.max(part, axis=0, keepdims=True) for part in scores]
        top = jnp.maximum(tops[1], jnp.maximum(tops[0] - far_below, tops[2] - far_above))
        offsets = (top + far_below, top, top + far_above)
        powers = [jnp.exp2((part - o) * factor) for part, o in zip(scores, offsets)]
        inverse = 1.0 / sum(jnp.sum(p, axis=0, keepdims=True) for p in powers)
        prob_grads = dot_last(values[blocks], g)
        prob_grads = [prob_grads[at * length : (at + 1) * length] for at in range(3)]
        delta = inverse * sum(
            jnp.sum(p * d, axis=0, keepdims=True) for p, d in zip(powers, prob_grads)
        )
        probs = [p * inverse for p in powers]
        score_grad = jnp.concatenate(
            [
                (p * scaling * (d - delta)).astype(jnp.bfloat16)
                for p, d in zip(probs, prob_grads)
            ],
            axis=0,
        )
        probs_half = jnp.concatenate([p.astype(jnp.bfloat16) for p in probs], axis=0)
        query_grads.append(dot_first(score_grad, near))
        for sums, part in ((key_sums, dot(score_grad, q)), (value_sums, dot(probs_half, g))):
            if e == 0:
                sums[blocks] = part
            else:
                held = slice(e * length, (e + 2) * length)
                sums[held] += part[: 2 * length]
                sums[(e + 2) * length : (e + 3) * length] = part[2 * length :]

    def by_view(sums):
        parts = [sums[at * length : (at + 1) * length] for at in range(6)]
        return (parts[1] + parts[5], parts[2], parts[3], parts[0] + parts[4])

    return query_grads, by_view(key_sums), by_view(value_sums)


def attention_kernel(scaling, kept, place_ref, own, mate_in, x_in, far_in, *refs):
    out_ref, keys, values, key_sums, value_sums = refs
    length = out_ref.shape[1]
    heads = own.shape[0]
    for head in range(heads):
        xs = [own.at[head], mate_in.at[head], x_in.at[head], far_in.at[head]]
        grads = one_head(
            scaling, place_ref[CORE], xs, length, keys, values, key_sums, value_sums
        )
        for at, e in enumerate(kept):
            for kind in range(3):
                out_ref[len(kept) * head + at, :, kind * HD : (kind + 1) * HD] = grads[kind][
                    e
                ].astype(out_ref.dtype)


def attention(place, kept, sources):
    heads, height, _ = sources[0].shape
    length = (height - FLAG_ROWS) // 4
    return pl.pallas_call(
        functools.partial(attention_kernel, HD ** (-0.5), kept),
        out_shape=jax.ShapeDtypeStruct((len(kept) * heads, length, 3 * HD), jnp.bfloat16),
        in_specs=[whole(pltpu.SMEM)] + [whole()] * 4,
        out_specs=whole(),
        scratch_shapes=[pltpu.VMEM((6 * length, HD), jnp.bfloat16)] * 2
        + [pltpu.VMEM((6 * length, HD), jnp.float32)] * 2,
        compiler_params=pltpu.CompilerParams(vmem_limit_bytes=8 * MIB),
        cost_estimate=pl.CostEstimate(
            flops=heads * 4 * 5 * 2 * length * 3 * length * HD * 2,
            bytes_accessed=heads * 2 * length * 7 * HD * 4,
            transcendentals=heads * 12 * length * length,
        ),
        name="attention_gradients",
    )(place, *sources)


def turn_kernel(place_ref, q_ref, k_ref, v_ref, out_ref):
    half = q_ref.shape[1] // HD // 2
    for side, base in enumerate((HERE, BESIDE)):
        for head in range(half):
            for kind, source in enumerate((q_ref, k_ref, v_ref)):
                at = ((side * half + head) * 3 + kind) * HD
                out_ref[at : at + HD] = source[:, lanes((place_ref[base] + head) * HD, HD)].T


def turned_weights(place, weights):
    rows, cols = weights[0].shape
    return pl.pallas_call(
        turn_kernel,
        out_shape=jax.ShapeDtypeStruct((3 * cols, rows), jnp.bfloat16),
        in_specs=[whole(pltpu.SMEM)] + [whole()] * 3,
        out_specs=whole(),
        compiler_params=pltpu.CompilerParams(vmem_limit_bytes=8 * MIB),
        name="turn_weights",
    )(place, *weights)


def join_kernel(place_ref, own_ref, mate_ref, out_ref):
    core = place_ref[CORE]
    rows = own_ref.shape[1]
    out_ref[:, lanes(core * rows, rows)] = own_ref[...]
    out_ref[:, lanes((1 - core) * rows, rows)] = mate_ref[...]


def joined_weights(place, own_weights, mate_weights):
    depth, rows = own_weights.shape
    return pl.pallas_call(
        join_kernel,
        out_shape=jax.ShapeDtypeStruct((depth, 2 * rows), jnp.bfloat16),
        in_specs=[whole(pltpu.SMEM)] + [whole()] * 2,
        out_specs=whole(),
        compiler_params=pltpu.CompilerParams(vmem_limit_bytes=12 * MIB),
        name="join_weights",
    )(place, own_weights, mate_weights)


def gathered(role, refs):
    sides = []
    for side in range(2):
        pieces = []
        for head in range(refs[0][0].shape[0] // 4):
            for maker in range(2):
                k = 2 * side + (maker ^ role)
                pieces.append([refs[k][0][4 * head + (e ^ k)] for e in range(4)])
        for at in range(refs[0][1].shape[0] // 2 if len(refs[0]) > 1 else 0):
            rows = []
            for e in range(4):
                k = 2 * side + e % 2
                rows.append(refs[k][1][2 * at + (e // 2 ^ side)])
            pieces.append(rows)
        sides.append(
            jnp.concatenate([jnp.concatenate(rows, axis=0) for rows in pieces], axis=1)
        )
    return sides


def by_role(refs, parts):
    made, inward, ahead, aside, relay_x, relay_y = [
        refs[at * parts : (at + 1) * parts] for at in range(6)
    ]
    return ((made, inward, ahead, aside), (ahead, aside, relay_x, relay_y))


def input_kernel(parts, place_ref, *refs):
    weights, out_refs, total = refs[6 * parts], refs[6 * parts + 1 : -1], refs[-1]
    length = out_refs[0].shape[0]
    for role, grads in enumerate(by_role(refs, parts)):

        @pl.when(place_ref[CORE] == role)
        def _():
            left = jnp.concatenate(gathered(role, grads), axis=1)
            for e in range(4):
                product = dot(left[e * length : (e + 1) * length], weights[...])
                total[e] = product.astype(total.dtype)

    for s, out_ref in enumerate(out_refs):
        out_ref[...] = total[jnp.bitwise_xor(place_ref[PLANE], s)]


def input_product(place, grads, weights):
    _, length, _ = grads[0].shape
    depth, rows = weights.shape
    out = jax.ShapeDtypeStruct((length, rows), jnp.bfloat16)
    return pl.pallas_call(
        functools.partial(input_kernel, len(grads) // 6),
        out_shape=[out] * 4,
        in_specs=[whole(pltpu.SMEM)] + [whole()] * (len(grads) + 1),
        out_specs=[whole()] * 4,
        scratch_shapes=[pltpu.VMEM((4, length, rows), jnp.bfloat16)],
        compiler_params=pltpu.CompilerParams(vmem_limit_bytes=12 * MIB),
        cost_estimate=pl.CostEstimate(
            flops=8 * length * rows * depth,
            bytes_accessed=8 * length * (rows + depth) + 2 * rows * depth,
            transcendentals=0,
        ),
        name="input_gradient",
    )(place, *grads, weights)


def weight_kernel(mine, mean_scale, parts, place_ref, *refs):
    own, mate_in, first, second, corner, corner_far = refs[:6]
    grad_refs, refs = refs[6 : 6 + 6 * parts], refs[6 + 6 * parts :]
    if mine:
        received, out_refs, turned = refs[:3], refs[3:6], refs[6]
    else:
        received, out_refs, turned = None, refs[:3], refs[3]
    core = place_ref[CORE]
    length = own.shape[1]
    part = core if mine else 1 - core
    tokens = ((own, mate_in, first, second), (first, second, corner, corner_far))
    for role, grads in enumerate(by_role(grad_refs, parts)):

        @pl.when(core == role)
        def _():
            for e, source in enumerate(tokens[role]):
                turned[:, e * length : (e + 1) * length] = source[part].T
            for base, side in zip((HERE, BESIDE), gathered(role, grads)):
                total = dot(turned[...], side)
                for head in range(side.shape[1] // (3 * HD)):
                    here = lanes((place_ref[base] + head) * HD, HD)
                    for kind, out in enumerate(out_refs):
                        at = (head * 3 + kind) * HD
                        value = total[:, at : at + HD]
                        if mine:
                            value = (value + received[kind][:, here]) * mean_scale
                        out[:, here] = value.astype(out.dtype)


def weight_product(place, mine, mean_scale, cols, tokens, grads, received=()):
    _, length, _ = grads[0].shape
    rows = tokens[0].shape[2]
    out = jax.ShapeDtypeStruct((rows, cols), jnp.float32 if mine else jnp.bfloat16)
    return pl.pallas_call(
        functools.partial(weight_kernel, mine, mean_scale, len(grads) // 6),
        out_shape=[out] * 3,
        in_specs=[whole(pltpu.SMEM)] + [whole()] * (6 + len(grads) + len(received)),
        out_specs=[whole()] * 3,
        scratch_shapes=[pltpu.VMEM((rows, 4 * length), jnp.bfloat16)],
        compiler_params=pltpu.CompilerParams(vmem_limit_bytes=12 * MIB),
        cost_estimate=pl.CostEstimate(
            flops=8 * rows * 3 * cols * length,
            bytes_accessed=8 * length * (rows + 3 * cols) + 12 * rows * cols,
            transcendentals=0,
        ),
        name="weight_gradient_own" if mine else "weight_gradient_mate",
    )(place, *tokens, *grads, *received)


def gather_body(
    normed,
    queries,
    saved_keys,
    saved_values,
    output_grad,
    view_links,
    query_weight,
    key_weight,
    value_weight,
):
    length, cols = queries.shape[2:]
    model_width = normed.shape[-1]
    rows = query_weight.shape[0]
    prompts, views, groups = (lax.axis_size(name) for name in ("dp", "view", "head"))
    mean_scale = 1.0 / (prompts * views)
    half = cols // HD // 2
    view = lax.axis_index("view")
    core = lax.rem(view, 2)
    side = view // 2
    chip = lax.axis_index("dp") * (views // 2) + side
    place = jnp.stack([core, lax.axis_index("head"), side * half, (1 - side) * half])
    place = place.astype(jnp.int32)
    arrays = tuple(a.reshape(length, cols) for a in (queries, saved_keys, saved_values, output_grad))

    own_heads, shared = half // 2, half % 2
    each = [2 * step for step in range(own_heads)]
    picks = [
        [(BESIDE, step, 1) for step in each],
        [(BESIDE, step + 1, -1) for step in each],
        [(HERE, step + 1, -1) for step in each],
        [(HERE, step, 1) for step in each],
    ]
    if shared:
        picks += [[(BESIDE, 2 * own_heads, 0)], [(HERE, 2 * own_heads, 0)]]
    packed = pack(picks, place, view_links, arrays)
    to_x, to_cross, to_mate, own = packed[:4]
    x_in = moved(to_x, along_x)
    cross_in = moved(to_cross, across_x)
    mate_in = moved(to_mate, mate)
    sets = [((0, 1, 2, 3), (own, mate_in, x_in, cross_in))]
    if shared:
        to_x, own = packed[4:]
        (to_x,) = after((to_x,), x_in)
        x_in = moved(to_x, along_x)
        sets.append(((0, 2), (own, moved(own, mate), x_in, moved(x_in, mate))))

    flat = normed.reshape(length, model_width)

    def columns(of_chip):
        columns = [
            lax.dynamic_slice_in_dim(flat, (2 * of_chip + part) * rows, rows, axis=1)
            for part in range(2)
        ]
        return jnp.stack(columns)

    toward_x, toward_y = jnp.bitwise_xor(chip, 1), jnp.bitwise_xor(chip, 2)
    here = columns(chip)
    to_straight = columns(jnp.where(core == 0, toward_x, toward_y))
    to_crossed = columns(jnp.where(core == 0, toward_y, toward_x))
    to_corner = columns(jnp.bitwise_xor(chip, 3))
    own_weights, turn = None, place
    parts = []
    for kept, sources in sets:
        made = attention(turn, kept, sources)
        if own_weights is None:
            ready = after((query_weight, key_weight, value_weight), made)
            own_weights = turned_weights(place, ready)
        (turn,) = after((place,), made, own_weights)
        ahead = moved(made, straight)
        aside = moved(made, crossed)
        inward = moved(made, only(1, mate))
        (sent,) = after((ahead,), aside, inward, here, to_straight, to_crossed, to_corner)
        relay_x = moved(sent, only(1, along_x))
        relay_y = moved(sent, only(0, across_y))
        parts.append((made, inward, ahead, aside, relay_x, relay_y))
    grads = [array for kind in zip(*parts) for array in kind]
    weights = joined_weights(place, own_weights, moved(own_weights, mate))

    slots = input_product(place, grads, weights)
    last = groups - 1
    far = lax.ppermute(slots[3], "head", [(0, 1), (last, last - 1)])
    nearest = lax.ppermute(slots[1], "head", [(z, z ^ 1) for z in range(groups)])
    inner = lax.ppermute(slots[3], "head", [(1, last - 1), (last - 1, 1)])
    joint = (slots[2].astype(jnp.float32) + far.astype(jnp.float32)).astype(jnp.bfloat16)
    across = lax.ppermute(joint, "head", [(z, z ^ 2) for z in range(groups)])
    arrived = [nearest, inner, across]
    total = sum(array.astype(jnp.float32) for array in (slots[0], *arrived))
    total = total.astype(jnp.bfloat16)

    to_straight, to_crossed = after((to_straight, to_crossed), *slots)
    normed_ahead = moved(to_straight, straight)
    normed_aside = moved(to_crossed, crossed)
    to_corner, sent = after((to_corner, here), normed_ahead, normed_aside)
    mate_here = moved(sent, only(1, mate))
    tokens = (
        here,
        mate_here,
        normed_ahead,
        normed_aside,
        moved(to_corner, corner_same),
        moved(to_corner, corner_cross),
    )
    (total,) = after((total,), *tokens)

    def spot(y, v, z):
        return (y * views + v) * groups + z

    corners = [(y, v, z) for y in range(prompts) for v in range(views) for z in range(groups)]
    beside = lax.ppermute(
        total,
        ("dp", "view", "head"),
        [(spot(y, v, z), spot(y ^ (v % 2), v ^ z, z)) for y, v, z in corners],
    )
    (turn,) = after((place,), arrived[0])
    for_mate = weight_product(turn, False, mean_scale, cols, tokens, grads)
    from_mate = [moved(part, mate) for part in for_mate]
    weight_grads = weight_product(place, True, mean_scale, cols, tokens, grads, from_mate)
    input_grad = lax.ppermute(
        beside,
        ("dp", "view", "head"),
        [
            (
                spot(y ^ (v % 2), v ^ z, z),
                spot(y ^ (v % 2), v ^ z, y * (views // 2) + v // 2),
            )
            for y, v, z in corners
        ],
    )

    (input_grad,) = after((input_grad,), *weight_grads)
    return (
        input_grad.reshape(1, 1, length, model_width // groups),
        *weight_grads,
    )


def solution(mesh):
    prompts, views, groups = (mesh.shape[name] for name in ("dp", "view", "head"))
    loop_of_four = prompts * 2 == views and prompts * views == 2 * groups and views == groups

    def choose(*arrays):
        batch, held, length, cols = arrays[1].shape
        if loop_of_four and batch == held == 1 and length % HD == 0 and cols % (2 * HD) == 0:
            return gather_body(*arrays)
        return halo_body(*arrays)

    placed = (
        P("dp", "view", None, None),
        P("dp", "view", None, "head"),
        P("dp", "view", None, "head"),
        P("dp", "view", None, "head"),
        P("dp", "view", None, "head"),
        P("view", None),
        P(("dp", "view"), "head"),
        P(("dp", "view"), "head"),
        P(("dp", "view"), "head"),
    )
    return jax.shard_map(
        choose,
        mesh=mesh,
        in_specs=placed,
        out_specs=(
            P("dp", "view", None, "head"),
            P(("dp", "view"), "head"),
            P(("dp", "view"), "head"),
            P(("dp", "view"), "head"),
        ),
        check_vma=False,
    )
```
